32 devices in a mesh: dp: 2 (over y), row: 4 (over x, core), col: 4 (over z).
Axes of the slice: x: 2, y: 2, z: 4, core: 2. Of those that a mesh axis runs over, the one named last changes fastest.
Arguments:
- first_homolog_features: bfloat16 [64, 6144], P(('dp', 'col'), 'row'), parts along dimension 0, may hold values from -18 to 18
- second_homolog_features: bfloat16 [64, 6144], P(('dp', 'row'), 'col'), parts along dimension 0, may hold values from -18 to 18
- final_projection_matrix: bfloat16 [1024, 128], replicated, may hold values from -0.1875 to 0.1875
- output_bias: float32 [128], replicated, may hold values from -3 to 3
- cotangent: bfloat16 [384, 192, 128], P(('dp', 'row'), 'col'), parts along dimension 0, may hold values from -6 to 6
Outputs:
- pair_map: bfloat16 [384, 192, 128], P(('dp', 'row'), 'col'), parts along dimension 0
- first_homolog_cotangent: float32 [64, 6144], P(('dp', 'col'), 'row'), parts along dimension 0
- right_grad: float32 [64, 6144], P(('dp', 'row'), 'col'), parts along dimension 0
- projection_cotangent: float32 [2048, 128], P('dp'), parts along dimension 0
- bias_grad: float32 [256], P('dp'), parts along dimension 0
The draws below stay inside these ranges and needn't reach their ends.
There are 2 independent parts, one for each index of `dp`. The reference program is written for one: setup_inputs(seed, part) draws one part's arguments, and reference() takes and returns one part's arrays. A program takes and returns all parts, laid end to end along the dimension named above; an argument that names none is the same for every part. Nothing has to cross between parts.
All inputs are finite; a program needn't handle non-finite values.
Results may differ from the reference program's by a relative error of at most 0.0048.
Values may be sent and summed in bfloat16 or wider, within the bound.
No kernel may reach another device: no remote copies, remote signals or barrier semaphores. Data moves between devices by JAX's collectives and lax.ppermute only.
A program may use at most 128 MiB of HBM per device.

```python
import jax
import jax.numpy as jnp
from jax import lax

PROJECTED_DEPTH = 32
PAIR_FEATURES = 128
PATCH_POSITIONS = 48
WINDOW_POSITIONS = 192
HOMOLOG_NUMBER = 32


def shard_levels(rng, extent, cuts, low, top_value):
    def one(position, parts):
        heights = jax.random.uniform(jax.random.fold_in(jax.random.fold_in(rng, 6), position), (parts,), jnp.float32, low / len(cuts), top_value / len(cuts))
        return jnp.repeat(jnp.exp(heights), extent[position] // parts).reshape((-1,) + (1,) * (len(extent) - position - 1))

    factor_of = one(*cuts[0])
    for cut in cuts[1:]:
        factor_of = factor_of * one(*cut)
    return factor_of


def normal_values(rng, extent, deviation, most, pieces=(), kind=jnp.bfloat16):
    drawn = jax.random.normal(rng, extent, jnp.float32) * deviation
    if len(pieces) > 0:
        drawn = shard_levels(rng, extent, pieces, -0.22, 0.18) * drawn
    return jnp.clip(drawn, min=-most, max=most).astype(kind)


def setup_inputs(seed: int = 0, part: int = 0) -> dict:
    key_of = jax.random.split(jax.random.key(seed), 6)
    own_keys = jax.random.split(jax.random.fold_in(key_of[5], part), 6)
    first_homolog_features = normal_values(own_keys[0], (HOMOLOG_NUMBER, WINDOW_POSITIONS * PROJECTED_DEPTH), 3.0, 18.0, ((0, 4), (1, 4)))
    second_homolog_features = normal_values(own_keys[1], (HOMOLOG_NUMBER, WINDOW_POSITIONS * PROJECTED_DEPTH), 3.0, 18.0, ((0, 4), (1, 4)))
    final_projection_matrix = normal_values(key_of[2], (PROJECTED_DEPTH * PROJECTED_DEPTH, PAIR_FEATURES), (PROJECTED_DEPTH * PROJECTED_DEPTH) ** -0.5, 0.1875)
    output_bias = normal_values(key_of[3], (PAIR_FEATURES,), 0.5, 3.0, (), jnp.float32)
    cotangent = normal_values(own_keys[4], (WINDOW_POSITIONS, WINDOW_POSITIONS, PAIR_FEATURES), 1.0, 6.0, ((0, 4), (1, 4)))
    return dict(first_homolog_features=first_homolog_features, second_homolog_features=second_homolog_features, final_projection_matrix=final_projection_matrix, output_bias=output_bias, cotangent=cotangent)


def reference(first_homolog_features, second_homolog_features, final_projection_matrix, output_bias, cotangent):
    projection_cuboid = final_projection_matrix.astype(jnp.float32).reshape(PROJECTED_DEPTH, PROJECTED_DEPTH, PAIR_FEATURES)
    block_count = WINDOW_POSITIONS // PATCH_POSITIONS

    def block_step(totals, portion_number):
        second_accumulator, projection_accumulator, bias_total = totals
        patch_displacement = (portion_number * PATCH_POSITIONS * PROJECTED_DEPTH).astype(jnp.int32)
        first_patch_portion = lax.dynamic_slice_in_dim(first_homolog_features, patch_displacement, PATCH_POSITIONS * PROJECTED_DEPTH, 1)
        kronecker_array = (jnp.dot(first_patch_portion.T, second_homolog_features, preferred_element_type=jnp.float32) / HOMOLOG_NUMBER).astype(jnp.bfloat16)
        kronecker_pieces = kronecker_array.astype(jnp.float32).reshape(PATCH_POSITIONS, PROJECTED_DEPTH, WINDOW_POSITIONS, PROJECTED_DEPTH)
        pair_block = (jnp.einsum('icje,cef->ijf', kronecker_pieces, projection_cuboid) + output_bias).astype(jnp.bfloat16)
        row_offset = (portion_number * PATCH_POSITIONS).astype(jnp.int32)
        cot_block = lax.dynamic_slice_in_dim(cotangent, row_offset, PATCH_POSITIONS, 0).astype(jnp.float32)
        kronecker_cotangent = jnp.einsum('ijf,cef->icje', cot_block, projection_cuboid).astype(jnp.bfloat16)
        kronecker_cotangent = kronecker_cotangent.reshape(PATCH_POSITIONS * PROJECTED_DEPTH, WINDOW_POSITIONS * PROJECTED_DEPTH)
        first_patch_cotangent = jnp.dot(second_homolog_features, kronecker_cotangent.T, preferred_element_type=jnp.float32) / HOMOLOG_NUMBER
        second_accumulator = second_accumulator + jnp.dot(first_patch_portion, kronecker_cotangent, preferred_element_type=jnp.float32) / HOMOLOG_NUMBER
        projection_accumulator = projection_accumulator + jnp.einsum('icje,ijf->cef', kronecker_pieces, cot_block)
        bias_total = bias_total + jnp.sum(cot_block, axis=(0, 1))
        return (second_accumulator, projection_accumulator, bias_total), (pair_block, first_patch_cotangent)

    initial_accumulators = (jnp.zeros((HOMOLOG_NUMBER, WINDOW_POSITIONS * PROJECTED_DEPTH), jnp.float32), jnp.zeros((PROJECTED_DEPTH, PROJECTED_DEPTH, PAIR_FEATURES), jnp.float32), jnp.zeros((PAIR_FEATURES,), jnp.float32))
    totals, stacked = lax.scan(block_step, initial_accumulators, jnp.arange(block_count, dtype=jnp.int32))
    right_grad, projection_accumulator, bias_total = totals
    pair_blocks, first_portions = stacked
    pair_map = pair_blocks.reshape(WINDOW_POSITIONS, WINDOW_POSITIONS, PAIR_FEATURES)
    first_homolog_cotangent = jnp.transpose(first_portions, (1, 0, 2)).reshape(HOMOLOG_NUMBER, WINDOW_POSITIONS * PROJECTED_DEPTH)
    projection_cotangent = projection_accumulator.reshape(PROJECTED_DEPTH * PROJECTED_DEPTH, PAIR_FEATURES) / WINDOW_POSITIONS
    bias_grad = bias_total / WINDOW_POSITIONS
    return pair_map, first_homolog_cotangent, right_grad, projection_cotangent, bias_grad
```

```python
import functools

import jax
import jax.numpy as jnp
from jax import lax
from jax.experimental import pallas as pl
from jax.experimental.pallas import tpu as pltpu
from jax.sharding import PartitionSpec as P

PROJECTED_DEPTH = 32
PAIR_FEATURES = 128
GROUP = 8
STEPS = 4
BIAS_ROWS = 16
LANES = 128
F32 = jnp.float32
BF16 = jnp.bfloat16
VMEM_BYTES = 60 * 1024 * 1024

ROWS_BY_ROWS = (((1,), (1,)), ((), ()))
COLS_BY_COLS = (((0,), (0,)), ((), ()))


def params():
    return pltpu.CompilerParams(vmem_limit_bytes=VMEM_BYTES)


def whole(shape):
    return pl.BlockSpec(shape, lambda t: (0,) * len(shape))


def dot(x, y, dims=(((1,), (0,)), ((), ()))):
    return lax.dot_general(x, y, dims, preferred_element_type=F32)


def prepare_kernel(i_n, j_n, w_ref, g_ref, y_ref, y2_ref, wt_ref, bias_ref, g32, gt, w32, we):
    depth = PROJECTED_DEPTH
    t = pl.program_id(0)

    @pl.when(t == 0)
    def _():
        g32[...] = g_ref[...].astype(F32)
        total = jnp.sum(g32[...], axis=0, keepdims=True)
        high = total.astype(BF16).astype(F32)
        row = lax.broadcasted_iota(jnp.int32, (BIAS_ROWS, PAIR_FEATURES), 0)
        bias_ref[...] = jnp.where(
            row == 0, high, jnp.where(row == 1, total - high, 0.0)
        ).astype(BF16)
        for j in range(j_n):
            gt[j * i_n : (j + 1) * i_n, :] = g32[pl.ds(j, i_n, stride=j_n), :].astype(BF16)
        w32[...] = w_ref[...].astype(F32)
        for e in range(depth):
            block = w32[pl.ds(e, depth, stride=depth), :]
            we[e * depth : (e + 1) * depth, :] = block.astype(BF16)
        wt_ref[...] = we[...].astype(F32).T.astype(BF16)

    size = y_ref.shape[0]
    rows = pl.ds(pl.multiple_of(t * size, size), size)
    y_ref[...] = dot(we[rows, :], g_ref[...], ROWS_BY_ROWS).astype(BF16)
    y2_ref[...] = dot(w_ref[rows, :], gt[...], ROWS_BY_ROWS).astype(BF16)


def prepare(w, g, i_n, j_n):
    pairs = i_n * j_n
    channels = w.shape[0]
    size = channels // STEPS
    return pl.pallas_call(
        functools.partial(prepare_kernel, i_n, j_n),
        grid=(STEPS,),
        in_specs=[whole(w.shape), whole(g.shape)],
        out_specs=[
            pl.BlockSpec((size, pairs), lambda t: (t, 0)),
            pl.BlockSpec((size, pairs), lambda t: (t, 0)),
            whole((PAIR_FEATURES, channels)),
            whole((BIAS_ROWS, PAIR_FEATURES)),
        ],
        out_shape=[
            jax.ShapeDtypeStruct((channels, pairs), BF16),
            jax.ShapeDtypeStruct((channels, pairs), BF16),
            jax.ShapeDtypeStruct((PAIR_FEATURES, channels), BF16),
            jax.ShapeDtypeStruct((BIAS_ROWS, PAIR_FEATURES), BF16),
        ],
        scratch_shapes=[
            pltpu.VMEM(g.shape, F32),
            pltpu.VMEM(g.shape, BF16),
            pltpu.VMEM(w.shape, F32),
            pltpu.VMEM(w.shape, BF16),
        ],
        compiler_params=params(),
        cost_estimate=pl.CostEstimate(
            flops=4 * pairs * channels * PAIR_FEATURES,
            bytes_accessed=4 * pairs * channels,
            transcendentals=0,
        ),
    )(w, g)


def join(pieces, axis, held):
    count = len(pieces)
    depth = pieces[0].shape[0]
    me = lax.axis_index(axis)
    for p, piece in enumerate(pieces):
        start = pl.multiple_of(lax.rem(me - p + count, count) * depth, depth)
        held[pl.ds(start, depth), :] = piece[...].astype(F32)


def repeat_matrix(sequences):
    shape = (sequences, GROUP * sequences)
    lane = lax.broadcasted_iota(jnp.int32, shape, 1)
    row = lax.broadcasted_iota(jnp.int32, shape, 0)
    return (lax.rem(lane, sequences) == row).astype(BF16)


def spread(held, wide):
    both = dot(held[...].T.astype(BF16), repeat_matrix(held.shape[0]))
    for l in range(wide.shape[0]):
        wide[l] = both[:, l * LANES : (l + 1) * LANES]


def tiles_of(sequences, tile):
    lane = lax.broadcasted_iota(jnp.int32, (1, LANES), 1) + tile * LANES
    return [
        (m, lax.div(lane, sequences) == m)
        for m in range(GROUP)
        if m * sequences < (tile + 1) * LANES and (m + 1) * sequences > tile * LANES
    ]


def fill_diagonal(wide, diagonal, slot, channel, positions, sequences):
    for l in range(wide.shape[0]):
        block = wide[l, pl.ds(channel, positions, stride=PROJECTED_DEPTH), :]
        for m, mask in tiles_of(sequences, l):
            diagonal[slot, m * positions : (m + 1) * positions, l * LANES : (l + 1) * LANES] = (
                jnp.where(mask, block, 0.0).astype(BF16)
            )


def outer_kernel(i_n, j_n, row_n, col_n, *refs):
    depth = PROJECTED_DEPTH
    a_pieces, refs = refs[:col_n], refs[col_n:]
    b_pieces, refs = refs[:row_n], refs[row_n:]
    (g_ref, bias_ref), refs = refs[:2], refs[2:]
    x_ref, refs = refs[0], refs[1:]
    messages, refs = refs[:row_n], refs[row_n:]
    a_held, b_held, wide, left, diagonal, total, ordered = refs
    sequences = a_held.shape[0]
    groups = i_n // GROUP
    per_step = depth // STEPS
    span = GROUP * j_n
    t = pl.program_id(0)

    @pl.when(t == 0)
    def _():
        join(a_pieces, "col", a_held)
        join(b_pieces, "row", b_held)
        spread(a_held, wide)
        for l in range(wide.shape[0]):
            members = tiles_of(sequences, l)
            for k in range(groups):
                block = jnp.zeros((depth, LANES), F32)
                for m, mask in members:
                    start = (k * GROUP + m) * depth
                    block = jnp.where(mask, wide[l, start : start + depth, :], block)
                left[k * depth : (k + 1) * depth, l * LANES : (l + 1) * LANES] = block.astype(BF16)
        spread(b_held, wide)
        diagonal[...] = jnp.zeros(diagonal.shape, BF16)

    for e in range(per_step):
        fill_diagonal(wide, diagonal, e, t * per_step + e, j_n, sequences)
    for e in range(0, per_step, 2):
        right = diagonal[e : e + 2].reshape(2 * span, diagonal.shape[2])
        product = dot(left[...], right, ROWS_BY_ROWS).astype(BF16)
        for n in range(2):
            for k in range(groups):
                x_ref[(e + n) * depth : (e + n + 1) * depth, k * span : (k + 1) * span] = product[
                    k * depth : (k + 1) * depth, n * span : (n + 1) * span
                ]
    size = x_ref.shape[0]
    total[pl.ds(pl.multiple_of(t * size, size), size), :] = dot(x_ref[...], g_ref[...])

    @pl.when(t == STEPS - 1)
    def _():
        for c in range(depth):
            ordered[c * depth : (c + 1) * depth, :] = total[pl.ds(c, depth, stride=depth), :]
        share = ordered.shape[0] // row_n
        me = lax.axis_index("row")
        for p, message in enumerate(messages):
            start = pl.multiple_of(lax.rem(me + p, row_n) * share, share)
            message[0:share, :] = ordered[pl.ds(start, share), :].astype(message.dtype)
            message[share:, :] = bias_ref[...].astype(message.dtype)


def outer(a_pieces, b_pieces, g, bias_rows, i_n, j_n, sequences):
    row_n, col_n = len(b_pieces), len(a_pieces)
    depth = PROJECTED_DEPTH
    channels = depth * depth
    pairs = i_n * j_n
    share = channels // row_n
    tiles = GROUP * sequences // LANES
    operands = [*a_pieces, *b_pieces, g, bias_rows]
    results = pl.pallas_call(
        functools.partial(outer_kernel, i_n, j_n, row_n, col_n),
        grid=(STEPS,),
        in_specs=[whole(x.shape) for x in operands],
        out_specs=[pl.BlockSpec((channels // STEPS, pairs), lambda t: (t, 0))]
        + [whole((share + BIAS_ROWS, PAIR_FEATURES))] * row_n,
        out_shape=[jax.ShapeDtypeStruct((channels, pairs), BF16)]
        + [
            jax.ShapeDtypeStruct((share + BIAS_ROWS, PAIR_FEATURES), F32 if p == 0 else BF16)
            for p in range(row_n)
        ],
        scratch_shapes=[
            pltpu.VMEM((sequences, i_n * depth), F32),
            pltpu.VMEM((sequences, j_n * depth), F32),
            pltpu.VMEM((tiles, i_n * depth, LANES), F32),
            pltpu.VMEM((i_n // GROUP * depth, GROUP * sequences), BF16),
            pltpu.VMEM((depth // STEPS, GROUP * j_n, GROUP * sequences), BF16),
            pltpu.VMEM((channels, PAIR_FEATURES), F32),
            pltpu.VMEM((channels, PAIR_FEATURES), F32),
        ],
        compiler_params=params(),
        cost_estimate=pl.CostEstimate(
            flops=4 * pairs * channels * PAIR_FEATURES,
            bytes_accessed=2 * pairs * channels,
            transcendentals=0,
        ),
    )(*operands)
    return results[0], results[1:]


def gradient_kernel(i_n, j_n, row_n, col_n, *refs):
    depth = PROJECTED_DEPTH
    a_pieces, refs = refs[:col_n], refs[col_n:]
    b_pieces, refs = refs[:row_n], refs[row_n:]
    (y_ref, y2_ref), refs = refs[:2], refs[2:]
    left_out, refs = refs[:col_n], refs[col_n:]
    right_out, refs = refs[:row_n], refs[row_n:]
    a_held, b_held, a_wide, b_wide, a_diagonal, b_diagonal, left, right, grown = refs
    sequences = a_held.shape[0]
    per_step = depth // STEPS
    t = pl.program_id(0)

    @pl.when(t == 0)
    def _():
        join(a_pieces, "col", a_held)
        join(b_pieces, "row", b_held)
        spread(a_held, a_wide)
        spread(b_held, b_wide)
        for ref in (a_diagonal, b_diagonal):
            ref[...] = jnp.zeros(ref.shape, BF16)
        for ref in (left, right):
            ref[...] = jnp.zeros(ref.shape, F32)

    def accumulate(source, wide, diagonal, result, positions, others):
        span = GROUP * positions
        for n in range(per_step):
            fill_diagonal(wide, diagonal, n, t * per_step + n, positions, sequences)
        for n in range(0, per_step, 2):
            rows = [
                jnp.concatenate(
                    [
                        source[m * depth : (m + 1) * depth, k * span : (k + 1) * span]
                        for m in (n, n + 1)
                    ],
                    axis=1,
                )
                for k in range(others // GROUP)
            ]
            result[...] += dot(
                jnp.concatenate(rows, axis=0),
                diagonal[n : n + 2].reshape(2 * span, diagonal.shape[2]),
            )

    accumulate(y_ref, b_wide, b_diagonal, left, j_n, i_n)
    accumulate(y2_ref, a_wide, a_diagonal, right, i_n, j_n)

    def deliver(result, held, outs, axis, positions):
        scaled = (result[...] * (1.0 / sequences)).astype(BF16)
        for l in range(scaled.shape[1] // LANES):
            members = dict(tiles_of(sequences, l))
            for k in range(positions // GROUP):
                block = scaled[k * depth : (k + 1) * depth, l * LANES : (l + 1) * LANES]
                for m in range(GROUP):
                    start = (k * GROUP + m) * depth
                    grown[start : start + depth, l * LANES : (l + 1) * LANES] = (
                        jnp.where(members[m], block.astype(F32), 0.0).astype(BF16)
                        if m in members
                        else jnp.zeros((depth, LANES), BF16)
                    )
        held[...] = dot(repeat_matrix(sequences), grown[...], ROWS_BY_ROWS)
        count = len(outs)
        share = sequences // count
        me = lax.axis_index(axis)
        for p, out in enumerate(outs):
            start = pl.multiple_of(lax.rem(me + p, count) * share, share)
            out[...] = held[pl.ds(start, share), :].astype(out.dtype)

    @pl.when(t == STEPS - 1)
    def _():
        deliver(left, a_held, left_out, "col", i_n)
        deliver(right, b_held, right_out, "row", j_n)


def gradients(a_pieces, b_pieces, y, y2, i_n, j_n, sequences):
    row_n, col_n = len(b_pieces), len(a_pieces)
    depth = PROJECTED_DEPTH
    channels, pairs = y.shape
    tiles = GROUP * sequences // LANES
    size = channels // STEPS
    pieces = [*a_pieces, *b_pieces]
    block = pl.BlockSpec((size, pairs), lambda t: (t, 0))

    def part(p, axis_n, positions):
        return jax.ShapeDtypeStruct((sequences // axis_n, positions * depth), F32 if p == 0 else BF16)

    shapes = [part(p, col_n, i_n) for p in range(col_n)] + [part(p, row_n, j_n) for p in range(row_n)]
    results = pl.pallas_call(
        functools.partial(gradient_kernel, i_n, j_n, row_n, col_n),
        grid=(STEPS,),
        in_specs=[whole(x.shape) for x in pieces] + [block, block],
        out_specs=[whole(x.shape) for x in shapes],
        out_shape=shapes,
        scratch_shapes=[
            pltpu.VMEM((sequences, i_n * depth), F32),
            pltpu.VMEM((sequences, j_n * depth), F32),
            pltpu.VMEM((tiles, i_n * depth, LANES), F32),
            pltpu.VMEM((tiles, j_n * depth, LANES), F32),
            pltpu.VMEM((depth // STEPS, GROUP * i_n, GROUP * sequences), BF16),
            pltpu.VMEM((depth // STEPS, GROUP * j_n, GROUP * sequences), BF16),
            pltpu.VMEM((i_n // GROUP * depth, GROUP * sequences), F32),
            pltpu.VMEM((j_n // GROUP * depth, GROUP * sequences), F32),
            pltpu.VMEM((i_n * depth, GROUP * sequences), BF16),
        ],
        compiler_params=params(),
        cost_estimate=pl.CostEstimate(
            flops=4 * pairs * channels * PAIR_FEATURES,
            bytes_accessed=4 * pairs * channels,
            transcendentals=0,
        ),
    )(*pieces, y, y2)
    return results[:col_n], results[col_n:]


def pair_kernel(sequences, x_ref, wt_ref, bias_ref, out_ref):
    product = dot(wt_ref[...], x_ref[...])
    out_ref[...] = (product.T * (1.0 / sequences) + bias_ref[...]).astype(BF16)


def pair(x, wt, output_bias, sequences):
    channels, pairs = x.shape
    count = 3
    size = pairs // count
    return pl.pallas_call(
        functools.partial(pair_kernel, sequences),
        grid=(count,),
        in_specs=[
            pl.BlockSpec((channels, size), lambda t: (0, t)),
            whole(wt.shape),
            whole((1, PAIR_FEATURES)),
        ],
        out_specs=pl.BlockSpec((size, PAIR_FEATURES), lambda t: (t, 0)),
        out_shape=jax.ShapeDtypeStruct((pairs, PAIR_FEATURES), BF16),
        compiler_params=params(),
        cost_estimate=pl.CostEstimate(
            flops=4 * pairs * channels * PAIR_FEATURES,
            bytes_accessed=2 * pairs * channels,
            transcendentals=0,
        ),
    )(x, wt, output_bias.reshape(1, PAIR_FEATURES))


def column_sum_kernel(res_total, *refs):
    pieces, (piece_out, bias_out, held) = refs[:-3], refs[-3:]
    count = len(pieces)
    me = lax.axis_index("col")
    for p, piece in enumerate(pieces):
        held[lax.rem(me - p + count, count)] = piece[...]
    total = held[0].astype(F32)
    for n in range(1, count):
        total += held[n].astype(F32)
    share = piece_out.shape[0]
    piece_out[...] = total[0:share].astype(BF16)
    bias_out[...] = (total[share : share + 1] + total[share + 1 : share + 2]) * (1.0 / res_total)


def column_sum(pieces, res_total):
    rows = pieces[0].shape[0]
    return pl.pallas_call(
        functools.partial(column_sum_kernel, res_total),
        out_shape=[
            jax.ShapeDtypeStruct((rows - BIAS_ROWS, PAIR_FEATURES), BF16),
            jax.ShapeDtypeStruct((1, PAIR_FEATURES), F32),
        ],
        scratch_shapes=[pltpu.VMEM((len(pieces), rows, PAIR_FEATURES), BF16)],
        compiler_params=params(),
    )(*pieces)


def place_kernel(scale, *refs):
    pieces, out_ref = refs[:-1], refs[-1]
    count = len(pieces)
    me = lax.axis_index("row")
    for p, piece in enumerate(pieces):
        share = piece.shape[0]
        start = pl.multiple_of(lax.rem(me - p + count, count) * share, share)
        out_ref[pl.ds(start, share), :] = piece[...].astype(F32) * scale


def place(pieces, scale):
    rows = pieces[0].shape[0] * len(pieces)
    return pl.pallas_call(
        functools.partial(place_kernel, scale),
        out_shape=jax.ShapeDtypeStruct((rows, PAIR_FEATURES), F32),
        compiler_params=params(),
    )(*pieces)


def shift(x, axis, distance):
    count = lax.axis_size(axis)
    return lax.ppermute(x, axis, [(n, (n + distance) % count) for n in range(count)])


def broadcast(x, axis):
    return [x] + [shift(x, axis, d) for d in range(1, lax.axis_size(axis))]


def exchange(parts, axis):
    return [parts[0]] + [shift(parts[d], axis, d) for d in range(1, len(parts))]


def total_of(parts):
    total = parts[0].astype(F32)
    for part in parts[1:]:
        total = total + part.astype(F32)
    return total


def local(
    first_homolog_features, second_homolog_features, final_projection_matrix, output_bias, cotangent
):
    i_n, j_n, _ = cotangent.shape
    sequences = second_homolog_features.shape[0] * lax.axis_size("row")
    res_total = i_n * lax.axis_size("row")
    g = cotangent.reshape(i_n * j_n, PAIR_FEATURES)
    a_pieces = broadcast(first_homolog_features, "col")
    b_pieces = broadcast(second_homolog_features, "row")
    y, y2, wt, bias_rows = prepare(final_projection_matrix, g, i_n, j_n)

    x, messages = outer(a_pieces, b_pieces, g, bias_rows, i_n, j_n, sequences)
    row_parts = exchange(messages, "row")

    left_parts, right_parts = gradients(a_pieces, b_pieces, y, y2, i_n, j_n, sequences)
    left_grad = total_of(exchange(left_parts, "col"))
    right_grad = total_of(exchange(right_parts, "row"))

    share = total_of(row_parts).astype(BF16)
    share, bias_grad = column_sum(broadcast(share, "col"), res_total)
    pair_map = pair(x, wt, output_bias, sequences)
    projection = place(broadcast(share, "row"), 1.0 / (sequences * res_total))
    return (
        pair_map.reshape(i_n, j_n, PAIR_FEATURES),
        left_grad,
        right_grad,
        projection,
        bias_grad.reshape(PAIR_FEATURES),
    )


def solution(mesh):
    return jax.shard_map(
        local,
        mesh=mesh,
        in_specs=(
            P(("dp", "col"), "row"),
            P(("dp", "row"), "col"),
            P(),
            P(),
            P(("dp", "row"), "col", None),
        ),
        out_specs=(
            P(("dp", "row"), "col", None),
            P(("dp", "col"), "row"),
            P(("dp", "row"), "col"),
            P("dp", None),
            P("dp"),
        ),
        check_vma=False,
    )
```

```python
import functools

import jax
import jax.numpy as jnp
from jax import lax
from jax.experimental import pallas as pl
from jax.experimental.pallas import tpu as pltpu
from jax.sharding import PartitionSpec as P

PROJECTED_DEPTH = 32
PAIR_FEATURES = 128
GROUP = 8
STEPS = 4
BIAS_ROWS = 16
LANES = 128
F32 = jnp.float32
BF16 = jnp.bfloat16
MIB = 1024 * 1024

ROWS_BY_ROWS = (((1,), (1,)), ((), ()))
COLS_BY_COLS = (((0,), (0,)), ((), ()))


def params(sequences=0):
    return pltpu.CompilerParams(vmem_limit_bytes=min(10 + 10 * sequences // 32, 50) * MIB + 2 * MIB)


def whole(shape):
    return pl.BlockSpec(shape, lambda t: (0,) * len(shape))


def dot(x, y, dims=(((1,), (0,)), ((), ()))):
    return lax.dot_general(x, y, dims, preferred_element_type=F32)


def prepare_kernel(i_n, j_n, w_ref, g_ref, y_ref, y2_ref, wt_ref, bias_ref, g32, gt, w32, we):
    depth = PROJECTED_DEPTH
    t = pl.program_id(0)

    @pl.when(t == 0)
    def _():
        g32[...] = g_ref[...].astype(F32)
        total = jnp.sum(g32[...], axis=0, keepdims=True)
        high = total.astype(BF16).astype(F32)
        row = lax.broadcasted_iota(jnp.int32, (BIAS_ROWS, PAIR_FEATURES), 0)
        bias_ref[...] = jnp.where(
            row == 0, high, jnp.where(row == 1, total - high, 0.0)
        ).astype(BF16)
        for j in range(j_n):
            gt[j * i_n : (j + 1) * i_n, :] = g32[pl.ds(j, i_n, stride=j_n), :].astype(BF16)
        w32[...] = w_ref[...].astype(F32)
        for e in range(depth):
            block = w32[pl.ds(e, depth, stride=depth), :]
            we[e * depth : (e + 1) * depth, :] = block.astype(BF16)
        wt_ref[...] = we[...].astype(F32).T.astype(BF16)

    size = y_ref.shape[0]
    rows = pl.ds(pl.multiple_of(t * size, size), size)
    y_ref[...] = dot(we[rows, :], g_ref[...], ROWS_BY_ROWS).astype(BF16)
    y2_ref[...] = dot(w_ref[rows, :], gt[...], ROWS_BY_ROWS).astype(BF16)


def prepare(w, g, i_n, j_n):
    pairs = i_n * j_n
    channels = w.shape[0]
    size = channels // STEPS
    return pl.pallas_call(
        functools.partial(prepare_kernel, i_n, j_n),
        grid=(STEPS,),
        in_specs=[whole(w.shape), whole(g.shape)],
        out_specs=[
            pl.BlockSpec((size, pairs), lambda t: (t, 0)),
            pl.BlockSpec((size, pairs), lambda t: (t, 0)),
            whole((PAIR_FEATURES, channels)),
            whole((BIAS_ROWS, PAIR_FEATURES)),
        ],
        out_shape=[
            jax.ShapeDtypeStruct((channels, pairs), BF16),
            jax.ShapeDtypeStruct((channels, pairs), BF16),
            jax.ShapeDtypeStruct((PAIR_FEATURES, channels), BF16),
            jax.ShapeDtypeStruct((BIAS_ROWS, PAIR_FEATURES), BF16),
        ],
        scratch_shapes=[
            pltpu.VMEM(g.shape, F32),
            pltpu.VMEM(g.shape, BF16),
            pltpu.VMEM(w.shape, F32),
            pltpu.VMEM(w.shape, BF16),
        ],
        compiler_params=params(32),
        cost_estimate=pl.CostEstimate(
            flops=4 * pairs * channels * PAIR_FEATURES,
            bytes_accessed=4 * pairs * channels,
            transcendentals=0,
        ),
    )(w, g)


def join(pieces, axis, held):
    count = len(pieces)
    depth = pieces[0].shape[0]
    me = lax.axis_index(axis)
    for p, piece in enumerate(pieces):
        start = pl.multiple_of(lax.rem(me - p + count, count) * depth, depth)
        held[pl.ds(start, depth), :] = piece[...].astype(F32)


def repeat_matrix(sequences):
    shape = (sequences, GROUP * sequences)
    lane = lax.broadcasted_iota(jnp.int32, shape, 1)
    row = lax.broadcasted_iota(jnp.int32, shape, 0)
    return (lax.rem(lane, sequences) == row).astype(BF16)


def spread(held, wide):
    both = dot(held[...].T.astype(BF16), repeat_matrix(held.shape[0]))
    for l in range(wide.shape[0]):
        wide[l] = both[:, l * LANES : (l + 1) * LANES]


def tiles_of(sequences, tile):
    lane = lax.broadcasted_iota(jnp.int32, (1, LANES), 1) + tile * LANES
    return [
        (m, lax.div(lane, sequences) == m)
        for m in range(GROUP)
        if m * sequences < (tile + 1) * LANES and (m + 1) * sequences > tile * LANES
    ]


def fill_diagonal(wide, diagonal, slot, channel, positions, sequences):
    for l in range(wide.shape[0]):
        block = wide[l, pl.ds(channel, positions, stride=PROJECTED_DEPTH), :]
        for m, mask in tiles_of(sequences, l):
            diagonal[slot, m * positions : (m + 1) * positions, l * LANES : (l + 1) * LANES] = (
                jnp.where(mask, block, 0.0).astype(BF16)
            )


def outer_kernel(i_n, j_n, row_n, col_n, *refs):
    depth = PROJECTED_DEPTH
    a_pieces, refs = refs[:col_n], refs[col_n:]
    b_pieces, refs = refs[:row_n], refs[row_n:]
    (g_ref, bias_ref), refs = refs[:2], refs[2:]
    x_ref, refs = refs[0], refs[1:]
    messages, refs = refs[:row_n], refs[row_n:]
    a_held, b_held, wide, left, diagonal, total, ordered = refs
    sequences = a_held.shape[0]
    groups = i_n // GROUP
    per_step = depth // STEPS
    span = GROUP * j_n
    t = pl.program_id(0)

    @pl.when(t == 0)
    def _():
        join(a_pieces, "col", a_held)
        join(b_pieces, "row", b_held)
        spread(a_held, wide)
        for l in range(wide.shape[0]):
            members = tiles_of(sequences, l)
            for k in range(groups):
                block = jnp.zeros((depth, LANES), F32)
                for m, mask in members:
                    start = (k * GROUP + m) * depth
                    block = jnp.where(mask, wide[l, start : start + depth, :], block)
                left[k * depth : (k + 1) * depth, l * LANES : (l + 1) * LANES] = block.astype(BF16)
        spread(b_held, wide)
        diagonal[...] = jnp.zeros(diagonal.shape, BF16)

    for e in range(per_step):
        fill_diagonal(wide, diagonal, e, t * per_step + e, j_n, sequences)
    for e in range(0, per_step, 2):
        right = diagonal[e : e + 2].reshape(2 * span, diagonal.shape[2])
        product = dot(left[...], right, ROWS_BY_ROWS).astype(BF16)
        for n in range(2):
            for k in range(groups):
                x_ref[(e + n) * depth : (e + n + 1) * depth, k * span : (k + 1) * span] = product[
                    k * depth : (k + 1) * depth, n * span : (n + 1) * span
                ]
    size = x_ref.shape[0]
    total[pl.ds(pl.multiple_of(t * size, size), size), :] = dot(x_ref[...], g_ref[...])

    @pl.when(t == STEPS - 1)
    def _():
        for c in range(depth):
            ordered[c * depth : (c + 1) * depth, :] = total[pl.ds(c, depth, stride=depth), :]
        share = ordered.shape[0] // row_n
        me = lax.axis_index("row")
        for p, message in enumerate(messages):
            start = pl.multiple_of(lax.rem(me + p, row_n) * share, share)
            message[0:share, :] = ordered[pl.ds(start, share), :].astype(message.dtype)
            message[share:, :] = bias_ref[...].astype(message.dtype)


def outer(a_pieces, b_pieces, g, bias_rows, i_n, j_n, sequences):
    row_n, col_n = len(b_pieces), len(a_pieces)
    depth = PROJECTED_DEPTH
    channels = depth * depth
    pairs = i_n * j_n
    share = channels // row_n
    tiles = GROUP * sequences // LANES
    operands = [*a_pieces, *b_pieces, g, bias_rows]
    results = pl.pallas_call(
        functools.partial(outer_kernel, i_n, j_n, row_n, col_n),
        grid=(STEPS,),
        in_specs=[whole(x.shape) for x in operands],
        out_specs=[pl.BlockSpec((channels // STEPS, pairs), lambda t: (t, 0))]
        + [whole((share + BIAS_ROWS, PAIR_FEATURES))] * row_n,
        out_shape=[jax.ShapeDtypeStruct((channels, pairs), BF16)]
        + [
            jax.ShapeDtypeStruct((share + BIAS_ROWS, PAIR_FEATURES), F32 if p == 0 else BF16)
            for p in range(row_n)
        ],
        scratch_shapes=[
            pltpu.VMEM((sequences, i_n * depth), F32),
            pltpu.VMEM((sequences, j_n * depth), F32),
            pltpu.VMEM((tiles, i_n * depth, LANES), F32),
            pltpu.VMEM((i_n // GROUP * depth, GROUP * sequences), BF16),
            pltpu.VMEM((depth // STEPS, GROUP * j_n, GROUP * sequences), BF16),
            pltpu.VMEM((channels, PAIR_FEATURES), F32),
            pltpu.VMEM((channels, PAIR_FEATURES), F32),
        ],
        compiler_params=params(sequences),
        cost_estimate=pl.CostEstimate(
            flops=4 * pairs * channels * PAIR_FEATURES,
            bytes_accessed=2 * pairs * channels,
            transcendentals=0,
        ),
    )(*operands)
    return results[0], results[1:]


def gradient_kernel(i_n, j_n, row_n, col_n, *refs):
    depth = PROJECTED_DEPTH
    a_pieces, refs = refs[:col_n], refs[col_n:]
    b_pieces, refs = refs[:row_n], refs[row_n:]
    (y_ref, y2_ref), refs = refs[:2], refs[2:]
    left_out, refs = refs[:col_n], refs[col_n:]
    right_out, refs = refs[:row_n], refs[row_n:]
    a_held, b_held, a_wide, b_wide, a_diagonal, b_diagonal, left, right, grown = refs
    sequences = a_held.shape[0]
    per_step = depth // STEPS
    t = pl.program_id(0)

    @pl.when(t == 0)
    def _():
        join(a_pieces, "col", a_held)
        join(b_pieces, "row", b_held)
        spread(a_held, a_wide)
        spread(b_held, b_wide)
        for ref in (a_diagonal, b_diagonal):
            ref[...] = jnp.zeros(ref.shape, BF16)
        for ref in (left, right):
            ref[...] = jnp.zeros(ref.shape, F32)

    def accumulate(source, wide, diagonal, result, positions, others):
        span = GROUP * positions
        for n in range(per_step):
            fill_diagonal(wide, diagonal, n, t * per_step + n, positions, sequences)
        for n in range(0, per_step, 2):
            rows = [
                jnp.concatenate(
                    [
                        source[m * depth : (m + 1) * depth, k * span : (k + 1) * span]
                        for m in (n, n + 1)
                    ],
                    axis=1,
                )
                for k in range(others // GROUP)
            ]
            result[...] += dot(
                jnp.concatenate(rows, axis=0),
                diagonal[n : n + 2].reshape(2 * span, diagonal.shape[2]),
            )

    accumulate(y_ref, b_wide, b_diagonal, left, j_n, i_n)
    accumulate(y2_ref, a_wide, a_diagonal, right, i_n, j_n)

    def deliver(result, held, outs, axis, positions):
        scaled = (result[...] * (1.0 / sequences)).astype(BF16)
        for l in range(scaled.shape[1] // LANES):
            members = dict(tiles_of(sequences, l))
            for k in range(positions // GROUP):
                block = scaled[k * depth : (k + 1) * depth, l * LANES : (l + 1) * LANES]
                for m in range(GROUP):
                    start = (k * GROUP + m) * depth
                    grown[start : start + depth, l * LANES : (l + 1) * LANES] = (
                        jnp.where(members[m], block.astype(F32), 0.0).astype(BF16)
                        if m in members
                        else jnp.zeros((depth, LANES), BF16)
                    )
        held[...] = dot(repeat_matrix(sequences), grown[...], ROWS_BY_ROWS)
        count = len(outs)
        share = sequences // count
        me = lax.axis_index(axis)
        for p, out in enumerate(outs):
            start = pl.multiple_of(lax.rem(me + p, count) * share, share)
            out[...] = held[pl.ds(start, share), :].astype(out.dtype)

    @pl.when(t == STEPS - 1)
    def _():
        deliver(left, a_held, left_out, "col", i_n)
        deliver(right, b_held, right_out, "row", j_n)


def gradients(a_pieces, b_pieces, y, y2, i_n, j_n, sequences):
    row_n, col_n = len(b_pieces), len(a_pieces)
    depth = PROJECTED_DEPTH
    channels, pairs = y.shape
    tiles = GROUP * sequences // LANES
    size = channels // STEPS
    pieces = [*a_pieces, *b_pieces]
    block = pl.BlockSpec((size, pairs), lambda t: (t, 0))

    def part(p, axis_n, positions):
        return jax.ShapeDtypeStruct((sequences // axis_n, positions * depth), F32 if p == 0 else BF16)

    shapes = [part(p, col_n, i_n) for p in range(col_n)] + [part(p, row_n, j_n) for p in range(row_n)]
    results = pl.pallas_call(
        functools.partial(gradient_kernel, i_n, j_n, row_n, col_n),
        grid=(STEPS,),
        in_specs=[whole(x.shape) for x in pieces] + [block, block],
        out_specs=[whole(x.shape) for x in shapes],
        out_shape=shapes,
        scratch_shapes=[
            pltpu.VMEM((sequences, i_n * depth), F32),
            pltpu.VMEM((sequences, j_n * depth), F32),
            pltpu.VMEM((tiles, i_n * depth, LANES), F32),
            pltpu.VMEM((tiles, j_n * depth, LANES), F32),
            pltpu.VMEM((depth // STEPS, GROUP * i_n, GROUP * sequences), BF16),
            pltpu.VMEM((depth // STEPS, GROUP * j_n, GROUP * sequences), BF16),
            pltpu.VMEM((i_n // GROUP * depth, GROUP * sequences), F32),
            pltpu.VMEM((j_n // GROUP * depth, GROUP * sequences), F32),
            pltpu.VMEM((i_n * depth, GROUP * sequences), BF16),
        ],
        compiler_params=params(sequences),
        cost_estimate=pl.CostEstimate(
            flops=4 * pairs * channels * PAIR_FEATURES,
            bytes_accessed=4 * pairs * channels,
            transcendentals=0,
        ),
    )(*pieces, y, y2)
    return results[:col_n], results[col_n:]


def pair_kernel(sequences, x_ref, wt_ref, bias_ref, out_ref):
    product = dot(wt_ref[...], x_ref[...])
    out_ref[...] = (product.T * (1.0 / sequences) + bias_ref[...]).astype(BF16)


def pair(x, wt, output_bias, sequences):
    channels, pairs = x.shape
    count = 3
    size = pairs // count
    return pl.pallas_call(
        functools.partial(pair_kernel, sequences),
        grid=(count,),
        in_specs=[
            pl.BlockSpec((channels, size), lambda t: (0, t)),
            whole(wt.shape),
            whole((1, PAIR_FEATURES)),
        ],
        out_specs=pl.BlockSpec((size, PAIR_FEATURES), lambda t: (t, 0)),
        out_shape=jax.ShapeDtypeStruct((pairs, PAIR_FEATURES), BF16),
        compiler_params=params(),
        cost_estimate=pl.CostEstimate(
            flops=4 * pairs * channels * PAIR_FEATURES,
            bytes_accessed=2 * pairs * channels,
            transcendentals=0,
        ),
    )(x, wt, output_bias.reshape(1, PAIR_FEATURES))


def column_sum_kernel(res_total, *refs):
    pieces, (piece_out, bias_out, held) = refs[:-3], refs[-3:]
    count = len(pieces)
    me = lax.axis_index("col")
    for p, piece in enumerate(pieces):
        held[lax.rem(me - p + count, count)] = piece[...]
    total = held[0].astype(F32)
    for n in range(1, count):
        total += held[n].astype(F32)
    share = piece_out.shape[0]
    piece_out[...] = total[0:share].astype(BF16)
    bias_out[...] = (total[share : share + 1] + total[share + 1 : share + 2]) * (1.0 / res_total)


def column_sum(pieces, res_total):
    rows = pieces[0].shape[0]
    return pl.pallas_call(
        functools.partial(column_sum_kernel, res_total),
        out_shape=[
            jax.ShapeDtypeStruct((rows - BIAS_ROWS, PAIR_FEATURES), BF16),
            jax.ShapeDtypeStruct((1, PAIR_FEATURES), F32),
        ],
        scratch_shapes=[pltpu.VMEM((len(pieces), rows, PAIR_FEATURES), BF16)],
        compiler_params=params(),
    )(*pieces)


def place_kernel(scale, *refs):
    pieces, out_ref = refs[:-1], refs[-1]
    count = len(pieces)
    me = lax.axis_index("row")
    for p, piece in enumerate(pieces):
        share = piece.shape[0]
        start = pl.multiple_of(lax.rem(me - p + count, count) * share, share)
        out_ref[pl.ds(start, share), :] = piece[...].astype(F32) * scale


def place(pieces, scale):
    rows = pieces[0].shape[0] * len(pieces)
    return pl.pallas_call(
        functools.partial(place_kernel, scale),
        out_shape=jax.ShapeDtypeStruct((rows, PAIR_FEATURES), F32),
        compiler_params=params(),
    )(*pieces)


def shift(x, axis, distance):
    count = lax.axis_size(axis)
    return lax.ppermute(x, axis, [(n, (n + distance) % count) for n in range(count)])


def broadcast(x, axis):
    return [x] + [shift(x, axis, d) for d in range(1, lax.axis_size(axis))]


def exchange(parts, axis):
    return [parts[0]] + [shift(parts[d], axis, d) for d in range(1, len(parts))]


def total_of(parts):
    total = parts[0].astype(F32)
    for part in parts[1:]:
        total = total + part.astype(F32)
    return total


def local(
    first_homolog_features, second_homolog_features, final_projection_matrix, output_bias, cotangent
):
    i_n, j_n, _ = cotangent.shape
    sequences = second_homolog_features.shape[0] * lax.axis_size("row")
    res_total = i_n * lax.axis_size("row")
    g = cotangent.reshape(i_n * j_n, PAIR_FEATURES)
    a_pieces = broadcast(first_homolog_features, "col")
    b_pieces = broadcast(second_homolog_features, "row")
    y, y2, wt, bias_rows = prepare(final_projection_matrix, g, i_n, j_n)

    x, messages = outer(a_pieces, b_pieces, g, bias_rows, i_n, j_n, sequences)
    row_parts = exchange(messages, "row")

    left_parts, right_parts = gradients(a_pieces, b_pieces, y, y2, i_n, j_n, sequences)
    left_grad = total_of(exchange(left_parts, "col"))
    right_grad = total_of(exchange(right_parts, "row"))

    share = total_of(row_parts).astype(BF16)
    share, bias_grad = column_sum(broadcast(share, "col"), res_total)
    pair_map = pair(x, wt, output_bias, sequences)
    projection = place(broadcast(share, "row"), 1.0 / (sequences * res_total))
    return (
        pair_map.reshape(i_n, j_n, PAIR_FEATURES),
        left_grad,
        right_grad,
        projection,
        bias_grad.reshape(PAIR_FEATURES),
    )


def solution(mesh):
    return jax.shard_map(
        local,
        mesh=mesh,
        in_specs=(
            P(("dp", "col"), "row"),
            P(("dp", "row"), "col"),
            P(),
            P(),
            P(("dp", "row"), "col", None),
        ),
        out_specs=(
            P(("dp", "row"), "col", None),
            P(("dp", "col"), "row"),
            P(("dp", "row"), "col"),
            P("dp", None),
            P("dp"),
        ),
        check_vma=False,
    )
```

```python
import functools

import jax
import jax.numpy as jnp
from jax import lax
from jax.experimental import pallas as pl
from jax.experimental.pallas import tpu as pltpu
from jax.sharding import PartitionSpec as P

PROJECTED_DEPTH = 32
PAIR_FEATURES = 128
GROUP = 8
STEPS = 4
BIAS_ROWS = 16
LANES = 128
F32 = jnp.float32
BF16 = jnp.bfloat16
MIB = 1024 * 1024

ROWS_BY_ROWS = (((1,), (1,)), ((), ()))
COLS_BY_COLS = (((0,), (0,)), ((), ()))


def params(sequences=0):
    return pltpu.CompilerParams(vmem_limit_bytes=min(10 + 10 * sequences // 32, 50) * MIB + 2 * MIB)


def whole(shape):
    return pl.BlockSpec(shape, lambda t: (0,) * len(shape))


def dot(x, y, dims=(((1,), (0,)), ((), ()))):
    return lax.dot_general(x, y, dims, preferred_element_type=F32)


def prepare_kernel(
    i_n, j_n, a_hbm, b_hbm, w_hbm, g_hbm, y_ref, y2_ref, wt_ref, bias_ref, a_ref, b_ref, g_ref,
    w_ref, g32, gt, w32, we, sems,
):
    depth = PROJECTED_DEPTH
    copies = [
        pltpu.make_async_copy(source, target, sems.at[n])
        for n, (source, target) in enumerate(
            [(w_hbm, w_ref), (g_hbm, g_ref), (a_hbm, a_ref), (b_hbm, b_ref)]
        )
    ]
    for copy in copies:
        copy.start()
    copies[0].wait()
    w32[...] = w_ref[...].astype(F32)
    for e in range(depth):
        block = w32[pl.ds(e, depth, stride=depth), :]
        we[e * depth : (e + 1) * depth, :] = block.astype(BF16)
    wt_ref[...] = we[...].astype(F32).T.astype(BF16)
    copies[1].wait()
    g32[...] = g_ref[...].astype(F32)
    total = jnp.sum(g32[...], axis=0, keepdims=True)
    high = total.astype(BF16).astype(F32)
    row = lax.broadcasted_iota(jnp.int32, (BIAS_ROWS, PAIR_FEATURES), 0)
    bias_ref[...] = jnp.where(row == 0, high, jnp.where(row == 1, total - high, 0.0)).astype(BF16)
    for j in range(j_n):
        gt[j * i_n : (j + 1) * i_n, :] = g32[pl.ds(j, i_n, stride=j_n), :].astype(BF16)

    size = y_ref.shape[0] // STEPS

    @pl.loop(0, STEPS)
    def _(t):
        rows = pl.ds(pl.multiple_of(t * size, size), size)
        y_ref[rows, :] = dot(we[rows, :], g_ref[...], ROWS_BY_ROWS).astype(BF16)
        y2_ref[rows, :] = dot(w_ref[rows, :], gt[...], ROWS_BY_ROWS).astype(BF16)

    copies[2].wait()
    copies[3].wait()


def in_vmem():
    return pl.BlockSpec(memory_space=pltpu.VMEM)


def prepare(a, b, w, g, i_n, j_n):
    pairs = i_n * j_n
    channels = w.shape[0]
    shapes = [
        jax.ShapeDtypeStruct((channels, pairs), BF16),
        jax.ShapeDtypeStruct((channels, pairs), BF16),
        jax.ShapeDtypeStruct((PAIR_FEATURES, channels), BF16),
        jax.ShapeDtypeStruct((BIAS_ROWS, PAIR_FEATURES), BF16),
        jax.ShapeDtypeStruct(a.shape, BF16),
        jax.ShapeDtypeStruct(b.shape, BF16),
        jax.ShapeDtypeStruct(g.shape, BF16),
    ]
    return pl.pallas_call(
        functools.partial(prepare_kernel, i_n, j_n),
        in_specs=[pl.BlockSpec(memory_space=pltpu.HBM)] * 4,
        out_specs=[in_vmem()] * len(shapes),
        out_shape=shapes,
        scratch_shapes=[
            pltpu.VMEM(w.shape, BF16),
            pltpu.VMEM(g.shape, F32),
            pltpu.VMEM(g.shape, BF16),
            pltpu.VMEM(w.shape, F32),
            pltpu.VMEM(w.shape, BF16),
            pltpu.SemaphoreType.DMA((4,)),
        ],
        compiler_params=params(32),
        cost_estimate=pl.CostEstimate(
            flops=4 * pairs * channels * PAIR_FEATURES,
            bytes_accessed=4 * pairs * channels,
            transcendentals=0,
        ),
    )(a, b, w, g)


def join(pieces, axis, held):
    count = len(pieces)
    depth = pieces[0].shape[0]
    me = lax.axis_index(axis)
    for p, piece in enumerate(pieces):
        start = pl.multiple_of(lax.rem(me - p + count, count) * depth, depth)
        held[pl.ds(start, depth), :] = piece[...].astype(F32)


def repeat_matrix(sequences):
    shape = (sequences, GROUP * sequences)
    lane = lax.broadcasted_iota(jnp.int32, shape, 1)
    row = lax.broadcasted_iota(jnp.int32, shape, 0)
    return (lax.rem(lane, sequences) == row).astype(BF16)


def spread(held, wide):
    both = dot(held[...].T.astype(BF16), repeat_matrix(held.shape[0]))
    for l in range(wide.shape[0]):
        wide[l] = both[:, l * LANES : (l + 1) * LANES]


def tiles_of(sequences, tile):
    lane = lax.broadcasted_iota(jnp.int32, (1, LANES), 1) + tile * LANES
    return [
        (m, lax.div(lane, sequences) == m)
        for m in range(GROUP)
        if m * sequences < (tile + 1) * LANES and (m + 1) * sequences > tile * LANES
    ]


def fill_diagonal(wide, diagonal, slot, channel, positions, sequences):
    for l in range(wide.shape[0]):
        block = wide[l, pl.ds(channel, positions, stride=PROJECTED_DEPTH), :]
        for m, mask in tiles_of(sequences, l):
            diagonal[slot, m * positions : (m + 1) * positions, l * LANES : (l + 1) * LANES] = (
                jnp.where(mask, block, 0.0).astype(BF16)
            )


def outer_kernel(i_n, j_n, row_n, col_n, *refs):
    depth = PROJECTED_DEPTH
    a_pieces, refs = refs[:col_n], refs[col_n:]
    b_pieces, refs = refs[:row_n], refs[row_n:]
    g_ref, bias_ref, x_ref, message = refs[:4]
    a_held, b_held, wide, left, diagonal, total, ordered = refs[4:]
    sequences = a_held.shape[0]
    groups = i_n // GROUP
    per_step = depth // STEPS
    span = GROUP * j_n

    join(a_pieces, "col", a_held)
    join(b_pieces, "row", b_held)
    spread(a_held, wide)
    for l in range(wide.shape[0]):
        members = tiles_of(sequences, l)
        for k in range(groups):
            block = jnp.zeros((depth, LANES), F32)
            for m, mask in members:
                start = (k * GROUP + m) * depth
                block = jnp.where(mask, wide[l, start : start + depth, :], block)
            left[k * depth : (k + 1) * depth, l * LANES : (l + 1) * LANES] = block.astype(BF16)
    spread(b_held, wide)
    diagonal[...] = jnp.zeros(diagonal.shape, BF16)

    @pl.loop(0, STEPS)
    def _(t):
        for e in range(per_step):
            fill_diagonal(wide, diagonal, e, t * per_step + e, j_n, sequences)
        size = per_step * depth
        first = pl.multiple_of(t * size, size)
        for e in range(0, per_step, 2):
            right = diagonal[e : e + 2].reshape(2 * span, diagonal.shape[2])
            product = dot(left[...], right, ROWS_BY_ROWS).astype(BF16)
            for n in range(2):
                for k in range(groups):
                    x_ref[pl.ds(first + (e + n) * depth, depth), k * span : (k + 1) * span] = product[
                        k * depth : (k + 1) * depth, n * span : (n + 1) * span
                    ]
        total[pl.ds(first, size), :] = dot(x_ref[pl.ds(first, size), :], g_ref[...])

    for c in range(depth):
        ordered[c * depth : (c + 1) * depth, :] = total[pl.ds(c, depth, stride=depth), :]
    share = ordered.shape[0] // row_n
    for p in range(row_n):
        message[p, 0:share, :] = ordered[p * share : (p + 1) * share, :].astype(BF16)
        message[p, share:, :] = bias_ref[...]


def outer(a_pieces, b_pieces, g, bias_rows, i_n, j_n, sequences):
    row_n, col_n = len(b_pieces), len(a_pieces)
    depth = PROJECTED_DEPTH
    channels = depth * depth
    pairs = i_n * j_n
    share = channels // row_n
    tiles = GROUP * sequences // LANES
    operands = [*a_pieces, *b_pieces, g, bias_rows]
    return pl.pallas_call(
        functools.partial(outer_kernel, i_n, j_n, row_n, col_n),
        in_specs=[in_vmem()] * len(operands),
        out_specs=[in_vmem()] * 2,
        out_shape=[
            jax.ShapeDtypeStruct((channels, pairs), BF16),
            jax.ShapeDtypeStruct((row_n, share + BIAS_ROWS, PAIR_FEATURES), BF16),
        ],
        scratch_shapes=[
            pltpu.VMEM((sequences, i_n * depth), F32),
            pltpu.VMEM((sequences, j_n * depth), F32),
            pltpu.VMEM((tiles, i_n * depth, LANES), F32),
            pltpu.VMEM((i_n // GROUP * depth, GROUP * sequences), BF16),
            pltpu.VMEM((depth // STEPS, GROUP * j_n, GROUP * sequences), BF16),
            pltpu.VMEM((channels, PAIR_FEATURES), F32),
            pltpu.VMEM((channels, PAIR_FEATURES), F32),
        ],
        compiler_params=params(sequences),
        cost_estimate=pl.CostEstimate(
            flops=4 * pairs * channels * PAIR_FEATURES,
            bytes_accessed=2 * pairs * channels,
            transcendentals=0,
        ),
    )(*operands)


def gradient_kernel(axis, count, positions, others, *refs):
    depth = PROJECTED_DEPTH
    pieces, source, out = refs[:count], refs[count], refs[count + 1]
    held, wide, diagonal, result, grown, grad = refs[count + 2 :]
    sequences = held.shape[0]
    per_step = depth // STEPS
    span = GROUP * others

    join(pieces, axis, held)
    spread(held, wide)
    diagonal[...] = jnp.zeros(diagonal.shape, BF16)
    result[...] = jnp.zeros(result.shape, F32)

    @pl.loop(0, STEPS)
    def _(t):
        for n in range(per_step):
            fill_diagonal(wide, diagonal, n, t * per_step + n, others, sequences)
        first = pl.multiple_of(t * per_step * depth, per_step * depth)
        for n in range(0, per_step, 2):
            rows = [
                jnp.concatenate(
                    [
                        source[pl.ds(first + m * depth, depth), k * span : (k + 1) * span]
                        for m in (n, n + 1)
                    ],
                    axis=1,
                )
                for k in range(positions // GROUP)
            ]
            result[...] += dot(
                jnp.concatenate(rows, axis=0),
                diagonal[n : n + 2].reshape(2 * span, diagonal.shape[2]),
            )

    scaled = (result[...] * (1.0 / sequences)).astype(BF16)
    for l in range(scaled.shape[1] // LANES):
        members = dict(tiles_of(sequences, l))
        for k in range(positions // GROUP):
            block = scaled[k * depth : (k + 1) * depth, l * LANES : (l + 1) * LANES]
            for m in range(GROUP):
                start = (k * GROUP + m) * depth
                grown[start : start + depth, l * LANES : (l + 1) * LANES] = (
                    jnp.where(members[m], block.astype(F32), 0.0).astype(BF16)
                    if m in members
                    else jnp.zeros((depth, LANES), BF16)
                )
    grad[...] = dot(repeat_matrix(sequences), grown[...], ROWS_BY_ROWS)
    share = sequences // out.shape[0]
    for p in range(out.shape[0]):
        mine = grad[p * share : (p + 1) * share, :]
        out[p] = jnp.concatenate(
            [mine[:, l * LANES : (l + 1) * LANES] for l in range(mine.shape[1] // LANES)], axis=0
        ).astype(BF16)


def gradient(pieces, axis, source, parts, positions, others, sequences):
    depth = PROJECTED_DEPTH
    channels, pairs = source.shape
    tiles = GROUP * sequences // LANES
    rows = sequences // parts * positions * depth // LANES
    return pl.pallas_call(
        functools.partial(gradient_kernel, axis, len(pieces), positions, others),
        in_specs=[in_vmem()] * (len(pieces) + 1),
        out_specs=in_vmem(),
        out_shape=jax.ShapeDtypeStruct((parts, rows, LANES), BF16),
        scratch_shapes=[
            pltpu.VMEM((sequences, others * depth), F32),
            pltpu.VMEM((tiles, others * depth, LANES), F32),
            pltpu.VMEM((depth // STEPS, GROUP * others, GROUP * sequences), BF16),
            pltpu.VMEM((positions // GROUP * depth, GROUP * sequences), F32),
            pltpu.VMEM((positions * depth, GROUP * sequences), BF16),
            pltpu.VMEM((sequences, positions * depth), F32),
        ],
        compiler_params=params(sequences),
        cost_estimate=pl.CostEstimate(
            flops=2 * pairs * channels * PAIR_FEATURES,
            bytes_accessed=2 * pairs * channels,
            transcendentals=0,
        ),
    )(*pieces, source)


def pair_kernel(sequences, x_ref, wt_ref, bias_ref, out_ref):
    product = dot(wt_ref[...], x_ref[...])
    out_ref[...] = (product.T * (1.0 / sequences) + bias_ref[...]).astype(BF16)


def pair(x, wt, output_bias, sequences):
    channels, pairs = x.shape
    count = 3
    size = pairs // count
    return pl.pallas_call(
        functools.partial(pair_kernel, sequences),
        grid=(count,),
        in_specs=[
            pl.BlockSpec((channels, size), lambda t: (0, t)),
            whole(wt.shape),
            whole((1, PAIR_FEATURES)),
        ],
        out_specs=pl.BlockSpec((size, PAIR_FEATURES), lambda t: (t, 0)),
        out_shape=jax.ShapeDtypeStruct((pairs, PAIR_FEATURES), BF16),
        compiler_params=params(),
        cost_estimate=pl.CostEstimate(
            flops=4 * pairs * channels * PAIR_FEATURES,
            bytes_accessed=2 * pairs * channels,
            transcendentals=0,
        ),
    )(x, wt, output_bias.reshape(1, PAIR_FEATURES))


def sum_parts(ref, start, stop):
    total = ref[0, start:stop, :].astype(F32)
    for n in range(1, ref.shape[0]):
        total += ref[n, start:stop, :].astype(F32)
    return total


def unfold(total, share, out):
    for l in range(out.shape[1] // LANES):
        out[:, l * LANES : (l + 1) * LANES] = total[l * share : (l + 1) * share, :]


def row_sum_kernel(parts, grads, message):
    rows = parts.shape[1]
    total = sum_parts(parts, 0, rows).astype(BF16)
    for p in range(message.shape[0]):
        message[p, 0:rows, :] = total
        message[p, rows:, :] = grads[p]


def row_sum(parts, grads):
    shape = (grads.shape[0], parts.shape[1] + grads.shape[1], LANES)
    return pl.pallas_call(
        row_sum_kernel,
        in_specs=[in_vmem()] * 2,
        out_specs=in_vmem(),
        out_shape=jax.ShapeDtypeStruct(shape, BF16),
        compiler_params=params(),
    )(parts, grads)


def column_sum_kernel(res_total, parts, grads, message, left_out, bias_out):
    share = message.shape[1] - grads.shape[1]
    total = sum_parts(parts, 0, share + BIAS_ROWS)
    piece = total[0:share].astype(BF16)
    for p in range(message.shape[0]):
        message[p, 0:share, :] = piece
        message[p, share:, :] = grads[p]
    bias_out[...] = (total[share : share + 1] + total[share + 1 : share + 2]) * (1.0 / res_total)
    unfold(sum_parts(parts, share + BIAS_ROWS, parts.shape[1]), left_out.shape[0], left_out)


def column_sum(parts, grads, share, left_shape, res_total):
    return pl.pallas_call(
        functools.partial(column_sum_kernel, res_total),
        in_specs=[in_vmem()] * 2,
        out_specs=[in_vmem()] * 3,
        out_shape=[
            jax.ShapeDtypeStruct((grads.shape[0], share + grads.shape[1], LANES), BF16),
            jax.ShapeDtypeStruct(left_shape, F32),
            jax.ShapeDtypeStruct((1, PAIR_FEATURES), F32),
        ],
        compiler_params=params(),
    )(parts, grads)


def finish_kernel(scale, parts, projection, right_out):
    count = parts.shape[0]
    share = projection.shape[0] // count
    for p in range(count):
        projection[p * share : (p + 1) * share, :] = parts[p, 0:share, :].astype(F32) * scale
    unfold(sum_parts(parts, share, parts.shape[1]), right_out.shape[0], right_out)


def finish(parts, channels, right_shape, scale):
    return pl.pallas_call(
        functools.partial(finish_kernel, scale),
        in_specs=[in_vmem()],
        out_specs=[in_vmem()] * 2,
        out_shape=[
            jax.ShapeDtypeStruct((channels, PAIR_FEATURES), F32),
            jax.ShapeDtypeStruct(right_shape, F32),
        ],
        compiler_params=params(),
    )(parts)


def shift(x, axis, distance):
    count = lax.axis_size(axis)
    return lax.ppermute(x, axis, [(n, (n + distance) % count) for n in range(count)])


def gather(x, axis):
    return [shift(x, axis, d) for d in range(1, lax.axis_size(axis))]


def exchange(parts, axis):
    return lax.all_to_all(parts, axis, 0, 0, tiled=True)


def local(
    first_homolog_features, second_homolog_features, final_projection_matrix, output_bias, cotangent
):
    i_n, j_n, _ = cotangent.shape
    row_n, col_n = lax.axis_size("row"), lax.axis_size("col")
    sequences = second_homolog_features.shape[0] * row_n
    channels = final_projection_matrix.shape[0]
    res_total = i_n * row_n
    a_pieces = gather(first_homolog_features, "col")
    b_pieces = gather(second_homolog_features, "row")
    y, y2, wt, bias_rows, a_own, b_own, g = prepare(
        first_homolog_features,
        second_homolog_features,
        final_projection_matrix,
        cotangent.reshape(i_n * j_n, PAIR_FEATURES),
        i_n,
        j_n,
    )
    a_pieces = [a_own] + a_pieces
    b_pieces = [b_own] + b_pieces

    x, message = outer(a_pieces, b_pieces, g, bias_rows, i_n, j_n, sequences)
    parts = exchange(message, "row")
    left_grads = gradient(b_pieces, "row", y, col_n, i_n, j_n, sequences)
    parts = exchange(row_sum(parts, left_grads), "col")
    right_grads = gradient(a_pieces, "col", y2, row_n, j_n, i_n, sequences)
    message, left_grad, bias_grad = column_sum(
        parts, right_grads, channels // row_n, first_homolog_features.shape, res_total
    )
    parts = exchange(message, "row")
    pair_map = pair(x, wt, output_bias, sequences)
    projection, right_grad = finish(
        parts, channels, second_homolog_features.shape, 1.0 / (sequences * res_total)
    )
    return (
        pair_map.reshape(i_n, j_n, PAIR_FEATURES),
        left_grad,
        right_grad,
        projection,
        bias_grad.reshape(PAIR_FEATURES),
    )


def solution(mesh):
    return jax.shard_map(
        local,
        mesh=mesh,
        in_specs=(
            P(("dp", "col"), "row"),
            P(("dp", "row"), "col"),
            P(),
            P(),
            P(("dp", "row"), "col", None),
        ),
        out_specs=(
            P(("dp", "row"), "col", None),
            P(("dp", "col"), "row"),
            P(("dp", "row"), "col"),
            P("dp", None),
            P("dp"),
        ),
        check_vma=False,
    )
```

```python
import functools

import jax
import jax.numpy as jnp
from jax import lax
from jax.experimental import pallas as pl
from jax.experimental.pallas import tpu as pltpu
from jax.sharding import PartitionSpec as P

PROJECTED_DEPTH = 32
PAIR_FEATURES = 128
GROUP = 8
STEPS = 4
BIAS_ROWS = 16
LANES = 128
F32 = jnp.float32
BF16 = jnp.bfloat16
MIB = 1024 * 1024

ROWS_BY_ROWS = (((1,), (1,)), ((), ()))
COLS_BY_COLS = (((0,), (0,)), ((), ()))


def params(sequences=0):
    return pltpu.CompilerParams(vmem_limit_bytes=min(10 + 10 * sequences // 32, 50) * MIB + 2 * MIB)


def whole(shape):
    return pl.BlockSpec(shape, lambda t: (0,) * len(shape))


def dot(x, y, dims=(((1,), (0,)), ((), ()))):
    return lax.dot_general(x, y, dims, preferred_element_type=F32)


def prepare_kernel(
    i_n, j_n, a_hbm, b_hbm, w_hbm, g_hbm, y_ref, y2_ref, wt_ref, bias_ref, a_ref, b_ref, g_ref,
    w_ref, g32, gt, w32, we, sems,
):
    depth = PROJECTED_DEPTH
    copies = [
        pltpu.make_async_copy(source, target, sems.at[n])
        for n, (source, target) in enumerate(
            [(w_hbm, w_ref), (g_hbm, g_ref), (a_hbm, a_ref), (b_hbm, b_ref)]
        )
    ]
    for copy in copies:
        copy.start()
    copies[0].wait()
    w32[...] = w_ref[...].astype(F32)
    for e in range(depth):
        block = w32[pl.ds(e, depth, stride=depth), :]
        we[e * depth : (e + 1) * depth, :] = block.astype(BF16)
    wt_ref[...] = we[...].astype(F32).T.astype(BF16)
    copies[1].wait()
    g32[...] = g_ref[...].astype(F32)
    total = jnp.sum(g32[...], axis=0, keepdims=True)
    high = total.astype(BF16).astype(F32)
    row = lax.broadcasted_iota(jnp.int32, (BIAS_ROWS, PAIR_FEATURES), 0)
    bias_ref[...] = jnp.where(row == 0, high, jnp.where(row == 1, total - high, 0.0)).astype(BF16)
    for j in range(j_n):
        gt[j * i_n : (j + 1) * i_n, :] = g32[pl.ds(j, i_n, stride=j_n), :].astype(BF16)

    size = y_ref.shape[0] // STEPS

    @pl.loop(0, STEPS)
    def _(t):
        rows = pl.ds(pl.multiple_of(t * size, size), size)
        y_ref[rows, :] = dot(we[rows, :], g_ref[...], ROWS_BY_ROWS).astype(BF16)
        y2_ref[rows, :] = dot(w_ref[rows, :], gt[...], ROWS_BY_ROWS).astype(BF16)

    copies[2].wait()
    copies[3].wait()


def in_vmem():
    return pl.BlockSpec(memory_space=pltpu.VMEM)


def prepare(a, b, w, g, i_n, j_n):
    pairs = i_n * j_n
    channels = w.shape[0]
    shapes = [
        jax.ShapeDtypeStruct((channels, pairs), BF16),
        jax.ShapeDtypeStruct((channels, pairs), BF16),
        jax.ShapeDtypeStruct((PAIR_FEATURES, channels), BF16),
        jax.ShapeDtypeStruct((BIAS_ROWS, PAIR_FEATURES), BF16),
        jax.ShapeDtypeStruct(a.shape, BF16),
        jax.ShapeDtypeStruct(b.shape, BF16),
        jax.ShapeDtypeStruct(g.shape, BF16),
    ]
    return pl.pallas_call(
        functools.partial(prepare_kernel, i_n, j_n),
        in_specs=[pl.BlockSpec(memory_space=pltpu.HBM)] * 4,
        out_specs=[in_vmem()] * len(shapes),
        out_shape=shapes,
        scratch_shapes=[
            pltpu.VMEM(w.shape, BF16),
            pltpu.VMEM(g.shape, F32),
            pltpu.VMEM(g.shape, BF16),
            pltpu.VMEM(w.shape, F32),
            pltpu.VMEM(w.shape, BF16),
            pltpu.SemaphoreType.DMA((4,)),
        ],
        compiler_params=params(32),
        cost_estimate=pl.CostEstimate(
            flops=4 * pairs * channels * PAIR_FEATURES,
            bytes_accessed=4 * pairs * channels,
            transcendentals=0,
        ),
    )(*[pltpu.with_memory_space_constraint(x, pltpu.HBM) for x in (a, b, w, g)])


def join(pieces, axis, held):
    count = len(pieces)
    depth = pieces[0].shape[0]
    me = lax.axis_index(axis)
    for p, piece in enumerate(pieces):
        start = pl.multiple_of(lax.rem(me - p + count, count) * depth, depth)
        held[pl.ds(start, depth), :] = piece[...].astype(F32)


def repeat_matrix(sequences):
    shape = (sequences, GROUP * sequences)
    lane = lax.broadcasted_iota(jnp.int32, shape, 1)
    row = lax.broadcasted_iota(jnp.int32, shape, 0)
    return (lax.rem(lane, sequences) == row).astype(BF16)


def spread(held, wide):
    both = dot(held[...].T.astype(BF16), repeat_matrix(held.shape[0]))
    for l in range(wide.shape[0]):
        wide[l] = both[:, l * LANES : (l + 1) * LANES]


def tiles_of(sequences, tile):
    lane = lax.broadcasted_iota(jnp.int32, (1, LANES), 1) + tile * LANES
    return [
        (m, lax.div(lane, sequences) == m)
        for m in range(GROUP)
        if m * sequences < (tile + 1) * LANES and (m + 1) * sequences > tile * LANES
    ]


def fill_diagonal(wide, diagonal, slot, channel, positions, sequences):
    for l in range(wide.shape[0]):
        block = wide[l, pl.ds(channel, positions, stride=PROJECTED_DEPTH), :]
        for m, mask in tiles_of(sequences, l):
            diagonal[slot, m * positions : (m + 1) * positions, l * LANES : (l + 1) * LANES] = (
                jnp.where(mask, block, 0.0).astype(BF16)
            )


def parts_shapes(count, rows):
    return [jax.ShapeDtypeStruct((rows, LANES), F32)] + [
        jax.ShapeDtypeStruct((rows, LANES), BF16)
    ] * (count - 1)


def outer_kernel(i_n, j_n, row_n, col_n, *refs):
    depth = PROJECTED_DEPTH
    a_pieces, refs = refs[:col_n], refs[col_n:]
    b_pieces, refs = refs[:row_n], refs[row_n:]
    (g_ref, bias_ref, x_ref), refs = refs[:3], refs[3:]
    messages, refs = refs[:row_n], refs[row_n:]
    a_held, b_held, wide, left, diagonal, total, ordered = refs
    sequences = a_held.shape[0]
    groups = i_n // GROUP
    per_step = depth // STEPS
    span = GROUP * j_n

    join(a_pieces, "col", a_held)
    join(b_pieces, "row", b_held)
    spread(a_held, wide)
    for l in range(wide.shape[0]):
        members = tiles_of(sequences, l)
        for k in range(groups):
            block = jnp.zeros((depth, LANES), F32)
            for m, mask in members:
                start = (k * GROUP + m) * depth
                block = jnp.where(mask, wide[l, start : start + depth, :], block)
            left[k * depth : (k + 1) * depth, l * LANES : (l + 1) * LANES] = block.astype(BF16)
    spread(b_held, wide)
    diagonal[...] = jnp.zeros(diagonal.shape, BF16)

    @pl.loop(0, STEPS)
    def _(t):
        for e in range(per_step):
            fill_diagonal(wide, diagonal, e, t * per_step + e, j_n, sequences)
        size = per_step * depth
        rows = pl.ds(pl.multiple_of(t * size, size), size)
        x_part = x_ref.at[rows]
        for e in range(0, per_step, 2):
            right = diagonal[e : e + 2].reshape(2 * span, diagonal.shape[2])
            product = dot(left[...], right, ROWS_BY_ROWS).astype(BF16)
            for n in range(2):
                for k in range(groups):
                    x_part[(e + n) * depth : (e + n + 1) * depth, k * span : (k + 1) * span] = product[
                        k * depth : (k + 1) * depth, n * span : (n + 1) * span
                    ]
        total[rows, :] = dot(x_part[...], g_ref[...])

    for c in range(depth):
        ordered[c * depth : (c + 1) * depth, :] = total[pl.ds(c, depth, stride=depth), :]
    share = ordered.shape[0] // row_n
    me = lax.axis_index("row")
    for p, message in enumerate(messages):
        start = pl.multiple_of(lax.rem(me + p, row_n) * share, share)
        message[0:share, :] = ordered[pl.ds(start, share), :].astype(message.dtype)
        message[share:, :] = bias_ref[...].astype(message.dtype)


def outer(a_pieces, b_pieces, g, bias_rows, i_n, j_n, sequences):
    row_n, col_n = len(b_pieces), len(a_pieces)
    depth = PROJECTED_DEPTH
    channels = depth * depth
    pairs = i_n * j_n
    share = channels // row_n
    tiles = GROUP * sequences // LANES
    operands = [*a_pieces, *b_pieces, g, bias_rows]
    shapes = [jax.ShapeDtypeStruct((channels, pairs), BF16)]
    shapes += parts_shapes(row_n, share + BIAS_ROWS)
    results = pl.pallas_call(
        functools.partial(outer_kernel, i_n, j_n, row_n, col_n),
        in_specs=[in_vmem()] * len(operands),
        out_specs=[in_vmem()] * len(shapes),
        out_shape=shapes,
        scratch_shapes=[
            pltpu.VMEM((sequences, i_n * depth), F32),
            pltpu.VMEM((sequences, j_n * depth), F32),
            pltpu.VMEM((tiles, i_n * depth, LANES), F32),
            pltpu.VMEM((i_n // GROUP * depth, GROUP * sequences), BF16),
            pltpu.VMEM((depth // STEPS, GROUP * j_n, GROUP * sequences), BF16),
            pltpu.VMEM((channels, PAIR_FEATURES), F32),
            pltpu.VMEM((channels, PAIR_FEATURES), F32),
        ],
        compiler_params=params(sequences),
        cost_estimate=pl.CostEstimate(
            flops=4 * pairs * channels * PAIR_FEATURES,
            bytes_accessed=2 * pairs * channels,
            transcendentals=0,
        ),
    )(*operands)
    return results[0], results[1:]


def gradient_kernel(axis, out_axis, count, parts, positions, others, *refs):
    depth = PROJECTED_DEPTH
    pieces, source, refs = refs[:count], refs[count], refs[count + 1 :]
    outs, refs = refs[:parts], refs[parts:]
    held, wide, diagonal, result, grown, grad = refs
    sequences = held.shape[0]
    per_step = depth // STEPS
    span = GROUP * others

    join(pieces, axis, held)
    spread(held, wide)
    diagonal[...] = jnp.zeros(diagonal.shape, BF16)
    result[...] = jnp.zeros(result.shape, F32)

    @pl.loop(0, STEPS)
    def _(t):
        for n in range(per_step):
            fill_diagonal(wide, diagonal, n, t * per_step + n, others, sequences)
        size = per_step * depth
        part = source.at[pl.ds(pl.multiple_of(t * size, size), size)]
        for n in range(0, per_step, 2):
            rows = [
                jnp.concatenate(
                    [
                        part[m * depth : (m + 1) * depth, k * span : (k + 1) * span]
                        for m in (n, n + 1)
                    ],
                    axis=1,
                )
                for k in range(positions // GROUP)
            ]
            result[...] += dot(
                jnp.concatenate(rows, axis=0),
                diagonal[n : n + 2].reshape(2 * span, diagonal.shape[2]),
            )

    scaled = (result[...] * (1.0 / sequences)).astype(BF16)
    for l in range(scaled.shape[1] // LANES):
        members = dict(tiles_of(sequences, l))
        for k in range(positions // GROUP):
            block = scaled[k * depth : (k + 1) * depth, l * LANES : (l + 1) * LANES]
            for m in range(GROUP):
                start = (k * GROUP + m) * depth
                grown[start : start + depth, l * LANES : (l + 1) * LANES] = (
                    jnp.where(members[m], block.astype(F32), 0.0).astype(BF16)
                    if m in members
                    else jnp.zeros((depth, LANES), BF16)
                )
    grad[...] = dot(repeat_matrix(sequences), grown[...], ROWS_BY_ROWS)
    share = sequences // parts
    me = lax.axis_index(out_axis)
    for p, out in enumerate(outs):
        mine = grad[pl.ds(pl.multiple_of(lax.rem(me + p, parts) * share, share), share), :]
        out[...] = jnp.concatenate(
            [mine[:, l * LANES : (l + 1) * LANES] for l in range(mine.shape[1] // LANES)], axis=0
        ).astype(out.dtype)


def gradient(pieces, axis, out_axis, source, parts, positions, others, sequences):
    depth = PROJECTED_DEPTH
    channels, pairs = source.shape
    tiles = GROUP * sequences // LANES
    rows = sequences // parts * positions * depth // LANES
    return pl.pallas_call(
        functools.partial(
            gradient_kernel, axis, out_axis, len(pieces), parts, positions, others
        ),
        in_specs=[in_vmem()] * (len(pieces) + 1),
        out_specs=[in_vmem()] * parts,
        out_shape=parts_shapes(parts, rows),
        scratch_shapes=[
            pltpu.VMEM((sequences, others * depth), F32),
            pltpu.VMEM((tiles, others * depth, LANES), F32),
            pltpu.VMEM((depth // STEPS, GROUP * others, GROUP * sequences), BF16),
            pltpu.VMEM((positions // GROUP * depth, GROUP * sequences), F32),
            pltpu.VMEM((positions * depth, GROUP * sequences), BF16),
            pltpu.VMEM((sequences, positions * depth), F32),
        ],
        compiler_params=params(sequences),
        cost_estimate=pl.CostEstimate(
            flops=2 * pairs * channels * PAIR_FEATURES,
            bytes_accessed=2 * pairs * channels,
            transcendentals=0,
        ),
    )(*pieces, source)


def pair_kernel(sequences, x_ref, wt_ref, bias_ref, out_ref):
    product = dot(wt_ref[...], x_ref[...])
    out_ref[...] = (product.T * (1.0 / sequences) + bias_ref[...]).astype(BF16)


def pair(x, wt, output_bias, sequences):
    channels, pairs = x.shape
    count = 3
    size = pairs // count
    return pl.pallas_call(
        functools.partial(pair_kernel, sequences),
        grid=(count,),
        in_specs=[
            pl.BlockSpec((channels, size), lambda t: (0, t)),
            whole(wt.shape),
            whole((1, PAIR_FEATURES)),
        ],
        out_specs=pl.BlockSpec((size, PAIR_FEATURES), lambda t: (t, 0)),
        out_shape=jax.ShapeDtypeStruct((pairs, PAIR_FEATURES), BF16),
        compiler_params=params(),
        cost_estimate=pl.CostEstimate(
            flops=4 * pairs * channels * PAIR_FEATURES,
            bytes_accessed=2 * pairs * channels,
            transcendentals=0,
        ),
    )(x, wt, output_bias.reshape(1, PAIR_FEATURES))


def unfold(total, share, out):
    for l in range(out.shape[1] // LANES):
        out[:, l * LANES : (l + 1) * LANES] = total[l * share : (l + 1) * share, :]


def row_sum_kernel(row_n, *refs):
    parts, refs = refs[:row_n], refs[row_n:]
    grads, messages = refs[: len(refs) // 2], refs[len(refs) // 2 :]
    rows = parts[0].shape[0]
    total = parts[0][...]
    for part in parts[1:]:
        total += part[...].astype(F32)
    total = total.astype(BF16)
    for message, grad in zip(messages, grads, strict=True):
        message[0:rows, :] = total
        message[rows:, :] = grad[...]


def row_sum(parts, grads):
    shape = (parts[0].shape[0] + grads[0].shape[0], LANES)
    return pl.pallas_call(
        functools.partial(row_sum_kernel, len(parts)),
        in_specs=[in_vmem()] * (len(parts) + len(grads)),
        out_specs=[in_vmem()] * len(grads),
        out_shape=[jax.ShapeDtypeStruct(shape, BF16)] * len(grads),
        compiler_params=params(),
    )(*parts, *grads)


def column_sum_kernel(res_total, col_n, *refs):
    parts, grad, refs = refs[: col_n - 1], refs[col_n - 1], refs[col_n:]
    own, refs = refs[0], refs[1:]
    grads, refs = refs[: (len(refs) - 4) // 2], refs[(len(refs) - 4) // 2 :]
    messages, (piece_out, left_out, bias_out, held) = refs[:-4], refs[-4:]
    share = piece_out.shape[0]
    rows = share + BIAS_ROWS
    me = lax.axis_index("col")
    for p, part in enumerate((own, *parts)):
        held[lax.rem(me - p + col_n, col_n)] = part[0:rows, :]
    total = held[0].astype(F32)
    for n in range(1, col_n):
        total += held[n].astype(F32)
    piece = total[0:share].astype(BF16)
    piece_out[...] = piece
    for message, other in zip(messages, grads, strict=True):
        message[0:share, :] = piece
        message[share:, :] = other[...]
    bias_out[...] = (total[share : share + 1] + total[share + 1 : share + 2]) * (1.0 / res_total)
    left = grad[...]
    for part in parts:
        left += part[rows:, :].astype(F32)
    unfold(left, left_out.shape[0], left_out)


def column_sum(parts, left_own, own, grads, share, left_shape, res_total):
    rows = share + grads[0].shape[0]
    operands = [*parts, left_own, own, *grads]
    shapes = [jax.ShapeDtypeStruct((rows, LANES), BF16)] * len(grads) + [
        jax.ShapeDtypeStruct((share, LANES), BF16),
        jax.ShapeDtypeStruct(left_shape, F32),
        jax.ShapeDtypeStruct((1, PAIR_FEATURES), F32),
    ]
    *messages, piece, left, bias = pl.pallas_call(
        functools.partial(column_sum_kernel, res_total, len(parts) + 1),
        in_specs=[in_vmem()] * len(operands),
        out_specs=[in_vmem()] * len(shapes),
        out_shape=shapes,
        scratch_shapes=[pltpu.VMEM((len(parts) + 1, share + BIAS_ROWS, LANES), BF16)],
        compiler_params=params(),
    )(*operands)
    return messages, piece, left, bias


def finish_kernel(scale, *refs):
    parts, (piece, grad, projection, right_out) = refs[:-4], refs[-4:]
    row_n = len(parts) + 1
    share = piece.shape[0]
    me = lax.axis_index("row")
    right = grad[...]
    for p, part in enumerate((piece, *parts)):
        start = pl.multiple_of(lax.rem(me - p + row_n, row_n) * share, share)
        projection[pl.ds(start, share), :] = part[0:share, :].astype(F32) * scale
        if p > 0:
            right += part[share:, :].astype(F32)
    unfold(right, right_out.shape[0], right_out)


def finish(parts, piece, right_own, right_shape, scale):
    operands = [*parts, piece, right_own]
    return pl.pallas_call(
        functools.partial(finish_kernel, scale),
        in_specs=[in_vmem()] * len(operands),
        out_specs=[in_vmem()] * 2,
        out_shape=[
            jax.ShapeDtypeStruct((piece.shape[0] * (len(parts) + 1), PAIR_FEATURES), F32),
            jax.ShapeDtypeStruct(right_shape, F32),
        ],
        compiler_params=params(),
    )(*operands)


def shift(x, axis, distance):
    count = lax.axis_size(axis)
    return lax.ppermute(x, axis, [(n, (n + distance) % count) for n in range(count)])


def gather(x, axis):
    return [shift(x, axis, d) for d in range(1, lax.axis_size(axis))]


def exchange(parts, axis):
    return [shift(part, axis, d) for d, part in enumerate(parts, 1)]


def local(
    first_homolog_features, second_homolog_features, final_projection_matrix, output_bias, cotangent
):
    i_n, j_n, _ = cotangent.shape
    row_n, col_n = lax.axis_size("row"), lax.axis_size("col")
    sequences = second_homolog_features.shape[0] * row_n
    channels = final_projection_matrix.shape[0]
    res_total = i_n * row_n
    a_pieces = gather(first_homolog_features, "col")
    b_pieces = gather(second_homolog_features, "row")
    y, y2, wt, bias_rows, a_own, b_own, g = prepare(
        first_homolog_features,
        second_homolog_features,
        final_projection_matrix,
        cotangent.reshape(i_n * j_n, PAIR_FEATURES),
        i_n,
        j_n,
    )
    a_pieces = [a_own] + a_pieces
    b_pieces = [b_own] + b_pieces

    x, (row_own, *messages) = outer(a_pieces, b_pieces, g, bias_rows, i_n, j_n, sequences)
    row_parts = [row_own] + exchange(messages, "row")
    left_own, *left_grads = gradient(b_pieces, "row", "col", y, col_n, i_n, j_n, sequences)
    messages = row_sum(row_parts, left_grads)
    col_parts = exchange(messages, "col")
    right_own, *right_grads = gradient(a_pieces, "col", "row", y2, row_n, j_n, i_n, sequences)
    messages, piece, left_grad, bias_grad = column_sum(
        col_parts,
        left_own,
        messages[0],
        right_grads,
        channels // row_n,
        first_homolog_features.shape,
        res_total,
    )
    row_parts = exchange(messages, "row")
    pair_map = pair(x, wt, output_bias, sequences)
    projection, right_grad = finish(
        row_parts,
        piece,
        right_own,
        second_homolog_features.shape,
        1.0 / (sequences * res_total),
    )
    return (
        pair_map.reshape(i_n, j_n, PAIR_FEATURES),
        left_grad,
        right_grad,
        projection,
        bias_grad.reshape(PAIR_FEATURES),
    )


def solution(mesh):
    return jax.shard_map(
        local,
        mesh=mesh,
        in_specs=(
            P(("dp", "col"), "row"),
            P(("dp", "row"), "col"),
            P(),
            P(),
            P(("dp", "row"), "col", None),
        ),
        out_specs=(
            P(("dp", "row"), "col", None),
            P(("dp", "col"), "row"),
            P(("dp", "row"), "col"),
            P("dp", None),
            P("dp"),
        ),
        check_vma=False,
    )
```

```python
import functools

import jax
import jax.numpy as jnp
from jax import lax
from jax.experimental import pallas as pl
from jax.experimental.pallas import tpu as pltpu
from jax.sharding import PartitionSpec as P

PROJECTED_DEPTH = 32
PAIR_FEATURES = 128
GROUP = 8
STEPS = 4
BIAS_ROWS = 16
LANES = 128
F32 = jnp.float32
BF16 = jnp.bfloat16
MIB = 1024 * 1024

ROWS_BY_ROWS = (((1,), (1,)), ((), ()))
COLS_BY_COLS = (((0,), (0,)), ((), ()))


def params(sequences=0):
    return pltpu.CompilerParams(vmem_limit_bytes=min(10 + 10 * sequences // 32, 50) * MIB + 2 * MIB)


def whole(shape):
    return pl.BlockSpec(shape, lambda t: (0,) * len(shape))


def dot(x, y, dims=(((1,), (0,)), ((), ()))):
    return lax.dot_general(x, y, dims, preferred_element_type=F32)


def load_kernel(a_hbm, b_hbm, w_hbm, g_hbm, we_ref, wt_ref, a_ref, b_ref, w_ref, g_ref, w32, sems):
    depth = PROJECTED_DEPTH
    copies = [
        pltpu.make_async_copy(source, target, sems.at[n])
        for n, (source, target) in enumerate(
            [(w_hbm, w_ref), (g_hbm, g_ref), (a_hbm, a_ref), (b_hbm, b_ref)]
        )
    ]
    for copy in copies:
        copy.start()
    copies[0].wait()
    w32[...] = w_ref[...].astype(F32)
    for e in range(depth):
        block = w32[pl.ds(e, depth, stride=depth), :]
        we_ref[e * depth : (e + 1) * depth, :] = block.astype(BF16)
    wt_ref[...] = we_ref[...].astype(F32).T.astype(BF16)
    for copy in copies[1:]:
        copy.wait()


def in_vmem():
    return pl.BlockSpec(memory_space=pltpu.VMEM)


def load(a, b, w, g):
    shapes = [
        jax.ShapeDtypeStruct(w.shape, BF16),
        jax.ShapeDtypeStruct(w.shape[::-1], BF16),
        *[jax.ShapeDtypeStruct(x.shape, BF16) for x in (a, b, w, g)],
    ]
    return pl.pallas_call(
        load_kernel,
        in_specs=[pl.BlockSpec(memory_space=pltpu.HBM)] * 4,
        out_specs=[in_vmem()] * len(shapes),
        out_shape=shapes,
        scratch_shapes=[pltpu.VMEM(w.shape, F32), pltpu.SemaphoreType.DMA((4,))],
        compiler_params=params(),
        cost_estimate=pl.CostEstimate(
            flops=1000 * w.size, bytes_accessed=16 * w.size, transcendentals=0
        ),
    )(*[pltpu.with_memory_space_constraint(x, pltpu.HBM) for x in (a, b, w, g)])


def stack_kernel(*refs):
    half = len(refs) * 2 // 3
    for n, out in enumerate(refs[half:]):
        first, second = refs[2 * n], refs[2 * n + 1]
        rows = first.shape[0]
        both = jnp.concatenate([first[...].astype(F32), second[...].astype(F32)], axis=0)
        out[...] = both.astype(BF16)


def stack(*pairs):
    shapes = [
        jax.ShapeDtypeStruct((2 * first.shape[0], first.shape[1]), BF16) for first, _ in pairs
    ]
    operands = [x for pair in pairs for x in pair]
    return pl.pallas_call(
        stack_kernel,
        in_specs=[in_vmem()] * len(operands),
        out_specs=[in_vmem()] * len(shapes),
        out_shape=shapes,
        compiler_params=params(),
    )(*operands)


def prepare_kernel(i_n, j_n, we_ref, g_ref, y_ref, gt_ref, bias_ref, g32):
    g32[...] = g_ref[...].astype(F32)
    total = jnp.sum(g32[...], axis=0, keepdims=True)
    high = total.astype(BF16).astype(F32)
    row = lax.broadcasted_iota(jnp.int32, (BIAS_ROWS, PAIR_FEATURES), 0)
    bias_ref[...] = jnp.where(row == 0, high, jnp.where(row == 1, total - high, 0.0)).astype(BF16)
    size = y_ref.shape[0] // STEPS

    @pl.loop(0, STEPS)
    def _(t):
        rows = pl.ds(pl.multiple_of(t * size, size), size)
        y_ref[rows, :] = dot(we_ref[rows, :], g_ref[...], ROWS_BY_ROWS).astype(BF16)


    for j in range(j_n):
        gt_ref[j * i_n : (j + 1) * i_n, :] = g32[pl.ds(j, i_n, stride=j_n), :].astype(BF16)


def prepare(we, g, i_n, j_n):
    pairs = i_n * j_n
    channels = we.shape[0]
    shapes = [
        jax.ShapeDtypeStruct((channels, pairs), BF16),
        jax.ShapeDtypeStruct(g.shape, BF16),
        jax.ShapeDtypeStruct((BIAS_ROWS, PAIR_FEATURES), BF16),
    ]
    return pl.pallas_call(
        functools.partial(prepare_kernel, i_n, j_n),
        in_specs=[in_vmem()] * 2,
        out_specs=[in_vmem()] * len(shapes),
        out_shape=shapes,
        scratch_shapes=[pltpu.VMEM(g.shape, F32)],
        compiler_params=params(16),
        cost_estimate=pl.CostEstimate(
            flops=2 * pairs * channels * PAIR_FEATURES,
            bytes_accessed=4 * pairs * channels,
            transcendentals=0,
        ),
    )(we, g)


def join(pieces, axis, held):
    count = len(pieces)
    depth = pieces[0].shape[0] // 2
    me = lax.axis_index(axis)
    odd = lax.rem(me, 2)
    home = lax.div(me, 2)
    for p, piece in enumerate(pieces):
        start = lax.rem(home - p + count, count) * 2 * depth
        both = piece[...].astype(F32)
        for n in range(2):
            place = start + (1 - odd if n else odd) * depth
            held[pl.ds(pl.multiple_of(place, depth), depth), :] = both[n * depth : (n + 1) * depth]


def repeat_matrix(sequences):
    shape = (sequences, GROUP * sequences)
    lane = lax.broadcasted_iota(jnp.int32, shape, 1)
    row = lax.broadcasted_iota(jnp.int32, shape, 0)
    return (lax.rem(lane, sequences) == row).astype(BF16)


def spread(held, wide):
    both = dot(held[...].T.astype(BF16), repeat_matrix(held.shape[0]))
    for l in range(wide.shape[0]):
        wide[l] = both[:, l * LANES : (l + 1) * LANES]


def tiles_of(sequences, tile):
    lane = lax.broadcasted_iota(jnp.int32, (1, LANES), 1) + tile * LANES
    return [
        (m, lax.div(lane, sequences) == m)
        for m in range(GROUP)
        if m * sequences < (tile + 1) * LANES and (m + 1) * sequences > tile * LANES
    ]


def fill_diagonal(wide, diagonal, slot, channel, positions, sequences):
    for l in range(wide.shape[0]):
        block = wide[l, pl.ds(channel, positions, stride=PROJECTED_DEPTH), :].astype(BF16)
        for m, mask in tiles_of(sequences, l):
            diagonal[slot, m * positions : (m + 1) * positions, l * LANES : (l + 1) * LANES] = (
                block * mask.astype(F32).astype(BF16)
            )


def parts_shapes(count, rows):
    return [jax.ShapeDtypeStruct((rows, LANES), F32)] + [
        jax.ShapeDtypeStruct((rows, LANES), BF16)
    ] * (count - 1)


def outer_kernel(i_n, j_n, row_n, col_n, *refs):
    depth = PROJECTED_DEPTH
    a_pieces, refs = refs[: col_n // 2], refs[col_n // 2 :]
    b_pieces, refs = refs[: row_n // 2], refs[row_n // 2 :]
    (g_ref, bias_ref, x_ref, a_wide, b_wide), refs = refs[:5], refs[5:]
    messages, refs = refs[:row_n], refs[row_n:]
    a_held, b_held, left, diagonal, total, ordered = refs
    sequences = a_held.shape[0]
    groups = i_n // GROUP
    per_step = depth // STEPS
    span = GROUP * j_n

    join(a_pieces, "col", a_held)
    join(b_pieces, "row", b_held)
    spread(a_held, a_wide)
    for l in range(a_wide.shape[0]):
        members = tiles_of(sequences, l)
        for k in range(groups):
            block = jnp.zeros((depth, LANES), F32)
            for m, mask in members:
                start = (k * GROUP + m) * depth
                block = jnp.where(mask, a_wide[l, start : start + depth, :], block)
            left[k * depth : (k + 1) * depth, l * LANES : (l + 1) * LANES] = block.astype(BF16)
    spread(b_held, b_wide)
    diagonal[...] = jnp.zeros(diagonal.shape, BF16)

    @pl.loop(0, STEPS)
    def _(t):
        for e in range(per_step):
            fill_diagonal(b_wide, diagonal, e, t * per_step + e, j_n, sequences)
        size = per_step * depth
        rows = pl.ds(pl.multiple_of(t * size, size), size)
        x_part = x_ref.at[rows]
        for e in range(0, per_step, 2):
            right = diagonal[e : e + 2].reshape(2 * span, diagonal.shape[2])
            product = dot(left[...], right, ROWS_BY_ROWS).astype(BF16)
            for n in range(2):
                for k in range(groups):
                    x_part[(e + n) * depth : (e + n + 1) * depth, k * span : (k + 1) * span] = product[
                        k * depth : (k + 1) * depth, n * span : (n + 1) * span
                    ]
        total[rows, :] = dot(x_part[...], g_ref[...])

    for c in range(depth):
        ordered[c * depth : (c + 1) * depth, :] = total[pl.ds(c, depth, stride=depth), :]
    share = ordered.shape[0] // row_n
    me = lax.axis_index("row")
    for p, message in enumerate(messages):
        start = pl.multiple_of(lax.rem(me + p, row_n) * share, share)
        message[0:share, :] = ordered[pl.ds(start, share), :].astype(message.dtype)
        message[share:, :] = bias_ref[...].astype(message.dtype)


def outer(a_pieces, b_pieces, g, bias_rows, i_n, j_n, sequences):
    row_n, col_n = 2 * len(b_pieces), 2 * len(a_pieces)
    depth = PROJECTED_DEPTH
    channels = depth * depth
    pairs = i_n * j_n
    share = channels // row_n
    tiles = GROUP * sequences // LANES
    operands = [*a_pieces, *b_pieces, g, bias_rows]
    shapes = [jax.ShapeDtypeStruct((channels, pairs), BF16)]
    shapes += [jax.ShapeDtypeStruct((tiles, n * depth, LANES), F32) for n in (i_n, j_n)]
    shapes += parts_shapes(row_n, share + BIAS_ROWS)
    results = pl.pallas_call(
        functools.partial(outer_kernel, i_n, j_n, row_n, col_n),
        in_specs=[in_vmem()] * len(operands),
        out_specs=[in_vmem()] * len(shapes),
        out_shape=shapes,
        scratch_shapes=[
            pltpu.VMEM((sequences, i_n * depth), F32),
            pltpu.VMEM((sequences, j_n * depth), F32),
            pltpu.VMEM((i_n // GROUP * depth, GROUP * sequences), BF16),
            pltpu.VMEM((depth // STEPS, GROUP * j_n, GROUP * sequences), BF16),
            pltpu.VMEM((channels, PAIR_FEATURES), F32),
            pltpu.VMEM((channels, PAIR_FEATURES), F32),
        ],
        compiler_params=params(sequences),
        cost_estimate=pl.CostEstimate(
            flops=4 * pairs * channels * PAIR_FEATURES,
            bytes_accessed=2 * pairs * channels,
            transcendentals=0,
        ),
    )(*operands)
    return *results[:3], results[3:]


def gradient_kernel(axis, positions, others, sequences, *refs):
    depth = PROJECTED_DEPTH
    wide, refs = refs[0], refs[1:]
    parts = lax.axis_size(axis)
    diagonal, result, grown, grad = refs[-4:]
    sources, outs = refs[: -4 - parts], refs[-4 - parts : -4]
    per_step = depth // STEPS
    span = GROUP * others

    diagonal[...] = jnp.zeros(diagonal.shape, BF16)
    result[...] = jnp.zeros(result.shape, F32)

    @pl.loop(0, STEPS)
    def _(t):
        for n in range(per_step):
            fill_diagonal(wide, diagonal, n, t * per_step + n, others, sequences)
        size = per_step * depth
        rows = pl.ds(pl.multiple_of(t * size, size), size)
        if len(sources) == 1:
            part = sources[0].at[rows]
        else:
            part = dot(sources[0][rows, :], sources[1][...], ROWS_BY_ROWS).astype(BF16)
        for n in range(0, per_step, 2):
            blocks = [
                jnp.concatenate(
                    [
                        part[m * depth : (m + 1) * depth, k * span : (k + 1) * span]
                        for m in (n, n + 1)
                    ],
                    axis=1,
                )
                for k in range(positions // GROUP)
            ]
            result[...] += dot(
                jnp.concatenate(blocks, axis=0),
                diagonal[n : n + 2].reshape(2 * span, diagonal.shape[2]),
            )

    scaled = (result[...] * (1.0 / sequences)).astype(BF16)
    for l in range(scaled.shape[1] // LANES):
        members = dict(tiles_of(sequences, l))
        for k in range(positions // GROUP):
            block = scaled[k * depth : (k + 1) * depth, l * LANES : (l + 1) * LANES]
            for m in range(GROUP):
                start = (k * GROUP + m) * depth
                grown[start : start + depth, l * LANES : (l + 1) * LANES] = (
                    block * members[m].astype(F32).astype(BF16)
                    if m in members
                    else jnp.zeros((depth, LANES), BF16)
                )
    grad[...] = dot(repeat_matrix(sequences), grown[...], ROWS_BY_ROWS)
    share = sequences // parts
    me = lax.axis_index(axis)
    for p, out in enumerate(outs):
        mine = grad[pl.ds(pl.multiple_of(lax.rem(me + p, parts) * share, share), share), :]
        out[...] = jnp.concatenate(
            [mine[:, l * LANES : (l + 1) * LANES] for l in range(mine.shape[1] // LANES)], axis=0
        ).astype(out.dtype)


def gradient(wide, sources, axis, positions, others, sequences):
    depth = PROJECTED_DEPTH
    channels, pairs = depth * depth, positions * others
    parts = lax.axis_size(axis)
    rows = sequences // parts * positions * depth // LANES
    return pl.pallas_call(
        functools.partial(gradient_kernel, axis, positions, others, sequences),
        in_specs=[in_vmem()] * (len(sources) + 1),
        out_specs=[in_vmem()] * parts,
        out_shape=parts_shapes(parts, rows),
        scratch_shapes=[
            pltpu.VMEM((depth // STEPS, GROUP * others, GROUP * sequences), BF16),
            pltpu.VMEM((positions // GROUP * depth, GROUP * sequences), F32),
            pltpu.VMEM((positions * depth, GROUP * sequences), BF16),
            pltpu.VMEM((sequences, positions * depth), F32),
        ],
        compiler_params=params(sequences),
        cost_estimate=pl.CostEstimate(
            flops=2 * len(sources) * pairs * channels * PAIR_FEATURES,
            bytes_accessed=2 * pairs * channels,
            transcendentals=0,
        ),
    )(wide, *sources)


def pair_kernel(sequences, x_ref, wt_ref, bias_ref, out_ref):
    product = dot(wt_ref[...], x_ref[...])
    out_ref[...] = (product.T * (1.0 / sequences) + bias_ref[...]).astype(BF16)


def pair(x, wt, output_bias, sequences):
    channels, pairs = x.shape
    count = 3
    size = pairs // count
    return pl.pallas_call(
        functools.partial(pair_kernel, sequences),
        grid=(count,),
        in_specs=[
            pl.BlockSpec((channels, size), lambda t: (0, t)),
            whole(wt.shape),
            whole((1, PAIR_FEATURES)),
        ],
        out_specs=pl.BlockSpec((size, PAIR_FEATURES), lambda t: (t, 0)),
        out_shape=jax.ShapeDtypeStruct((pairs, PAIR_FEATURES), BF16),
        compiler_params=params(),
        cost_estimate=pl.CostEstimate(
            flops=4 * pairs * channels * PAIR_FEATURES,
            bytes_accessed=2 * pairs * channels,
            transcendentals=0,
        ),
    )(x, wt, output_bias.reshape(1, PAIR_FEATURES))


def unfold(total, share, out):
    for l in range(out.shape[1] // LANES):
        out[:, l * LANES : (l + 1) * LANES] = total[l * share : (l + 1) * share, :]


def row_sum_kernel(row_n, *refs):
    parts, refs = refs[:row_n], refs[row_n:]
    grads, messages = refs[: len(refs) // 2], refs[len(refs) // 2 :]
    rows = parts[0].shape[0]
    total = parts[0][...]
    for part in parts[1:]:
        total += part[...].astype(F32)
    total = total.astype(BF16)
    for message, grad in zip(messages, grads, strict=True):
        message[0:rows, :] = total
        message[rows:, :] = grad[...]


def row_sum(parts, grads):
    shape = (parts[0].shape[0] + grads[0].shape[0], LANES)
    return pl.pallas_call(
        functools.partial(row_sum_kernel, len(parts)),
        in_specs=[in_vmem()] * (len(parts) + len(grads)),
        out_specs=[in_vmem()] * len(grads),
        out_shape=[jax.ShapeDtypeStruct(shape, BF16)] * len(grads),
        compiler_params=params(),
    )(*parts, *grads)


def column_sum_kernel(res_total, col_n, *refs):
    parts, grad, refs = refs[: col_n - 1], refs[col_n - 1], refs[col_n:]
    own, refs = refs[0], refs[1:]
    grads, refs = refs[: (len(refs) - 4) // 2], refs[(len(refs) - 4) // 2 :]
    messages, (piece_out, left_out, bias_out, held) = refs[:-4], refs[-4:]
    share = piece_out.shape[0]
    rows = share + BIAS_ROWS
    me = lax.axis_index("col")
    for p, part in enumerate((own, *parts)):
        held[lax.rem(me - p + col_n, col_n)] = part[0:rows, :]
    total = held[0].astype(F32)
    for n in range(1, col_n):
        total += held[n].astype(F32)
    piece = total[0:share].astype(BF16)
    piece_out[...] = piece
    for message, other in zip(messages, grads, strict=True):
        message[0:share, :] = piece
        message[share:, :] = other[...]
    bias_out[...] = (total[share : share + 1] + total[share + 1 : share + 2]) * (1.0 / res_total)
    left = grad[...]
    for part in parts:
        left += part[rows:, :].astype(F32)
    unfold(left, left_out.shape[0], left_out)


def column_sum(parts, left_own, own, grads, share, left_shape, res_total):
    rows = share + grads[0].shape[0]
    operands = [*parts, left_own, own, *grads]
    shapes = [jax.ShapeDtypeStruct((rows, LANES), BF16)] * len(grads) + [
        jax.ShapeDtypeStruct((share, LANES), BF16),
        jax.ShapeDtypeStruct(left_shape, F32),
        jax.ShapeDtypeStruct((1, PAIR_FEATURES), F32),
    ]
    *messages, piece, left, bias = pl.pallas_call(
        functools.partial(column_sum_kernel, res_total, len(parts) + 1),
        in_specs=[in_vmem()] * len(operands),
        out_specs=[in_vmem()] * len(shapes),
        out_shape=shapes,
        scratch_shapes=[pltpu.VMEM((len(parts) + 1, share + BIAS_ROWS, LANES), BF16)],
        compiler_params=params(),
    )(*operands)
    return messages, piece, left, bias


def finish_kernel(scale, *refs):
    parts, (piece, grad, projection, right_out) = refs[:-4], refs[-4:]
    row_n = len(parts) + 1
    share = piece.shape[0]
    me = lax.axis_index("row")
    right = grad[...]
    for p, part in enumerate((piece, *parts)):
        start = pl.multiple_of(lax.rem(me - p + row_n, row_n) * share, share)
        projection[pl.ds(start, share), :] = part[0:share, :].astype(F32) * scale
        if p > 0:
            right += part[share:, :].astype(F32)
    unfold(right, right_out.shape[0], right_out)


def finish(parts, piece, right_own, right_shape, scale):
    operands = [*parts, piece, right_own]
    return pl.pallas_call(
        functools.partial(finish_kernel, scale),
        in_specs=[in_vmem()] * len(operands),
        out_specs=[in_vmem()] * 2,
        out_shape=[
            jax.ShapeDtypeStruct((piece.shape[0] * (len(parts) + 1), PAIR_FEATURES), F32),
            jax.ShapeDtypeStruct(right_shape, F32),
        ],
        compiler_params=params(),
    )(*operands)


def shift(x, axis, distance):
    count = lax.axis_size(axis)
    return lax.ppermute(x, axis, [(n, (n + distance) % count) for n in range(count)])


def neighbour(x, axis):
    return lax.ppermute(x, axis, [(n, n ^ 1) for n in range(lax.axis_size(axis))])


def shift_pairs(x, axis):
    return [x] + [shift(x, axis, d) for d in range(2, lax.axis_size(axis), 2)]


def exchange(parts, axis):
    return [shift(part, axis, d) for d, part in enumerate(parts, 1)]


def local(
    first_homolog_features, second_homolog_features, final_projection_matrix, output_bias, cotangent
):
    i_n, j_n, _ = cotangent.shape
    row_n = lax.axis_size("row")
    sequences = second_homolog_features.shape[0] * row_n
    channels = final_projection_matrix.shape[0]
    res_total = i_n * row_n
    a_near = neighbour(first_homolog_features, "col")
    b_near = neighbour(second_homolog_features, "row")
    we, wt, a, b, w, g = load(
        first_homolog_features,
        second_homolog_features,
        final_projection_matrix,
        cotangent.reshape(i_n * j_n, PAIR_FEATURES),
    )
    a_pair, b_pair = stack((a, a_near), (b, b_near))
    a_pieces = shift_pairs(a_pair, "col")
    b_pieces = shift_pairs(b_pair, "row")
    y, gt, bias_rows = prepare(we, g, i_n, j_n)

    x, a_wide, b_wide, (row_own, *messages) = outer(
        a_pieces, b_pieces, g, bias_rows, i_n, j_n, sequences
    )
    row_parts = [row_own] + exchange(messages, "row")
    left_own, *left_grads = gradient(b_wide, [y], "col", i_n, j_n, sequences)
    messages = row_sum(row_parts, left_grads)
    col_parts = exchange(messages, "col")
    right_own, *right_grads = gradient(a_wide, [w, gt], "row", j_n, i_n, sequences)
    messages, piece, left_grad, bias_grad = column_sum(
        col_parts,
        left_own,
        messages[0],
        right_grads,
        channels // row_n,
        first_homolog_features.shape,
        res_total,
    )
    row_parts = exchange(messages, "row")
    pair_map = pair(x, wt, output_bias, sequences)
    projection, right_grad = finish(
        row_parts,
        piece,
        right_own,
        second_homolog_features.shape,
        1.0 / (sequences * res_total),
    )
    return (
        pair_map.reshape(i_n, j_n, PAIR_FEATURES),
        left_grad,
        right_grad,
        projection,
        bias_grad.reshape(PAIR_FEATURES),
    )


def solution(mesh):
    return jax.shard_map(
        local,
        mesh=mesh,
        in_specs=(
            P(("dp", "col"), "row"),
            P(("dp", "row"), "col"),
            P(),
            P(),
            P(("dp", "row"), "col", None),
        ),
        out_specs=(
            P(("dp", "row"), "col", None),
            P(("dp", "col"), "row"),
            P(("dp", "row"), "col"),
            P("dp", None),
            P("dp"),
        ),
        check_vma=False,
    )
```

```python
import functools

import jax
import jax.numpy as jnp
from jax import lax
from jax.experimental import pallas as pl
from jax.experimental.pallas import tpu as pltpu
from jax.sharding import PartitionSpec as P

PROJECTED_DEPTH = 32
PAIR_FEATURES = 128
GROUP = 8
STEPS = 4
CHUNKS = 2
BIAS_ROWS = 16
LANES = 128
F32 = jnp.float32
BF16 = jnp.bfloat16
MIB = 1024 * 1024

ROWS_BY_ROWS = (((1,), (1,)), ((), ()))
COLS_BY_COLS = (((0,), (0,)), ((), ()))


def params(sequences=0):
    return pltpu.CompilerParams(vmem_limit_bytes=min(10 + 10 * sequences // 32, 50) * MIB + 2 * MIB)


def whole(shape):
    return pl.BlockSpec(shape, lambda t: (0,) * len(shape))


def dot(x, y, dims=(((1,), (0,)), ((), ()))):
    return lax.dot_general(x, y, dims, preferred_element_type=F32)


def load_kernel(a_hbm, b_hbm, w_hbm, g_hbm, we_ref, wt_ref, a_ref, b_ref, w_ref, g_ref, w32, sems):
    depth = PROJECTED_DEPTH
    copies = [
        pltpu.make_async_copy(source, target, sems.at[n])
        for n, (source, target) in enumerate(
            [(w_hbm, w_ref), (g_hbm, g_ref), (a_hbm, a_ref), (b_hbm, b_ref)]
        )
    ]
    for copy in copies:
        copy.start()
    copies[0].wait()
    w32[...] = w_ref[...].astype(F32)
    for e in range(depth):
        block = w32[pl.ds(e, depth, stride=depth), :]
        we_ref[e * depth : (e + 1) * depth, :] = block.astype(BF16)
    wt_ref[...] = we_ref[...].astype(F32).T.astype(BF16)
    for copy in copies[1:]:
        copy.wait()


def in_vmem():
    return pl.BlockSpec(memory_space=pltpu.VMEM)


def load(a, b, w, g):
    shapes = [
        jax.ShapeDtypeStruct(w.shape, BF16),
        jax.ShapeDtypeStruct(w.shape[::-1], BF16),
        *[jax.ShapeDtypeStruct(x.shape, BF16) for x in (a, b, w, g)],
    ]
    return pl.pallas_call(
        load_kernel,
        in_specs=[pl.BlockSpec(memory_space=pltpu.HBM)] * 4,
        out_specs=[in_vmem()] * len(shapes),
        out_shape=shapes,
        scratch_shapes=[pltpu.VMEM(w.shape, F32), pltpu.SemaphoreType.DMA((4,))],
        compiler_params=params(),
        cost_estimate=pl.CostEstimate(
            flops=1000 * w.size, bytes_accessed=16 * w.size, transcendentals=0
        ),
    )(*[pltpu.with_memory_space_constraint(x, pltpu.HBM) for x in (a, b, w, g)])


def stack_kernel(*refs):
    half = len(refs) * 2 // 3
    for n, out in enumerate(refs[half:]):
        first, second = refs[2 * n], refs[2 * n + 1]
        rows = first.shape[0]
        both = jnp.concatenate([first[...].astype(F32), second[...].astype(F32)], axis=0)
        out[...] = both.astype(BF16)


def stack(*pairs):
    shapes = [
        jax.ShapeDtypeStruct((2 * first.shape[0], first.shape[1]), BF16) for first, _ in pairs
    ]
    operands = [x for pair in pairs for x in pair]
    return pl.pallas_call(
        stack_kernel,
        in_specs=[in_vmem()] * len(operands),
        out_specs=[in_vmem()] * len(shapes),
        out_shape=shapes,
        compiler_params=params(),
    )(*operands)


def prepare_kernel(i_n, j_n, we_ref, g_ref, y_ref, gt_ref, bias_ref, g32):
    g32[...] = g_ref[...].astype(F32)
    total = jnp.sum(g32[...], axis=0, keepdims=True)
    high = total.astype(BF16).astype(F32)
    row = lax.broadcasted_iota(jnp.int32, (BIAS_ROWS, PAIR_FEATURES), 0)
    bias_ref[...] = jnp.where(row == 0, high, jnp.where(row == 1, total - high, 0.0)).astype(BF16)
    size = y_ref.shape[0] // STEPS

    @pl.loop(0, STEPS)
    def _(t):
        rows = pl.ds(pl.multiple_of(t * size, size), size)
        y_ref[rows, :] = dot(we_ref[rows, :], g_ref[...], ROWS_BY_ROWS).astype(BF16)


    for j in range(j_n):
        gt_ref[j * i_n : (j + 1) * i_n, :] = g32[pl.ds(j, i_n, stride=j_n), :].astype(BF16)


def prepare(we, g, i_n, j_n):
    pairs = i_n * j_n
    channels = we.shape[0]
    shapes = [
        jax.ShapeDtypeStruct((channels, pairs), BF16),
        jax.ShapeDtypeStruct(g.shape, BF16),
        jax.ShapeDtypeStruct((BIAS_ROWS, PAIR_FEATURES), BF16),
    ]
    return pl.pallas_call(
        functools.partial(prepare_kernel, i_n, j_n),
        in_specs=[in_vmem()] * 2,
        out_specs=[in_vmem()] * len(shapes),
        out_shape=shapes,
        scratch_shapes=[pltpu.VMEM(g.shape, F32)],
        compiler_params=params(16),
        cost_estimate=pl.CostEstimate(
            flops=2 * pairs * channels * PAIR_FEATURES,
            bytes_accessed=4 * pairs * channels,
            transcendentals=0,
        ),
    )(we, g)


def join(pieces, axis, held):
    count = len(pieces)
    depth = pieces[0].shape[0] // 2
    me = lax.axis_index(axis)
    odd = lax.rem(me, 2)
    home = lax.div(me, 2)
    for p, piece in enumerate(pieces):
        start = lax.rem(home - p + count, count) * 2 * depth
        both = piece[...].astype(F32)
        for n in range(2):
            place = start + (1 - odd if n else odd) * depth
            held[pl.ds(pl.multiple_of(place, depth), depth), :] = both[n * depth : (n + 1) * depth]


def repeat_matrix(sequences):
    shape = (sequences, GROUP * sequences)
    lane = lax.broadcasted_iota(jnp.int32, shape, 1)
    row = lax.broadcasted_iota(jnp.int32, shape, 0)
    return (lax.rem(lane, sequences) == row).astype(BF16)


def spread(held, wide):
    both = dot(held[...].T.astype(BF16), repeat_matrix(held.shape[0]))
    for l in range(wide.shape[0]):
        wide[l] = both[:, l * LANES : (l + 1) * LANES]


def tiles_of(sequences, tile):
    lane = lax.broadcasted_iota(jnp.int32, (1, LANES), 1) + tile * LANES
    return [
        (m, lax.div(lane, sequences) == m)
        for m in range(GROUP)
        if m * sequences < (tile + 1) * LANES and (m + 1) * sequences > tile * LANES
    ]


def fill_diagonal(wide, diagonal, slot, channel, positions, sequences):
    for l in range(wide.shape[0]):
        block = wide[l, pl.ds(channel, positions, stride=PROJECTED_DEPTH), :].astype(BF16)
        for m, mask in tiles_of(sequences, l):
            diagonal[slot, m * positions : (m + 1) * positions, l * LANES : (l + 1) * LANES] = (
                block * mask.astype(F32).astype(BF16)
            )


def parts_shapes(count, rows):
    return [jax.ShapeDtypeStruct((rows, LANES), F32)] + [
        jax.ShapeDtypeStruct((rows, LANES), BF16)
    ] * (count - 1)


def outer_kernel(i_n, j_n, row_n, col_n, *refs):
    depth = PROJECTED_DEPTH
    a_pieces, refs = refs[: col_n // 2], refs[col_n // 2 :]
    b_pieces, refs = refs[: row_n // 2], refs[row_n // 2 :]
    (g_ref, bias_ref, x_ref, a_wide, b_wide), refs = refs[:5], refs[5:]
    messages, refs = refs[:row_n], refs[row_n:]
    a_held, b_held, left, diagonal, total, ordered = refs
    sequences = a_held.shape[0]
    groups = i_n // GROUP
    per_step = depth // CHUNKS
    span = GROUP * j_n

    join(a_pieces, "col", a_held)
    join(b_pieces, "row", b_held)
    spread(a_held, a_wide)
    for l in range(a_wide.shape[0]):
        members = tiles_of(sequences, l)
        for k in range(groups):
            block = jnp.zeros((depth, LANES), F32)
            for m, mask in members:
                start = (k * GROUP + m) * depth
                block = jnp.where(mask, a_wide[l, start : start + depth, :], block)
            left[k * depth : (k + 1) * depth, l * LANES : (l + 1) * LANES] = block.astype(BF16)
    spread(b_held, b_wide)
    diagonal[...] = jnp.zeros(diagonal.shape, BF16)

    @pl.loop(0, CHUNKS)
    def _(t):
        for e in range(per_step):
            fill_diagonal(b_wide, diagonal, e, t * per_step + e, j_n, sequences)
        size = per_step * depth
        rows = pl.ds(pl.multiple_of(t * size, size), size)
        x_part = x_ref.at[rows]
        for e in range(0, per_step, 2):
            right = diagonal[e : e + 2].reshape(2 * span, diagonal.shape[2])
            product = dot(left[...], right, ROWS_BY_ROWS).astype(BF16)
            for n in range(2):
                for k in range(groups):
                    x_part[(e + n) * depth : (e + n + 1) * depth, k * span : (k + 1) * span] = product[
                        k * depth : (k + 1) * depth, n * span : (n + 1) * span
                    ]
        total[rows, :] = dot(x_part[...], g_ref[...])

    for c in range(depth):
        ordered[c * depth : (c + 1) * depth, :] = total[pl.ds(c, depth, stride=depth), :]
    share = ordered.shape[0] // row_n
    me = lax.axis_index("row")
    for p, message in enumerate(messages):
        start = pl.multiple_of(lax.rem(me + p, row_n) * share, share)
        message[0:share, :] = ordered[pl.ds(start, share), :].astype(message.dtype)
        message[share:, :] = bias_ref[...].astype(message.dtype)


def outer(a_pieces, b_pieces, g, bias_rows, i_n, j_n, sequences):
    row_n, col_n = 2 * len(b_pieces), 2 * len(a_pieces)
    depth = PROJECTED_DEPTH
    channels = depth * depth
    pairs = i_n * j_n
    share = channels // row_n
    tiles = GROUP * sequences // LANES
    operands = [*a_pieces, *b_pieces, g, bias_rows]
    shapes = [jax.ShapeDtypeStruct((channels, pairs), BF16)]
    shapes += [jax.ShapeDtypeStruct((tiles, n * depth, LANES), F32) for n in (i_n, j_n)]
    shapes += parts_shapes(row_n, share + BIAS_ROWS)
    results = pl.pallas_call(
        functools.partial(outer_kernel, i_n, j_n, row_n, col_n),
        in_specs=[in_vmem()] * len(operands),
        out_specs=[in_vmem()] * len(shapes),
        out_shape=shapes,
        scratch_shapes=[
            pltpu.VMEM((sequences, i_n * depth), F32),
            pltpu.VMEM((sequences, j_n * depth), F32),
            pltpu.VMEM((i_n // GROUP * depth, GROUP * sequences), BF16),
            pltpu.VMEM((depth // CHUNKS, GROUP * j_n, GROUP * sequences), BF16),
            pltpu.VMEM((channels, PAIR_FEATURES), F32),
            pltpu.VMEM((channels, PAIR_FEATURES), F32),
        ],
        compiler_params=params(sequences),
        cost_estimate=pl.CostEstimate(
            flops=4 * pairs * channels * PAIR_FEATURES,
            bytes_accessed=2 * pairs * channels,
            transcendentals=0,
        ),
    )(*operands)
    return *results[:3], results[3:]


def gradient_kernel(axis, positions, others, sequences, *refs):
    depth = PROJECTED_DEPTH
    wide, refs = refs[0], refs[1:]
    parts = lax.axis_size(axis)
    diagonal, result, grown, grad, product = refs[-5:]
    sources, outs = refs[: -5 - parts], refs[-5 - parts : -5]
    per_step = depth // CHUNKS
    span = GROUP * others

    diagonal[...] = jnp.zeros(diagonal.shape, BF16)
    result[...] = jnp.zeros(result.shape, F32)

    @pl.loop(0, CHUNKS)
    def _(t):
        for n in range(per_step):
            fill_diagonal(wide, diagonal, n, t * per_step + n, others, sequences)
        size = per_step * depth
        rows = pl.ds(pl.multiple_of(t * size, size), size)
        if len(sources) == 1:
            part = sources[0].at[rows]
        else:
            part = product
            for n in range(0, size, size // 2):
                block = sources[0][pl.ds(pl.multiple_of(t * size + n, size // 2), size // 2), :]
                part[n : n + size // 2, :] = dot(block, sources[1][...], ROWS_BY_ROWS).astype(BF16)
        for n in range(0, per_step, 2):
            blocks = [
                jnp.concatenate(
                    [
                        part[m * depth : (m + 1) * depth, k * span : (k + 1) * span]
                        for m in (n, n + 1)
                    ],
                    axis=1,
                )
                for k in range(positions // GROUP)
            ]
            result[...] += dot(
                jnp.concatenate(blocks, axis=0),
                diagonal[n : n + 2].reshape(2 * span, diagonal.shape[2]),
            )

    scaled = (result[...] * (1.0 / sequences)).astype(BF16)
    for l in range(scaled.shape[1] // LANES):
        members = dict(tiles_of(sequences, l))
        for k in range(positions // GROUP):
            block = scaled[k * depth : (k + 1) * depth, l * LANES : (l + 1) * LANES]
            for m in range(GROUP):
                start = (k * GROUP + m) * depth
                grown[start : start + depth, l * LANES : (l + 1) * LANES] = (
                    block * members[m].astype(F32).astype(BF16)
                    if m in members
                    else jnp.zeros((depth, LANES), BF16)
                )
    grad[...] = dot(repeat_matrix(sequences), grown[...], ROWS_BY_ROWS)
    share = sequences // parts
    me = lax.axis_index(axis)
    for p, out in enumerate(outs):
        mine = grad[pl.ds(pl.multiple_of(lax.rem(me + p, parts) * share, share), share), :]
        out[...] = jnp.concatenate(
            [mine[:, l * LANES : (l + 1) * LANES] for l in range(mine.shape[1] // LANES)], axis=0
        ).astype(out.dtype)


def gradient(wide, sources, axis, positions, others, sequences):
    depth = PROJECTED_DEPTH
    channels, pairs = depth * depth, positions * others
    parts = lax.axis_size(axis)
    rows = sequences // parts * positions * depth // LANES
    return pl.pallas_call(
        functools.partial(gradient_kernel, axis, positions, others, sequences),
        in_specs=[in_vmem()] * (len(sources) + 1),
        out_specs=[in_vmem()] * parts,
        out_shape=parts_shapes(parts, rows),
        scratch_shapes=[
            pltpu.VMEM((depth // CHUNKS, GROUP * others, GROUP * sequences), BF16),
            pltpu.VMEM((positions // GROUP * depth, GROUP * sequences), F32),
            pltpu.VMEM((positions * depth, GROUP * sequences), BF16),
            pltpu.VMEM((sequences, positions * depth), F32),
            pltpu.VMEM((channels // CHUNKS if len(sources) > 1 else 16, pairs), BF16),
        ],
        compiler_params=params(sequences),
        cost_estimate=pl.CostEstimate(
            flops=2 * len(sources) * pairs * channels * PAIR_FEATURES,
            bytes_accessed=2 * pairs * channels,
            transcendentals=0,
        ),
    )(wide, *sources)


def pair_kernel(sequences, x_ref, wt_ref, bias_ref, out_ref):
    product = dot(wt_ref[...], x_ref[...])
    out_ref[...] = (product.T * (1.0 / sequences) + bias_ref[...]).astype(BF16)


def pair(x, wt, output_bias, sequences):
    channels, pairs = x.shape
    count = 3
    size = pairs // count
    return pl.pallas_call(
        functools.partial(pair_kernel, sequences),
        grid=(count,),
        in_specs=[
            pl.BlockSpec((channels, size), lambda t: (0, t)),
            whole(wt.shape),
            whole((1, PAIR_FEATURES)),
        ],
        out_specs=pl.BlockSpec((size, PAIR_FEATURES), lambda t: (t, 0)),
        out_shape=jax.ShapeDtypeStruct((pairs, PAIR_FEATURES), BF16),
        compiler_params=params(),
        cost_estimate=pl.CostEstimate(
            flops=4 * pairs * channels * PAIR_FEATURES,
            bytes_accessed=2 * pairs * channels,
            transcendentals=0,
        ),
    )(x, wt, output_bias.reshape(1, PAIR_FEATURES))


def unfold(total, share, out):
    for l in range(out.shape[1] // LANES):
        out[:, l * LANES : (l + 1) * LANES] = total[l * share : (l + 1) * share, :]


def row_sum_kernel(row_n, *refs):
    parts, refs = refs[:row_n], refs[row_n:]
    grads, messages = refs[: len(refs) // 2], refs[len(refs) // 2 :]
    rows = parts[0].shape[0]
    total = parts[0][...]
    for part in parts[1:]:
        total += part[...].astype(F32)
    total = total.astype(BF16)
    for message, grad in zip(messages, grads, strict=True):
        message[0:rows, :] = total
        message[rows:, :] = grad[...]


def row_sum(parts, grads):
    shape = (parts[0].shape[0] + grads[0].shape[0], LANES)
    return pl.pallas_call(
        functools.partial(row_sum_kernel, len(parts)),
        in_specs=[in_vmem()] * (len(parts) + len(grads)),
        out_specs=[in_vmem()] * len(grads),
        out_shape=[jax.ShapeDtypeStruct(shape, BF16)] * len(grads),
        compiler_params=params(),
    )(*parts, *grads)


def column_sum_kernel(res_total, col_n, *refs):
    parts, grad, refs = refs[: col_n - 1], refs[col_n - 1], refs[col_n:]
    own, refs = refs[0], refs[1:]
    grads, refs = refs[: (len(refs) - 4) // 2], refs[(len(refs) - 4) // 2 :]
    messages, (piece_out, left_out, bias_out, held) = refs[:-4], refs[-4:]
    share = piece_out.shape[0]
    rows = share + BIAS_ROWS
    me = lax.axis_index("col")
    for p, part in enumerate((own, *parts)):
        held[lax.rem(me - p + col_n, col_n)] = part[0:rows, :]
    total = held[0].astype(F32)
    for n in range(1, col_n):
        total += held[n].astype(F32)
    piece = total[0:share].astype(BF16)
    piece_out[...] = piece
    for message, other in zip(messages, grads, strict=True):
        message[0:share, :] = piece
        message[share:, :] = other[...]
    bias_out[...] = (total[share : share + 1] + total[share + 1 : share + 2]) * (1.0 / res_total)
    left = grad[...]
    for part in parts:
        left += part[rows:, :].astype(F32)
    unfold(left, left_out.shape[0], left_out)


def column_sum(parts, left_own, own, grads, share, left_shape, res_total):
    rows = share + grads[0].shape[0]
    operands = [*parts, left_own, own, *grads]
    shapes = [jax.ShapeDtypeStruct((rows, LANES), BF16)] * len(grads) + [
        jax.ShapeDtypeStruct((share, LANES), BF16),
        jax.ShapeDtypeStruct(left_shape, F32),
        jax.ShapeDtypeStruct((1, PAIR_FEATURES), F32),
    ]
    *messages, piece, left, bias = pl.pallas_call(
        functools.partial(column_sum_kernel, res_total, len(parts) + 1),
        in_specs=[in_vmem()] * len(operands),
        out_specs=[in_vmem()] * len(shapes),
        out_shape=shapes,
        scratch_shapes=[pltpu.VMEM((len(parts) + 1, share + BIAS_ROWS, LANES), BF16)],
        compiler_params=params(),
    )(*operands)
    return messages, piece, left, bias


def finish_kernel(scale, *refs):
    parts, (piece, grad, projection, right_out) = refs[:-4], refs[-4:]
    row_n = len(parts) + 1
    share = piece.shape[0]
    me = lax.axis_index("row")
    right = grad[...]
    for p, part in enumerate((piece, *parts)):
        start = pl.multiple_of(lax.rem(me - p + row_n, row_n) * share, share)
        projection[pl.ds(start, share), :] = part[0:share, :].astype(F32) * scale
        if p > 0:
            right += part[share:, :].astype(F32)
    unfold(right, right_out.shape[0], right_out)


def finish(parts, piece, right_own, right_shape, scale):
    operands = [*parts, piece, right_own]
    return pl.pallas_call(
        functools.partial(finish_kernel, scale),
        in_specs=[in_vmem()] * len(operands),
        out_specs=[in_vmem()] * 2,
        out_shape=[
            jax.ShapeDtypeStruct((piece.shape[0] * (len(parts) + 1), PAIR_FEATURES), F32),
            jax.ShapeDtypeStruct(right_shape, F32),
        ],
        compiler_params=params(),
    )(*operands)


def shift(x, axis, distance):
    count = lax.axis_size(axis)
    return lax.ppermute(x, axis, [(n, (n + distance) % count) for n in range(count)])


def neighbour(x, axis):
    return lax.ppermute(x, axis, [(n, n ^ 1) for n in range(lax.axis_size(axis))])


def shift_pairs(x, axis):
    return [x] + [shift(x, axis, d) for d in range(2, lax.axis_size(axis), 2)]


def exchange(parts, axis):
    return [shift(part, axis, d) for d, part in enumerate(parts, 1)]


def local(
    first_homolog_features, second_homolog_features, final_projection_matrix, output_bias, cotangent
):
    i_n, j_n, _ = cotangent.shape
    row_n = lax.axis_size("row")
    sequences = second_homolog_features.shape[0] * row_n
    channels = final_projection_matrix.shape[0]
    res_total = i_n * row_n
    a_near = neighbour(first_homolog_features, "col")
    b_near = neighbour(second_homolog_features, "row")
    we, wt, a, b, w, g = load(
        first_homolog_features,
        second_homolog_features,
        final_projection_matrix,
        cotangent.reshape(i_n * j_n, PAIR_FEATURES),
    )
    a_pair, b_pair = stack((a, a_near), (b, b_near))
    a_pieces = shift_pairs(a_pair, "col")
    b_pieces = shift_pairs(b_pair, "row")
    y, gt, bias_rows = prepare(we, g, i_n, j_n)

    x, a_wide, b_wide, (row_own, *messages) = outer(
        a_pieces, b_pieces, g, bias_rows, i_n, j_n, sequences
    )
    row_parts = [row_own] + exchange(messages, "row")
    left_own, *left_grads = gradient(b_wide, [y], "col", i_n, j_n, sequences)
    messages = row_sum(row_parts, left_grads)
    col_parts = exchange(messages, "col")
    right_own, *right_grads = gradient(a_wide, [w, gt], "row", j_n, i_n, sequences)
    messages, piece, left_grad, bias_grad = column_sum(
        col_parts,
        left_own,
        messages[0],
        right_grads,
        channels // row_n,
        first_homolog_features.shape,
        res_total,
    )
    row_parts = exchange(messages, "row")
    pair_map = pair(x, wt, output_bias, sequences)
    projection, right_grad = finish(
        row_parts,
        piece,
        right_own,
        second_homolog_features.shape,
        1.0 / (sequences * res_total),
    )
    return (
        pair_map.reshape(i_n, j_n, PAIR_FEATURES),
        left_grad,
        right_grad,
        projection,
        bias_grad.reshape(PAIR_FEATURES),
    )


def solution(mesh):
    return jax.shard_map(
        local,
        mesh=mesh,
        in_specs=(
            P(("dp", "col"), "row"),
            P(("dp", "row"), "col"),
            P(),
            P(),
            P(("dp", "row"), "col", None),
        ),
        out_specs=(
            P(("dp", "row"), "col", None),
            P(("dp", "col"), "row"),
            P(("dp", "row"), "col"),
            P("dp", None),
            P("dp"),
        ),
        check_vma=False,
    )
```

```python
import functools

import jax
import jax.numpy as jnp
from jax import lax
from jax.experimental import pallas as pl
from jax.experimental.pallas import tpu as pltpu
from jax.sharding import PartitionSpec as P

PROJECTED_DEPTH = 32
PAIR_FEATURES = 128
GROUP = 8
STEPS = 4
CHUNKS = 2
BIAS_ROWS = 16
LANES = 128
F32 = jnp.float32
BF16 = jnp.bfloat16
MIB = 1024 * 1024

ROWS_BY_ROWS = (((1,), (1,)), ((), ()))
COLS_BY_COLS = (((0,), (0,)), ((), ()))


def params(sequences=0):
    return pltpu.CompilerParams(vmem_limit_bytes=min(10 + 10 * sequences // 32, 50) * MIB + 2 * MIB)


def whole(shape):
    return pl.BlockSpec(shape, lambda t: (0,) * len(shape))


def dot(x, y, dims=(((1,), (0,)), ((), ()))):
    return lax.dot_general(x, y, dims, preferred_element_type=F32)


def load_kernel(a_hbm, b_hbm, w_hbm, g_hbm, we_ref, wt_ref, a_ref, b_ref, w_ref, g_ref, w32, sems):
    depth = PROJECTED_DEPTH
    copies = [
        pltpu.make_async_copy(source, target, sems.at[n])
        for n, (source, target) in enumerate(
            [(w_hbm, w_ref), (g_hbm, g_ref), (a_hbm, a_ref), (b_hbm, b_ref)]
        )
    ]
    for copy in copies:
        copy.start()
    copies[0].wait()
    w32[...] = w_ref[...].astype(F32)
    for e in range(depth):
        block = w32[pl.ds(e, depth, stride=depth), :]
        we_ref[e * depth : (e + 1) * depth, :] = block.astype(BF16)
    wt_ref[...] = we_ref[...].astype(F32).T.astype(BF16)
    for copy in copies[1:]:
        copy.wait()


def in_vmem():
    return pl.BlockSpec(memory_space=pltpu.VMEM)


def load(a, b, w, g):
    shapes = [
        jax.ShapeDtypeStruct(w.shape, BF16),
        jax.ShapeDtypeStruct(w.shape[::-1], BF16),
        *[jax.ShapeDtypeStruct(x.shape, BF16) for x in (a, b, w, g)],
    ]
    return pl.pallas_call(
        load_kernel,
        in_specs=[pl.BlockSpec(memory_space=pltpu.HBM)] * 4,
        out_specs=[in_vmem()] * len(shapes),
        out_shape=shapes,
        scratch_shapes=[pltpu.VMEM(w.shape, F32), pltpu.SemaphoreType.DMA((4,))],
        compiler_params=params(),
        cost_estimate=pl.CostEstimate(
            flops=1000 * w.size, bytes_accessed=16 * w.size, transcendentals=0
        ),
    )(*[pltpu.with_memory_space_constraint(x, pltpu.HBM) for x in (a, b, w, g)])


def stack_kernel(*refs):
    half = len(refs) * 2 // 3
    for n, out in enumerate(refs[half:]):
        first, second = refs[2 * n], refs[2 * n + 1]
        rows = first.shape[0]
        both = jnp.concatenate([first[...].astype(F32), second[...].astype(F32)], axis=0)
        out[...] = both.astype(BF16)


def stack(*pairs):
    shapes = [
        jax.ShapeDtypeStruct((2 * first.shape[0], first.shape[1]), BF16) for first, _ in pairs
    ]
    operands = [x for pair in pairs for x in pair]
    return pl.pallas_call(
        stack_kernel,
        in_specs=[in_vmem()] * len(operands),
        out_specs=[in_vmem()] * len(shapes),
        out_shape=shapes,
        compiler_params=params(),
    )(*operands)


def prepare_kernel(i_n, j_n, we_ref, g_ref, y_ref, gt_ref, bias_ref, g32):
    g32[...] = g_ref[...].astype(F32)
    total = jnp.sum(g32[...], axis=0, keepdims=True)
    high = total.astype(BF16).astype(F32)
    row = lax.broadcasted_iota(jnp.int32, (BIAS_ROWS, PAIR_FEATURES), 0)
    bias_ref[...] = jnp.where(row == 0, high, jnp.where(row == 1, total - high, 0.0)).astype(BF16)
    size = y_ref.shape[0] // STEPS

    @pl.loop(0, STEPS)
    def _(t):
        rows = pl.ds(pl.multiple_of(t * size, size), size)
        y_ref[rows, :] = dot(we_ref[rows, :], g_ref[...], ROWS_BY_ROWS).astype(BF16)


    for j in range(j_n):
        gt_ref[j * i_n : (j + 1) * i_n, :] = g32[pl.ds(j, i_n, stride=j_n), :].astype(BF16)


def prepare(we, g, i_n, j_n):
    pairs = i_n * j_n
    channels = we.shape[0]
    shapes = [
        jax.ShapeDtypeStruct((channels, pairs), BF16),
        jax.ShapeDtypeStruct(g.shape, BF16),
        jax.ShapeDtypeStruct((BIAS_ROWS, PAIR_FEATURES), BF16),
    ]
    return pl.pallas_call(
        functools.partial(prepare_kernel, i_n, j_n),
        in_specs=[in_vmem()] * 2,
        out_specs=[in_vmem()] * len(shapes),
        out_shape=shapes,
        scratch_shapes=[pltpu.VMEM(g.shape, F32)],
        compiler_params=params(16),
        cost_estimate=pl.CostEstimate(
            flops=2 * pairs * channels * PAIR_FEATURES,
            bytes_accessed=4 * pairs * channels,
            transcendentals=0,
        ),
    )(we, g)


def join(pieces, axis, held):
    count = len(pieces)
    depth = pieces[0].shape[0] // 2
    me = lax.axis_index(axis)
    odd = lax.rem(me, 2)
    home = lax.div(me, 2)
    for p, piece in enumerate(pieces):
        start = lax.rem(home - p + count, count) * 2 * depth
        both = piece[...].astype(F32)
        for n in range(2):
            place = start + (1 - odd if n else odd) * depth
            held[pl.ds(pl.multiple_of(place, depth), depth), :] = both[n * depth : (n + 1) * depth]


def repeat_matrix(sequences):
    shape = (sequences, GROUP * sequences)
    lane = lax.broadcasted_iota(jnp.int32, shape, 1)
    row = lax.broadcasted_iota(jnp.int32, shape, 0)
    return (lax.rem(lane, sequences) == row).astype(BF16)


def spread(held, wide):
    both = dot(held[...].T.astype(BF16), repeat_matrix(held.shape[0]))
    for l in range(wide.shape[0]):
        wide[l] = both[:, l * LANES : (l + 1) * LANES]


def tiles_of(sequences, tile):
    lane = lax.broadcasted_iota(jnp.int32, (1, LANES), 1) + tile * LANES
    return [
        (m, lax.div(lane, sequences) == m)
        for m in range(GROUP)
        if m * sequences < (tile + 1) * LANES and (m + 1) * sequences > tile * LANES
    ]


def fill_diagonal(wide, diagonal, slot, channel, positions, sequences):
    for l in range(wide.shape[0]):
        block = wide[l, pl.ds(channel, positions, stride=PROJECTED_DEPTH), :].astype(BF16)
        for m, mask in tiles_of(sequences, l):
            diagonal[slot, m * positions : (m + 1) * positions, l * LANES : (l + 1) * LANES] = (
                block * mask.astype(F32).astype(BF16)
            )


def parts_shapes(count, rows):
    return [jax.ShapeDtypeStruct((rows, LANES), F32)] + [
        jax.ShapeDtypeStruct((rows, LANES), BF16)
    ] * (count - 1)


def outer_kernel(i_n, j_n, row_n, col_n, *refs):
    depth = PROJECTED_DEPTH
    a_pieces, refs = refs[: col_n // 2], refs[col_n // 2 :]
    b_pieces, refs = refs[: row_n // 2], refs[row_n // 2 :]
    (g_ref, bias_ref, x_ref, a_wide, b_wide), refs = refs[:5], refs[5:]
    messages, refs = refs[:row_n], refs[row_n:]
    a_held, b_held, left, diagonal, total = refs
    sequences = a_held.shape[0]
    groups = i_n // GROUP
    per_step = depth // CHUNKS
    span = GROUP * j_n

    join(a_pieces, "col", a_held)
    join(b_pieces, "row", b_held)
    spread(a_held, a_wide)
    for l in range(a_wide.shape[0]):
        members = tiles_of(sequences, l)
        for k in range(groups):
            block = jnp.zeros((depth, LANES), F32)
            for m, mask in members:
                start = (k * GROUP + m) * depth
                block = jnp.where(mask, a_wide[l, start : start + depth, :], block)
            left[k * depth : (k + 1) * depth, l * LANES : (l + 1) * LANES] = block.astype(BF16)
    spread(b_held, b_wide)
    diagonal[...] = jnp.zeros(diagonal.shape, BF16)

    @pl.loop(0, CHUNKS)
    def _(t):
        for e in range(per_step):
            fill_diagonal(b_wide, diagonal, e, t * per_step + e, j_n, sequences)
        size = per_step * depth
        rows = pl.ds(pl.multiple_of(t * size, size), size)
        x_part = x_ref.at[rows]
        for e in range(0, per_step, 2):
            right = diagonal[e : e + 2].reshape(2 * span, diagonal.shape[2])
            product = dot(left[...], right, ROWS_BY_ROWS).astype(BF16)
            for n in range(2):
                for k in range(groups):
                    x_part[(e + n) * depth : (e + n + 1) * depth, k * span : (k + 1) * span] = product[
                        k * depth : (k + 1) * depth, n * span : (n + 1) * span
                    ]
        total[rows, :] = dot(x_part[...], g_ref[...])

    share = total.shape[0] // row_n
    me = lax.axis_index("row")
    for p, message in enumerate(messages):
        start = lax.rem(me + p, row_n) * (share // depth)
        for n in range(share // depth):
            block = total[pl.ds(start + n, depth, stride=depth), :]
            message[n * depth : (n + 1) * depth, :] = block.astype(message.dtype)
        message[share:, :] = bias_ref[...].astype(message.dtype)


def outer(a_pieces, b_pieces, g, bias_rows, i_n, j_n, sequences):
    row_n, col_n = 2 * len(b_pieces), 2 * len(a_pieces)
    depth = PROJECTED_DEPTH
    channels = depth * depth
    pairs = i_n * j_n
    share = channels // row_n
    tiles = GROUP * sequences // LANES
    operands = [*a_pieces, *b_pieces, g, bias_rows]
    shapes = [jax.ShapeDtypeStruct((channels, pairs), BF16)]
    shapes += [jax.ShapeDtypeStruct((tiles, n * depth, LANES), F32) for n in (i_n, j_n)]
    shapes += parts_shapes(row_n, share + BIAS_ROWS)
    results = pl.pallas_call(
        functools.partial(outer_kernel, i_n, j_n, row_n, col_n),
        in_specs=[in_vmem()] * len(operands),
        out_specs=[in_vmem()] * len(shapes),
        out_shape=shapes,
        scratch_shapes=[
            pltpu.VMEM((sequences, i_n * depth), F32),
            pltpu.VMEM((sequences, j_n * depth), F32),
            pltpu.VMEM((i_n // GROUP * depth, GROUP * sequences), BF16),
            pltpu.VMEM((depth // CHUNKS, GROUP * j_n, GROUP * sequences), BF16),
            pltpu.VMEM((channels, PAIR_FEATURES), F32),
        ],
        compiler_params=params(sequences),
        cost_estimate=pl.CostEstimate(
            flops=4 * pairs * channels * PAIR_FEATURES,
            bytes_accessed=2 * pairs * channels,
            transcendentals=0,
        ),
    )(*operands)
    return *results[:3], results[3:]


def in_order(count):
    return lambda me: ([me], [[lax.rem(me + d, count)] for d in range(1, count)])


def in_pairs(count):
    def plan(me):
        near = me + 1 - 2 * lax.rem(me, 2)
        steps = range(0, count, 2)
        return [lax.rem(me + d, count) for d in steps], [[lax.rem(near + d, count) for d in steps]]

    return plan


def gradient_kernel(axis, plan, kept, positions, others, sequences, *refs):
    depth = PROJECTED_DEPTH
    wide, source, _ = refs[:3]
    outs = refs[3:-4]
    diagonal, result, grown, grad = refs[-4:]
    parts = lax.axis_size(axis)
    per_step = depth // CHUNKS
    span = GROUP * others

    diagonal[...] = jnp.zeros(diagonal.shape, BF16)
    result[...] = jnp.zeros(result.shape, F32)

    @pl.loop(0, CHUNKS)
    def _(t):
        for n in range(per_step):
            fill_diagonal(wide, diagonal, n, t * per_step + n, others, sequences)
        size = per_step * depth
        rows = pl.ds(pl.multiple_of(t * size, size), size)
        part = source.at[rows]
        for n in range(0, per_step, 2):
            blocks = [
                jnp.concatenate(
                    [
                        part[m * depth : (m + 1) * depth, k * span : (k + 1) * span]
                        for m in (n, n + 1)
                    ],
                    axis=1,
                )
                for k in range(positions // GROUP)
            ]
            result[...] += dot(
                jnp.concatenate(blocks, axis=0),
                diagonal[n : n + 2].reshape(2 * span, diagonal.shape[2]),
            )

    scaled = (result[...] * (1.0 / sequences)).astype(BF16)
    for l in range(scaled.shape[1] // LANES):
        members = dict(tiles_of(sequences, l))
        for k in range(positions // GROUP):
            block = scaled[k * depth : (k + 1) * depth, l * LANES : (l + 1) * LANES]
            for m in range(GROUP):
                start = (k * GROUP + m) * depth
                grown[start : start + depth, l * LANES : (l + 1) * LANES] = (
                    block * members[m].astype(F32).astype(BF16)
                    if m in members
                    else jnp.zeros((depth, LANES), BF16)
                )
    grad[...] = dot(repeat_matrix(sequences), grown[...], ROWS_BY_ROWS)
    share = sequences // parts

    def rows_of(p):
        mine = grad[pl.ds(pl.multiple_of(p * share, share), share), :]
        return jnp.concatenate(
            [mine[:, l * LANES : (l + 1) * LANES] for l in range(mine.shape[1] // LANES)], axis=0
        )

    stay, go = plan(lax.axis_index(axis))
    for p, out in zip(stay, outs[:kept], strict=True):
        out[...] = rows_of(p)
    for group, out in zip(go, outs[kept:], strict=True):
        size = out.shape[0] // len(group)
        for n, p in enumerate(group):
            out[n * size : (n + 1) * size, :] = rows_of(p).astype(BF16)


def gradient(wide, source, after, axis, plan, kept, groups, positions, others, sequences):
    depth = PROJECTED_DEPTH
    channels, pairs = depth * depth, positions * others
    parts = lax.axis_size(axis)
    rows = sequences // parts * positions * depth // LANES
    group = (parts - kept) // groups
    shapes = [jax.ShapeDtypeStruct((rows, LANES), F32)] * kept
    shapes += [jax.ShapeDtypeStruct((group * rows, LANES), BF16)] * groups
    results = pl.pallas_call(
        functools.partial(gradient_kernel, axis, plan, kept, positions, others, sequences),
        in_specs=[in_vmem(), in_vmem(), pl.BlockSpec(memory_space=pl.ANY)],
        out_specs=[in_vmem()] * len(shapes),
        out_shape=shapes,
        scratch_shapes=[
            pltpu.VMEM((depth // CHUNKS, GROUP * others, GROUP * sequences), BF16),
            pltpu.VMEM((positions // GROUP * depth, GROUP * sequences), F32),
            pltpu.VMEM((positions * depth, GROUP * sequences), BF16),
            pltpu.VMEM((sequences, positions * depth), F32),
        ],
        compiler_params=params(sequences),
        cost_estimate=pl.CostEstimate(
            flops=2 * pairs * channels * PAIR_FEATURES,
            bytes_accessed=2 * pairs * channels,
            transcendentals=0,
        ),
    )(wide, source, after)
    return results[:kept], results[kept:]


def product_kernel(left_ref, right_ref, _, out_ref):
    size = out_ref.shape[0] // STEPS

    @pl.loop(0, STEPS)
    def _(t):
        rows = pl.ds(pl.multiple_of(t * size, size), size)
        out_ref[rows, :] = dot(left_ref[rows, :], right_ref[...], ROWS_BY_ROWS).astype(BF16)


def product(left, right, after):
    shape = (left.shape[0], right.shape[0])
    return pl.pallas_call(
        product_kernel,
        in_specs=[in_vmem(), in_vmem(), pl.BlockSpec(memory_space=pl.ANY)],
        out_specs=in_vmem(),
        out_shape=jax.ShapeDtypeStruct(shape, BF16),
        compiler_params=params(16),
        cost_estimate=pl.CostEstimate(
            flops=2 * shape[0] * shape[1] * left.shape[1],
            bytes_accessed=4 * shape[0] * shape[1],
            transcendentals=0,
        ),
    )(left, right, after)


def pair_kernel(sequences, x_ref, wt_ref, bias_ref, out_ref):
    product = dot(wt_ref[...], x_ref[...])
    out_ref[...] = (product.T * (1.0 / sequences) + bias_ref[...]).astype(BF16)


def pair(x, wt, output_bias, sequences):
    channels, pairs = x.shape
    count = 3
    size = pairs // count
    return pl.pallas_call(
        functools.partial(pair_kernel, sequences),
        grid=(count,),
        in_specs=[
            pl.BlockSpec((channels, size), lambda t: (0, t)),
            whole(wt.shape),
            whole((1, PAIR_FEATURES)),
        ],
        out_specs=pl.BlockSpec((size, PAIR_FEATURES), lambda t: (t, 0)),
        out_shape=jax.ShapeDtypeStruct((pairs, PAIR_FEATURES), BF16),
        compiler_params=params(),
        cost_estimate=pl.CostEstimate(
            flops=4 * pairs * channels * PAIR_FEATURES,
            bytes_accessed=2 * pairs * channels,
            transcendentals=0,
        ),
    )(x, wt, output_bias.reshape(1, PAIR_FEATURES))


def unfold(total, share, out):
    for l in range(out.shape[1] // LANES):
        out[:, l * LANES : (l + 1) * LANES] = total[l * share : (l + 1) * share, :]


def row_sum_kernel(*refs):
    parts, grad, message = refs[:-2], refs[-2], refs[-1]
    rows = parts[0].shape[0]
    total = parts[0][...]
    for part in parts[1:]:
        total += part[...].astype(F32)
    message[0:rows, :] = total.astype(BF16)
    message[rows:, :] = grad[...]


def row_sum(parts, grad):
    shape = (parts[0].shape[0] + grad.shape[0], LANES)
    return pl.pallas_call(
        row_sum_kernel,
        in_specs=[in_vmem()] * (len(parts) + 1),
        out_specs=in_vmem(),
        out_shape=jax.ShapeDtypeStruct(shape, BF16),
        compiler_params=params(),
    )(*parts, grad)


def pair_sum_kernel(rows, own, near, _, *refs):
    count = len(refs) // 2
    grads, left_out, messages = refs[:count], refs[count], refs[count + 1 :]
    total = (own[0:rows, :].astype(F32) + near[0:rows, :].astype(F32)).astype(BF16)
    size = left_out.shape[0]
    for n, grad in enumerate(grads):
        both = grad[...] + near[rows + n * size : rows + (n + 1) * size, :].astype(F32)
        if n == 0:
            left_out[...] = both
        else:
            messages[n - 1][0:rows, :] = total
            messages[n - 1][rows:, :] = both.astype(BF16)


def pair_sum(own, near, after, grads, rows):
    size = grads[0].shape[0]
    shapes = [jax.ShapeDtypeStruct((size, LANES), F32)]
    shapes += [jax.ShapeDtypeStruct((rows + size, LANES), BF16)] * (len(grads) - 1)
    left, *messages = pl.pallas_call(
        functools.partial(pair_sum_kernel, rows),
        in_specs=[in_vmem()] * 2 + [pl.BlockSpec(memory_space=pl.ANY)] + [in_vmem()] * len(grads),
        out_specs=[in_vmem()] * len(shapes),
        out_shape=shapes,
        compiler_params=params(),
    )(own, near, after, *grads)
    return left, messages


def column_sum_kernel(res_total, count, *refs):
    parts, grad, refs = refs[: count - 1], refs[count - 1], refs[count:]
    own, refs = refs[0], refs[1:]
    grads, refs = refs[: (len(refs) - 4) // 2], refs[(len(refs) - 4) // 2 :]
    messages, (piece_out, left_out, bias_out, held) = refs[:-4], refs[-4:]
    share = piece_out.shape[0]
    rows = share + BIAS_ROWS
    home = lax.div(lax.axis_index("col"), 2)
    for p, part in enumerate((own, *parts)):
        held[lax.rem(home - p + count, count)] = part[0:rows, :]
    total = held[0].astype(F32)
    for n in range(1, count):
        total += held[n].astype(F32)
    piece = total[0:share].astype(BF16)
    piece_out[...] = piece
    for message, other in zip(messages, grads, strict=True):
        message[0:share, :] = piece
        message[share:, :] = other[...]
    bias_out[...] = (total[share : share + 1] + total[share + 1 : share + 2]) * (1.0 / res_total)
    left = grad[...]
    for part in parts:
        left += part[rows:, :].astype(F32)
    unfold(left, left_out.shape[0], left_out)


def column_sum(parts, left_own, own, grads, share, left_shape, res_total):
    rows = share + grads[0].shape[0]
    operands = [*parts, left_own, own, *grads]
    shapes = [jax.ShapeDtypeStruct((rows, LANES), BF16)] * len(grads) + [
        jax.ShapeDtypeStruct((share, LANES), BF16),
        jax.ShapeDtypeStruct(left_shape, F32),
        jax.ShapeDtypeStruct((1, PAIR_FEATURES), F32),
    ]
    *messages, piece, left, bias = pl.pallas_call(
        functools.partial(column_sum_kernel, res_total, len(parts) + 1),
        in_specs=[in_vmem()] * len(operands),
        out_specs=[in_vmem()] * len(shapes),
        out_shape=shapes,
        scratch_shapes=[pltpu.VMEM((len(parts) + 1, share + BIAS_ROWS, LANES), BF16)],
        compiler_params=params(),
    )(*operands)
    return messages, piece, left, bias


def finish_kernel(scale, *refs):
    parts, (piece, grad, projection, right_out) = refs[:-4], refs[-4:]
    row_n = len(parts) + 1
    share = piece.shape[0]
    me = lax.axis_index("row")
    right = grad[...]
    for p, part in enumerate((piece, *parts)):
        start = pl.multiple_of(lax.rem(me - p + row_n, row_n) * share, share)
        projection[pl.ds(start, share), :] = part[0:share, :].astype(F32) * scale
        if p > 0:
            right += part[share:, :].astype(F32)
    unfold(right, right_out.shape[0], right_out)


def finish(parts, piece, right_own, right_shape, scale):
    operands = [*parts, piece, right_own]
    return pl.pallas_call(
        functools.partial(finish_kernel, scale),
        in_specs=[in_vmem()] * len(operands),
        out_specs=[in_vmem()] * 2,
        out_shape=[
            jax.ShapeDtypeStruct((piece.shape[0] * (len(parts) + 1), PAIR_FEATURES), F32),
            jax.ShapeDtypeStruct(right_shape, F32),
        ],
        compiler_params=params(),
    )(*operands)


def shift(x, axis, distance):
    count = lax.axis_size(axis)
    return lax.ppermute(x, axis, [(n, (n + distance) % count) for n in range(count)])


def neighbour(x, axis):
    return lax.ppermute(x, axis, [(n, n ^ 1) for n in range(lax.axis_size(axis))])


def shift_pairs(x, axis):
    return [x] + [shift(x, axis, d) for d in range(2, lax.axis_size(axis), 2)]


def exchange(parts, axis):
    return [shift(part, axis, d) for d, part in enumerate(parts, 1)]


def local(
    first_homolog_features, second_homolog_features, final_projection_matrix, output_bias, cotangent
):
    i_n, j_n, _ = cotangent.shape
    row_n, col_n = lax.axis_size("row"), lax.axis_size("col")
    sequences = second_homolog_features.shape[0] * row_n
    channels = final_projection_matrix.shape[0]
    res_total = i_n * row_n
    a_near = neighbour(first_homolog_features, "col")
    b_near = neighbour(second_homolog_features, "row")
    we, wt, a, b, w, g = load(
        first_homolog_features,
        second_homolog_features,
        final_projection_matrix,
        cotangent.reshape(i_n * j_n, PAIR_FEATURES),
    )
    a_pair, b_pair = stack((a, a_near), (b, b_near))
    a_pieces = shift_pairs(a_pair, "col")
    b_pieces = shift_pairs(b_pair, "row")
    y, gt, bias_rows = prepare(we, g, i_n, j_n)

    x, a_wide, b_wide, (row_own, *messages) = outer(
        a_pieces, b_pieces, g, bias_rows, i_n, j_n, sequences
    )
    row_parts = [row_own] + exchange(messages, "row")
    left_kept, (left_sent,) = gradient(
        b_wide, y, row_own, "col", in_pairs(col_n), col_n // 2, 1, i_n, j_n, sequences
    )
    message = row_sum(row_parts, left_sent)
    near = neighbour(message, "col")
    y2 = product(w, gt, message)
    left_own, messages = pair_sum(message, near, y2, left_kept, row_own.shape[0])
    col_parts = [shift(part, "col", 2 * d) for d, part in enumerate(messages, 1)]
    (right_own,), right_grads = gradient(
        a_wide, y2, messages[0], "row", in_order(row_n), 1, row_n - 1, j_n, i_n, sequences
    )
    messages, piece, left_grad, bias_grad = column_sum(
        col_parts,
        left_own,
        messages[0],
        right_grads,
        channels // row_n,
        first_homolog_features.shape,
        res_total,
    )
    row_parts = exchange(messages, "row")
    pair_map = pair(x, wt, output_bias, sequences)
    projection, right_grad = finish(
        row_parts,
        piece,
        right_own,
        second_homolog_features.shape,
        1.0 / (sequences * res_total),
    )
    return (
        pair_map.reshape(i_n, j_n, PAIR_FEATURES),
        left_grad,
        right_grad,
        projection,
        bias_grad.reshape(PAIR_FEATURES),
    )


def solution(mesh):
    return jax.shard_map(
        local,
        mesh=mesh,
        in_specs=(
            P(("dp", "col"), "row"),
            P(("dp", "row"), "col"),
            P(),
            P(),
            P(("dp", "row"), "col", None),
        ),
        out_specs=(
            P(("dp", "row"), "col", None),
            P(("dp", "col"), "row"),
            P(("dp", "row"), "col"),
            P("dp", None),
            P("dp"),
        ),
        check_vma=False,
    )
```

```python
import functools

import jax
import jax.numpy as jnp
from jax import lax
from jax.experimental import pallas as pl
from jax.experimental.pallas import tpu as pltpu
from jax.sharding import PartitionSpec as P

PROJECTED_DEPTH = 32
PAIR_FEATURES = 128
GROUP = 8
MULTIPLY_ROWS = 384
CHUNKS = 2
BIAS_ROWS = 16
LANES = 128
F32 = jnp.float32
BF16 = jnp.bfloat16
MIB = 1024 * 1024

ROWS_BY_ROWS = (((1,), (1,)), ((), ()))
COLS_BY_COLS = (((0,), (0,)), ((), ()))


def params(sequences=0):
    return pltpu.CompilerParams(vmem_limit_bytes=min(10 + 10 * sequences // 32, 50) * MIB + 2 * MIB)


def whole(shape):
    return pl.BlockSpec(shape, lambda t: (0,) * len(shape))


def dot(x, y, dims=(((1,), (0,)), ((), ()))):
    return lax.dot_general(x, y, dims, preferred_element_type=F32)


def load_kernel(a_hbm, b_hbm, w_hbm, g_hbm, we_ref, wt_ref, a_ref, b_ref, w_ref, g_ref, w32, sems):
    depth = PROJECTED_DEPTH
    copies = [
        pltpu.make_async_copy(source, target, sems.at[n])
        for n, (source, target) in enumerate(
            [(w_hbm, w_ref), (g_hbm, g_ref), (a_hbm, a_ref), (b_hbm, b_ref)]
        )
    ]
    for copy in copies:
        copy.start()
    copies[0].wait()
    w32[...] = w_ref[...].astype(F32)
    for e in range(depth):
        block = w32[pl.ds(e, depth, stride=depth), :]
        we_ref[e * depth : (e + 1) * depth, :] = block.astype(BF16)
    wt_ref[...] = we_ref[...].astype(F32).T.astype(BF16)
    for copy in copies[1:]:
        copy.wait()


def in_vmem():
    return pl.BlockSpec(memory_space=pltpu.VMEM)


def load(a, b, w, g):
    shapes = [
        jax.ShapeDtypeStruct(w.shape, BF16),
        jax.ShapeDtypeStruct(w.shape[::-1], BF16),
        *[jax.ShapeDtypeStruct(x.shape, BF16) for x in (a, b, w, g)],
    ]
    return pl.pallas_call(
        load_kernel,
        in_specs=[pl.BlockSpec(memory_space=pltpu.HBM)] * 4,
        out_specs=[in_vmem()] * len(shapes),
        out_shape=shapes,
        scratch_shapes=[pltpu.VMEM(w.shape, F32), pltpu.SemaphoreType.DMA((4,))],
        compiler_params=params(),
        cost_estimate=pl.CostEstimate(
            flops=1000 * w.size, bytes_accessed=16 * w.size, transcendentals=0
        ),
    )(*[pltpu.with_memory_space_constraint(x, pltpu.HBM) for x in (a, b, w, g)])


def stack_kernel(*refs):
    half = len(refs) * 2 // 3
    for n, out in enumerate(refs[half:]):
        first, second = refs[2 * n], refs[2 * n + 1]
        rows = first.shape[0]
        both = jnp.concatenate([first[...].astype(F32), second[...].astype(F32)], axis=0)
        out[...] = both.astype(BF16)


def stack(*pairs):
    shapes = [
        jax.ShapeDtypeStruct((2 * first.shape[0], first.shape[1]), BF16) for first, _ in pairs
    ]
    operands = [x for pair in pairs for x in pair]
    return pl.pallas_call(
        stack_kernel,
        in_specs=[in_vmem()] * len(operands),
        out_specs=[in_vmem()] * len(shapes),
        out_shape=shapes,
        compiler_params=params(),
    )(*operands)


def split(total):
    high = total.astype(BF16).astype(F32)
    row = lax.broadcasted_iota(jnp.int32, (BIAS_ROWS, PAIR_FEATURES), 0)
    return jnp.where(row == 0, high, jnp.where(row == 1, total - high, 0.0)).astype(BF16)


def joined(block):
    block = block.astype(F32)
    return block[0:1] + block[1:2]


def multiply(left_ref, right_ref, out_ref):
    for n in range(0, right_ref.shape[0], MULTIPLY_ROWS):
        rows = slice(n, n + MULTIPLY_ROWS)
        out_ref[:, rows] = dot(left_ref[...], right_ref[rows, :], ROWS_BY_ROWS).astype(BF16)


def prepare_kernel(i_n, j_n, we_ref, g_ref, y_ref, gt_ref, bias_ref, g32):
    g32[...] = g_ref[...].astype(F32)
    bias_ref[...] = split(jnp.sum(g32[...], axis=0, keepdims=True))
    multiply(we_ref, g_ref, y_ref)

    for j in range(j_n):
        gt_ref[j * i_n : (j + 1) * i_n, :] = g32[pl.ds(j, i_n, stride=j_n), :].astype(BF16)


def prepare(we, g, i_n, j_n):
    pairs = i_n * j_n
    channels = we.shape[0]
    shapes = [
        jax.ShapeDtypeStruct((channels, pairs), BF16),
        jax.ShapeDtypeStruct(g.shape, BF16),
        jax.ShapeDtypeStruct((BIAS_ROWS, PAIR_FEATURES), BF16),
    ]
    return pl.pallas_call(
        functools.partial(prepare_kernel, i_n, j_n),
        in_specs=[in_vmem()] * 2,
        out_specs=[in_vmem()] * len(shapes),
        out_shape=shapes,
        scratch_shapes=[pltpu.VMEM(g.shape, F32)],
        compiler_params=params(16),
        cost_estimate=pl.CostEstimate(
            flops=2 * pairs * channels * PAIR_FEATURES,
            bytes_accessed=4 * pairs * channels,
            transcendentals=0,
        ),
    )(we, g)


def join(pieces, axis, held):
    count = len(pieces)
    depth = pieces[0].shape[0] // 2
    me = lax.axis_index(axis)
    odd = lax.rem(me, 2)
    home = lax.div(me, 2)
    for p, piece in enumerate(pieces):
        start = lax.rem(home - p + count, count) * 2 * depth
        both = piece[...].astype(F32)
        for n in range(2):
            place = start + (1 - odd if n else odd) * depth
            held[pl.ds(pl.multiple_of(place, depth), depth), :] = both[n * depth : (n + 1) * depth]


def repeat_matrix(sequences):
    shape = (sequences, GROUP * sequences)
    lane = lax.broadcasted_iota(jnp.int32, shape, 1)
    row = lax.broadcasted_iota(jnp.int32, shape, 0)
    return (lax.rem(lane, sequences) == row).astype(BF16)


def spread(held, wide):
    both = dot(held[...].T.astype(BF16), repeat_matrix(held.shape[0]))
    for l in range(wide.shape[0]):
        wide[l] = both[:, l * LANES : (l + 1) * LANES]


def tiles_of(sequences, tile):
    lane = lax.broadcasted_iota(jnp.int32, (1, LANES), 1) + tile * LANES
    return [
        (m, lax.div(lane, sequences) == m)
        for m in range(GROUP)
        if m * sequences < (tile + 1) * LANES and (m + 1) * sequences > tile * LANES
    ]


def clear_off_diagonal(diagonal, positions, sequences):
    for l in range(diagonal.shape[2] // LANES):
        members = dict(tiles_of(sequences, l))
        for m in range(GROUP):
            if m not in members:
                rows = slice(m * positions, (m + 1) * positions)
                shape = (diagonal.shape[0], positions, LANES)
                diagonal[:, rows, l * LANES : (l + 1) * LANES] = jnp.zeros(shape, BF16)


def fill_diagonal(wide, diagonal, slot, channel, positions, sequences):
    for l in range(wide.shape[0]):
        block = wide[l, pl.ds(channel, positions, stride=PROJECTED_DEPTH), :].astype(BF16)
        for m, mask in tiles_of(sequences, l):
            diagonal[slot, m * positions : (m + 1) * positions, l * LANES : (l + 1) * LANES] = (
                block * mask.astype(F32).astype(BF16)
            )


def near_of(me):
    return me + 1 - 2 * lax.rem(me, 2)


def by_pairs(count):
    def plan(me):
        groups = [
            [lax.rem(me + d, count), lax.rem(near_of(me) + d, count)] for d in range(0, count, 2)
        ]
        return groups[0], groups[1:]

    return plan


def in_pairs(count):
    def plan(me):
        steps = range(0, count, 2)
        near = near_of(me)
        return [lax.rem(me + d, count) for d in steps], [[lax.rem(near + d, count) for d in steps]]

    return plan


def outer_kernel(i_n, j_n, row_n, col_n, *refs):
    depth = PROJECTED_DEPTH
    a_pieces, refs = refs[: col_n // 2], refs[col_n // 2 :]
    b_pieces, refs = refs[: row_n // 2], refs[row_n // 2 :]
    g_ref, bias_ref, x_ref, a_wide, b_wide, kept, message = refs[:7]
    a_held, b_held, left, diagonal, total = refs[7:]
    sequences = a_held.shape[0]
    groups = i_n // GROUP
    per_step = depth // CHUNKS
    span = GROUP * j_n

    join(a_pieces, "col", a_held)
    join(b_pieces, "row", b_held)
    spread(a_held, a_wide)
    for l in range(a_wide.shape[0]):
        members = tiles_of(sequences, l)
        for k in range(groups):
            block = jnp.zeros((depth, LANES), F32)
            for m, mask in members:
                start = (k * GROUP + m) * depth
                block = jnp.where(mask, a_wide[l, start : start + depth, :], block)
            left[k * depth : (k + 1) * depth, l * LANES : (l + 1) * LANES] = block.astype(BF16)
    spread(b_held, b_wide)
    clear_off_diagonal(diagonal, j_n, sequences)

    @pl.loop(0, CHUNKS)
    def _(t):
        for e in range(per_step):
            fill_diagonal(b_wide, diagonal, e, t * per_step + e, j_n, sequences)
        size = per_step * depth
        rows = pl.ds(pl.multiple_of(t * size, size), size)
        x_part = x_ref.at[rows]
        for e in range(0, per_step, 2):
            right = diagonal[e : e + 2].reshape(2 * span, diagonal.shape[2])
            product = dot(left[...], right, ROWS_BY_ROWS).astype(BF16)
            for n in range(2):
                for k in range(groups):
                    x_part[(e + n) * depth : (e + n + 1) * depth, k * span : (k + 1) * span] = product[
                        k * depth : (k + 1) * depth, n * span : (n + 1) * span
                    ]
        total[rows, :] = dot(x_part[...], g_ref[...])

    share = total.shape[0] // row_n
    me = lax.axis_index("row")
    stay, (go,) = in_pairs(row_n)(me)
    for out, parts in ((kept, stay), (message, go)):
        for p, part in enumerate(parts):
            for n in range(share // depth):
                block = total[pl.ds(part * (share // depth) + n, depth, stride=depth), :]
                first = p * share + n * depth
                out[first : first + depth, :] = block.astype(out.dtype)
    message[len(go) * share :, :] = bias_ref[...]


def outer(a_pieces, b_pieces, g, bias_rows, i_n, j_n, sequences):
    row_n, col_n = 2 * len(b_pieces), 2 * len(a_pieces)
    depth = PROJECTED_DEPTH
    channels = depth * depth
    pairs = i_n * j_n
    tiles = GROUP * sequences // LANES
    operands = [*a_pieces, *b_pieces, g, bias_rows]
    shapes = [jax.ShapeDtypeStruct((channels, pairs), BF16)]
    shapes += [jax.ShapeDtypeStruct((tiles, n * depth, LANES), F32) for n in (i_n, j_n)]
    shapes += [
        jax.ShapeDtypeStruct((channels // 2, LANES), F32),
        jax.ShapeDtypeStruct((channels // 2 + BIAS_ROWS, LANES), BF16),
    ]
    return pl.pallas_call(
        functools.partial(outer_kernel, i_n, j_n, row_n, col_n),
        in_specs=[in_vmem()] * len(operands),
        out_specs=[in_vmem()] * len(shapes),
        out_shape=shapes,
        scratch_shapes=[
            pltpu.VMEM((sequences, i_n * depth), F32),
            pltpu.VMEM((sequences, j_n * depth), F32),
            pltpu.VMEM((i_n // GROUP * depth, GROUP * sequences), BF16),
            pltpu.VMEM((depth // CHUNKS, GROUP * j_n, GROUP * sequences), BF16),
            pltpu.VMEM((channels, PAIR_FEATURES), F32),
        ],
        compiler_params=params(sequences),
        cost_estimate=pl.CostEstimate(
            flops=4 * pairs * channels * PAIR_FEATURES,
            bytes_accessed=2 * pairs * channels,
            transcendentals=0,
        ),
    )(*operands)


def gradient_kernel(axis, plan, kept, positions, others, sequences, chunks, *refs):
    depth = PROJECTED_DEPTH
    wide, source, _ = refs[:3]
    first, last = chunks[0] == 0, chunks[-1] == CHUNKS - 1
    before, refs = (None, refs[3:]) if first else (refs[3], refs[4:])
    if last:
        outs, (diagonal, result, grown, grad) = refs[:-4], refs[-4:]
    else:
        result, diagonal = refs
    parts = lax.axis_size(axis)
    per_step = depth // CHUNKS
    span = GROUP * others

    clear_off_diagonal(diagonal, others, sequences)
    result[...] = jnp.zeros(result.shape, F32) if first else before[...]

    @pl.loop(chunks[0], chunks[-1] + 1)
    def _(t):
        for n in range(per_step):
            fill_diagonal(wide, diagonal, n, t * per_step + n, others, sequences)
        size = per_step * depth
        rows = pl.ds(pl.multiple_of(t * size, size), size)
        part = source.at[rows]
        for n in range(0, per_step, 2):
            blocks = [
                jnp.concatenate(
                    [
                        part[m * depth : (m + 1) * depth, k * span : (k + 1) * span]
                        for m in (n, n + 1)
                    ],
                    axis=1,
                )
                for k in range(positions // GROUP)
            ]
            result[...] += dot(
                jnp.concatenate(blocks, axis=0),
                diagonal[n : n + 2].reshape(2 * span, diagonal.shape[2]),
            )

    if not last:
        return
    scaled = (result[...] * (1.0 / sequences)).astype(BF16)
    for l in range(scaled.shape[1] // LANES):
        members = dict(tiles_of(sequences, l))
        for k in range(positions // GROUP):
            block = scaled[k * depth : (k + 1) * depth, l * LANES : (l + 1) * LANES]
            for m in range(GROUP):
                start = (k * GROUP + m) * depth
                grown[start : start + depth, l * LANES : (l + 1) * LANES] = (
                    block * members[m].astype(F32).astype(BF16)
                    if m in members
                    else jnp.zeros((depth, LANES), BF16)
                )
    grad[...] = dot(repeat_matrix(sequences), grown[...], ROWS_BY_ROWS)
    share = sequences // parts

    def rows_of(p):
        mine = grad[pl.ds(pl.multiple_of(p * share, share), share), :]
        return jnp.concatenate(
            [mine[:, l * LANES : (l + 1) * LANES] for l in range(mine.shape[1] // LANES)], axis=0
        )

    stay, go = plan(lax.axis_index(axis))
    for p, out in zip(stay, outs[:kept], strict=True):
        out[...] = rows_of(p)
    for group, out in zip(go, outs[kept:], strict=True):
        size = out.shape[0] // len(group)
        for n, p in enumerate(group):
            out[n * size : (n + 1) * size, :] = rows_of(p).astype(BF16)


def gradient_call(kernel, operands, after, shapes, scratch, others, sequences, flops):
    specs = [in_vmem()] * len(operands)
    specs.insert(2, pl.BlockSpec(memory_space=pl.ANY))
    diagonal = pltpu.VMEM((PROJECTED_DEPTH // CHUNKS, GROUP * others, GROUP * sequences), BF16)
    return pl.pallas_call(
        kernel,
        in_specs=specs,
        out_specs=[in_vmem()] * len(shapes),
        out_shape=shapes,
        scratch_shapes=[diagonal, *scratch],
        compiler_params=params(sequences),
        cost_estimate=pl.CostEstimate(
            flops=flops, bytes_accessed=2 * operands[1].size, transcendentals=0
        ),
    )(*operands[:2], after, *operands[2:])


def gradient_start(wide, source, after, axis, positions, others, sequences):
    shape = (positions // GROUP * PROJECTED_DEPTH, GROUP * sequences)
    chunks = range(CHUNKS // 2)
    (before,) = gradient_call(
        functools.partial(gradient_kernel, axis, None, 0, positions, others, sequences, chunks),
        [wide, source],
        after,
        [jax.ShapeDtypeStruct(shape, F32)],
        [],
        others,
        sequences,
        source.size * PAIR_FEATURES,
    )
    return before


def gradient(wide, source, after, axis, plan, kept, groups, positions, others, sequences, before=None):
    depth = PROJECTED_DEPTH
    parts = lax.axis_size(axis)
    rows = sequences // parts * positions * depth // LANES
    shapes = [jax.ShapeDtypeStruct((rows, LANES), F32)] * kept
    if groups > 0:
        group = (parts - kept) // groups
        shapes += [jax.ShapeDtypeStruct((group * rows, LANES), BF16)] * groups
    chunks = range(0 if before is None else CHUNKS // 2, CHUNKS)
    results = gradient_call(
        functools.partial(gradient_kernel, axis, plan, kept, positions, others, sequences, chunks),
        [wide, source] + ([] if before is None else [before]),
        after,
        shapes,
        [
            pltpu.VMEM((positions // GROUP * depth, GROUP * sequences), F32),
            pltpu.VMEM((positions * depth, GROUP * sequences), BF16),
            pltpu.VMEM((sequences, positions * depth), F32),
        ],
        others,
        sequences,
        2 * source.size * PAIR_FEATURES,
    )
    return results[:kept], results[kept:]


def product_kernel(left_ref, right_ref, _, out_ref):
    multiply(left_ref, right_ref, out_ref)


def product(left, right, after):
    shape = (left.shape[0], right.shape[0])
    return pl.pallas_call(
        product_kernel,
        in_specs=[in_vmem(), in_vmem(), pl.BlockSpec(memory_space=pl.ANY)],
        out_specs=in_vmem(),
        out_shape=jax.ShapeDtypeStruct(shape, BF16),
        compiler_params=params(16),
        cost_estimate=pl.CostEstimate(
            flops=2 * shape[0] * shape[1] * left.shape[1],
            bytes_accessed=4 * shape[0] * shape[1],
            transcendentals=0,
        ),
    )(left, right, after)


def pair_kernel(sequences, x_ref, wt_ref, bias_ref, out_ref, done_ref):
    done_ref[...] = jnp.zeros(done_ref.shape, F32)
    product = dot(wt_ref[...], x_ref[...])
    out_ref[...] = (product.T * (1.0 / sequences) + bias_ref[...]).astype(BF16)


def pair(x, wt, output_bias, sequences):
    channels, pairs = x.shape
    count = 3
    size = pairs // count
    return pl.pallas_call(
        functools.partial(pair_kernel, sequences),
        grid=(count,),
        in_specs=[
            pl.BlockSpec((channels, size), lambda t: (0, t)),
            whole(wt.shape),
            whole((1, PAIR_FEATURES)),
        ],
        out_specs=[pl.BlockSpec((size, PAIR_FEATURES), lambda t: (t, 0)), whole((8, LANES))],
        out_shape=[
            jax.ShapeDtypeStruct((pairs, PAIR_FEATURES), BF16),
            jax.ShapeDtypeStruct((8, LANES), F32),
        ],
        compiler_params=params(),
        cost_estimate=pl.CostEstimate(
            flops=4 * pairs * channels * PAIR_FEATURES,
            bytes_accessed=2 * pairs * channels,
            transcendentals=0,
        ),
    )(x, wt, output_bias.reshape(1, PAIR_FEATURES))


def unfold(total, share, out):
    for l in range(out.shape[1] // LANES):
        out[:, l * LANES : (l + 1) * LANES] = total[l * share : (l + 1) * share, :]


def call(kernel, operands, shapes, after=()):
    specs = [in_vmem()] * len(operands) + [pl.BlockSpec(memory_space=pl.ANY)] * len(after)
    return pl.pallas_call(
        kernel,
        in_specs=specs,
        out_specs=[in_vmem()] * len(shapes),
        out_shape=[jax.ShapeDtypeStruct(shape, kind) for shape, kind in shapes],
        compiler_params=params(),
    )(*operands, *after)


def row_pair_sum(kept, bias, near, after, share):
    count = kept.shape[0] // share

    def kernel(kept, bias, near, _, own, bias_out, *messages):
        total = split(joined(bias[...]) + joined(near[count * share :, :]))
        bias_out[...] = total
        for p in range(count):
            rows = slice(p * share, (p + 1) * share)
            both = kept[rows, :] + near[rows, :].astype(F32)
            if p == 0:
                own[...] = both
            else:
                messages[p - 1][0:share, :] = both.astype(BF16)
                messages[p - 1][share:, :] = total

    shapes = [((share, LANES), F32), (bias.shape, BF16)]
    shapes += [((share + BIAS_ROWS, LANES), BF16)] * (count - 1)
    own, bias, *messages = call(kernel, [kept, bias, near], shapes, [after])
    return own, bias, messages


def row_sum(own, bias, parts, grad):
    share = own.shape[0]

    def kernel(own, bias, *refs):
        parts, grad, message = refs[:-2], refs[-2], refs[-1]
        total, bias_total = own[...], joined(bias[...])
        for part in parts:
            total += part[0:share, :].astype(F32)
            bias_total += joined(part[share:, :])
        message[0:share, :] = total.astype(BF16)
        message[share : share + BIAS_ROWS, :] = split(bias_total)
        message[share + BIAS_ROWS :, :] = grad[...]

    shape = (share + BIAS_ROWS + grad.shape[0], LANES)
    (message,) = call(kernel, [own, bias, *parts, grad], [(shape, BF16)])
    return message


def column_pair_sum(own, near, grads, after, share):
    rows = share + BIAS_ROWS
    size = grads[0].shape[0]

    def kernel(own, near, *refs):
        grads, left_out, messages = refs[: len(grad_list)], refs[len(grad_list) + 1], refs[len(grad_list) + 2 :]
        total = (own[0:share, :].astype(F32) + near[0:share, :].astype(F32)).astype(BF16)
        bias = split(joined(own[share:rows, :]) + joined(near[share:rows, :]))
        for n, grad in enumerate(grads):
            both = grad[...] + near[rows + n * size : rows + (n + 1) * size, :].astype(F32)
            if n == 0:
                left_out[...] = both
            else:
                messages[n - 1][0:share, :] = total
                messages[n - 1][share:rows, :] = bias
                messages[n - 1][rows:, :] = both.astype(BF16)

    grad_list = list(grads)
    shapes = [((size, LANES), F32)] + [((rows + size, LANES), BF16)] * (len(grad_list) - 1)
    left, *messages = call(kernel, [own, near, *grad_list], shapes, [after])
    return left, messages


def column_sum(parts, left_own, own, grads, share, left_shape, res_total):
    rows = share + BIAS_ROWS
    count = len(parts) + 1

    def kernel(*refs):
        parts, grad, own, refs = refs[: count - 1], refs[count - 1], refs[count], refs[count + 1 :]
        grads, refs = refs[: len(grad_list)], refs[len(grad_list) :]
        messages, (piece_out, left_out, bias_out, held) = refs[:-4], refs[-4:]
        home = lax.div(lax.axis_index("col"), 2)
        for p, part in enumerate((own, *parts)):
            held[lax.rem(home - p + count, count)] = part[0:rows, :]
        total, bias = held[0, 0:share, :].astype(F32), joined(held[0, share:, :])
        for n in range(1, count):
            total += held[n, 0:share, :].astype(F32)
            bias += joined(held[n, share:, :])
        piece = total.astype(BF16)
        piece_out[...] = piece
        for message, other in zip(messages, grads, strict=True):
            message[0:share, :] = piece
            message[share:, :] = other[...]
        bias_out[...] = bias * (1.0 / res_total)
        left = grad[...]
        for part in parts:
            left += part[rows:, :].astype(F32)
        unfold(left, left_out.shape[0], left_out)

    grad_list = list(grads)
    operands = [*parts, left_own, own, *grad_list]
    shapes = [
        jax.ShapeDtypeStruct((share + grad.shape[0], LANES), BF16) for grad in grad_list
    ] + [
        jax.ShapeDtypeStruct((share, LANES), BF16),
        jax.ShapeDtypeStruct(left_shape, F32),
        jax.ShapeDtypeStruct((1, PAIR_FEATURES), F32),
    ]
    *messages, piece, left, bias = pl.pallas_call(
        kernel,
        in_specs=[in_vmem()] * len(operands),
        out_specs=[in_vmem()] * len(shapes),
        out_shape=shapes,
        scratch_shapes=[pltpu.VMEM((count, rows, LANES), BF16)],
        compiler_params=params(),
    )(*operands)
    return messages, piece, left, bias


def finish_pairs(piece, grads, parts, after):
    share, size = piece.shape[0], grads[0].shape[0]
    count = len(parts) + 1

    def kernel(piece, own, other, *refs):
        parts, (message, right_out) = refs[: count - 1], refs[-2:]
        message[0:share, :] = piece[...]
        mine, theirs = own[...], other[...]
        for p, part in enumerate(parts, 1):
            message[p * share : (p + 1) * share, :] = part[0:share, :]
            mine += part[share : share + size, :].astype(F32)
            theirs += part[share + size :, :].astype(F32)
        message[count * share :, :] = theirs.astype(BF16)
        right_out[...] = mine

    shapes = [((count * share + size, LANES), BF16), ((size, LANES), F32)]
    return call(kernel, [piece, *grads, *parts], shapes, [after])


def finish(own, near, right_own, right_shape, share, scale):
    count = lax.axis_size("row") // 2

    def kernel(own, near, right_own, projection, right_out):
        me = lax.axis_index("row")
        home, odd = lax.div(me, 2), lax.rem(me, 2)
        for ref, parity in ((own, odd), (near, 1 - odd)):
            for p in range(count):
                place = 2 * lax.rem(home - p + count, count) + parity
                rows = pl.ds(pl.multiple_of(place * share, share), share)
                projection[rows, :] = ref[p * share : (p + 1) * share, :].astype(F32) * scale
        right = right_own[...] + near[count * share :, :].astype(F32)
        unfold(right, right_out.shape[0], right_out)

    shapes = [((2 * count * share, PAIR_FEATURES), F32), (right_shape, F32)]
    return call(kernel, [own, near, right_own], shapes)


def shift(x, axis, distance):
    count = lax.axis_size(axis)
    return lax.ppermute(x, axis, [(n, (n + distance) % count) for n in range(count)])


def neighbour(x, axis):
    return lax.ppermute(x, axis, [(n, n ^ 1) for n in range(lax.axis_size(axis))])


def shift_pairs(x, axis):
    return [x] + [shift(x, axis, d) for d in range(2, lax.axis_size(axis), 2)]


def send_pairs(parts, axis):
    return [shift(part, axis, 2 * p) for p, part in enumerate(parts, 1)]


def local(
    first_homolog_features, second_homolog_features, final_projection_matrix, output_bias, cotangent
):
    i_n, j_n, _ = cotangent.shape
    row_n, col_n = lax.axis_size("row"), lax.axis_size("col")
    sequences = second_homolog_features.shape[0] * row_n
    channels = final_projection_matrix.shape[0]
    res_total = i_n * row_n
    a_near = neighbour(first_homolog_features, "col")
    b_near = neighbour(second_homolog_features, "row")
    we, wt, a, b, w, g = load(
        first_homolog_features,
        second_homolog_features,
        final_projection_matrix,
        cotangent.reshape(i_n * j_n, PAIR_FEATURES),
    )
    a_pair, b_pair = stack((a, a_near), (b, b_near))
    a_pieces = shift_pairs(a_pair, "col")
    b_pieces = shift_pairs(b_pair, "row")
    y, gt, bias_rows = prepare(we, g, i_n, j_n)

    x, a_wide, b_wide, kept, message = outer(
        a_pieces, b_pieces, g, bias_rows, i_n, j_n, sequences
    )
    share = channels // row_n

    near = neighbour(message, "row")
    before = gradient_start(b_wide, y, message, "col", i_n, j_n, sequences)
    own, bias, messages = row_pair_sum(kept, bias_rows, near, before, share)
    parts = send_pairs(messages, "row")
    left_kept, (left_sent,) = gradient(
        b_wide, y, bias, "col", in_pairs(col_n), col_n // 2, 1, i_n, j_n, sequences, before
    )

    message = row_sum(own, bias, parts, left_sent)
    near = neighbour(message, "col")
    y2 = product(w, gt, message)
    left_own, messages = column_pair_sum(message, near, left_kept, y2, share)
    parts = send_pairs(messages, "col")
    right_kept, right_sent = gradient(
        a_wide, y2, left_own, "row", by_pairs(row_n), 2, row_n // 2 - 1, j_n, i_n, sequences
    )

    messages, piece, left_grad, bias_grad = column_sum(
        parts, left_own, messages[0], right_sent, share, first_homolog_features.shape, res_total
    )
    parts = send_pairs(messages, "row")
    pair_map, pair_done = pair(x, wt, output_bias, sequences)
    message, right_own = finish_pairs(piece, right_kept, parts, pair_done)
    near = neighbour(message, "row")
    projection, right_grad = finish(
        message,
        near,
        right_own,
        second_homolog_features.shape,
        share,
        1.0 / (sequences * res_total),
    )
    return (
        pair_map.reshape(i_n, j_n, PAIR_FEATURES),
        left_grad,
        right_grad,
        projection,
        bias_grad.reshape(PAIR_FEATURES),
    )


def solution(mesh):
    return jax.shard_map(
        local,
        mesh=mesh,
        in_specs=(
            P(("dp", "col"), "row"),
            P(("dp", "row"), "col"),
            P(),
            P(),
            P(("dp", "row"), "col", None),
        ),
        out_specs=(
            P(("dp", "row"), "col", None),
            P(("dp", "col"), "row"),
            P(("dp", "row"), "col"),
            P("dp", None),
            P("dp"),
        ),
        check_vma=False,
    )
```

```python
import functools

import jax
import jax.numpy as jnp
from jax import lax
from jax.experimental import pallas as pl
from jax.experimental.pallas import tpu as pltpu
from jax.sharding import PartitionSpec as P

PROJECTED_DEPTH = 32
PAIR_FEATURES = 128
GROUP = 8
MULTIPLY_ROWS = 384
CHUNKS = 2
BIAS_ROWS = 16
LANES = 128
F32 = jnp.float32
BF16 = jnp.bfloat16
MIB = 1024 * 1024

ROWS_BY_ROWS = (((1,), (1,)), ((), ()))
COLS_BY_COLS = (((0,), (0,)), ((), ()))


def params(sequences=0):
    return pltpu.CompilerParams(vmem_limit_bytes=min(10 + 10 * sequences // 32, 50) * MIB + 2 * MIB)


def whole(shape):
    return pl.BlockSpec(shape, lambda t: (0,) * len(shape))


def dot(x, y, dims=(((1,), (0,)), ((), ()))):
    return lax.dot_general(x, y, dims, preferred_element_type=F32)


def load_kernel(a_hbm, b_hbm, w_hbm, g_hbm, we_ref, wt_ref, a_ref, b_ref, w_ref, g_ref, w32, sems):
    depth = PROJECTED_DEPTH
    copies = [
        pltpu.make_async_copy(source, target, sems.at[n])
        for n, (source, target) in enumerate(
            [(w_hbm, w_ref), (g_hbm, g_ref), (a_hbm, a_ref), (b_hbm, b_ref)]
        )
    ]
    for copy in copies:
        copy.start()
    copies[0].wait()
    w32[...] = w_ref[...].astype(F32)
    for e in range(depth):
        block = w32[pl.ds(e, depth, stride=depth), :]
        we_ref[e * depth : (e + 1) * depth, :] = block.astype(BF16)
    wt_ref[...] = we_ref[...].astype(F32).T.astype(BF16)
    for copy in copies[1:]:
        copy.wait()


def in_vmem():
    return pl.BlockSpec(memory_space=pltpu.VMEM)


def load(a, b, w, g):
    shapes = [
        jax.ShapeDtypeStruct(w.shape, BF16),
        jax.ShapeDtypeStruct(w.shape[::-1], BF16),
        *[jax.ShapeDtypeStruct(x.shape, BF16) for x in (a, b, w, g)],
    ]
    return pl.pallas_call(
        load_kernel,
        in_specs=[pl.BlockSpec(memory_space=pltpu.HBM)] * 4,
        out_specs=[in_vmem()] * len(shapes),
        out_shape=shapes,
        scratch_shapes=[pltpu.VMEM(w.shape, F32), pltpu.SemaphoreType.DMA((4,))],
        compiler_params=params(),
        cost_estimate=pl.CostEstimate(
            flops=1000 * w.size, bytes_accessed=16 * w.size, transcendentals=0
        ),
    )(*[pltpu.with_memory_space_constraint(x, pltpu.HBM) for x in (a, b, w, g)])


def stack_kernel(*refs):
    half = len(refs) * 2 // 3
    for n, out in enumerate(refs[half:]):
        first, second = refs[2 * n], refs[2 * n + 1]
        rows = first.shape[0]
        both = jnp.concatenate([first[...].astype(F32), second[...].astype(F32)], axis=0)
        out[...] = both.astype(BF16)


def stack(*pairs):
    shapes = [
        jax.ShapeDtypeStruct((2 * first.shape[0], first.shape[1]), BF16) for first, _ in pairs
    ]
    operands = [x for pair in pairs for x in pair]
    return pl.pallas_call(
        stack_kernel,
        in_specs=[in_vmem()] * len(operands),
        out_specs=[in_vmem()] * len(shapes),
        out_shape=shapes,
        compiler_params=params(),
    )(*operands)


def split(total):
    high = total.astype(BF16).astype(F32)
    row = lax.broadcasted_iota(jnp.int32, (BIAS_ROWS, PAIR_FEATURES), 0)
    return jnp.where(row == 0, high, jnp.where(row == 1, total - high, 0.0)).astype(BF16)


def joined(block):
    block = block.astype(F32)
    return block[0:1] + block[1:2]


def multiply(left_ref, right_ref, out_ref):
    for n in range(0, right_ref.shape[0], MULTIPLY_ROWS):
        rows = slice(n, n + MULTIPLY_ROWS)
        out_ref[:, rows] = dot(left_ref[...], right_ref[rows, :], ROWS_BY_ROWS).astype(BF16)


def prepare_kernel(i_n, j_n, we_ref, g_ref, y_ref, gt_ref, bias_ref, g32):
    g32[...] = g_ref[...].astype(F32)
    bias_ref[...] = split(jnp.sum(g32[...], axis=0, keepdims=True))
    multiply(we_ref, g_ref, y_ref)

    for j in range(j_n):
        gt_ref[j * i_n : (j + 1) * i_n, :] = g32[pl.ds(j, i_n, stride=j_n), :].astype(BF16)


def prepare(we, g, i_n, j_n):
    pairs = i_n * j_n
    channels = we.shape[0]
    shapes = [
        jax.ShapeDtypeStruct((channels, pairs), BF16),
        jax.ShapeDtypeStruct(g.shape, BF16),
        jax.ShapeDtypeStruct((BIAS_ROWS, PAIR_FEATURES), BF16),
    ]
    return pl.pallas_call(
        functools.partial(prepare_kernel, i_n, j_n),
        in_specs=[in_vmem()] * 2,
        out_specs=[in_vmem()] * len(shapes),
        out_shape=shapes,
        scratch_shapes=[pltpu.VMEM(g.shape, F32)],
        compiler_params=params(16),
        cost_estimate=pl.CostEstimate(
            flops=2 * pairs * channels * PAIR_FEATURES,
            bytes_accessed=4 * pairs * channels,
            transcendentals=0,
        ),
    )(we, g)


def join(pieces, axis, held):
    count = len(pieces)
    depth = pieces[0].shape[0] // 2
    me = lax.axis_index(axis)
    odd = lax.rem(me, 2)
    home = lax.div(me, 2)
    for p, piece in enumerate(pieces):
        start = lax.rem(home - p + count, count) * 2 * depth
        both = piece[...].astype(F32)
        for n in range(2):
            place = start + (1 - odd if n else odd) * depth
            held[pl.ds(pl.multiple_of(place, depth), depth), :] = both[n * depth : (n + 1) * depth]


def repeat_matrix(sequences):
    shape = (sequences, GROUP * sequences)
    lane = lax.broadcasted_iota(jnp.int32, shape, 1)
    row = lax.broadcasted_iota(jnp.int32, shape, 0)
    return (lax.rem(lane, sequences) == row).astype(BF16)


def spread(held, wide):
    both = dot(held[...].T.astype(BF16), repeat_matrix(held.shape[0]))
    for l in range(wide.shape[0]):
        wide[l] = both[:, l * LANES : (l + 1) * LANES]


def tiles_of(sequences, tile):
    lane = lax.broadcasted_iota(jnp.int32, (1, LANES), 1) + tile * LANES
    return [
        (m, lax.div(lane, sequences) == m)
        for m in range(GROUP)
        if m * sequences < (tile + 1) * LANES and (m + 1) * sequences > tile * LANES
    ]


def diagonal_of(wide, channel, positions, sequences):
    columns = []
    for l in range(wide.shape[0]):
        block = wide[l, pl.ds(channel, positions, stride=PROJECTED_DEPTH), :].astype(BF16)
        members = dict(tiles_of(sequences, l))
        columns.append(
            jnp.concatenate(
                [
                    block * members[m].astype(F32).astype(BF16)
                    if m in members
                    else jnp.zeros(block.shape, BF16)
                    for m in range(GROUP)
                ],
                axis=0,
            )
        )
    return jnp.concatenate(columns, axis=1)


def near_of(me):
    return me + 1 - 2 * lax.rem(me, 2)


def in_order(count):
    return lambda me: ([me], [[lax.rem(me + d, count)] for d in range(1, count)])


def in_pairs(count):
    def plan(me):
        steps = range(0, count, 2)
        near = near_of(me)
        return [lax.rem(me + d, count) for d in steps], [[lax.rem(near + d, count) for d in steps]]

    return plan


def outer_kernel(i_n, j_n, row_n, col_n, *refs):
    depth = PROJECTED_DEPTH
    a_pieces, refs = refs[: col_n // 2], refs[col_n // 2 :]
    b_pieces, refs = refs[: row_n // 2], refs[row_n // 2 :]
    g_ref, bias_ref, x_ref, a_held, b_wide = refs[:5]
    messages, (b_held, left, total) = refs[5 : 5 + row_n], refs[5 + row_n :]
    sequences = a_held.shape[0]
    groups = i_n // GROUP
    per_step = depth // CHUNKS
    span = GROUP * j_n

    join(a_pieces, "col", a_held)
    join(b_pieces, "row", b_held)
    spread(b_held, b_wide)
    turned = a_held[...].T.astype(BF16)
    shape = (sequences, GROUP * sequences)
    shifted = lax.broadcasted_iota(jnp.int32, shape, 1) - lax.broadcasted_iota(jnp.int32, shape, 0)
    value = jnp.zeros(left.shape, F32)
    for m in range(GROUP):
        rows = [
            turned[(k * GROUP + m) * depth : (k * GROUP + m + 1) * depth, :] for k in range(groups)
        ]
        value += dot(jnp.concatenate(rows, axis=0), (shifted == m * sequences).astype(BF16))
    left[...] = value.astype(BF16)

    @pl.loop(0, CHUNKS)
    def _(t):
        size = per_step * depth
        rows = pl.ds(pl.multiple_of(t * size, size), size)
        x_part = x_ref.at[rows]
        for e in range(0, per_step, 2):
            right = [diagonal_of(b_wide, t * per_step + e + n, j_n, sequences) for n in range(2)]
            product = dot(
                left[...], jnp.concatenate(right, axis=0), ROWS_BY_ROWS
            ).astype(BF16)
            for n in range(2):
                for k in range(groups):
                    x_part[(e + n) * depth : (e + n + 1) * depth, k * span : (k + 1) * span] = product[
                        k * depth : (k + 1) * depth, n * span : (n + 1) * span
                    ]
        total[rows, :] = dot(x_part[...], g_ref[...])

    share = total.shape[0] // row_n
    me = lax.axis_index("row")
    stay, go = in_order(row_n)(me)
    for message, (part,) in zip(messages, [stay, *go], strict=True):
        for n in range(share // depth):
            block = total[pl.ds(part * (share // depth) + n, depth, stride=depth), :]
            message[n * depth : (n + 1) * depth, :] = block.astype(message.dtype)
        message[share:, :] = bias_ref[...].astype(message.dtype)


def outer(a_pieces, b_pieces, g, bias_rows, i_n, j_n, sequences):
    row_n, col_n = 2 * len(b_pieces), 2 * len(a_pieces)
    depth = PROJECTED_DEPTH
    channels = depth * depth
    pairs = i_n * j_n
    tiles = GROUP * sequences // LANES
    operands = [*a_pieces, *b_pieces, g, bias_rows]
    shapes = [jax.ShapeDtypeStruct((channels, pairs), BF16)]
    shapes += [
        jax.ShapeDtypeStruct((sequences, i_n * depth), F32),
        jax.ShapeDtypeStruct((tiles, j_n * depth, LANES), F32),
    ]
    shapes += [
        jax.ShapeDtypeStruct((channels // row_n + BIAS_ROWS, LANES), BF16 if p else F32)
        for p in range(row_n)
    ]
    results = pl.pallas_call(
        functools.partial(outer_kernel, i_n, j_n, row_n, col_n),
        in_specs=[in_vmem()] * len(operands),
        out_specs=[in_vmem()] * len(shapes),
        out_shape=shapes,
        scratch_shapes=[
            pltpu.VMEM((sequences, j_n * depth), F32),
            pltpu.VMEM((i_n // GROUP * depth, GROUP * sequences), BF16),
            pltpu.VMEM((channels, PAIR_FEATURES), F32),
        ],
        compiler_params=params(sequences),
        cost_estimate=pl.CostEstimate(
            flops=4 * pairs * channels * PAIR_FEATURES,
            bytes_accessed=2 * pairs * channels,
            transcendentals=0,
        ),
    )(*operands)
    return *results[:3], results[3:]


def gradient_kernel(axis, plan, kept, positions, others, sequences, *refs):
    depth = PROJECTED_DEPTH
    wide, source = refs[:2]
    outs, (result, grown, grad, own_wide) = refs[3:-4], refs[-4:]
    if len(wide.shape) == 2:
        spread(wide, own_wide)
        wide = own_wide
    parts = lax.axis_size(axis)
    per_step = depth // CHUNKS
    span = GROUP * others

    result[...] = jnp.zeros(result.shape, F32)

    @pl.loop(0, CHUNKS)
    def _(t):
        size = per_step * depth
        rows = pl.ds(pl.multiple_of(t * size, size), size)
        part = source.at[rows]
        for n in range(0, per_step, 2):
            blocks = [
                jnp.concatenate(
                    [
                        part[m * depth : (m + 1) * depth, k * span : (k + 1) * span]
                        for m in (n, n + 1)
                    ],
                    axis=1,
                )
                for k in range(positions // GROUP)
            ]
            right = [
                diagonal_of(wide, t * per_step + m, others, sequences) for m in (n, n + 1)
            ]
            result[...] += dot(jnp.concatenate(blocks, axis=0), jnp.concatenate(right, axis=0))

    scaled = (result[...] * (1.0 / sequences)).astype(BF16)
    for l in range(scaled.shape[1] // LANES):
        members = dict(tiles_of(sequences, l))
        for k in range(positions // GROUP):
            block = scaled[k * depth : (k + 1) * depth, l * LANES : (l + 1) * LANES]
            for m in range(GROUP):
                start = (k * GROUP + m) * depth
                grown[start : start + depth, l * LANES : (l + 1) * LANES] = (
                    block * members[m].astype(F32).astype(BF16)
                    if m in members
                    else jnp.zeros((depth, LANES), BF16)
                )
    grad[...] = dot(repeat_matrix(sequences), grown[...], ROWS_BY_ROWS)
    share = sequences // parts

    def rows_of(p):
        mine = grad[pl.ds(pl.multiple_of(p * share, share), share), :]
        return jnp.concatenate(
            [mine[:, l * LANES : (l + 1) * LANES] for l in range(mine.shape[1] // LANES)], axis=0
        )

    stay, go = plan(lax.axis_index(axis))
    for p, out in zip(stay, outs[:kept], strict=True):
        out[...] = rows_of(p)
    for group, out in zip(go, outs[kept:], strict=True):
        size = out.shape[0] // len(group)
        for n, p in enumerate(group):
            out[n * size : (n + 1) * size, :] = rows_of(p).astype(BF16)


def gradient(wide, source, after, axis, plan, kept, groups, positions, others, sequences):
    depth = PROJECTED_DEPTH
    parts = lax.axis_size(axis)
    rows = sequences // parts * positions * depth // LANES
    shapes = [jax.ShapeDtypeStruct((rows, LANES), F32)] * kept
    group = (parts - kept) // groups
    shapes += [jax.ShapeDtypeStruct((group * rows, LANES), BF16)] * groups
    tiles = GROUP * sequences // LANES if wide.ndim == 2 else 1
    results = pl.pallas_call(
        functools.partial(gradient_kernel, axis, plan, kept, positions, others, sequences),
        in_specs=[in_vmem(), in_vmem(), pl.BlockSpec(memory_space=pl.ANY)],
        out_specs=[in_vmem()] * len(shapes),
        out_shape=shapes,
        scratch_shapes=[
            pltpu.VMEM((positions // GROUP * depth, GROUP * sequences), F32),
            pltpu.VMEM((positions * depth, GROUP * sequences), BF16),
            pltpu.VMEM((sequences, positions * depth), F32),
            pltpu.VMEM((tiles, others * depth if wide.ndim == 2 else 8, LANES), F32),
        ],
        compiler_params=params(sequences),
        cost_estimate=pl.CostEstimate(
            flops=2 * source.size * PAIR_FEATURES,
            bytes_accessed=2 * source.size,
            transcendentals=0,
        ),
    )(wide, source, after)
    return results[:kept], results[kept:]


def product_kernel(left_ref, right_ref, _, out_ref):
    multiply(left_ref, right_ref, out_ref)


def product(left, right, after):
    shape = (left.shape[0], right.shape[0])
    return pl.pallas_call(
        product_kernel,
        in_specs=[in_vmem(), in_vmem(), pl.BlockSpec(memory_space=pl.ANY)],
        out_specs=in_vmem(),
        out_shape=jax.ShapeDtypeStruct(shape, BF16),
        compiler_params=params(16),
        cost_estimate=pl.CostEstimate(
            flops=2 * shape[0] * shape[1] * left.shape[1],
            bytes_accessed=4 * shape[0] * shape[1],
            transcendentals=0,
        ),
    )(left, right, after)


def pair_kernel(sequences, x_ref, wt_ref, bias_ref, out_ref):
    product = dot(wt_ref[...], x_ref[...])
    out_ref[...] = (product.T * (1.0 / sequences) + bias_ref[...]).astype(BF16)


def pair(x, wt, output_bias, sequences):
    channels, pairs = x.shape
    count = 3
    size = pairs // count
    return pl.pallas_call(
        functools.partial(pair_kernel, sequences),
        grid=(count,),
        in_specs=[
            pl.BlockSpec((channels, size), lambda t: (0, t)),
            whole(wt.shape),
            whole((1, PAIR_FEATURES)),
        ],
        out_specs=pl.BlockSpec((size, PAIR_FEATURES), lambda t: (t, 0)),
        out_shape=jax.ShapeDtypeStruct((pairs, PAIR_FEATURES), BF16),
        compiler_params=params(),
        cost_estimate=pl.CostEstimate(
            flops=4 * pairs * channels * PAIR_FEATURES,
            bytes_accessed=2 * pairs * channels,
            transcendentals=0,
        ),
    )(x, wt, output_bias.reshape(1, PAIR_FEATURES))


def unfold(total, share, out):
    for l in range(out.shape[1] // LANES):
        out[:, l * LANES : (l + 1) * LANES] = total[l * share : (l + 1) * share, :]


def call(kernel, operands, shapes, after=(), scratch=()):
    specs = [in_vmem()] * len(operands) + [pl.BlockSpec(memory_space=pl.ANY)] * len(after)
    return pl.pallas_call(
        kernel,
        in_specs=specs,
        out_specs=[in_vmem()] * len(shapes),
        out_shape=[jax.ShapeDtypeStruct(shape, kind) for shape, kind in shapes],
        scratch_shapes=scratch,
        compiler_params=params(),
    )(*operands, *after)


def row_sum(parts, grad, share):
    count = len(parts)

    def kernel(*refs):
        parts, (grad, message, held) = refs[:count], refs[count:]
        me = lax.axis_index("row")
        total = parts[0][0:share, :]
        for p, part in enumerate(parts):
            held[lax.rem(me - p + count, count)] = part[share:, :].astype(F32)
            if p > 0:
                total += part[0:share, :].astype(F32)
        bias = joined(held[0])
        for n in range(1, count):
            bias += joined(held[n])
        message[0:share, :] = total.astype(BF16)
        message[share : share + BIAS_ROWS, :] = split(bias)
        message[share + BIAS_ROWS :, :] = grad[...]

    shape = (share + BIAS_ROWS + grad.shape[0], LANES)
    scratch = [pltpu.VMEM((count, BIAS_ROWS, LANES), F32)]
    (message,) = call(kernel, [*parts, grad], [(shape, BF16)], scratch=scratch)
    return message


def column_pair_sum(own, near, grads, after, share):
    rows = share + BIAS_ROWS
    size = grads[0].shape[0]

    def kernel(own, near, *refs):
        grads, left_out, messages = refs[: len(grad_list)], refs[len(grad_list) + 1], refs[len(grad_list) + 2 :]
        total = (own[0:share, :].astype(F32) + near[0:share, :].astype(F32)).astype(BF16)
        bias = split(joined(own[share:rows, :]) + joined(near[share:rows, :]))
        for n, grad in enumerate(grads):
            both = grad[...] + near[rows + n * size : rows + (n + 1) * size, :].astype(F32)
            if n == 0:
                left_out[...] = both
            else:
                messages[n - 1][0:share, :] = total
                messages[n - 1][share:rows, :] = bias
                messages[n - 1][rows:, :] = both.astype(BF16)

    grad_list = list(grads)
    shapes = [((size, LANES), F32)] + [((rows + size, LANES), BF16)] * (len(grad_list) - 1)
    left, *messages = call(kernel, [own, near, *grad_list], shapes, [after])
    return left, messages


def column_sum(parts, left_own, own, grads, share):
    rows = share + BIAS_ROWS
    count = len(parts) + 1
    sent = len(grads)

    def kernel(*refs):
        parts, (grad, own), refs = refs[: count - 1], refs[count - 1 : count + 1], refs[count + 1 :]
        grads, messages, (piece_out, left_out, bias_out, held) = refs[:sent], refs[sent:-4], refs[-4:]
        home = lax.div(lax.axis_index("col"), 2)
        for p, part in enumerate((own, *parts)):
            held[lax.rem(home - p + count, count)] = part[0:rows, :]
        total, bias = held[0, 0:share, :].astype(F32), joined(held[0, share:, :])
        for n in range(1, count):
            total += held[n, 0:share, :].astype(F32)
            bias += joined(held[n, share:, :])
        piece = total.astype(BF16)
        piece_out[...] = piece
        for message, other in zip(messages, grads, strict=True):
            message[0:share, :] = piece
            message[share:, :] = other[...]
        bias_out[...] = jnp.broadcast_to(bias, bias_out.shape)
        left = grad[...]
        for part in parts:
            left += part[rows:, :].astype(F32)
        left_out[...] = left

    shapes = [((share + grad.shape[0], LANES), BF16) for grad in grads]
    shapes += [((share, LANES), BF16), (left_own.shape, F32), ((8, LANES), F32)]
    scratch = [pltpu.VMEM((count, rows, LANES), BF16)]
    *messages, piece, left, bias = call(
        kernel, [*parts, left_own, own, *grads], shapes, scratch=scratch
    )
    return messages, piece, left, bias


def finish(parts, piece, left, right_own, bias, left_shape, right_shape, scale, bias_scale):
    count = len(parts) + 1
    share = piece.shape[0]

    def kernel(*refs):
        parts, refs = refs[: count - 1], refs[count - 1 :]
        piece, left, right_own, bias, projection, left_out, right_out, bias_out = refs
        me = lax.axis_index("row")
        right = right_own[...]
        for p, part in enumerate((piece, *parts)):
            rows = pl.ds(pl.multiple_of(lax.rem(me - p + count, count) * share, share), share)
            projection[rows, :] = part[0:share, :].astype(F32) * scale
            if p > 0:
                right += part[share:, :].astype(F32)
        unfold(left[...], left_out.shape[0], left_out)
        unfold(right, right_out.shape[0], right_out)
        bias_out[...] = bias[0:1, :] * bias_scale

    shapes = [
        ((count * share, PAIR_FEATURES), F32),
        (left_shape, F32),
        (right_shape, F32),
        ((1, PAIR_FEATURES), F32),
    ]
    return call(kernel, [*parts, piece, left, right_own, bias], shapes)


def shift(x, axis, distance):
    count = lax.axis_size(axis)
    return lax.ppermute(x, axis, [(n, (n + distance) % count) for n in range(count)])


def neighbour(x, axis):
    return lax.ppermute(x, axis, [(n, n ^ 1) for n in range(lax.axis_size(axis))])


def shift_pairs(x, axis):
    return [x] + [shift(x, axis, d) for d in range(2, lax.axis_size(axis), 2)]


def send(parts, axis):
    return [shift(part, axis, d) for d, part in enumerate(parts, 1)]


def send_pairs(parts, axis):
    return [shift(part, axis, 2 * p) for p, part in enumerate(parts, 1)]


def local(
    first_homolog_features, second_homolog_features, final_projection_matrix, output_bias, cotangent
):
    i_n, j_n, _ = cotangent.shape
    row_n, col_n = lax.axis_size("row"), lax.axis_size("col")
    sequences = second_homolog_features.shape[0] * row_n
    channels = final_projection_matrix.shape[0]
    res_total = i_n * row_n
    a_near = neighbour(first_homolog_features, "col")
    b_near = neighbour(second_homolog_features, "row")
    we, wt, a, b, w, g = load(
        first_homolog_features,
        second_homolog_features,
        final_projection_matrix,
        cotangent.reshape(i_n * j_n, PAIR_FEATURES),
    )
    a_pair, b_pair = stack((a, a_near), (b, b_near))
    a_pieces = shift_pairs(a_pair, "col")
    b_pieces = shift_pairs(b_pair, "row")
    y, gt, bias_rows = prepare(we, g, i_n, j_n)

    x, a_held, b_wide, (own, *messages) = outer(
        a_pieces, b_pieces, g, bias_rows, i_n, j_n, sequences
    )
    share = channels // row_n

    parts = [own] + send(messages, "row")
    left_kept, (left_sent,) = gradient(
        b_wide, y, own, "col", in_pairs(col_n), col_n // 2, 1, i_n, j_n, sequences
    )

    message = row_sum(parts, left_sent, share)
    near = neighbour(message, "col")
    y2 = product(w, gt, message)
    left_own, messages = column_pair_sum(message, near, left_kept, y2, share)
    parts = send_pairs(messages, "col")
    (right_own,), right_sent = gradient(
        a_held, y2, left_own, "row", in_order(row_n), 1, row_n - 1, j_n, i_n, sequences
    )

    messages, piece, left_own, bias = column_sum(parts, left_own, messages[0], right_sent, share)
    parts = send(messages, "row")
    pair_map = pair(x, wt, output_bias, sequences)
    projection, left_grad, right_grad, bias_grad = finish(
        parts,
        piece,
        left_own,
        right_own,
        bias,
        first_homolog_features.shape,
        second_homolog_features.shape,
        1.0 / (sequences * res_total),
        1.0 / res_total,
    )
    return (
        pair_map.reshape(i_n, j_n, PAIR_FEATURES),
        left_grad,
        right_grad,
        projection,
        bias_grad.reshape(PAIR_FEATURES),
    )


def solution(mesh):
    return jax.shard_map(
        local,
        mesh=mesh,
        in_specs=(
            P(("dp", "col"), "row"),
            P(("dp", "row"), "col"),
            P(),
            P(),
            P(("dp", "row"), "col", None),
        ),
        out_specs=(
            P(("dp", "row"), "col", None),
            P(("dp", "col"), "row"),
            P(("dp", "row"), "col"),
            P("dp", None),
            P("dp"),
        ),
        check_vma=False,
    )
```

```python
import functools

import jax
import jax.numpy as jnp
from jax import lax
from jax.experimental import pallas as pl
from jax.experimental.pallas import tpu as pltpu
from jax.sharding import PartitionSpec as P

PROJECTED_DEPTH = 32
PAIR_FEATURES = 128
GROUP = 8
MULTIPLY_ROWS = 384
CHUNKS = 2
BIAS_ROWS = 16
LANES = 128
F32 = jnp.float32
BF16 = jnp.bfloat16
MIB = 1024 * 1024

ROWS_BY_ROWS = (((1,), (1,)), ((), ()))
COLS_BY_COLS = (((0,), (0,)), ((), ()))


def params(sequences=0):
    return pltpu.CompilerParams(vmem_limit_bytes=min(10 + 10 * sequences // 32, 50) * MIB + 2 * MIB)


def whole(shape):
    return pl.BlockSpec(shape, lambda t: (0,) * len(shape))


def dot(x, y, dims=(((1,), (0,)), ((), ()))):
    return lax.dot_general(x, y, dims, preferred_element_type=F32)


def load_kernel(a_hbm, b_hbm, w_hbm, g_hbm, we_ref, wt_ref, a_ref, b_ref, w_ref, g_ref, w32, sems):
    depth = PROJECTED_DEPTH
    copies = [
        pltpu.make_async_copy(source, target, sems.at[n])
        for n, (source, target) in enumerate(
            [(w_hbm, w_ref), (g_hbm, g_ref), (a_hbm, a_ref), (b_hbm, b_ref)]
        )
    ]
    for copy in copies:
        copy.start()
    copies[0].wait()
    w32[...] = w_ref[...].astype(F32)
    for e in range(depth):
        block = w32[pl.ds(e, depth, stride=depth), :]
        we_ref[e * depth : (e + 1) * depth, :] = block.astype(BF16)
    wt_ref[...] = we_ref[...].astype(F32).T.astype(BF16)
    for copy in copies[1:]:
        copy.wait()


def in_vmem():
    return pl.BlockSpec(memory_space=pltpu.VMEM)


def load(a, b, w, g):
    shapes = [
        jax.ShapeDtypeStruct(w.shape, BF16),
        jax.ShapeDtypeStruct(w.shape[::-1], BF16),
        *[jax.ShapeDtypeStruct(x.shape, BF16) for x in (a, b, w, g)],
    ]
    return pl.pallas_call(
        load_kernel,
        in_specs=[pl.BlockSpec(memory_space=pltpu.HBM)] * 4,
        out_specs=[in_vmem()] * len(shapes),
        out_shape=shapes,
        scratch_shapes=[pltpu.VMEM(w.shape, F32), pltpu.SemaphoreType.DMA((4,))],
        compiler_params=params(),
        cost_estimate=pl.CostEstimate(
            flops=1000 * w.size, bytes_accessed=16 * w.size, transcendentals=0
        ),
    )(*[pltpu.with_memory_space_constraint(x, pltpu.HBM) for x in (a, b, w, g)])


def stack(*groups):
    def kernel(*refs):
        refs, outs = refs[: -len(groups)], refs[-len(groups) :]
        for group, out in zip(groups, outs, strict=True):
            blocks = [ref[...].astype(F32) for ref in refs[: len(group)]]
            refs = refs[len(group) :]
            out[...] = jnp.concatenate(blocks, axis=0).astype(BF16)

    shapes = [((len(group) * group[0].shape[0], group[0].shape[1]), BF16) for group in groups]
    return call(kernel, [x for group in groups for x in group], shapes)


def split(total):
    high = total.astype(BF16).astype(F32)
    row = lax.broadcasted_iota(jnp.int32, (BIAS_ROWS, PAIR_FEATURES), 0)
    return jnp.where(row == 0, high, jnp.where(row == 1, total - high, 0.0)).astype(BF16)


def joined(block):
    block = block.astype(F32)
    return block[0:1] + block[1:2]


def multiply(left_ref, right_ref, out_ref):
    for n in range(0, right_ref.shape[0], MULTIPLY_ROWS):
        rows = slice(n, n + MULTIPLY_ROWS)
        out_ref[:, rows] = dot(left_ref[...], right_ref[rows, :], ROWS_BY_ROWS).astype(BF16)


def prepare_kernel(i_n, j_n, we_ref, g_ref, y_ref, gt_ref, bias_ref, g32):
    g32[...] = g_ref[...].astype(F32)
    bias_ref[...] = split(jnp.sum(g32[...], axis=0, keepdims=True))
    multiply(we_ref, g_ref, y_ref)

    for j in range(j_n):
        gt_ref[j * i_n : (j + 1) * i_n, :] = g32[pl.ds(j, i_n, stride=j_n), :].astype(BF16)


def prepare(we, g, i_n, j_n):
    pairs = i_n * j_n
    channels = we.shape[0]
    shapes = [
        jax.ShapeDtypeStruct((channels, pairs), BF16),
        jax.ShapeDtypeStruct(g.shape, BF16),
        jax.ShapeDtypeStruct((BIAS_ROWS, PAIR_FEATURES), BF16),
    ]
    return pl.pallas_call(
        functools.partial(prepare_kernel, i_n, j_n),
        in_specs=[in_vmem()] * 2,
        out_specs=[in_vmem()] * len(shapes),
        out_shape=shapes,
        scratch_shapes=[pltpu.VMEM(g.shape, F32)],
        compiler_params=params(16),
        cost_estimate=pl.CostEstimate(
            flops=2 * pairs * channels * PAIR_FEATURES,
            bytes_accessed=4 * pairs * channels,
            transcendentals=0,
        ),
    )(we, g)


def join(pieces, axis, held):
    half = lax.axis_size(axis) // 2
    depth = pieces[0].shape[0] // half
    me = lax.axis_index(axis)
    odd, home = lax.rem(me, 2), lax.div(me, 2)
    for piece, parity in zip(pieces, (odd, 1 - odd), strict=True):
        block = piece[...].astype(F32)
        for p in range(half):
            place = (2 * lax.rem(home - p + half, half) + parity) * depth
            held[pl.ds(pl.multiple_of(place, depth), depth), :] = block[p * depth : (p + 1) * depth]


def repeat_matrix(sequences):
    shape = (sequences, GROUP * sequences)
    lane = lax.broadcasted_iota(jnp.int32, shape, 1)
    row = lax.broadcasted_iota(jnp.int32, shape, 0)
    return (lax.rem(lane, sequences) == row).astype(BF16)


def spread(held, wide):
    both = dot(held[...].T.astype(BF16), repeat_matrix(held.shape[0]))
    for l in range(wide.shape[0]):
        wide[l] = both[:, l * LANES : (l + 1) * LANES]


def tiles_of(sequences, tile):
    lane = lax.broadcasted_iota(jnp.int32, (1, LANES), 1) + tile * LANES
    return [
        (m, lax.div(lane, sequences) == m)
        for m in range(GROUP)
        if m * sequences < (tile + 1) * LANES and (m + 1) * sequences > tile * LANES
    ]


def diagonal_of(wide, channel, positions, sequences):
    columns = []
    for l in range(wide.shape[0]):
        block = wide[l, pl.ds(channel, positions, stride=PROJECTED_DEPTH), :].astype(BF16)
        members = dict(tiles_of(sequences, l))
        columns.append(
            jnp.concatenate(
                [
                    block * members[m].astype(F32).astype(BF16)
                    if m in members
                    else jnp.zeros(block.shape, BF16)
                    for m in range(GROUP)
                ],
                axis=0,
            )
        )
    return jnp.concatenate(columns, axis=1)


def near_of(me):
    return me + 1 - 2 * lax.rem(me, 2)


def outer_kernel(i_n, j_n, *refs):
    depth = PROJECTED_DEPTH
    row_n = lax.axis_size("row")
    a_pieces, b_pieces, refs = refs[:2], refs[2:4], refs[4:]
    g_ref, bias_ref, x_ref, a_held, b_wide = refs[:5]
    messages, (b_held, left, total) = refs[5 : 5 + row_n], refs[5 + row_n :]
    sequences = a_held.shape[0]
    groups = i_n // GROUP
    per_step = depth // CHUNKS
    span = GROUP * j_n

    join(a_pieces, "col", a_held)
    join(b_pieces, "row", b_held)
    spread(b_held, b_wide)
    turned = a_held[...].T.astype(BF16)
    shape = (sequences, GROUP * sequences)
    shifted = lax.broadcasted_iota(jnp.int32, shape, 1) - lax.broadcasted_iota(jnp.int32, shape, 0)
    value = jnp.zeros(left.shape, F32)
    for m in range(GROUP):
        rows = [
            turned[(k * GROUP + m) * depth : (k * GROUP + m + 1) * depth, :] for k in range(groups)
        ]
        value += dot(jnp.concatenate(rows, axis=0), (shifted == m * sequences).astype(BF16))
    left[...] = value.astype(BF16)

    @pl.loop(0, CHUNKS)
    def _(t):
        size = per_step * depth
        rows = pl.ds(pl.multiple_of(t * size, size), size)
        x_part = x_ref.at[rows]
        for e in range(0, per_step, 2):
            right = [diagonal_of(b_wide, t * per_step + e + n, j_n, sequences) for n in range(2)]
            product = dot(
                left[...], jnp.concatenate(right, axis=0), ROWS_BY_ROWS
            ).astype(BF16)
            for n in range(2):
                for k in range(groups):
                    x_part[(e + n) * depth : (e + n + 1) * depth, k * span : (k + 1) * span] = product[
                        k * depth : (k + 1) * depth, n * span : (n + 1) * span
                    ]
        total[rows, :] = dot(x_part[...], g_ref[...])

    share = total.shape[0] // row_n
    me = lax.axis_index("row")
    for p, message in enumerate(messages):
        part = lax.rem(me + p, row_n)
        for n in range(share // depth):
            block = total[pl.ds(part * (share // depth) + n, depth, stride=depth), :]
            message[n * depth : (n + 1) * depth, :] = block.astype(message.dtype)
        message[share:, :] = bias_ref[...].astype(message.dtype)


def outer(a_pieces, b_pieces, g, bias_rows, i_n, j_n, sequences):
    row_n = lax.axis_size("row")
    depth = PROJECTED_DEPTH
    channels = depth * depth
    pairs = i_n * j_n
    tiles = GROUP * sequences // LANES
    operands = [*a_pieces, *b_pieces, g, bias_rows]
    shapes = [jax.ShapeDtypeStruct((channels, pairs), BF16)]
    shapes += [
        jax.ShapeDtypeStruct((sequences, i_n * depth), F32),
        jax.ShapeDtypeStruct((tiles, j_n * depth, LANES), F32),
    ]
    shapes += [
        jax.ShapeDtypeStruct((channels // row_n + BIAS_ROWS, LANES), BF16 if p else F32)
        for p in range(row_n)
    ]
    results = pl.pallas_call(
        functools.partial(outer_kernel, i_n, j_n),
        in_specs=[in_vmem()] * len(operands),
        out_specs=[in_vmem()] * len(shapes),
        out_shape=shapes,
        scratch_shapes=[
            pltpu.VMEM((sequences, j_n * depth), F32),
            pltpu.VMEM((i_n // GROUP * depth, GROUP * sequences), BF16),
            pltpu.VMEM((channels, PAIR_FEATURES), F32),
        ],
        compiler_params=params(sequences),
        cost_estimate=pl.CostEstimate(
            flops=4 * pairs * channels * PAIR_FEATURES,
            bytes_accessed=2 * pairs * channels,
            transcendentals=0,
        ),
    )(*operands)
    return *results[:3], results[3:]


def gradient_kernel(axis, positions, others, sequences, *refs):
    depth = PROJECTED_DEPTH
    wide, source = refs[:2]
    outs, (result, grown, grad, own_wide) = refs[3:-4], refs[-4:]
    if len(wide.shape) == 2:
        spread(wide, own_wide)
        wide = own_wide
    parts = lax.axis_size(axis)
    per_step = depth // CHUNKS
    span = GROUP * others

    result[...] = jnp.zeros(result.shape, F32)

    @pl.loop(0, CHUNKS)
    def _(t):
        size = per_step * depth
        rows = pl.ds(pl.multiple_of(t * size, size), size)
        part = source.at[rows]
        for n in range(0, per_step, 2):
            blocks = [
                jnp.concatenate(
                    [
                        part[m * depth : (m + 1) * depth, k * span : (k + 1) * span]
                        for m in (n, n + 1)
                    ],
                    axis=1,
                )
                for k in range(positions // GROUP)
            ]
            right = [
                diagonal_of(wide, t * per_step + m, others, sequences) for m in (n, n + 1)
            ]
            result[...] += dot(jnp.concatenate(blocks, axis=0), jnp.concatenate(right, axis=0))

    scaled = (result[...] * (1.0 / sequences)).astype(BF16)
    for l in range(scaled.shape[1] // LANES):
        members = dict(tiles_of(sequences, l))
        for k in range(positions // GROUP):
            block = scaled[k * depth : (k + 1) * depth, l * LANES : (l + 1) * LANES]
            for m in range(GROUP):
                start = (k * GROUP + m) * depth
                grown[start : start + depth, l * LANES : (l + 1) * LANES] = (
                    block * members[m].astype(F32).astype(BF16)
                    if m in members
                    else jnp.zeros((depth, LANES), BF16)
                )
    grad[...] = dot(repeat_matrix(sequences), grown[...], ROWS_BY_ROWS)
    share = sequences // parts

    def rows_of(p):
        mine = grad[pl.ds(pl.multiple_of(p * share, share), share), :]
        return jnp.concatenate(
            [mine[:, l * LANES : (l + 1) * LANES] for l in range(mine.shape[1] // LANES)], axis=0
        )

    me = lax.axis_index(axis)
    near = me + 1 - 2 * lax.rem(me, 2)
    *kept, message = outs
    size = kept[0].shape[0]
    for p, out in enumerate(kept):
        out[...] = rows_of(lax.rem(me + 2 * p, parts))
        message[p * size : (p + 1) * size, :] = rows_of(lax.rem(near + 2 * p, parts)).astype(BF16)


def gradient(wide, source, after, axis, positions, others, sequences):
    depth = PROJECTED_DEPTH
    parts = lax.axis_size(axis)
    rows = sequences // parts * positions * depth // LANES
    shapes = [jax.ShapeDtypeStruct((rows, LANES), F32)] * (parts // 2)
    shapes += [jax.ShapeDtypeStruct((parts // 2 * rows, LANES), BF16)]
    tiles = GROUP * sequences // LANES if wide.ndim == 2 else 1
    *kept, message = pl.pallas_call(
        functools.partial(gradient_kernel, axis, positions, others, sequences),
        in_specs=[in_vmem(), in_vmem(), pl.BlockSpec(memory_space=pl.ANY)],
        out_specs=[in_vmem()] * len(shapes),
        out_shape=shapes,
        scratch_shapes=[
            pltpu.VMEM((positions // GROUP * depth, GROUP * sequences), F32),
            pltpu.VMEM((positions * depth, GROUP * sequences), BF16),
            pltpu.VMEM((sequences, positions * depth), F32),
            pltpu.VMEM((tiles, others * depth if wide.ndim == 2 else 8, LANES), F32),
        ],
        compiler_params=params(sequences),
        cost_estimate=pl.CostEstimate(
            flops=2 * source.size * PAIR_FEATURES,
            bytes_accessed=2 * source.size,
            transcendentals=0,
        ),
    )(wide, source, after)
    return kept, message


def product_kernel(left_ref, right_ref, _, out_ref):
    multiply(left_ref, right_ref, out_ref)


def product(left, right, after):
    shape = (left.shape[0], right.shape[0])
    return pl.pallas_call(
        product_kernel,
        in_specs=[in_vmem(), in_vmem(), pl.BlockSpec(memory_space=pl.ANY)],
        out_specs=in_vmem(),
        out_shape=jax.ShapeDtypeStruct(shape, BF16),
        compiler_params=params(16),
        cost_estimate=pl.CostEstimate(
            flops=2 * shape[0] * shape[1] * left.shape[1],
            bytes_accessed=4 * shape[0] * shape[1],
            transcendentals=0,
        ),
    )(left, right, after)


def pair_kernel(sequences, x_ref, wt_ref, bias_ref, _, out_ref, done_ref):
    done_ref[...] = jnp.zeros(done_ref.shape, F32)
    product = dot(wt_ref[...], x_ref[...])
    out_ref[...] = (product.T * (1.0 / sequences) + bias_ref[...]).astype(BF16)


def pair(x, wt, output_bias, after, sequences):
    channels, pairs = x.shape
    count = 3
    size = pairs // count
    return pl.pallas_call(
        functools.partial(pair_kernel, sequences),
        grid=(count,),
        in_specs=[
            pl.BlockSpec((channels, size), lambda t: (0, t)),
            whole(wt.shape),
            whole((1, PAIR_FEATURES)),
            pl.BlockSpec(memory_space=pl.ANY),
        ],
        out_specs=[pl.BlockSpec((size, PAIR_FEATURES), lambda t: (t, 0)), whole((8, LANES))],
        out_shape=[
            jax.ShapeDtypeStruct((pairs, PAIR_FEATURES), BF16),
            jax.ShapeDtypeStruct((8, LANES), F32),
        ],
        compiler_params=params(),
        cost_estimate=pl.CostEstimate(
            flops=4 * pairs * channels * PAIR_FEATURES,
            bytes_accessed=2 * pairs * channels,
            transcendentals=0,
        ),
    )(x, wt, output_bias.reshape(1, PAIR_FEATURES), after)


def unfold(total, share, out):
    for l in range(out.shape[1] // LANES):
        out[:, l * LANES : (l + 1) * LANES] = total[l * share : (l + 1) * share, :]


def call(kernel, operands, shapes, after=(), scratch=()):
    specs = [in_vmem()] * len(operands) + [pl.BlockSpec(memory_space=pl.ANY)] * len(after)
    return pl.pallas_call(
        kernel,
        in_specs=specs,
        out_specs=[in_vmem()] * len(shapes),
        out_shape=[jax.ShapeDtypeStruct(shape, kind) for shape, kind in shapes],
        scratch_shapes=scratch,
        compiler_params=params(),
    )(*operands, *after)


def row_sum(parts, after, share):
    count = len(parts)

    def kernel(*refs):
        parts, (_, message, held) = refs[:count], refs[count:]
        me = lax.axis_index("row")
        total = parts[0][0:share, :]
        for p, part in enumerate(parts):
            held[lax.rem(me - p + count, count)] = part[share:, :].astype(F32)
            if p > 0:
                total += part[0:share, :].astype(F32)
        bias = joined(held[0])
        for n in range(1, count):
            bias += joined(held[n])
        message[0:share, :] = total.astype(BF16)
        message[share:, :] = split(bias)

    scratch = [pltpu.VMEM((count, BIAS_ROWS, LANES), F32)]
    (message,) = call(kernel, parts, [((share + BIAS_ROWS, LANES), BF16)], [after], scratch)
    return message


def add_near(kept, near, own, messages):
    size = own.shape[0]
    for p, part in enumerate(kept):
        both = part[...] + near[p * size : (p + 1) * size, :].astype(F32)
        if p == 0:
            own[...] = both
        else:
            messages[p - 1][...] = both.astype(BF16)


def column_pair_sum(own, near, kept, grad_near, passed, share):
    count = len(kept)

    def kernel(own, near, grad_near, passed, *refs):
        kept, (message, passed_on, grad_own), messages = (
            refs[:count],
            refs[count : count + 3],
            refs[count + 3 :],
        )
        passed_on[...] = passed[...]
        total = own[0:share, :].astype(F32) + near[0:share, :].astype(F32)
        message[0:share, :] = total.astype(BF16)
        message[share:, :] = split(joined(own[share:, :]) + joined(near[share:, :]))
        add_near(kept, grad_near, grad_own, messages)

    size = kept[0].shape
    shapes = [(own.shape, BF16), (passed.shape, BF16), (size, F32)] + [(size, BF16)] * (count - 1)
    message, passed, grad_own, *messages = call(
        kernel, [own, near, grad_near, passed, *kept], shapes
    )
    return message, passed, grad_own, messages


def column_sum(parts, kept, grad_near, after, share):
    rows = share + BIAS_ROWS
    count = len(parts)
    kept_n = len(kept)

    def kernel(grad_near, *refs):
        parts, kept = refs[:count], refs[count : count + kept_n]
        refs = refs[count + kept_n + len(after) :]
        piece_out, bias_out, grad_own, *messages, held = refs
        home = lax.div(lax.axis_index("col"), 2)
        for p, part in enumerate(parts):
            held[lax.rem(home - p + count, count)] = part[...]
        total, bias = held[0, 0:share, :].astype(F32), joined(held[0, share:, :])
        for n in range(1, count):
            total += held[n, 0:share, :].astype(F32)
            bias += joined(held[n, share:, :])
        piece_out[...] = total.astype(BF16)
        bias_out[...] = jnp.broadcast_to(bias, bias_out.shape)
        add_near(kept, grad_near, grad_own, messages)

    size = kept[0].shape
    shapes = [((share, LANES), BF16), ((8, LANES), F32), (size, F32)] + [(size, BF16)] * (kept_n - 1)
    scratch = [pltpu.VMEM((count, rows, LANES), BF16)]
    piece, bias, grad_own, *messages = call(
        kernel, [grad_near, *parts, *kept], shapes, after, scratch
    )
    return piece, bias, grad_own, messages


def finish(pieces, left, right, bias, left_shape, right_shape, scale, bias_scale):
    count, left_n = len(pieces), len(left)
    share = pieces[0].shape[0]

    def kernel(*refs):
        pieces, left, right = refs[:count], refs[count : count + left_n], refs[count + left_n : -5]
        bias, projection, left_out, right_out, bias_out = refs[-5:]
        me = lax.axis_index("row")
        for p, piece in enumerate(pieces):
            rows = pl.ds(pl.multiple_of(lax.rem(me - p + count, count) * share, share), share)
            projection[rows, :] = piece[...].astype(F32) * scale
        for terms, out in ((left, left_out), (right, right_out)):
            total = terms[0][...]
            for term in terms[1:]:
                total += term[...].astype(F32)
            unfold(total, out.shape[0], out)
        bias_out[...] = bias[0:1, :] * bias_scale

    shapes = [
        ((count * share, PAIR_FEATURES), F32),
        (left_shape, F32),
        (right_shape, F32),
        ((1, PAIR_FEATURES), F32),
    ]
    return call(kernel, [*pieces, *left, *right, bias], shapes)


def shift(x, axis, distance):
    count = lax.axis_size(axis)
    return lax.ppermute(x, axis, [(n, (n + distance) % count) for n in range(count)])


def neighbour(x, axis):
    return lax.ppermute(x, axis, [(n, n ^ 1) for n in range(lax.axis_size(axis))])


def send(parts, axis):
    return [shift(part, axis, d) for d, part in enumerate(parts, 1)]


def spread_pairs(x, axis):
    return send_pairs([x] * (lax.axis_size(axis) // 2 - 1), axis)


def send_pairs(parts, axis):
    return [shift(part, axis, 2 * p) for p, part in enumerate(parts, 1)]


def local(
    first_homolog_features, second_homolog_features, final_projection_matrix, output_bias, cotangent
):
    i_n, j_n, _ = cotangent.shape
    row_n = lax.axis_size("row")
    sequences = second_homolog_features.shape[0] * row_n
    channels = final_projection_matrix.shape[0]
    res_total = i_n * row_n
    a_far = spread_pairs(first_homolog_features, "col")
    b_far = spread_pairs(second_homolog_features, "row")
    we, wt, a, b, w, g = load(
        first_homolog_features,
        second_homolog_features,
        final_projection_matrix,
        cotangent.reshape(i_n * j_n, PAIR_FEATURES),
    )
    a, b = stack([a, *a_far], [b, *b_far])
    a_pieces = [a, neighbour(a, "col")]
    b_pieces = [b, neighbour(b, "row")]
    y, gt, bias_rows = prepare(we, g, i_n, j_n)

    x, a_held, b_wide, (own, *messages) = outer(
        a_pieces, b_pieces, g, bias_rows, i_n, j_n, sequences
    )
    share = channels // row_n

    parts = [own] + send(messages, "row")
    y2 = product(w, gt, own)
    right_kept, message = gradient(a_held, y2, own, "row", j_n, i_n, sequences)
    right_near = neighbour(message, "row")

    message = row_sum(parts, message, share)
    near = neighbour(message, "col")
    left_kept, left_message = gradient(b_wide, y, message, "col", i_n, j_n, sequences)
    message, left_message, right_own, right_messages = column_pair_sum(
        message, near, right_kept, right_near, left_message, share
    )

    parts = [message] + spread_pairs(message, "col")
    left_near = neighbour(left_message, "col")
    right = [right_own] + send_pairs(right_messages, "row")
    pair_map, pair_done = pair(x, wt, output_bias, message, sequences)
    piece, bias, left_own, left_messages = column_sum(
        parts, left_kept, left_near, [pair_done, *right[1:]], share
    )

    pieces = [piece] + send([piece] * (row_n - 1), "row")
    left = [left_own] + send_pairs(left_messages, "col")
    projection, left_grad, right_grad, bias_grad = finish(
        pieces,
        left,
        right,
        bias,
        first_homolog_features.shape,
        second_homolog_features.shape,
        1.0 / (sequences * res_total),
        1.0 / res_total,
    )
    return (
        pair_map.reshape(i_n, j_n, PAIR_FEATURES),
        left_grad,
        right_grad,
        projection,
        bias_grad.reshape(PAIR_FEATURES),
    )


def solution(mesh):
    return jax.shard_map(
        local,
        mesh=mesh,
        in_specs=(
            P(("dp", "col"), "row"),
            P(("dp", "row"), "col"),
            P(),
            P(),
            P(("dp", "row"), "col", None),
        ),
        out_specs=(
            P(("dp", "row"), "col", None),
            P(("dp", "col"), "row"),
            P(("dp", "row"), "col"),
            P("dp", None),
            P("dp"),
        ),
        check_vma=False,
    )
```

```python
import functools

import jax
import jax.numpy as jnp
from jax import lax
from jax.experimental import pallas as pl
from jax.experimental.pallas import tpu as pltpu
from jax.sharding import PartitionSpec as P

PROJECTED_DEPTH = 32
PAIR_FEATURES = 128
GROUP = 8
MULTIPLY_ROWS = 384
CHUNKS = 2
BIAS_ROWS = 16
LANES = 128
F32 = jnp.float32
BF16 = jnp.bfloat16
MIB = 1024 * 1024

ROWS_BY_ROWS = (((1,), (1,)), ((), ()))
COLS_BY_COLS = (((0,), (0,)), ((), ()))


def params(sequences=0):
    return pltpu.CompilerParams(vmem_limit_bytes=min(10 + 10 * sequences // 32, 50) * MIB + 2 * MIB)


def whole(shape):
    return pl.BlockSpec(shape, lambda t: (0,) * len(shape))


def dot(x, y, dims=(((1,), (0,)), ((), ()))):
    return lax.dot_general(x, y, dims, preferred_element_type=F32)


def load_kernel(a_hbm, b_hbm, w_hbm, g_hbm, we_ref, wt_ref, a_ref, b_ref, w_ref, g_ref, w32, sems):
    depth = PROJECTED_DEPTH
    copies = [
        pltpu.make_async_copy(source, target, sems.at[n])
        for n, (source, target) in enumerate(
            [(w_hbm, w_ref), (g_hbm, g_ref), (a_hbm, a_ref), (b_hbm, b_ref)]
        )
    ]
    for copy in copies:
        copy.start()
    copies[0].wait()
    w32[...] = w_ref[...].astype(F32)
    for e in range(depth):
        block = w32[pl.ds(e, depth, stride=depth), :]
        we_ref[e * depth : (e + 1) * depth, :] = block.astype(BF16)
    wt_ref[...] = we_ref[...].astype(F32).T.astype(BF16)
    for copy in copies[1:]:
        copy.wait()


def in_vmem():
    return pl.BlockSpec(memory_space=pltpu.VMEM)


def load(a, b, w, g):
    shapes = [
        jax.ShapeDtypeStruct(w.shape, BF16),
        jax.ShapeDtypeStruct(w.shape[::-1], BF16),
        *[jax.ShapeDtypeStruct(x.shape, BF16) for x in (a, b, w, g)],
    ]
    return pl.pallas_call(
        load_kernel,
        in_specs=[pl.BlockSpec(memory_space=pltpu.HBM)] * 4,
        out_specs=[in_vmem()] * len(shapes),
        out_shape=shapes,
        scratch_shapes=[pltpu.VMEM(w.shape, F32), pltpu.SemaphoreType.DMA((4,))],
        compiler_params=params(),
        cost_estimate=pl.CostEstimate(
            flops=1000 * w.size, bytes_accessed=16 * w.size, transcendentals=0
        ),
    )(*[pltpu.with_memory_space_constraint(x, pltpu.HBM) for x in (a, b, w, g)])


def stack(*groups):
    def kernel(*refs):
        refs, outs = refs[: -len(groups)], refs[-len(groups) :]
        for group, out in zip(groups, outs, strict=True):
            blocks = [ref[...].astype(F32) for ref in refs[: len(group)]]
            refs = refs[len(group) :]
            out[...] = jnp.concatenate(blocks, axis=0).astype(BF16)

    shapes = [((len(group) * group[0].shape[0], group[0].shape[1]), BF16) for group in groups]
    return call(kernel, [x for group in groups for x in group], shapes)


def split(total):
    high = total.astype(BF16).astype(F32)
    row = lax.broadcasted_iota(jnp.int32, (BIAS_ROWS, PAIR_FEATURES), 0)
    return jnp.where(row == 0, high, jnp.where(row == 1, total - high, 0.0)).astype(BF16)


def joined(block):
    block = block.astype(F32)
    return block[0:1] + block[1:2]


def multiply(left_ref, right_ref, out_ref):
    for n in range(0, right_ref.shape[0], MULTIPLY_ROWS):
        rows = slice(n, n + MULTIPLY_ROWS)
        out_ref[:, rows] = dot(left_ref[...], right_ref[rows, :], ROWS_BY_ROWS).astype(BF16)


def prepare_kernel(i_n, j_n, we_ref, g_ref, y_ref, gt_ref, bias_ref, g32):
    g32[...] = g_ref[...].astype(F32)
    bias_ref[...] = split(jnp.sum(g32[...], axis=0, keepdims=True))
    multiply(we_ref, g_ref, y_ref)

    for j in range(j_n):
        gt_ref[j * i_n : (j + 1) * i_n, :] = g32[pl.ds(j, i_n, stride=j_n), :].astype(BF16)


def prepare(we, g, i_n, j_n):
    pairs = i_n * j_n
    channels = we.shape[0]
    shapes = [
        jax.ShapeDtypeStruct((channels, pairs), BF16),
        jax.ShapeDtypeStruct(g.shape, BF16),
        jax.ShapeDtypeStruct((BIAS_ROWS, PAIR_FEATURES), BF16),
    ]
    return pl.pallas_call(
        functools.partial(prepare_kernel, i_n, j_n),
        in_specs=[in_vmem()] * 2,
        out_specs=[in_vmem()] * len(shapes),
        out_shape=shapes,
        scratch_shapes=[pltpu.VMEM(g.shape, F32)],
        compiler_params=params(16),
        cost_estimate=pl.CostEstimate(
            flops=2 * pairs * channels * PAIR_FEATURES,
            bytes_accessed=4 * pairs * channels,
            transcendentals=0,
        ),
    )(we, g)


def join(pieces, axis, held):
    half = lax.axis_size(axis) // 2
    depth = pieces[0].shape[0] // half
    me = lax.axis_index(axis)
    odd, home = lax.rem(me, 2), lax.div(me, 2)
    for piece, parity in zip(pieces, (odd, 1 - odd), strict=True):
        block = piece[...].astype(F32)
        for p in range(half):
            place = (2 * lax.rem(home - p + half, half) + parity) * depth
            held[pl.ds(pl.multiple_of(place, depth), depth), :] = block[p * depth : (p + 1) * depth]


def repeat_matrix(sequences):
    shape = (sequences, GROUP * sequences)
    lane = lax.broadcasted_iota(jnp.int32, shape, 1)
    row = lax.broadcasted_iota(jnp.int32, shape, 0)
    return (lax.rem(lane, sequences) == row).astype(BF16)


def spread(held, wide):
    both = dot(held[...].T.astype(BF16), repeat_matrix(held.shape[0]))
    for l in range(wide.shape[0]):
        wide[l] = both[:, l * LANES : (l + 1) * LANES]


def tiles_of(sequences, tile):
    lane = lax.broadcasted_iota(jnp.int32, (1, LANES), 1) + tile * LANES
    return [
        (m, lax.div(lane, sequences) == m)
        for m in range(GROUP)
        if m * sequences < (tile + 1) * LANES and (m + 1) * sequences > tile * LANES
    ]


def diagonal_of(wide, channel, positions, sequences):
    columns = []
    for l in range(wide.shape[0]):
        block = wide[l, pl.ds(channel, positions, stride=PROJECTED_DEPTH), :].astype(BF16)
        members = dict(tiles_of(sequences, l))
        columns.append(
            jnp.concatenate(
                [
                    block * members[m].astype(F32).astype(BF16)
                    if m in members
                    else jnp.zeros(block.shape, BF16)
                    for m in range(GROUP)
                ],
                axis=0,
            )
        )
    return jnp.concatenate(columns, axis=1)


def near_of(me):
    return me + 1 - 2 * lax.rem(me, 2)


def near_of(me):
    return me + 1 - 2 * lax.rem(me, 2)


def in_order(count):
    return lambda me: ([me], [[lax.rem(me + d, count)] for d in range(1, count)])


def in_pairs(count):
    def plan(me):
        steps = range(0, count, 2)
        near = near_of(me)
        return [lax.rem(me + d, count) for d in steps], [[lax.rem(near + d, count) for d in steps]]

    return plan


def outer_kernel(i_n, j_n, *refs):
    depth = PROJECTED_DEPTH
    row_n = lax.axis_size("row")
    a_pieces, b_pieces, refs = refs[:2], refs[2:4], refs[4:]
    g_ref, bias_ref, x_ref, a_held, b_wide = refs[:5]
    messages, (b_held, left, total) = refs[5 : 5 + row_n], refs[5 + row_n :]
    sequences = a_held.shape[0]
    groups = i_n // GROUP
    per_step = depth // CHUNKS
    span = GROUP * j_n

    join(a_pieces, "col", a_held)
    join(b_pieces, "row", b_held)
    spread(b_held, b_wide)
    turned = a_held[...].T.astype(BF16)
    shape = (sequences, GROUP * sequences)
    shifted = lax.broadcasted_iota(jnp.int32, shape, 1) - lax.broadcasted_iota(jnp.int32, shape, 0)
    value = jnp.zeros(left.shape, F32)
    for m in range(GROUP):
        rows = [
            turned[(k * GROUP + m) * depth : (k * GROUP + m + 1) * depth, :] for k in range(groups)
        ]
        value += dot(jnp.concatenate(rows, axis=0), (shifted == m * sequences).astype(BF16))
    left[...] = value.astype(BF16)

    @pl.loop(0, CHUNKS)
    def _(t):
        size = per_step * depth
        rows = pl.ds(pl.multiple_of(t * size, size), size)
        x_part = x_ref.at[rows]
        for e in range(0, per_step, 2):
            right = [diagonal_of(b_wide, t * per_step + e + n, j_n, sequences) for n in range(2)]
            product = dot(
                left[...], jnp.concatenate(right, axis=0), ROWS_BY_ROWS
            ).astype(BF16)
            for n in range(2):
                for k in range(groups):
                    x_part[(e + n) * depth : (e + n + 1) * depth, k * span : (k + 1) * span] = product[
                        k * depth : (k + 1) * depth, n * span : (n + 1) * span
                    ]
        total[rows, :] = dot(x_part[...], g_ref[...])

    share = total.shape[0] // row_n
    me = lax.axis_index("row")
    for p, message in enumerate(messages):
        part = lax.rem(me + p, row_n)
        for n in range(share // depth):
            block = total[pl.ds(part * (share // depth) + n, depth, stride=depth), :]
            message[n * depth : (n + 1) * depth, :] = block.astype(message.dtype)
        message[share:, :] = bias_ref[...].astype(message.dtype)


def outer(a_pieces, b_pieces, g, bias_rows, i_n, j_n, sequences):
    row_n = lax.axis_size("row")
    depth = PROJECTED_DEPTH
    channels = depth * depth
    pairs = i_n * j_n
    tiles = GROUP * sequences // LANES
    operands = [*a_pieces, *b_pieces, g, bias_rows]
    shapes = [jax.ShapeDtypeStruct((channels, pairs), BF16)]
    shapes += [
        jax.ShapeDtypeStruct((sequences, i_n * depth), F32),
        jax.ShapeDtypeStruct((tiles, j_n * depth, LANES), F32),
    ]
    shapes += [
        jax.ShapeDtypeStruct((channels // row_n + BIAS_ROWS, LANES), BF16 if p else F32)
        for p in range(row_n)
    ]
    results = pl.pallas_call(
        functools.partial(outer_kernel, i_n, j_n),
        in_specs=[in_vmem()] * len(operands),
        out_specs=[in_vmem()] * len(shapes),
        out_shape=shapes,
        scratch_shapes=[
            pltpu.VMEM((sequences, j_n * depth), F32),
            pltpu.VMEM((i_n // GROUP * depth, GROUP * sequences), BF16),
            pltpu.VMEM((channels, PAIR_FEATURES), F32),
        ],
        compiler_params=params(sequences),
        cost_estimate=pl.CostEstimate(
            flops=4 * pairs * channels * PAIR_FEATURES,
            bytes_accessed=2 * pairs * channels,
            transcendentals=0,
        ),
    )(*operands)
    return *results[:3], results[3:]


def gradient_kernel(axis, plan, kept, positions, others, sequences, *refs):
    depth = PROJECTED_DEPTH
    wide, source = refs[:2]
    outs, (result, grown, grad, own_wide) = refs[3:-4], refs[-4:]
    if len(wide.shape) == 2:
        spread(wide, own_wide)
        wide = own_wide
    parts = lax.axis_size(axis)
    per_step = depth // CHUNKS
    span = GROUP * others

    result[...] = jnp.zeros(result.shape, F32)

    @pl.loop(0, CHUNKS)
    def _(t):
        size = per_step * depth
        rows = pl.ds(pl.multiple_of(t * size, size), size)
        part = source.at[rows]
        for n in range(0, per_step, 2):
            blocks = [
                jnp.concatenate(
                    [
                        part[m * depth : (m + 1) * depth, k * span : (k + 1) * span]
                        for m in (n, n + 1)
                    ],
                    axis=1,
                )
                for k in range(positions // GROUP)
            ]
            right = [
                diagonal_of(wide, t * per_step + m, others, sequences) for m in (n, n + 1)
            ]
            result[...] += dot(jnp.concatenate(blocks, axis=0), jnp.concatenate(right, axis=0))

    scaled = (result[...] * (1.0 / sequences)).astype(BF16)
    for l in range(scaled.shape[1] // LANES):
        members = dict(tiles_of(sequences, l))
        for k in range(positions // GROUP):
            block = scaled[k * depth : (k + 1) * depth, l * LANES : (l + 1) * LANES]
            for m in range(GROUP):
                start = (k * GROUP + m) * depth
                grown[start : start + depth, l * LANES : (l + 1) * LANES] = (
                    block * members[m].astype(F32).astype(BF16)
                    if m in members
                    else jnp.zeros((depth, LANES), BF16)
                )
    grad[...] = dot(repeat_matrix(sequences), grown[...], ROWS_BY_ROWS)
    share = sequences // parts

    def rows_of(p):
        mine = grad[pl.ds(pl.multiple_of(p * share, share), share), :]
        return jnp.concatenate(
            [mine[:, l * LANES : (l + 1) * LANES] for l in range(mine.shape[1] // LANES)], axis=0
        )

    stay, go = plan(lax.axis_index(axis))
    for p, out in zip(stay, outs[:kept], strict=True):
        out[...] = rows_of(p)
    for group, out in zip(go, outs[kept:], strict=True):
        size = out.shape[0] // len(group)
        for n, p in enumerate(group):
            out[n * size : (n + 1) * size, :] = rows_of(p).astype(BF16)


def gradient(wide, source, after, axis, plan, kept, groups, positions, others, sequences):
    depth = PROJECTED_DEPTH
    parts = lax.axis_size(axis)
    rows = sequences // parts * positions * depth // LANES
    shapes = [jax.ShapeDtypeStruct((rows, LANES), F32)] * kept
    group = (parts - kept) // groups
    shapes += [jax.ShapeDtypeStruct((group * rows, LANES), BF16)] * groups
    tiles = GROUP * sequences // LANES if wide.ndim == 2 else 1
    results = pl.pallas_call(
        functools.partial(gradient_kernel, axis, plan, kept, positions, others, sequences),
        in_specs=[in_vmem(), in_vmem(), pl.BlockSpec(memory_space=pl.ANY)],
        out_specs=[in_vmem()] * len(shapes),
        out_shape=shapes,
        scratch_shapes=[
            pltpu.VMEM((positions // GROUP * depth, GROUP * sequences), F32),
            pltpu.VMEM((positions * depth, GROUP * sequences), BF16),
            pltpu.VMEM((sequences, positions * depth), F32),
            pltpu.VMEM((tiles, others * depth if wide.ndim == 2 else 8, LANES), F32),
        ],
        compiler_params=params(sequences),
        cost_estimate=pl.CostEstimate(
            flops=2 * source.size * PAIR_FEATURES,
            bytes_accessed=2 * source.size,
            transcendentals=0,
        ),
    )(wide, source, after)
    return results[:kept], results[kept:]


def product_kernel(left_ref, right_ref, _, out_ref):
    multiply(left_ref, right_ref, out_ref)


def product(left, right, after):
    shape = (left.shape[0], right.shape[0])
    return pl.pallas_call(
        product_kernel,
        in_specs=[in_vmem(), in_vmem(), pl.BlockSpec(memory_space=pl.ANY)],
        out_specs=in_vmem(),
        out_shape=jax.ShapeDtypeStruct(shape, BF16),
        compiler_params=params(16),
        cost_estimate=pl.CostEstimate(
            flops=2 * shape[0] * shape[1] * left.shape[1],
            bytes_accessed=4 * shape[0] * shape[1],
            transcendentals=0,
        ),
    )(left, right, after)


def pair_kernel(sequences, x_ref, wt_ref, bias_ref, _, out_ref):
    product = dot(wt_ref[...], x_ref[...])
    out_ref[...] = (product.T * (1.0 / sequences) + bias_ref[...]).astype(BF16)


def pair(x, wt, output_bias, after, sequences):
    channels, pairs = x.shape
    count = 3
    size = pairs // count
    return pl.pallas_call(
        functools.partial(pair_kernel, sequences),
        grid=(count,),
        in_specs=[
            pl.BlockSpec((channels, size), lambda t: (0, t)),
            whole(wt.shape),
            whole((1, PAIR_FEATURES)),
            pl.BlockSpec(memory_space=pl.ANY),
        ],
        out_specs=pl.BlockSpec((size, PAIR_FEATURES), lambda t: (t, 0)),
        out_shape=jax.ShapeDtypeStruct((pairs, PAIR_FEATURES), BF16),
        compiler_params=params(),
        cost_estimate=pl.CostEstimate(
            flops=4 * pairs * channels * PAIR_FEATURES,
            bytes_accessed=2 * pairs * channels,
            transcendentals=0,
        ),
    )(x, wt, output_bias.reshape(1, PAIR_FEATURES), after)


def unfold(total, share, out):
    for l in range(out.shape[1] // LANES):
        out[:, l * LANES : (l + 1) * LANES] = total[l * share : (l + 1) * share, :]


def call(kernel, operands, shapes, after=(), scratch=()):
    specs = [in_vmem()] * len(operands) + [pl.BlockSpec(memory_space=pl.ANY)] * len(after)
    return pl.pallas_call(
        kernel,
        in_specs=specs,
        out_specs=[in_vmem()] * len(shapes),
        out_shape=[jax.ShapeDtypeStruct(shape, kind) for shape, kind in shapes],
        scratch_shapes=scratch,
        compiler_params=params(),
    )(*operands, *after)


def row_sum(parts, after, share):
    count = len(parts)

    def kernel(*refs):
        parts, (_, message, held) = refs[:count], refs[count:]
        me = lax.axis_index("row")
        total = parts[0][0:share, :]
        for p, part in enumerate(parts):
            held[lax.rem(me - p + count, count)] = part[share:, :].astype(F32)
            if p > 0:
                total += part[0:share, :].astype(F32)
        bias = joined(held[0])
        for n in range(1, count):
            bias += joined(held[n])
        message[0:share, :] = total.astype(BF16)
        message[share:, :] = split(bias)

    scratch = [pltpu.VMEM((count, BIAS_ROWS, LANES), F32)]
    (message,) = call(kernel, parts, [((share + BIAS_ROWS, LANES), BF16)], [after], scratch)
    return message


def pair_sum(kept, near, after):
    def kernel(*refs):
        kept, near, (own, *messages) = refs[:count], refs[count], refs[count + 2 :]
        size = own.shape[0]
        for p, part in enumerate(kept):
            both = part[...] + near[p * size : (p + 1) * size, :].astype(F32)
            if p == 0:
                own[...] = both
            else:
                messages[p - 1][...] = both.astype(BF16)

    count = len(kept)
    shapes = [(kept[0].shape, F32)] + [(kept[0].shape, BF16)] * (count - 1)
    own, *messages = call(kernel, [*kept, near], shapes, [after])
    return own, messages


def column_pair_sum(own, near, after, share):
    def kernel(own, near, _, message):
        total = own[0:share, :].astype(F32) + near[0:share, :].astype(F32)
        message[0:share, :] = total.astype(BF16)
        message[share:, :] = split(joined(own[share:, :]) + joined(near[share:, :]))

    (message,) = call(kernel, [own, near], [(own.shape, BF16)], [after])
    return message


def column_sum(parts, grads, share):
    rows = share + BIAS_ROWS
    count, sent = len(parts), len(grads)

    def kernel(*refs):
        parts, grads, refs = refs[:count], refs[count : count + sent], refs[count + sent :]
        messages, (piece_out, bias_out, held) = refs[:sent], refs[sent:]
        home = lax.div(lax.axis_index("col"), 2)
        for p, part in enumerate(parts):
            held[lax.rem(home - p + count, count)] = part[...]
        total, bias = held[0, 0:share, :].astype(F32), joined(held[0, share:, :])
        for n in range(1, count):
            total += held[n, 0:share, :].astype(F32)
            bias += joined(held[n, share:, :])
        piece = total.astype(BF16)
        piece_out[...] = piece
        for message, grad in zip(messages, grads, strict=True):
            message[0:share, :] = piece
            message[share:, :] = grad[...]
        bias_out[...] = jnp.broadcast_to(bias, bias_out.shape)

    shapes = [((share + grad.shape[0], LANES), BF16) for grad in grads]
    shapes += [((share, LANES), BF16), ((8, LANES), F32)]
    scratch = [pltpu.VMEM((count, rows, LANES), BF16)]
    *messages, piece, bias = call(kernel, [*parts, *grads], shapes, scratch=scratch)
    return messages, piece, bias


def finish(pieces, left, right_own, bias, left_shape, right_shape, scale, bias_scale):
    count, left_n = len(pieces), len(left)
    share = pieces[0].shape[0]

    def kernel(*refs):
        pieces, left, refs = refs[:count], refs[count : count + left_n], refs[count + left_n :]
        right_own, bias, projection, left_out, right_out, bias_out = refs
        me = lax.axis_index("row")
        right_total = right_own[...]
        for p, piece in enumerate(pieces):
            rows = pl.ds(pl.multiple_of(lax.rem(me - p + count, count) * share, share), share)
            projection[rows, :] = piece[0:share, :].astype(F32) * scale
            if p > 0:
                right_total += piece[share:, :].astype(F32)
        left_total = left[0][...]
        for term in left[1:]:
            left_total += term[...].astype(F32)
        unfold(left_total, left_out.shape[0], left_out)
        unfold(right_total, right_out.shape[0], right_out)
        bias_out[...] = bias[0:1, :] * bias_scale

    shapes = [
        ((count * share, PAIR_FEATURES), F32),
        (left_shape, F32),
        (right_shape, F32),
        ((1, PAIR_FEATURES), F32),
    ]
    return call(kernel, [*pieces, *left, right_own, bias], shapes)


def shift(x, axis, distance):
    count = lax.axis_size(axis)
    return lax.ppermute(x, axis, [(n, (n + distance) % count) for n in range(count)])


def neighbour(x, axis):
    return lax.ppermute(x, axis, [(n, n ^ 1) for n in range(lax.axis_size(axis))])


def send(parts, axis):
    return [shift(part, axis, d) for d, part in enumerate(parts, 1)]


def spread_pairs(x, axis):
    return send_pairs([x] * (lax.axis_size(axis) // 2 - 1), axis)


def send_pairs(parts, axis):
    return [shift(part, axis, 2 * p) for p, part in enumerate(parts, 1)]


def local(
    first_homolog_features, second_homolog_features, final_projection_matrix, output_bias, cotangent
):
    i_n, j_n, _ = cotangent.shape
    row_n, col_n = lax.axis_size("row"), lax.axis_size("col")
    sequences = second_homolog_features.shape[0] * row_n
    channels = final_projection_matrix.shape[0]
    res_total = i_n * row_n
    a_far = spread_pairs(first_homolog_features, "col")
    b_far = spread_pairs(second_homolog_features, "row")
    we, wt, a, b, w, g = load(
        first_homolog_features,
        second_homolog_features,
        final_projection_matrix,
        cotangent.reshape(i_n * j_n, PAIR_FEATURES),
    )
    a, b = stack([a, *a_far], [b, *b_far])
    a_pieces = [a, neighbour(a, "col")]
    b_pieces = [b, neighbour(b, "row")]
    y, gt, bias_rows = prepare(we, g, i_n, j_n)

    x, a_held, b_wide, (own, *messages) = outer(
        a_pieces, b_pieces, g, bias_rows, i_n, j_n, sequences
    )
    share = channels // row_n

    parts = [own] + send(messages, "row")
    left_kept, (message,) = gradient(
        b_wide, y, own, "col", in_pairs(col_n), col_n // 2, 1, i_n, j_n, sequences
    )
    left_near = neighbour(message, "col")

    message = row_sum(parts, message, share)
    near = neighbour(message, "col")
    left_own, left_messages = pair_sum(left_kept, left_near, message)
    left = [left_own] + send_pairs(left_messages, "col")
    y2 = product(w, gt, left_own)

    message = column_pair_sum(message, near, y2, share)
    parts = [message] + spread_pairs(message, "col")
    (right_own,), right_sent = gradient(
        a_held, y2, message, "row", in_order(row_n), 1, row_n - 1, j_n, i_n, sequences
    )

    messages, piece, bias = column_sum(parts, right_sent, share)
    pieces = [piece] + send(messages, "row")
    pair_map = pair(x, wt, output_bias, piece, sequences)
    projection, left_grad, right_grad, bias_grad = finish(
        pieces,
        left,
        right_own,
        bias,
        first_homolog_features.shape,
        second_homolog_features.shape,
        1.0 / (sequences * res_total),
        1.0 / res_total,
    )
    return (
        pair_map.reshape(i_n, j_n, PAIR_FEATURES),
        left_grad,
        right_grad,
        projection,
        bias_grad.reshape(PAIR_FEATURES),
    )


def solution(mesh):
    return jax.shard_map(
        local,
        mesh=mesh,
        in_specs=(
            P(("dp", "col"), "row"),
            P(("dp", "row"), "col"),
            P(),
            P(),
            P(("dp", "row"), "col", None),
        ),
        out_specs=(
            P(("dp", "row"), "col", None),
            P(("dp", "col"), "row"),
            P(("dp", "row"), "col"),
            P("dp", None),
            P("dp"),
        ),
        check_vma=False,
    )
```

```python
import functools

import jax
import jax.numpy as jnp
from jax import lax
from jax.experimental import pallas as pl
from jax.experimental.pallas import tpu as pltpu
from jax.sharding import PartitionSpec as P

PROJECTED_DEPTH = 32
PAIR_FEATURES = 128
GROUP = 8
MULTIPLY_ROWS = 384
CHUNKS = 1
BIAS_ROWS = 16
LANES = 128
F32 = jnp.float32
BF16 = jnp.bfloat16
MIB = 1024 * 1024

ROWS_BY_ROWS = (((1,), (1,)), ((), ()))
COLS_BY_COLS = (((0,), (0,)), ((), ()))


def params(sequences=0):
    return pltpu.CompilerParams(vmem_limit_bytes=min(10 + 10 * sequences // 32, 50) * MIB + 2 * MIB)


def whole(shape):
    return pl.BlockSpec(shape, lambda t: (0,) * len(shape))


def dot(x, y, dims=(((1,), (0,)), ((), ()))):
    return lax.dot_general(x, y, dims, preferred_element_type=F32)


def load_kernel(a_hbm, b_hbm, w_hbm, g_hbm, we_ref, wt_ref, a_ref, b_ref, w_ref, g_ref, w32, sems):
    depth = PROJECTED_DEPTH
    copies = [
        pltpu.make_async_copy(source, target, sems.at[n])
        for n, (source, target) in enumerate(
            [(w_hbm, w_ref), (g_hbm, g_ref), (a_hbm, a_ref), (b_hbm, b_ref)]
        )
    ]
    for copy in copies:
        copy.start()
    copies[0].wait()
    w32[...] = w_ref[...].astype(F32)
    for e in range(depth):
        block = w32[pl.ds(e, depth, stride=depth), :]
        we_ref[e * depth : (e + 1) * depth, :] = block.astype(BF16)
    wt_ref[...] = we_ref[...].astype(F32).T.astype(BF16)
    for copy in copies[1:]:
        copy.wait()


def in_vmem():
    return pl.BlockSpec(memory_space=pltpu.VMEM)


def load(a, b, w, g):
    shapes = [
        jax.ShapeDtypeStruct(w.shape, BF16),
        jax.ShapeDtypeStruct(w.shape[::-1], BF16),
        *[jax.ShapeDtypeStruct(x.shape, BF16) for x in (a, b, w, g)],
    ]
    return pl.pallas_call(
        load_kernel,
        in_specs=[pl.BlockSpec(memory_space=pltpu.HBM)] * 4,
        out_specs=[in_vmem()] * len(shapes),
        out_shape=shapes,
        scratch_shapes=[pltpu.VMEM(w.shape, F32), pltpu.SemaphoreType.DMA((4,))],
        compiler_params=params(),
        cost_estimate=pl.CostEstimate(
            flops=1000 * w.size, bytes_accessed=16 * w.size, transcendentals=0
        ),
    )(*[pltpu.with_memory_space_constraint(x, pltpu.HBM) for x in (a, b, w, g)])


def stack(*groups):
    def kernel(*refs):
        refs, outs = refs[: -len(groups)], refs[-len(groups) :]
        for group, out in zip(groups, outs, strict=True):
            blocks = [ref[...].astype(F32) for ref in refs[: len(group)]]
            refs = refs[len(group) :]
            out[...] = jnp.concatenate(blocks, axis=0).astype(BF16)

    shapes = [((len(group) * group[0].shape[0], group[0].shape[1]), BF16) for group in groups]
    return call(kernel, [x for group in groups for x in group], shapes)


def split(total):
    high = total.astype(BF16).astype(F32)
    row = lax.broadcasted_iota(jnp.int32, (BIAS_ROWS, PAIR_FEATURES), 0)
    return jnp.where(row == 0, high, jnp.where(row == 1, total - high, 0.0)).astype(BF16)


def joined(block):
    block = block.astype(F32)
    return block[0:1] + block[1:2]


def multiply(left_ref, right_ref, out_ref):
    for n in range(0, right_ref.shape[0], MULTIPLY_ROWS):
        rows = slice(n, n + MULTIPLY_ROWS)
        out_ref[:, rows] = dot(left_ref[...], right_ref[rows, :], ROWS_BY_ROWS).astype(BF16)


def prepare_kernel(i_n, j_n, we_ref, g_ref, y_ref, gt_ref, bias_ref, g32):
    g32[...] = g_ref[...].astype(F32)
    bias_ref[...] = split(jnp.sum(g32[...], axis=0, keepdims=True))
    multiply(we_ref, g_ref, y_ref)

    for j in range(j_n):
        gt_ref[j * i_n : (j + 1) * i_n, :] = g32[pl.ds(j, i_n, stride=j_n), :].astype(BF16)


def prepare(we, g, i_n, j_n):
    pairs = i_n * j_n
    channels = we.shape[0]
    shapes = [
        jax.ShapeDtypeStruct((channels, pairs), BF16),
        jax.ShapeDtypeStruct(g.shape, BF16),
        jax.ShapeDtypeStruct((BIAS_ROWS, PAIR_FEATURES), BF16),
    ]
    return pl.pallas_call(
        functools.partial(prepare_kernel, i_n, j_n),
        in_specs=[in_vmem()] * 2,
        out_specs=[in_vmem()] * len(shapes),
        out_shape=shapes,
        scratch_shapes=[pltpu.VMEM(g.shape, F32)],
        compiler_params=params(16),
        cost_estimate=pl.CostEstimate(
            flops=2 * pairs * channels * PAIR_FEATURES,
            bytes_accessed=4 * pairs * channels,
            transcendentals=0,
        ),
    )(we, g)


def join(pieces, axis, held):
    half = lax.axis_size(axis) // 2
    depth = pieces[0].shape[0] // half
    me = lax.axis_index(axis)
    odd, home = lax.rem(me, 2), lax.div(me, 2)
    for piece, parity in zip(pieces, (odd, 1 - odd), strict=True):
        block = piece[...].astype(F32)
        for p in range(half):
            place = (2 * lax.bitwise_xor(home, p) + parity) * depth
            held[pl.ds(pl.multiple_of(place, depth), depth), :] = block[p * depth : (p + 1) * depth]


def repeat_matrix(sequences):
    shape = (sequences, GROUP * sequences)
    lane = lax.broadcasted_iota(jnp.int32, shape, 1)
    row = lax.broadcasted_iota(jnp.int32, shape, 0)
    return (lax.rem(lane, sequences) == row).astype(BF16)


def spread(held, wide):
    both = dot(held[...].T.astype(BF16), repeat_matrix(held.shape[0]))
    for l in range(wide.shape[0]):
        wide[l] = both[:, l * LANES : (l + 1) * LANES]


def tiles_of(sequences, tile):
    lane = lax.broadcasted_iota(jnp.int32, (1, LANES), 1) + tile * LANES
    return [
        (m, lax.div(lane, sequences) == m)
        for m in range(GROUP)
        if m * sequences < (tile + 1) * LANES and (m + 1) * sequences > tile * LANES
    ]


def chunks(body):
    if CHUNKS == 1:
        body(0)
    else:
        pl.loop(0, CHUNKS)(body)


def diagonal_of(wide, channel, positions, sequences):
    columns = []
    for l in range(wide.shape[0]):
        block = wide[l, pl.ds(channel, positions, stride=PROJECTED_DEPTH), :].astype(BF16)
        members = dict(tiles_of(sequences, l))
        columns.append(
            jnp.concatenate(
                [
                    block * members[m].astype(F32).astype(BF16)
                    if m in members
                    else jnp.zeros(block.shape, BF16)
                    for m in range(GROUP)
                ],
                axis=0,
            )
        )
    return jnp.concatenate(columns, axis=1)


def alone(count):
    return lambda me: ([me], [[lax.bitwise_xor(me, d)] for d in range(1, count)])


def in_pairs(count):
    def plan(me):
        evens = range(0, count, 2)
        return [lax.bitwise_xor(me, d) for d in evens], [
            [lax.bitwise_xor(me, d + 1) for d in evens]
        ]

    return plan


def outer_kernel(i_n, j_n, *refs):
    depth = PROJECTED_DEPTH
    row_n = lax.axis_size("row")
    a_pieces, b_pieces, refs = refs[:2], refs[2:4], refs[4:]
    g_ref, bias_ref, x_ref, a_held, b_wide = refs[:5]
    messages, (b_held, left, total) = refs[5 : 5 + row_n], refs[5 + row_n :]
    sequences = a_held.shape[0]
    groups = i_n // GROUP
    per_step = depth // CHUNKS
    span = GROUP * j_n

    join(a_pieces, "col", a_held)
    join(b_pieces, "row", b_held)
    spread(b_held, b_wide)
    turned = a_held[...].T.astype(BF16)
    shape = (sequences, GROUP * sequences)
    shifted = lax.broadcasted_iota(jnp.int32, shape, 1) - lax.broadcasted_iota(jnp.int32, shape, 0)
    value = jnp.zeros(left.shape, F32)
    for m in range(GROUP):
        rows = [
            turned[(k * GROUP + m) * depth : (k * GROUP + m + 1) * depth, :] for k in range(groups)
        ]
        value += dot(jnp.concatenate(rows, axis=0), (shifted == m * sequences).astype(BF16))
    left[...] = value.astype(BF16)

    @chunks
    def _(t):
        size = per_step * depth
        rows = pl.ds(t * size if CHUNKS == 1 else pl.multiple_of(t * size, size), size)
        x_part = x_ref.at[rows]
        for e in range(0, per_step, 2):
            right = [diagonal_of(b_wide, t * per_step + e + n, j_n, sequences) for n in range(2)]
            product = dot(
                left[...], jnp.concatenate(right, axis=0), ROWS_BY_ROWS
            ).astype(BF16)
            for n in range(2):
                for k in range(groups):
                    x_part[(e + n) * depth : (e + n + 1) * depth, k * span : (k + 1) * span] = product[
                        k * depth : (k + 1) * depth, n * span : (n + 1) * span
                    ]
        total[rows, :] = dot(x_part[...], g_ref[...])

    share = total.shape[0] // row_n
    me = lax.axis_index("row")
    for p, message in enumerate(messages):
        part = lax.bitwise_xor(me, p)
        for n in range(share // depth):
            block = total[pl.ds(part * (share // depth) + n, depth, stride=depth), :]
            message[n * depth : (n + 1) * depth, :] = block.astype(message.dtype)
        message[share:, :] = bias_ref[...].astype(message.dtype)


def outer(a_pieces, b_pieces, g, bias_rows, i_n, j_n, sequences):
    row_n = lax.axis_size("row")
    depth = PROJECTED_DEPTH
    channels = depth * depth
    pairs = i_n * j_n
    tiles = GROUP * sequences // LANES
    operands = [*a_pieces, *b_pieces, g, bias_rows]
    shapes = [jax.ShapeDtypeStruct((channels, pairs), BF16)]
    shapes += [
        jax.ShapeDtypeStruct((sequences, i_n * depth), F32),
        jax.ShapeDtypeStruct((tiles, j_n * depth, LANES), F32),
    ]
    shapes += [
        jax.ShapeDtypeStruct((channels // row_n + BIAS_ROWS, LANES), BF16 if p else F32)
        for p in range(row_n)
    ]
    results = pl.pallas_call(
        functools.partial(outer_kernel, i_n, j_n),
        in_specs=[in_vmem()] * len(operands),
        out_specs=[in_vmem()] * len(shapes),
        out_shape=shapes,
        scratch_shapes=[
            pltpu.VMEM((sequences, j_n * depth), F32),
            pltpu.VMEM((i_n // GROUP * depth, GROUP * sequences), BF16),
            pltpu.VMEM((channels, PAIR_FEATURES), F32),
        ],
        compiler_params=params(sequences),
        cost_estimate=pl.CostEstimate(
            flops=4 * pairs * channels * PAIR_FEATURES,
            bytes_accessed=2 * pairs * channels,
            transcendentals=0,
        ),
    )(*operands)
    return *results[:3], results[3:]


def gradient_kernel(axis, plan, kept, positions, others, sequences, *refs):
    depth = PROJECTED_DEPTH
    wide, source = refs[:2]
    outs, (result, grown, grad) = refs[3:-3], refs[-3:]
    parts = lax.axis_size(axis)
    per_step = depth // CHUNKS
    span = GROUP * others

    result[...] = jnp.zeros(result.shape, F32)

    @chunks
    def _(t):
        size = per_step * depth
        rows = pl.ds(t * size if CHUNKS == 1 else pl.multiple_of(t * size, size), size)
        part = source.at[rows]
        for n in range(0, per_step, 2):
            blocks = [
                jnp.concatenate(
                    [
                        part[m * depth : (m + 1) * depth, k * span : (k + 1) * span]
                        for m in (n, n + 1)
                    ],
                    axis=1,
                )
                for k in range(positions // GROUP)
            ]
            right = [
                diagonal_of(wide, t * per_step + m, others, sequences) for m in (n, n + 1)
            ]
            result[...] += dot(jnp.concatenate(blocks, axis=0), jnp.concatenate(right, axis=0))

    scaled = (result[...] * (1.0 / sequences)).astype(BF16)
    for l in range(scaled.shape[1] // LANES):
        members = dict(tiles_of(sequences, l))
        for k in range(positions // GROUP):
            block = scaled[k * depth : (k + 1) * depth, l * LANES : (l + 1) * LANES]
            for m in range(GROUP):
                start = (k * GROUP + m) * depth
                grown[start : start + depth, l * LANES : (l + 1) * LANES] = (
                    block * members[m].astype(F32).astype(BF16)
                    if m in members
                    else jnp.zeros((depth, LANES), BF16)
                )
    grad[...] = dot(repeat_matrix(sequences), grown[...], ROWS_BY_ROWS)
    share = sequences // parts

    def rows_of(p):
        mine = grad[pl.ds(pl.multiple_of(p * share, share), share), :]
        return jnp.concatenate(
            [mine[:, l * LANES : (l + 1) * LANES] for l in range(mine.shape[1] // LANES)], axis=0
        )

    stay, go = plan(lax.axis_index(axis))
    for p, out in zip(stay, outs[:kept], strict=True):
        out[...] = rows_of(p)
    for group, out in zip(go, outs[kept:], strict=True):
        size = out.shape[0] // len(group)
        for n, p in enumerate(group):
            out[n * size : (n + 1) * size, :] = rows_of(p).astype(BF16)


def gradient(wide, source, after, axis, plan, kept, groups, positions, others, sequences):
    depth = PROJECTED_DEPTH
    parts = lax.axis_size(axis)
    rows = sequences // parts * positions * depth // LANES
    shapes = [jax.ShapeDtypeStruct((rows, LANES), F32)] * kept
    group = (parts - kept) // groups
    shapes += [jax.ShapeDtypeStruct((group * rows, LANES), BF16)] * groups
    results = pl.pallas_call(
        functools.partial(gradient_kernel, axis, plan, kept, positions, others, sequences),
        in_specs=[in_vmem(), in_vmem(), pl.BlockSpec(memory_space=pl.ANY)],
        out_specs=[in_vmem()] * len(shapes),
        out_shape=shapes,
        scratch_shapes=[
            pltpu.VMEM((positions // GROUP * depth, GROUP * sequences), F32),
            pltpu.VMEM((positions * depth, GROUP * sequences), BF16),
            pltpu.VMEM((sequences, positions * depth), F32),
        ],
        compiler_params=params(sequences),
        cost_estimate=pl.CostEstimate(
            flops=2 * source.size * PAIR_FEATURES,
            bytes_accessed=2 * source.size,
            transcendentals=0,
        ),
    )(wide, source, after)
    return results[:kept], results[kept:]


def product_kernel(left_ref, right_ref, held, _, out_ref, wide):
    spread(held, wide)
    multiply(left_ref, right_ref, out_ref)


def product(left, right, held, after):
    shape = (left.shape[0], right.shape[0])
    spread_shape = (GROUP * held.shape[0] // LANES, held.shape[1], LANES)
    return pl.pallas_call(
        product_kernel,
        in_specs=[in_vmem()] * 3 + [pl.BlockSpec(memory_space=pl.ANY)],
        out_specs=[in_vmem()] * 2,
        out_shape=[jax.ShapeDtypeStruct(shape, BF16), jax.ShapeDtypeStruct(spread_shape, F32)],
        compiler_params=params(32),
        cost_estimate=pl.CostEstimate(
            flops=2 * shape[0] * shape[1] * left.shape[1],
            bytes_accessed=4 * shape[0] * shape[1],
            transcendentals=0,
        ),
    )(left, right, held, after)


def pair_kernel(sequences, x_ref, wt_ref, bias_ref, _, out_ref):
    product = dot(wt_ref[...], x_ref[...])
    out_ref[...] = (product.T * (1.0 / sequences) + bias_ref[...]).astype(BF16)


def pair(x, wt, output_bias, after, sequences):
    channels, pairs = x.shape
    count = 3
    size = pairs // count
    return pl.pallas_call(
        functools.partial(pair_kernel, sequences),
        grid=(count,),
        in_specs=[
            pl.BlockSpec((channels, size), lambda t: (0, t)),
            whole(wt.shape),
            whole((1, PAIR_FEATURES)),
            pl.BlockSpec(memory_space=pl.ANY),
        ],
        out_specs=pl.BlockSpec((size, PAIR_FEATURES), lambda t: (t, 0)),
        out_shape=jax.ShapeDtypeStruct((pairs, PAIR_FEATURES), BF16),
        compiler_params=params(),
        cost_estimate=pl.CostEstimate(
            flops=4 * pairs * channels * PAIR_FEATURES,
            bytes_accessed=2 * pairs * channels,
            transcendentals=0,
        ),
    )(x, wt, output_bias.reshape(1, PAIR_FEATURES), after)


def unfold(total, share, out):
    for l in range(out.shape[1] // LANES):
        out[:, l * LANES : (l + 1) * LANES] = total[l * share : (l + 1) * share, :]


def call(kernel, operands, shapes, after=(), scratch=()):
    specs = [in_vmem()] * len(operands) + [pl.BlockSpec(memory_space=pl.ANY)] * len(after)
    return pl.pallas_call(
        kernel,
        in_specs=specs,
        out_specs=[in_vmem()] * len(shapes),
        out_shape=[jax.ShapeDtypeStruct(shape, kind) for shape, kind in shapes],
        scratch_shapes=scratch,
        compiler_params=params(),
    )(*operands, *after)


def partners(count):
    return [0, *range(count - 1, 0, -1)]


def row_sum(parts, after, share):
    count = len(parts)

    def kernel(*refs):
        parts, (_, message, held) = refs[:count], refs[count:]
        me = lax.axis_index("row")
        total = parts[0][0:share, :]
        for p, part in zip(partners(count), parts, strict=True):
            held[lax.bitwise_xor(me, p)] = part[share:, :].astype(F32)
            if p > 0:
                total += part[0:share, :].astype(F32)
        bias = joined(held[0])
        for n in range(1, count):
            bias += joined(held[n])
        message[0:share, :] = total.astype(BF16)
        message[share:, :] = split(bias)

    scratch = [pltpu.VMEM((count, BIAS_ROWS, LANES), F32)]
    (message,) = call(kernel, parts, [((share + BIAS_ROWS, LANES), BF16)], [after], scratch)
    return message


def pair_sum(kept, near, after):
    def kernel(*refs):
        kept, near, (own, *messages) = refs[:count], refs[count], refs[count + 2 :]
        size = own.shape[0]
        for p, part in enumerate(kept):
            both = part[...] + near[p * size : (p + 1) * size, :].astype(F32)
            if p == 0:
                own[...] = both
            else:
                messages[p - 1][...] = both.astype(BF16)

    count = len(kept)
    shapes = [(kept[0].shape, F32)] + [(kept[0].shape, BF16)] * (count - 1)
    own, *messages = call(kernel, [*kept, near], shapes, [after])
    return own, messages


def column_pair_sum(own, near, after, share):
    def kernel(own, near, _, message):
        total = own[0:share, :].astype(F32) + near[0:share, :].astype(F32)
        message[0:share, :] = total.astype(BF16)
        message[share:, :] = split(joined(own[share:, :]) + joined(near[share:, :]))

    (message,) = call(kernel, [own, near], [(own.shape, BF16)], [after])
    return message


def column_sum(parts, grads, share):
    rows = share + BIAS_ROWS
    count, sent = len(parts), len(grads)

    def kernel(*refs):
        parts, grads, refs = refs[:count], refs[count : count + sent], refs[count + sent :]
        messages, (piece_out, bias_out, held) = refs[:sent], refs[sent:]
        home = lax.div(lax.axis_index("col"), 2)
        for p, part in enumerate(parts):
            held[lax.bitwise_xor(home, p)] = part[...]
        total, bias = held[0, 0:share, :].astype(F32), joined(held[0, share:, :])
        for n in range(1, count):
            total += held[n, 0:share, :].astype(F32)
            bias += joined(held[n, share:, :])
        piece = total.astype(BF16)
        piece_out[...] = piece
        for message, grad in zip(messages, grads, strict=True):
            message[0:share, :] = piece
            message[share:, :] = grad[...]
        bias_out[...] = jnp.broadcast_to(bias, bias_out.shape)

    shapes = [((share + grad.shape[0], LANES), BF16) for grad in grads]
    shapes += [((share, LANES), BF16), ((8, LANES), F32)]
    scratch = [pltpu.VMEM((count, rows, LANES), BF16)]
    *messages, piece, bias = call(kernel, [*parts, *grads], shapes, scratch=scratch)
    return messages, piece, bias


def finish(pieces, left, right_own, bias, left_shape, right_shape, scale, bias_scale):
    count, left_n = len(pieces), len(left)
    share = pieces[0].shape[0]

    def kernel(*refs):
        pieces, left, refs = refs[:count], refs[count : count + left_n], refs[count + left_n :]
        right_own, bias, projection, left_out, right_out, bias_out = refs
        me = lax.axis_index("row")
        right_total = right_own[...]
        for p, piece in zip(partners(count), pieces, strict=True):
            rows = pl.ds(pl.multiple_of(lax.bitwise_xor(me, p) * share, share), share)
            projection[rows, :] = piece[0:share, :].astype(F32) * scale
            if p > 0:
                right_total += piece[share:, :].astype(F32)
        left_total = left[0][...]
        for term in left[1:]:
            left_total += term[...].astype(F32)
        unfold(left_total, left_out.shape[0], left_out)
        unfold(right_total, right_out.shape[0], right_out)
        bias_out[...] = bias[0:1, :] * bias_scale

    shapes = [
        ((count * share, PAIR_FEATURES), F32),
        (left_shape, F32),
        (right_shape, F32),
        ((1, PAIR_FEATURES), F32),
    ]
    return call(kernel, [*pieces, *left, right_own, bias], shapes)


def swap(x, axis, p):
    return lax.ppermute(x, axis, [(n, n ^ p) for n in range(lax.axis_size(axis))])


def swap_each(parts, axis, step=1):
    count = len(parts)
    return [swap(parts[n - 1], axis, n * step) for n in range(count, 0, -1)][::-1]


def from_evens(x, axis):
    return swap_each([x] * (lax.axis_size(axis) // 2 - 1), axis, 2)


def local(
    first_homolog_features, second_homolog_features, final_projection_matrix, output_bias, cotangent
):
    i_n, j_n, _ = cotangent.shape
    row_n, col_n = lax.axis_size("row"), lax.axis_size("col")
    sequences = second_homolog_features.shape[0] * row_n
    channels = final_projection_matrix.shape[0]
    res_total = i_n * row_n
    a_far = from_evens(first_homolog_features, "col")
    b_far = from_evens(second_homolog_features, "row")
    we, wt, a, b, w, g = load(
        first_homolog_features,
        second_homolog_features,
        final_projection_matrix,
        cotangent.reshape(i_n * j_n, PAIR_FEATURES),
    )
    a, b = stack([a, *a_far], [b, *b_far])
    a_pieces = [a, swap(a, "col", 1)]
    b_pieces = [b, swap(b, "row", 1)]
    y, gt, bias_rows = prepare(we, g, i_n, j_n)

    x, a_held, b_wide, (own, *messages) = outer(
        a_pieces, b_pieces, g, bias_rows, i_n, j_n, sequences
    )
    share = channels // row_n

    parts = [own] + swap_each(messages, "row")[::-1]
    left_kept, (message,) = gradient(
        b_wide, y, own, "col", in_pairs(col_n), col_n // 2, 1, i_n, j_n, sequences
    )
    left_near = swap(message, "col", 1)

    message = row_sum(parts, message, share)
    near = swap(message, "col", 1)
    left_own, left_messages = pair_sum(left_kept, left_near, message)
    left = [left_own] + swap_each(left_messages, "col", 2)
    y2, a_wide = product(w, gt, a_held, left_own)

    message = column_pair_sum(message, near, y2, share)
    parts = [message] + from_evens(message, "col")
    (right_own,), right_sent = gradient(
        a_wide, y2, message, "row", alone(row_n), 1, row_n - 1, j_n, i_n, sequences
    )

    messages, piece, bias = column_sum(parts, right_sent, share)
    pieces = [piece] + swap_each(messages, "row")[::-1]
    pair_map = pair(x, wt, output_bias, piece, sequences)
    projection, left_grad, right_grad, bias_grad = finish(
        pieces,
        left,
        right_own,
        bias,
        first_homolog_features.shape,
        second_homolog_features.shape,
        1.0 / (sequences * res_total),
        1.0 / res_total,
    )
    return (
        pair_map.reshape(i_n, j_n, PAIR_FEATURES),
        left_grad,
        right_grad,
        projection,
        bias_grad.reshape(PAIR_FEATURES),
    )


def solution(mesh):
    return jax.shard_map(
        local,
        mesh=mesh,
        in_specs=(
            P(("dp", "col"), "row"),
            P(("dp", "row"), "col"),
            P(),
            P(),
            P(("dp", "row"), "col", None),
        ),
        out_specs=(
            P(("dp", "row"), "col", None),
            P(("dp", "col"), "row"),
            P(("dp", "row"), "col"),
            P("dp", None),
            P("dp"),
        ),
        check_vma=False,
    )
```

```python
import functools

import jax
import jax.numpy as jnp
from jax import lax
from jax.experimental import pallas as pl
from jax.experimental.pallas import tpu as pltpu
from jax.sharding import PartitionSpec as P

PROJECTED_DEPTH = 32
PAIR_FEATURES = 128
GROUP = 8
MULTIPLY_ROWS = 384
CHUNKS = 2
BIAS_ROWS = 16
LANES = 128
F32 = jnp.float32
BF16 = jnp.bfloat16
MIB = 1024 * 1024

ROWS_BY_ROWS = (((1,), (1,)), ((), ()))
COLS_BY_COLS = (((0,), (0,)), ((), ()))


def params(sequences=0):
    return pltpu.CompilerParams(vmem_limit_bytes=min(10 + 10 * sequences // 32, 50) * MIB + 2 * MIB)


def whole(shape):
    return pl.BlockSpec(shape, lambda t: (0,) * len(shape))


def dot(x, y, dims=(((1,), (0,)), ((), ()))):
    return lax.dot_general(x, y, dims, preferred_element_type=F32)


def in_vmem():
    return pl.BlockSpec(memory_space=pltpu.VMEM)


def split(total):
    high = total.astype(BF16).astype(F32)
    row = lax.broadcasted_iota(jnp.int32, (BIAS_ROWS, PAIR_FEATURES), 0)
    return jnp.where(row == 0, high, jnp.where(row == 1, total - high, 0.0)).astype(BF16)


def joined(block):
    block = block.astype(F32)
    return block[0:1] + block[1:2]


def multiply(left_ref, right_ref, out_ref):
    for n in range(0, right_ref.shape[0], MULTIPLY_ROWS):
        rows = slice(n, n + MULTIPLY_ROWS)
        out_ref[:, rows] = dot(left_ref[...], right_ref[rows, :], ROWS_BY_ROWS).astype(BF16)


def prepare_kernel(
    i_n, j_n, a_hbm, b_hbm, w_hbm, g_hbm, y_ref, gt_ref, wt_ref, bias_ref, a_ref, b_ref, w_ref, g_ref,
    w32, we, g32, sems,
):
    depth = PROJECTED_DEPTH
    copies = [
        pltpu.make_async_copy(source, target, sems.at[n])
        for n, (source, target) in enumerate(
            [(w_hbm, w_ref), (g_hbm, g_ref), (a_hbm, a_ref), (b_hbm, b_ref)]
        )
    ]
    for copy in copies:
        copy.start()
    copies[0].wait()
    w32[...] = w_ref[...].astype(F32)
    for e in range(depth):
        block = w32[pl.ds(e, depth, stride=depth), :]
        we[e * depth : (e + 1) * depth, :] = block.astype(BF16)
    wt_ref[...] = we[...].astype(F32).T.astype(BF16)
    copies[1].wait()
    g32[...] = g_ref[...].astype(F32)
    bias_ref[...] = split(jnp.sum(g32[...], axis=0, keepdims=True))
    multiply(we, g_ref, y_ref)
    for j in range(j_n):
        gt_ref[j * i_n : (j + 1) * i_n, :] = g32[pl.ds(j, i_n, stride=j_n), :].astype(BF16)
    for copy in copies[2:]:
        copy.wait()


def prepare(a, b, w, g, i_n, j_n):
    channels, pairs = w.shape[0], g.shape[0]
    shapes = [
        jax.ShapeDtypeStruct((channels, pairs), BF16),
        jax.ShapeDtypeStruct(g.shape, BF16),
        jax.ShapeDtypeStruct(w.shape[::-1], BF16),
        jax.ShapeDtypeStruct((BIAS_ROWS, PAIR_FEATURES), BF16),
        *[jax.ShapeDtypeStruct(x.shape, BF16) for x in (a, b, w, g)],
    ]
    return pl.pallas_call(
        functools.partial(prepare_kernel, i_n, j_n),
        in_specs=[pl.BlockSpec(memory_space=pltpu.HBM)] * 4,
        out_specs=[in_vmem()] * len(shapes),
        out_shape=shapes,
        scratch_shapes=[
            pltpu.VMEM(w.shape, F32),
            pltpu.VMEM(w.shape, BF16),
            pltpu.VMEM(g.shape, F32),
            pltpu.SemaphoreType.DMA((4,)),
        ],
        compiler_params=params(16),
        cost_estimate=pl.CostEstimate(
            flops=2 * pairs * channels * PAIR_FEATURES,
            bytes_accessed=4 * pairs * channels,
            transcendentals=0,
        ),
    )(*[pltpu.with_memory_space_constraint(x, pltpu.HBM) for x in (a, b, w, g)])


def join(pieces, axis, held):
    depth = pieces[0].shape[0]
    me = lax.axis_index(axis)
    for p, piece in enumerate(pieces):
        place = lax.bitwise_xor(me, p) * depth
        held[pl.ds(pl.multiple_of(place, depth), depth), :] = piece[...].astype(F32)


def repeat_matrix(sequences):
    shape = (sequences, GROUP * sequences)
    lane = lax.broadcasted_iota(jnp.int32, shape, 1)
    row = lax.broadcasted_iota(jnp.int32, shape, 0)
    return (lax.rem(lane, sequences) == row).astype(BF16)


def spread(held, wide):
    both = dot(held[...].T.astype(BF16), repeat_matrix(held.shape[0]))
    for l in range(wide.shape[0]):
        wide[l] = both[:, l * LANES : (l + 1) * LANES]


def tiles_of(sequences, tile):
    lane = lax.broadcasted_iota(jnp.int32, (1, LANES), 1) + tile * LANES
    return [
        (m, lax.div(lane, sequences) == m)
        for m in range(GROUP)
        if m * sequences < (tile + 1) * LANES and (m + 1) * sequences > tile * LANES
    ]


def chunks(body):
    if CHUNKS == 1:
        body(0)
    else:
        pl.loop(0, CHUNKS)(body)


def diagonal_of(wide, channel, positions, sequences):
    columns = []
    for l in range(wide.shape[0]):
        block = wide[l, pl.ds(channel, positions, stride=PROJECTED_DEPTH), :].astype(BF16)
        members = dict(tiles_of(sequences, l))
        columns.append(
            jnp.concatenate(
                [
                    block * members[m].astype(F32).astype(BF16)
                    if m in members
                    else jnp.zeros(block.shape, BF16)
                    for m in range(GROUP)
                ],
                axis=0,
            )
        )
    return jnp.concatenate(columns, axis=1)


def alone(count):
    return lambda me: ([me], [[lax.bitwise_xor(me, d)] for d in range(1, count)])


def in_pairs(count):
    def plan(me):
        evens = range(0, count, 2)
        return [lax.bitwise_xor(me, d) for d in evens], [
            [lax.bitwise_xor(me, d + 1) for d in evens]
        ]

    return plan


def outer_kernel(i_n, j_n, *refs):
    depth = PROJECTED_DEPTH
    row_n, col_n = lax.axis_size("row"), lax.axis_size("col")
    a_pieces, b_pieces, refs = refs[:col_n], refs[col_n : col_n + row_n], refs[col_n + row_n :]
    g_ref, bias_ref, x_ref, a_held, b_wide = refs[:5]
    messages, (b_held, left, total) = refs[5 : 5 + row_n], refs[5 + row_n :]
    sequences = a_held.shape[0]
    groups = i_n // GROUP
    per_step = depth // CHUNKS
    span = GROUP * j_n

    join(a_pieces, "col", a_held)
    join(b_pieces, "row", b_held)
    spread(b_held, b_wide)
    turned = a_held[...].T.astype(BF16)
    shape = (sequences, GROUP * sequences)
    shifted = lax.broadcasted_iota(jnp.int32, shape, 1) - lax.broadcasted_iota(jnp.int32, shape, 0)
    value = jnp.zeros(left.shape, F32)
    for m in range(GROUP):
        rows = [
            turned[(k * GROUP + m) * depth : (k * GROUP + m + 1) * depth, :] for k in range(groups)
        ]
        value += dot(jnp.concatenate(rows, axis=0), (shifted == m * sequences).astype(BF16))
    left[...] = value.astype(BF16)

    @chunks
    def _(t):
        size = per_step * depth
        rows = pl.ds(t * size if CHUNKS == 1 else pl.multiple_of(t * size, size), size)
        x_part = x_ref.at[rows]
        for e in range(0, per_step, 2):
            right = [diagonal_of(b_wide, t * per_step + e + n, j_n, sequences) for n in range(2)]
            product = dot(
                left[...], jnp.concatenate(right, axis=0), ROWS_BY_ROWS
            ).astype(BF16)
            for n in range(2):
                for k in range(groups):
                    x_part[(e + n) * depth : (e + n + 1) * depth, k * span : (k + 1) * span] = product[
                        k * depth : (k + 1) * depth, n * span : (n + 1) * span
                    ]
        total[rows, :] = dot(x_part[...], g_ref[...])

    share = total.shape[0] // row_n
    me = lax.axis_index("row")
    for p, message in enumerate(messages):
        part = lax.bitwise_xor(me, p)
        for n in range(share // depth):
            block = total[pl.ds(part * (share // depth) + n, depth, stride=depth), :]
            message[n * depth : (n + 1) * depth, :] = block.astype(message.dtype)
        message[share:, :] = bias_ref[...].astype(message.dtype)


def outer(a_pieces, b_pieces, g, bias_rows, i_n, j_n, sequences):
    row_n = lax.axis_size("row")
    depth = PROJECTED_DEPTH
    channels = depth * depth
    pairs = i_n * j_n
    tiles = GROUP * sequences // LANES
    operands = [*a_pieces, *b_pieces, g, bias_rows]
    shapes = [jax.ShapeDtypeStruct((channels, pairs), BF16)]
    shapes += [
        jax.ShapeDtypeStruct((sequences, i_n * depth), F32),
        jax.ShapeDtypeStruct((tiles, j_n * depth, LANES), F32),
    ]
    shapes += [
        jax.ShapeDtypeStruct((channels // row_n + BIAS_ROWS, LANES), BF16 if p else F32)
        for p in range(row_n)
    ]
    results = pl.pallas_call(
        functools.partial(outer_kernel, i_n, j_n),
        in_specs=[in_vmem()] * len(operands),
        out_specs=[in_vmem()] * len(shapes),
        out_shape=shapes,
        scratch_shapes=[
            pltpu.VMEM((sequences, j_n * depth), F32),
            pltpu.VMEM((i_n // GROUP * depth, GROUP * sequences), BF16),
            pltpu.VMEM((channels, PAIR_FEATURES), F32),
        ],
        compiler_params=params(sequences),
        cost_estimate=pl.CostEstimate(
            flops=4 * pairs * channels * PAIR_FEATURES,
            bytes_accessed=2 * pairs * channels,
            transcendentals=0,
        ),
    )(*operands)
    return *results[:3], results[3:]


def gradient_kernel(axis, plan, kept, positions, others, sequences, *refs):
    depth = PROJECTED_DEPTH
    wide, source = refs[:2]
    outs, (result, grown, grad) = refs[3:-3], refs[-3:]
    parts = lax.axis_size(axis)
    per_step = depth // CHUNKS
    span = GROUP * others

    result[...] = jnp.zeros(result.shape, F32)

    @chunks
    def _(t):
        size = per_step * depth
        rows = pl.ds(t * size if CHUNKS == 1 else pl.multiple_of(t * size, size), size)
        part = source.at[rows]
        for n in range(0, per_step, 2):
            blocks = [
                jnp.concatenate(
                    [
                        part[m * depth : (m + 1) * depth, k * span : (k + 1) * span]
                        for m in (n, n + 1)
                    ],
                    axis=1,
                )
                for k in range(positions // GROUP)
            ]
            right = [
                diagonal_of(wide, t * per_step + m, others, sequences) for m in (n, n + 1)
            ]
            result[...] += dot(jnp.concatenate(blocks, axis=0), jnp.concatenate(right, axis=0))

    scaled = (result[...] * (1.0 / sequences)).astype(BF16)
    for l in range(scaled.shape[1] // LANES):
        members = dict(tiles_of(sequences, l))
        for k in range(positions // GROUP):
            block = scaled[k * depth : (k + 1) * depth, l * LANES : (l + 1) * LANES]
            for m in range(GROUP):
                start = (k * GROUP + m) * depth
                grown[start : start + depth, l * LANES : (l + 1) * LANES] = (
                    block * members[m].astype(F32).astype(BF16)
                    if m in members
                    else jnp.zeros((depth, LANES), BF16)
                )
    grad[...] = dot(repeat_matrix(sequences), grown[...], ROWS_BY_ROWS)
    share = sequences // parts

    def rows_of(p):
        mine = grad[pl.ds(pl.multiple_of(p * share, share), share), :]
        return jnp.concatenate(
            [mine[:, l * LANES : (l + 1) * LANES] for l in range(mine.shape[1] // LANES)], axis=0
        )

    stay, go = plan(lax.axis_index(axis))
    for p, out in zip(stay, outs[:kept], strict=True):
        out[...] = rows_of(p)
    for group, out in zip(go, outs[kept:], strict=True):
        size = out.shape[0] // len(group)
        for n, p in enumerate(group):
            out[n * size : (n + 1) * size, :] = rows_of(p).astype(BF16)


def gradient(wide, source, after, axis, plan, kept, groups, positions, others, sequences):
    depth = PROJECTED_DEPTH
    parts = lax.axis_size(axis)
    rows = sequences // parts * positions * depth // LANES
    shapes = [jax.ShapeDtypeStruct((rows, LANES), F32)] * kept
    group = (parts - kept) // groups
    shapes += [jax.ShapeDtypeStruct((group * rows, LANES), BF16)] * groups
    results = pl.pallas_call(
        functools.partial(gradient_kernel, axis, plan, kept, positions, others, sequences),
        in_specs=[in_vmem(), in_vmem(), pl.BlockSpec(memory_space=pl.ANY)],
        out_specs=[in_vmem()] * len(shapes),
        out_shape=shapes,
        scratch_shapes=[
            pltpu.VMEM((positions // GROUP * depth, GROUP * sequences), F32),
            pltpu.VMEM((positions * depth, GROUP * sequences), BF16),
            pltpu.VMEM((sequences, positions * depth), F32),
        ],
        compiler_params=params(sequences),
        cost_estimate=pl.CostEstimate(
            flops=2 * source.size * PAIR_FEATURES,
            bytes_accessed=2 * source.size,
            transcendentals=0,
        ),
    )(wide, source, after)
    return results[:kept], results[kept:]


def product_kernel(left_ref, right_ref, held, _, out_ref, wide):
    spread(held, wide)
    multiply(left_ref, right_ref, out_ref)


def product(left, right, held, after):
    shape = (left.shape[0], right.shape[0])
    spread_shape = (GROUP * held.shape[0] // LANES, held.shape[1], LANES)
    return pl.pallas_call(
        product_kernel,
        in_specs=[in_vmem()] * 3 + [pl.BlockSpec(memory_space=pl.ANY)],
        out_specs=[in_vmem()] * 2,
        out_shape=[jax.ShapeDtypeStruct(shape, BF16), jax.ShapeDtypeStruct(spread_shape, F32)],
        compiler_params=params(32),
        cost_estimate=pl.CostEstimate(
            flops=2 * shape[0] * shape[1] * left.shape[1],
            bytes_accessed=4 * shape[0] * shape[1],
            transcendentals=0,
        ),
    )(left, right, held, after)


def pair_kernel(sequences, x_ref, wt_ref, bias_ref, _, out_ref):
    product = dot(wt_ref[...], x_ref[...])
    out_ref[...] = (product.T * (1.0 / sequences) + bias_ref[...]).astype(BF16)


def pair(x, wt, output_bias, after, sequences):
    channels, pairs = x.shape
    count = 3
    size = pairs // count
    return pl.pallas_call(
        functools.partial(pair_kernel, sequences),
        grid=(count,),
        in_specs=[
            pl.BlockSpec((channels, size), lambda t: (0, t)),
            whole(wt.shape),
            whole((1, PAIR_FEATURES)),
            pl.BlockSpec(memory_space=pl.ANY),
        ],
        out_specs=pl.BlockSpec((size, PAIR_FEATURES), lambda t: (t, 0)),
        out_shape=jax.ShapeDtypeStruct((pairs, PAIR_FEATURES), BF16),
        compiler_params=params(),
        cost_estimate=pl.CostEstimate(
            flops=4 * pairs * channels * PAIR_FEATURES,
            bytes_accessed=2 * pairs * channels,
            transcendentals=0,
        ),
    )(x, wt, output_bias.reshape(1, PAIR_FEATURES), after)


def unfold(total, share, out):
    for l in range(out.shape[1] // LANES):
        out[:, l * LANES : (l + 1) * LANES] = total[l * share : (l + 1) * share, :]


def call(kernel, operands, shapes, after=(), scratch=()):
    specs = [in_vmem()] * len(operands) + [pl.BlockSpec(memory_space=pl.ANY)] * len(after)
    return pl.pallas_call(
        kernel,
        in_specs=specs,
        out_specs=[in_vmem()] * len(shapes),
        out_shape=[jax.ShapeDtypeStruct(shape, kind) for shape, kind in shapes],
        scratch_shapes=scratch,
        compiler_params=params(),
    )(*operands, *after)


def partners(count):
    return [0, *range(count - 1, 0, -1)]


def row_sum(parts, after, share):
    count = len(parts)

    def kernel(*refs):
        parts, (_, message, held) = refs[:count], refs[count:]
        me = lax.axis_index("row")
        total = parts[0][0:share, :]
        for p, part in zip(partners(count), parts, strict=True):
            held[lax.bitwise_xor(me, p)] = part[share:, :].astype(F32)
            if p > 0:
                total += part[0:share, :].astype(F32)
        bias = joined(held[0])
        for n in range(1, count):
            bias += joined(held[n])
        message[0:share, :] = total.astype(BF16)
        message[share:, :] = split(bias)

    scratch = [pltpu.VMEM((count, BIAS_ROWS, LANES), F32)]
    (message,) = call(kernel, parts, [((share + BIAS_ROWS, LANES), BF16)], [after], scratch)
    return message


def column_pair_sum(own, near, kept, grad_near, after, share):
    rows = share + BIAS_ROWS
    count = len(kept)
    size = kept[0].shape[0]

    def kernel(own, near, grad_near, *refs):
        kept, (_, grad_own), messages = refs[:count], refs[count : count + 2], refs[count + 2 :]
        total = own[0:share, :].astype(F32) + near[0:share, :].astype(F32)
        bias = split(joined(own[share:, :]) + joined(near[share:, :]))
        grad_own[...] = kept[0][...] + grad_near[0:size, :].astype(F32)
        for p, message in enumerate(messages, 1):
            message[0:share, :] = total.astype(BF16)
            message[share:rows, :] = bias
            part = kept[p][...] + grad_near[p * size : (p + 1) * size, :].astype(F32)
            message[rows:, :] = part.astype(BF16)

    shapes = [((size, LANES), F32)] + [((rows + size, LANES), BF16)] * (count - 1)
    grad_own, *messages = call(kernel, [own, near, grad_near, *kept], shapes, [after])
    return grad_own, messages


def column_sum(own, parts, left_own, grads, share):
    rows = share + BIAS_ROWS
    count, sent = len(parts) + 1, len(grads)

    def kernel(own, left_own, *refs):
        parts, grads, refs = refs[: count - 1], refs[count - 1 : count - 1 + sent], refs[count - 1 + sent :]
        messages, (piece_out, left_out, bias_out, held) = refs[:sent], refs[sent:]
        home = lax.div(lax.axis_index("col"), 2)
        left = left_own[...]
        for p, part in enumerate((own, *parts)):
            held[lax.bitwise_xor(home, p)] = part[0:rows, :]
            if p > 0:
                left += part[rows:, :].astype(F32)
        left_out[...] = left
        total, bias = held[0, 0:share, :].astype(F32), joined(held[0, share:, :])
        for n in range(1, count):
            total += held[n, 0:share, :].astype(F32)
            bias += joined(held[n, share:, :])
        piece = total.astype(BF16)
        piece_out[...] = piece
        for message, grad in zip(messages, grads, strict=True):
            message[0:share, :] = piece
            message[share:, :] = grad[...]
        bias_out[...] = jnp.broadcast_to(bias, bias_out.shape)

    shapes = [((share + grad.shape[0], LANES), BF16) for grad in grads]
    shapes += [((share, LANES), BF16), (left_own.shape, F32), ((8, LANES), F32)]
    scratch = [pltpu.VMEM((count, rows, LANES), BF16)]
    *messages, piece, left, bias = call(
        kernel, [own, left_own, *parts, *grads], shapes, scratch=scratch
    )
    return messages, piece, left, bias


def finish(pieces, left, right_own, bias, left_shape, right_shape, scale, bias_scale):
    count = len(pieces)
    share = pieces[0].shape[0]

    def kernel(*refs):
        pieces, refs = refs[:count], refs[count:]
        left, right_own, bias, projection, left_out, right_out, bias_out = refs
        me = lax.axis_index("row")
        right_total = right_own[...]
        for p, piece in zip(partners(count), pieces, strict=True):
            rows = pl.ds(pl.multiple_of(lax.bitwise_xor(me, p) * share, share), share)
            projection[rows, :] = piece[0:share, :].astype(F32) * scale
            if p > 0:
                right_total += piece[share:, :].astype(F32)
        unfold(left[...], left_out.shape[0], left_out)
        unfold(right_total, right_out.shape[0], right_out)
        bias_out[...] = bias[0:1, :] * bias_scale

    shapes = [
        ((count * share, PAIR_FEATURES), F32),
        (left_shape, F32),
        (right_shape, F32),
        ((1, PAIR_FEATURES), F32),
    ]
    return call(kernel, [*pieces, left, right_own, bias], shapes)


def swap(x, axis, p):
    return lax.ppermute(x, axis, [(n, n ^ p) for n in range(lax.axis_size(axis))])


def swap_each(parts, axis, step=1):
    count = len(parts)
    return [swap(parts[n - 1], axis, n * step) for n in range(count, 0, -1)][::-1]


def local(
    first_homolog_features, second_homolog_features, final_projection_matrix, output_bias, cotangent
):
    i_n, j_n, _ = cotangent.shape
    row_n, col_n = lax.axis_size("row"), lax.axis_size("col")
    sequences = second_homolog_features.shape[0] * row_n
    channels = final_projection_matrix.shape[0]
    res_total = i_n * row_n
    gathered = {}
    for axis, x in (("col", first_homolog_features), ("row", second_homolog_features)):
        count = lax.axis_size(axis)
        gathered[axis] = swap_each([x] * (count - 1), axis)
    y, gt, wt, bias_rows, a, b, w, g = prepare(
        first_homolog_features,
        second_homolog_features,
        final_projection_matrix,
        cotangent.reshape(i_n * j_n, PAIR_FEATURES),
        i_n,
        j_n,
    )
    a_pieces = [a] + gathered["col"]
    b_pieces = [b] + gathered["row"]

    x, a_held, b_wide, (own, *messages) = outer(
        a_pieces, b_pieces, g, bias_rows, i_n, j_n, sequences
    )
    share = channels // row_n

    parts = [own] + swap_each(messages, "row")[::-1]
    left_kept, (message,) = gradient(
        b_wide, y, own, "col", in_pairs(col_n), col_n // 2, 1, i_n, j_n, sequences
    )
    left_near = swap(message, "col", 1)

    message = row_sum(parts, message, share)
    near = swap(message, "col", 1)
    y2, a_wide = product(w, gt, a_held, message)
    left_own, messages = column_pair_sum(message, near, left_kept, left_near, y2, share)
    parts = swap_each(messages, "col", 2)
    (right_own,), right_sent = gradient(
        a_wide, y2, left_own, "row", alone(row_n), 1, row_n - 1, j_n, i_n, sequences
    )

    messages, piece, left_own, bias = column_sum(messages[0], parts, left_own, right_sent, share)
    pieces = [piece] + swap_each(messages, "row")[::-1]
    pair_map = pair(x, wt, output_bias, piece, sequences)
    projection, left_grad, right_grad, bias_grad = finish(
        pieces,
        left_own,
        right_own,
        bias,
        first_homolog_features.shape,
        second_homolog_features.shape,
        1.0 / (sequences * res_total),
        1.0 / res_total,
    )
    return (
        pair_map.reshape(i_n, j_n, PAIR_FEATURES),
        left_grad,
        right_grad,
        projection,
        bias_grad.reshape(PAIR_FEATURES),
    )


def solution(mesh):
    return jax.shard_map(
        local,
        mesh=mesh,
        in_specs=(
            P(("dp", "col"), "row"),
            P(("dp", "row"), "col"),
            P(),
            P(),
            P(("dp", "row"), "col", None),
        ),
        out_specs=(
            P(("dp", "row"), "col", None),
            P(("dp", "col"), "row"),
            P(("dp", "row"), "col"),
            P("dp", None),
            P("dp"),
        ),
        check_vma=False,
    )
```

```python
import functools

import jax
import jax.numpy as jnp
from jax import lax
from jax.experimental import pallas as pl
from jax.experimental.pallas import tpu as pltpu
from jax.sharding import PartitionSpec as P

PROJECTED_DEPTH = 32
PAIR_FEATURES = 128
GROUP = 8
MULTIPLY_ROWS = 384
CHUNKS = 2
BIAS_ROWS = 16
LANES = 128
F32 = jnp.float32
BF16 = jnp.bfloat16
MIB = 1024 * 1024

ROWS_BY_ROWS = (((1,), (1,)), ((), ()))
COLS_BY_COLS = (((0,), (0,)), ((), ()))


def params(sequences=0):
    return pltpu.CompilerParams(vmem_limit_bytes=min(10 + 10 * sequences // 32, 50) * MIB + 2 * MIB)


def whole(shape):
    return pl.BlockSpec(shape, lambda t: (0,) * len(shape))


def dot(x, y, dims=(((1,), (0,)), ((), ()))):
    return lax.dot_general(x, y, dims, preferred_element_type=F32)


def load_kernel(a_hbm, b_hbm, w_hbm, g_hbm, we_ref, wt_ref, a_ref, b_ref, w_ref, g_ref, w32, sems):
    depth = PROJECTED_DEPTH
    copies = [
        pltpu.make_async_copy(source, target, sems.at[n])
        for n, (source, target) in enumerate(
            [(w_hbm, w_ref), (g_hbm, g_ref), (a_hbm, a_ref), (b_hbm, b_ref)]
        )
    ]
    for copy in copies:
        copy.start()
    copies[0].wait()
    w32[...] = w_ref[...].astype(F32)
    for e in range(depth):
        block = w32[pl.ds(e, depth, stride=depth), :]
        we_ref[e * depth : (e + 1) * depth, :] = block.astype(BF16)
    wt_ref[...] = we_ref[...].astype(F32).T.astype(BF16)
    for copy in copies[1:]:
        copy.wait()


def in_vmem():
    return pl.BlockSpec(memory_space=pltpu.VMEM)


def load(a, b, w, g):
    shapes = [
        jax.ShapeDtypeStruct(w.shape, BF16),
        jax.ShapeDtypeStruct(w.shape[::-1], BF16),
        *[jax.ShapeDtypeStruct(x.shape, BF16) for x in (a, b, w, g)],
    ]
    return pl.pallas_call(
        load_kernel,
        in_specs=[pl.BlockSpec(memory_space=pltpu.HBM)] * 4,
        out_specs=[in_vmem()] * len(shapes),
        out_shape=shapes,
        scratch_shapes=[pltpu.VMEM(w.shape, F32), pltpu.SemaphoreType.DMA((4,))],
        compiler_params=params(),
        cost_estimate=pl.CostEstimate(
            flops=1000 * w.size, bytes_accessed=16 * w.size, transcendentals=0
        ),
    )(*[pltpu.with_memory_space_constraint(x, pltpu.HBM) for x in (a, b, w, g)])


def stack(*groups):
    def kernel(*refs):
        refs, outs = refs[: -len(groups)], refs[-len(groups) :]
        for group, out in zip(groups, outs, strict=True):
            blocks = [ref[...].astype(F32) for ref in refs[: len(group)]]
            refs = refs[len(group) :]
            out[...] = jnp.concatenate(blocks, axis=0).astype(BF16)

    shapes = [((len(group) * group[0].shape[0], group[0].shape[1]), BF16) for group in groups]
    return call(kernel, [x for group in groups for x in group], shapes)


def split(total):
    high = total.astype(BF16).astype(F32)
    row = lax.broadcasted_iota(jnp.int32, (BIAS_ROWS, PAIR_FEATURES), 0)
    return jnp.where(row == 0, high, jnp.where(row == 1, total - high, 0.0)).astype(BF16)


def joined(block):
    block = block.astype(F32)
    return block[0:1] + block[1:2]


def multiply(left_ref, right_ref, out_ref):
    for n in range(0, right_ref.shape[0], MULTIPLY_ROWS):
        rows = slice(n, n + MULTIPLY_ROWS)
        out_ref[:, rows] = dot(left_ref[...], right_ref[rows, :], ROWS_BY_ROWS).astype(BF16)


def prepare_kernel(i_n, j_n, we_ref, g_ref, y_ref, gt_ref, bias_ref, g32):
    g32[...] = g_ref[...].astype(F32)
    bias_ref[...] = split(jnp.sum(g32[...], axis=0, keepdims=True))
    multiply(we_ref, g_ref, y_ref)

    for j in range(j_n):
        gt_ref[j * i_n : (j + 1) * i_n, :] = g32[pl.ds(j, i_n, stride=j_n), :].astype(BF16)


def prepare(we, g, i_n, j_n):
    pairs = i_n * j_n
    channels = we.shape[0]
    shapes = [
        jax.ShapeDtypeStruct((channels, pairs), BF16),
        jax.ShapeDtypeStruct(g.shape, BF16),
        jax.ShapeDtypeStruct((BIAS_ROWS, PAIR_FEATURES), BF16),
    ]
    return pl.pallas_call(
        functools.partial(prepare_kernel, i_n, j_n),
        in_specs=[in_vmem()] * 2,
        out_specs=[in_vmem()] * len(shapes),
        out_shape=shapes,
        scratch_shapes=[pltpu.VMEM(g.shape, F32)],
        compiler_params=params(16),
        cost_estimate=pl.CostEstimate(
            flops=2 * pairs * channels * PAIR_FEATURES,
            bytes_accessed=4 * pairs * channels,
            transcendentals=0,
        ),
    )(we, g)


def join(pieces, axis, held):
    half = lax.axis_size(axis) // 2
    depth = pieces[0].shape[0] // half
    me = lax.axis_index(axis)
    odd, home = lax.rem(me, 2), lax.div(me, 2)
    for piece, parity in zip(pieces, (odd, 1 - odd), strict=True):
        block = piece[...].astype(F32)
        for p in range(half):
            place = (2 * lax.bitwise_xor(home, p) + parity) * depth
            held[pl.ds(pl.multiple_of(place, depth), depth), :] = block[p * depth : (p + 1) * depth]


def repeat_matrix(sequences):
    shape = (sequences, GROUP * sequences)
    lane = lax.broadcasted_iota(jnp.int32, shape, 1)
    row = lax.broadcasted_iota(jnp.int32, shape, 0)
    return (lax.rem(lane, sequences) == row).astype(BF16)


def tile_count(sequences):
    return GROUP * sequences // LANES, max(1, sequences // LANES)


def spread(held, wide):
    repeated = repeat_matrix(held.shape[0])[:, : wide.shape[0] * LANES]
    both = dot(held[...].T.astype(BF16), repeated)
    for l in range(wide.shape[0]):
        wide[l] = both[:, l * LANES : (l + 1) * LANES]


def tiles_of(sequences, tile):
    lane = lax.broadcasted_iota(jnp.int32, (1, LANES), 1) + tile * LANES
    return [
        (m, lax.div(lane, sequences) == m)
        for m in range(GROUP)
        if m * sequences < (tile + 1) * LANES and (m + 1) * sequences > tile * LANES
    ]


def chunks(body):
    if CHUNKS == 1:
        body(0)
    else:
        pl.loop(0, CHUNKS)(body)


def diagonal_of(wide, channel, positions, sequences):
    columns = []
    blocks = [
        wide[l, pl.ds(channel, positions, stride=PROJECTED_DEPTH), :].astype(BF16)
        for l in range(wide.shape[0])
    ]
    for l in range(tile_count(sequences)[0]):
        block = blocks[l % len(blocks)]
        members = dict(tiles_of(sequences, l))
        columns.append(
            jnp.concatenate(
                [
                    block * members[m].astype(F32).astype(BF16)
                    if m in members
                    else jnp.zeros(block.shape, BF16)
                    for m in range(GROUP)
                ],
                axis=0,
            )
        )
    return jnp.concatenate(columns, axis=1)


def alone(count):
    return lambda me: ([me], [[lax.bitwise_xor(me, d)] for d in range(1, count)])


def in_pairs(count):
    def plan(me):
        evens = range(0, count, 2)
        return [lax.bitwise_xor(me, d) for d in evens], [
            [lax.bitwise_xor(me, d + 1) for d in evens]
        ]

    return plan


def outer_kernel(i_n, j_n, *refs):
    depth = PROJECTED_DEPTH
    row_n = lax.axis_size("row")
    a_pieces, b_pieces, refs = refs[:2], refs[2:4], refs[4:]
    g_ref, bias_ref, x_ref, a_held, b_wide = refs[:5]
    messages, (b_held, left, total) = refs[5 : 5 + row_n], refs[5 + row_n :]
    sequences = a_held.shape[0]
    groups = i_n // GROUP
    per_step = depth // CHUNKS
    span = GROUP * j_n

    join(a_pieces, "col", a_held)
    join(b_pieces, "row", b_held)
    spread(b_held, b_wide)
    turned = a_held[...].T.astype(BF16)
    shape = (sequences, GROUP * sequences)
    shifted = lax.broadcasted_iota(jnp.int32, shape, 1) - lax.broadcasted_iota(jnp.int32, shape, 0)
    value = jnp.zeros(left.shape, F32)
    for m in range(GROUP):
        rows = [
            turned[(k * GROUP + m) * depth : (k * GROUP + m + 1) * depth, :] for k in range(groups)
        ]
        value += dot(jnp.concatenate(rows, axis=0), (shifted == m * sequences).astype(BF16))
    left[...] = value.astype(BF16)

    @chunks
    def _(t):
        size = per_step * depth
        rows = pl.ds(t * size if CHUNKS == 1 else pl.multiple_of(t * size, size), size)
        x_part = x_ref.at[rows]
        for e in range(0, per_step, 2):
            right = [diagonal_of(b_wide, t * per_step + e + n, j_n, sequences) for n in range(2)]
            product = dot(
                left[...], jnp.concatenate(right, axis=0), ROWS_BY_ROWS
            ).astype(BF16)
            for n in range(2):
                for k in range(groups):
                    x_part[(e + n) * depth : (e + n + 1) * depth, k * span : (k + 1) * span] = product[
                        k * depth : (k + 1) * depth, n * span : (n + 1) * span
                    ]
        total[rows, :] = dot(x_part[...], g_ref[...])

    share = total.shape[0] // row_n
    me = lax.axis_index("row")
    for p, message in enumerate(messages):
        part = lax.bitwise_xor(me, p)
        for n in range(share // depth):
            block = total[pl.ds(part * (share // depth) + n, depth, stride=depth), :]
            message[n * depth : (n + 1) * depth, :] = block.astype(message.dtype)
        message[share:, :] = bias_ref[...].astype(message.dtype)


def outer(a_pieces, b_pieces, g, bias_rows, i_n, j_n, sequences):
    row_n = lax.axis_size("row")
    depth = PROJECTED_DEPTH
    channels = depth * depth
    pairs = i_n * j_n
    tiles = tile_count(sequences)[1]
    operands = [*a_pieces, *b_pieces, g, bias_rows]
    shapes = [jax.ShapeDtypeStruct((channels, pairs), BF16)]
    shapes += [
        jax.ShapeDtypeStruct((sequences, i_n * depth), F32),
        jax.ShapeDtypeStruct((tiles, j_n * depth, LANES), F32),
    ]
    shapes += [
        jax.ShapeDtypeStruct((channels // row_n + BIAS_ROWS, LANES), BF16 if p else F32)
        for p in range(row_n)
    ]
    results = pl.pallas_call(
        functools.partial(outer_kernel, i_n, j_n),
        in_specs=[in_vmem()] * len(operands),
        out_specs=[in_vmem()] * len(shapes),
        out_shape=shapes,
        scratch_shapes=[
            pltpu.VMEM((sequences, j_n * depth), F32),
            pltpu.VMEM((i_n // GROUP * depth, GROUP * sequences), BF16),
            pltpu.VMEM((channels, PAIR_FEATURES), F32),
        ],
        compiler_params=params(sequences),
        cost_estimate=pl.CostEstimate(
            flops=4 * pairs * channels * PAIR_FEATURES,
            bytes_accessed=2 * pairs * channels,
            transcendentals=0,
        ),
    )(*operands)
    return *results[:3], results[3:]


def gradient_kernel(axis, plan, kept, positions, others, sequences, *refs):
    depth = PROJECTED_DEPTH
    wide, source = refs[:2]
    outs, (result, grown, grad) = refs[3:-3], refs[-3:]
    parts = lax.axis_size(axis)
    per_step = depth // CHUNKS
    span = GROUP * others

    result[...] = jnp.zeros(result.shape, F32)

    @chunks
    def _(t):
        size = per_step * depth
        rows = pl.ds(t * size if CHUNKS == 1 else pl.multiple_of(t * size, size), size)
        part = source.at[rows]
        for n in range(0, per_step, 2):
            blocks = [
                jnp.concatenate(
                    [
                        part[m * depth : (m + 1) * depth, k * span : (k + 1) * span]
                        for m in (n, n + 1)
                    ],
                    axis=1,
                )
                for k in range(positions // GROUP)
            ]
            right = [
                diagonal_of(wide, t * per_step + m, others, sequences) for m in (n, n + 1)
            ]
            result[...] += dot(jnp.concatenate(blocks, axis=0), jnp.concatenate(right, axis=0))

    scaled = (result[...] * (1.0 / sequences)).astype(BF16)
    for l in range(scaled.shape[1] // LANES):
        members = dict(tiles_of(sequences, l))
        for k in range(positions // GROUP):
            block = scaled[k * depth : (k + 1) * depth, l * LANES : (l + 1) * LANES]
            for m in range(GROUP):
                start = (k * GROUP + m) * depth
                grown[start : start + depth, l * LANES : (l + 1) * LANES] = (
                    block * members[m].astype(F32).astype(BF16)
                    if m in members
                    else jnp.zeros((depth, LANES), BF16)
                )
    grad[...] = dot(repeat_matrix(sequences), grown[...], ROWS_BY_ROWS)
    share = sequences // parts

    def rows_of(p):
        mine = grad[pl.ds(pl.multiple_of(p * share, share), share), :]
        return jnp.concatenate(
            [mine[:, l * LANES : (l + 1) * LANES] for l in range(mine.shape[1] // LANES)], axis=0
        )

    stay, go = plan(lax.axis_index(axis))
    for p, out in zip(stay, outs[:kept], strict=True):
        out[...] = rows_of(p)
    for group, out in zip(go, outs[kept:], strict=True):
        size = out.shape[0] // len(group)
        for n, p in enumerate(group):
            out[n * size : (n + 1) * size, :] = rows_of(p).astype(BF16)


def gradient(wide, source, after, axis, plan, kept, groups, positions, others, sequences):
    depth = PROJECTED_DEPTH
    parts = lax.axis_size(axis)
    rows = sequences // parts * positions * depth // LANES
    shapes = [jax.ShapeDtypeStruct((rows, LANES), F32)] * kept
    group = (parts - kept) // groups
    shapes += [jax.ShapeDtypeStruct((group * rows, LANES), BF16)] * groups
    results = pl.pallas_call(
        functools.partial(gradient_kernel, axis, plan, kept, positions, others, sequences),
        in_specs=[in_vmem(), in_vmem(), pl.BlockSpec(memory_space=pl.ANY)],
        out_specs=[in_vmem()] * len(shapes),
        out_shape=shapes,
        scratch_shapes=[
            pltpu.VMEM((positions // GROUP * depth, GROUP * sequences), F32),
            pltpu.VMEM((positions * depth, GROUP * sequences), BF16),
            pltpu.VMEM((sequences, positions * depth), F32),
        ],
        compiler_params=params(sequences),
        cost_estimate=pl.CostEstimate(
            flops=2 * source.size * PAIR_FEATURES,
            bytes_accessed=2 * source.size,
            transcendentals=0,
        ),
    )(wide, source, after)
    return results[:kept], results[kept:]


def product_kernel(left_ref, right_ref, held, _, out_ref, wide):
    spread(held, wide)
    multiply(left_ref, right_ref, out_ref)


def product(left, right, held, after):
    shape = (left.shape[0], right.shape[0])
    spread_shape = (tile_count(held.shape[0])[1], held.shape[1], LANES)
    return pl.pallas_call(
        product_kernel,
        in_specs=[in_vmem()] * 3 + [pl.BlockSpec(memory_space=pl.ANY)],
        out_specs=[in_vmem()] * 2,
        out_shape=[jax.ShapeDtypeStruct(shape, BF16), jax.ShapeDtypeStruct(spread_shape, F32)],
        compiler_params=params(32),
        cost_estimate=pl.CostEstimate(
            flops=2 * shape[0] * shape[1] * left.shape[1],
            bytes_accessed=4 * shape[0] * shape[1],
            transcendentals=0,
        ),
    )(left, right, held, after)


def pair_kernel(sequences, x_ref, wt_ref, bias_ref, _, out_ref):
    product = dot(wt_ref[...], x_ref[...])
    out_ref[...] = (product.T * (1.0 / sequences) + bias_ref[...]).astype(BF16)


def pair(x, wt, output_bias, after, sequences):
    channels, pairs = x.shape
    count = 3
    size = pairs // count
    return pl.pallas_call(
        functools.partial(pair_kernel, sequences),
        grid=(count,),
        in_specs=[
            pl.BlockSpec((channels, size), lambda t: (0, t)),
            whole(wt.shape),
            whole((1, PAIR_FEATURES)),
            pl.BlockSpec(memory_space=pl.ANY),
        ],
        out_specs=pl.BlockSpec((size, PAIR_FEATURES), lambda t: (t, 0)),
        out_shape=jax.ShapeDtypeStruct((pairs, PAIR_FEATURES), BF16),
        compiler_params=params(),
        cost_estimate=pl.CostEstimate(
            flops=4 * pairs * channels * PAIR_FEATURES,
            bytes_accessed=2 * pairs * channels,
            transcendentals=0,
        ),
    )(x, wt, output_bias.reshape(1, PAIR_FEATURES), after)


def unfold(total, share, out):
    for l in range(out.shape[1] // LANES):
        out[:, l * LANES : (l + 1) * LANES] = total[l * share : (l + 1) * share, :]


def call(kernel, operands, shapes, after=(), scratch=()):
    specs = [in_vmem()] * len(operands) + [pl.BlockSpec(memory_space=pl.ANY)] * len(after)
    return pl.pallas_call(
        kernel,
        in_specs=specs,
        out_specs=[in_vmem()] * len(shapes),
        out_shape=[jax.ShapeDtypeStruct(shape, kind) for shape, kind in shapes],
        scratch_shapes=scratch,
        compiler_params=params(),
    )(*operands, *after)


def partners(count):
    return [0, *range(count - 1, 0, -1)]


def row_sum(parts, after, share):
    count = len(parts)

    def kernel(*refs):
        parts, (_, message, held) = refs[:count], refs[count:]
        me = lax.axis_index("row")
        total = parts[0][0:share, :]
        for p, part in zip(partners(count), parts, strict=True):
            held[lax.bitwise_xor(me, p)] = part[share:, :].astype(F32)
            if p > 0:
                total += part[0:share, :].astype(F32)
        bias = joined(held[0])
        for n in range(1, count):
            bias += joined(held[n])
        message[0:share, :] = total.astype(BF16)
        message[share:, :] = split(bias)

    scratch = [pltpu.VMEM((count, BIAS_ROWS, LANES), F32)]
    (message,) = call(kernel, parts, [((share + BIAS_ROWS, LANES), BF16)], [after], scratch)
    return message


def pair_sum(kept, near, after):
    def kernel(*refs):
        kept, near, (own, *messages) = refs[:count], refs[count], refs[count + 2 :]
        size = own.shape[0]
        for p, part in enumerate(kept):
            both = part[...] + near[p * size : (p + 1) * size, :].astype(F32)
            if p == 0:
                own[...] = both
            else:
                messages[p - 1][...] = both.astype(BF16)

    count = len(kept)
    shapes = [(kept[0].shape, F32)] + [(kept[0].shape, BF16)] * (count - 1)
    own, *messages = call(kernel, [*kept, near], shapes, [after])
    return own, messages


def column_pair_sum(own, near, after, share):
    def kernel(own, near, _, message):
        total = own[0:share, :].astype(F32) + near[0:share, :].astype(F32)
        message[0:share, :] = total.astype(BF16)
        message[share:, :] = split(joined(own[share:, :]) + joined(near[share:, :]))

    (message,) = call(kernel, [own, near], [(own.shape, BF16)], [after])
    return message


def column_sum(parts, grads, share):
    rows = share + BIAS_ROWS
    count, sent = len(parts), len(grads)

    def kernel(*refs):
        parts, grads, refs = refs[:count], refs[count : count + sent], refs[count + sent :]
        messages, (piece_out, bias_out, held) = refs[:sent], refs[sent:]
        home = lax.div(lax.axis_index("col"), 2)
        for p, part in enumerate(parts):
            held[lax.bitwise_xor(home, p)] = part[...]
        total, bias = held[0, 0:share, :].astype(F32), joined(held[0, share:, :])
        for n in range(1, count):
            total += held[n, 0:share, :].astype(F32)
            bias += joined(held[n, share:, :])
        piece = total.astype(BF16)
        piece_out[...] = piece
        for message, grad in zip(messages, grads, strict=True):
            message[0:share, :] = piece
            message[share:, :] = grad[...]
        bias_out[...] = jnp.broadcast_to(bias, bias_out.shape)

    shapes = [((share + grad.shape[0], LANES), BF16) for grad in grads]
    shapes += [((share, LANES), BF16), ((8, LANES), F32)]
    scratch = [pltpu.VMEM((count, rows, LANES), BF16)]
    *messages, piece, bias = call(kernel, [*parts, *grads], shapes, scratch=scratch)
    return messages, piece, bias


def finish(pieces, left, right_own, bias, left_shape, right_shape, scale, bias_scale):
    count, left_n = len(pieces), len(left)
    share = pieces[0].shape[0]

    def kernel(*refs):
        pieces, left, refs = refs[:count], refs[count : count + left_n], refs[count + left_n :]
        right_own, bias, projection, left_out, right_out, bias_out = refs
        me = lax.axis_index("row")
        right_total = right_own[...]
        for p, piece in zip(partners(count), pieces, strict=True):
            rows = pl.ds(pl.multiple_of(lax.bitwise_xor(me, p) * share, share), share)
            projection[rows, :] = piece[0:share, :].astype(F32) * scale
            if p > 0:
                right_total += piece[share:, :].astype(F32)
        left_total = left[0][...]
        for term in left[1:]:
            left_total += term[...].astype(F32)
        unfold(left_total, left_out.shape[0], left_out)
        unfold(right_total, right_out.shape[0], right_out)
        bias_out[...] = bias[0:1, :] * bias_scale

    shapes = [
        ((count * share, PAIR_FEATURES), F32),
        (left_shape, F32),
        (right_shape, F32),
        ((1, PAIR_FEATURES), F32),
    ]
    return call(kernel, [*pieces, *left, right_own, bias], shapes)


def swap(x, axis, p):
    return lax.ppermute(x, axis, [(n, n ^ p) for n in range(lax.axis_size(axis))])


def swap_each(parts, axis, step=1):
    count = len(parts)
    return [swap(parts[n - 1], axis, n * step) for n in range(count, 0, -1)][::-1]


def from_evens(x, axis):
    return swap_each([x] * (lax.axis_size(axis) // 2 - 1), axis, 2)


def local(
    first_homolog_features, second_homolog_features, final_projection_matrix, output_bias, cotangent
):
    i_n, j_n, _ = cotangent.shape
    row_n, col_n = lax.axis_size("row"), lax.axis_size("col")
    sequences = second_homolog_features.shape[0] * row_n
    channels = final_projection_matrix.shape[0]
    res_total = i_n * row_n
    a_far = from_evens(first_homolog_features, "col")
    b_far = from_evens(second_homolog_features, "row")
    we, wt, a, b, w, g = load(
        first_homolog_features,
        second_homolog_features,
        final_projection_matrix,
        cotangent.reshape(i_n * j_n, PAIR_FEATURES),
    )
    a, b = stack([a, *a_far], [b, *b_far])
    a_pieces = [a, swap(a, "col", 1)]
    b_pieces = [b, swap(b, "row", 1)]
    y, gt, bias_rows = prepare(we, g, i_n, j_n)

    x, a_held, b_wide, (own, *messages) = outer(
        a_pieces, b_pieces, g, bias_rows, i_n, j_n, sequences
    )
    share = channels // row_n

    parts = [own] + swap_each(messages, "row")[::-1]
    left_kept, (message,) = gradient(
        b_wide, y, own, "col", in_pairs(col_n), col_n // 2, 1, i_n, j_n, sequences
    )
    left_near = swap(message, "col", 1)

    message = row_sum(parts, message, share)
    near = swap(message, "col", 1)
    left_own, left_messages = pair_sum(left_kept, left_near, message)
    left = [left_own] + swap_each(left_messages, "col", 2)
    y2, a_wide = product(w, gt, a_held, left_own)

    message = column_pair_sum(message, near, y2, share)
    parts = [message] + from_evens(message, "col")
    (right_own,), right_sent = gradient(
        a_wide, y2, message, "row", alone(row_n), 1, row_n - 1, j_n, i_n, sequences
    )

    messages, piece, bias = column_sum(parts, right_sent, share)
    pieces = [piece] + swap_each(messages, "row")[::-1]
    pair_map = pair(x, wt, output_bias, piece, sequences)
    projection, left_grad, right_grad, bias_grad = finish(
        pieces,
        left,
        right_own,
        bias,
        first_homolog_features.shape,
        second_homolog_features.shape,
        1.0 / (sequences * res_total),
        1.0 / res_total,
    )
    return (
        pair_map.reshape(i_n, j_n, PAIR_FEATURES),
        left_grad,
        right_grad,
        projection,
        bias_grad.reshape(PAIR_FEATURES),
    )


def solution(mesh):
    return jax.shard_map(
        local,
        mesh=mesh,
        in_specs=(
            P(("dp", "col"), "row"),
            P(("dp", "row"), "col"),
            P(),
            P(),
            P(("dp", "row"), "col", None),
        ),
        out_specs=(
            P(("dp", "row"), "col", None),
            P(("dp", "col"), "row"),
            P(("dp", "row"), "col"),
            P("dp", None),
            P("dp"),
        ),
        check_vma=False,
    )
```

```python
import functools

import jax
import jax.numpy as jnp
from jax import lax
from jax.experimental import pallas as pl
from jax.experimental.pallas import tpu as pltpu
from jax.sharding import PartitionSpec as P

PROJECTED_DEPTH = 32
PAIR_FEATURES = 128
GROUP = 8
MULTIPLY_ROWS = 384
PAIR_BLOCKS = 3
CHUNKS = 2
BIAS_ROWS = 16
LANES = 128
F32 = jnp.float32
BF16 = jnp.bfloat16
MIB = 1024 * 1024

ROWS_BY_ROWS = (((1,), (1,)), ((), ()))
COLS_BY_COLS = (((0,), (0,)), ((), ()))


def params(sequences=0):
    return pltpu.CompilerParams(vmem_limit_bytes=min(10 + 10 * sequences // 32, 50) * MIB + 2 * MIB)


def whole(shape):
    return pl.BlockSpec(shape, lambda t: (0,) * len(shape))


def dot(x, y, dims=(((1,), (0,)), ((), ()))):
    return lax.dot_general(x, y, dims, preferred_element_type=F32)


def load_kernel(a_hbm, b_hbm, w_hbm, g_hbm, we_ref, wt_ref, a_ref, b_ref, w_ref, g_ref, w32, sems):
    depth = PROJECTED_DEPTH
    copies = [
        pltpu.make_async_copy(source, target, sems.at[n])
        for n, (source, target) in enumerate(
            [(w_hbm, w_ref), (g_hbm, g_ref), (a_hbm, a_ref), (b_hbm, b_ref)]
        )
    ]
    for copy in copies:
        copy.start()
    copies[0].wait()
    w32[...] = w_ref[...].astype(F32)
    for e in range(depth):
        block = w32[pl.ds(e, depth, stride=depth), :]
        we_ref[e * depth : (e + 1) * depth, :] = block.astype(BF16)
    wt_ref[...] = we_ref[...].astype(F32).T.astype(BF16)
    for copy in copies[1:]:
        copy.wait()


def in_vmem():
    return pl.BlockSpec(memory_space=pltpu.VMEM)


def load(a, b, w, g):
    shapes = [
        jax.ShapeDtypeStruct(w.shape, BF16),
        jax.ShapeDtypeStruct(w.shape[::-1], BF16),
        *[jax.ShapeDtypeStruct(x.shape, BF16) for x in (a, b, w, g)],
    ]
    return pl.pallas_call(
        load_kernel,
        in_specs=[pl.BlockSpec(memory_space=pltpu.HBM)] * 4,
        out_specs=[in_vmem()] * len(shapes),
        out_shape=shapes,
        scratch_shapes=[pltpu.VMEM(w.shape, F32), pltpu.SemaphoreType.DMA((4,))],
        compiler_params=params(),
        cost_estimate=pl.CostEstimate(
            flops=1000 * w.size, bytes_accessed=16 * w.size, transcendentals=0
        ),
    )(*[pltpu.with_memory_space_constraint(x, pltpu.HBM) for x in (a, b, w, g)])


def stack(*groups):
    def kernel(*refs):
        refs, outs = refs[: -len(groups)], refs[-len(groups) :]
        for group, out in zip(groups, outs, strict=True):
            blocks = [ref[...].astype(F32) for ref in refs[: len(group)]]
            refs = refs[len(group) :]
            out[...] = jnp.concatenate(blocks, axis=0).astype(BF16)

    shapes = [((len(group) * group[0].shape[0], group[0].shape[1]), BF16) for group in groups]
    return call(kernel, [x for group in groups for x in group], shapes)


def split(total):
    high = total.astype(BF16).astype(F32)
    row = lax.broadcasted_iota(jnp.int32, (BIAS_ROWS, PAIR_FEATURES), 0)
    return jnp.where(row == 0, high, jnp.where(row == 1, total - high, 0.0)).astype(BF16)


def joined(block):
    block = block.astype(F32)
    return block[0:1] + block[1:2]


def multiply(left_ref, right_ref, out_ref):
    for n in range(0, right_ref.shape[0], MULTIPLY_ROWS):
        rows = slice(n, n + MULTIPLY_ROWS)
        out_ref[:, rows] = dot(left_ref[...], right_ref[rows, :], ROWS_BY_ROWS).astype(BF16)


def prepare_kernel(i_n, j_n, we_ref, g_ref, y_ref, gt_ref, bias_ref, g32):
    g32[...] = g_ref[...].astype(F32)
    bias_ref[...] = split(jnp.sum(g32[...], axis=0, keepdims=True))
    multiply(we_ref, g_ref, y_ref)

    for j in range(j_n):
        gt_ref[j * i_n : (j + 1) * i_n, :] = g32[pl.ds(j, i_n, stride=j_n), :].astype(BF16)


def prepare(we, g, i_n, j_n):
    pairs = i_n * j_n
    channels = we.shape[0]
    shapes = [
        jax.ShapeDtypeStruct((channels, pairs), BF16),
        jax.ShapeDtypeStruct(g.shape, BF16),
        jax.ShapeDtypeStruct((BIAS_ROWS, PAIR_FEATURES), BF16),
    ]
    return pl.pallas_call(
        functools.partial(prepare_kernel, i_n, j_n),
        in_specs=[in_vmem()] * 2,
        out_specs=[in_vmem()] * len(shapes),
        out_shape=shapes,
        scratch_shapes=[pltpu.VMEM(g.shape, F32)],
        compiler_params=params(16),
        cost_estimate=pl.CostEstimate(
            flops=2 * pairs * channels * PAIR_FEATURES,
            bytes_accessed=4 * pairs * channels,
            transcendentals=0,
        ),
    )(we, g)


def join(pieces, axis, held):
    half = lax.axis_size(axis) // 2
    depth = pieces[0].shape[0] // half
    me = lax.axis_index(axis)
    odd, home = lax.rem(me, 2), lax.div(me, 2)
    for piece, parity in zip(pieces, (odd, 1 - odd), strict=True):
        block = piece[...].astype(F32)
        for p in range(half):
            place = (2 * lax.bitwise_xor(home, p) + parity) * depth
            held[pl.ds(pl.multiple_of(place, depth), depth), :] = block[p * depth : (p + 1) * depth]


def repeat_matrix(sequences):
    shape = (sequences, GROUP * sequences)
    lane = lax.broadcasted_iota(jnp.int32, shape, 1)
    row = lax.broadcasted_iota(jnp.int32, shape, 0)
    return (lax.rem(lane, sequences) == row).astype(BF16)


def tile_count(sequences):
    return GROUP * sequences // LANES, max(1, sequences // LANES)


def spread(held, wide):
    repeated = repeat_matrix(held.shape[0])[:, : wide.shape[0] * LANES]
    both = dot(held[...].T.astype(BF16), repeated)
    for l in range(wide.shape[0]):
        wide[l] = both[:, l * LANES : (l + 1) * LANES]


def tiles_of(sequences, tile):
    lane = lax.broadcasted_iota(jnp.int32, (1, LANES), 1) + tile * LANES
    return [
        (m, lax.div(lane, sequences) == m)
        for m in range(GROUP)
        if m * sequences < (tile + 1) * LANES and (m + 1) * sequences > tile * LANES
    ]


def chunks(body):
    if CHUNKS == 1:
        body(0)
    else:
        pl.loop(0, CHUNKS)(body)


def diagonal_of(wide, channel, positions, sequences):
    columns = []
    blocks = [
        wide[l, pl.ds(channel, positions, stride=PROJECTED_DEPTH), :].astype(BF16)
        for l in range(wide.shape[0])
    ]
    for l in range(tile_count(sequences)[0]):
        block = blocks[l % len(blocks)]
        members = dict(tiles_of(sequences, l))
        columns.append(
            jnp.concatenate(
                [
                    block * members[m].astype(F32).astype(BF16)
                    if m in members
                    else jnp.zeros(block.shape, BF16)
                    for m in range(GROUP)
                ],
                axis=0,
            )
        )
    return jnp.concatenate(columns, axis=1)


def alone(count):
    return lambda me: ([me], [[lax.bitwise_xor(me, d)] for d in range(1, count)])


def in_pairs(count):
    def plan(me):
        evens = range(0, count, 2)
        return [lax.bitwise_xor(me, d) for d in evens], [
            [lax.bitwise_xor(me, d + 1) for d in evens]
        ]

    return plan


def outer_kernel(i_n, j_n, *refs):
    depth = PROJECTED_DEPTH
    row_n = lax.axis_size("row")
    a_pieces, b_pieces, refs = refs[:2], refs[2:4], refs[4:]
    g_ref, bias_ref, x_ref, a_held, b_wide = refs[:5]
    messages, (b_held, left, total) = refs[5 : 5 + row_n], refs[5 + row_n :]
    sequences = a_held.shape[0]
    groups = i_n // GROUP
    per_step = depth // CHUNKS
    span = GROUP * j_n

    join(a_pieces, "col", a_held)
    join(b_pieces, "row", b_held)
    spread(b_held, b_wide)
    turned = a_held[...].T.astype(BF16)
    shape = (sequences, GROUP * sequences)
    shifted = lax.broadcasted_iota(jnp.int32, shape, 1) - lax.broadcasted_iota(jnp.int32, shape, 0)
    value = jnp.zeros(left.shape, F32)
    for m in range(GROUP):
        rows = [
            turned[(k * GROUP + m) * depth : (k * GROUP + m + 1) * depth, :] for k in range(groups)
        ]
        value += dot(jnp.concatenate(rows, axis=0), (shifted == m * sequences).astype(BF16))
    left[...] = value.astype(BF16)

    @chunks
    def _(t):
        size = per_step * depth
        rows = pl.ds(t * size if CHUNKS == 1 else pl.multiple_of(t * size, size), size)
        x_part = x_ref.at[rows]
        for e in range(0, per_step, 2):
            right = [diagonal_of(b_wide, t * per_step + e + n, j_n, sequences) for n in range(2)]
            product = dot(
                left[...], jnp.concatenate(right, axis=0), ROWS_BY_ROWS
            ).astype(BF16)
            for n in range(2):
                for k in range(groups):
                    x_part[(e + n) * depth : (e + n + 1) * depth, k * span : (k + 1) * span] = product[
                        k * depth : (k + 1) * depth, n * span : (n + 1) * span
                    ]
        total[rows, :] = dot(x_part[...], g_ref[...])

    share = total.shape[0] // row_n
    me = lax.axis_index("row")
    for p, message in enumerate(messages):
        part = lax.bitwise_xor(me, p)
        for n in range(share // depth):
            block = total[pl.ds(part * (share // depth) + n, depth, stride=depth), :]
            message[n * depth : (n + 1) * depth, :] = block.astype(message.dtype)
        message[share:, :] = bias_ref[...].astype(message.dtype)


def outer(a_pieces, b_pieces, g, bias_rows, i_n, j_n, sequences):
    row_n = lax.axis_size("row")
    depth = PROJECTED_DEPTH
    channels = depth * depth
    pairs = i_n * j_n
    tiles = tile_count(sequences)[1]
    operands = [*a_pieces, *b_pieces, g, bias_rows]
    shapes = [jax.ShapeDtypeStruct((channels, pairs), BF16)]
    shapes += [
        jax.ShapeDtypeStruct((sequences, i_n * depth), F32),
        jax.ShapeDtypeStruct((tiles, j_n * depth, LANES), F32),
    ]
    shapes += [
        jax.ShapeDtypeStruct((channels // row_n + BIAS_ROWS, LANES), BF16 if p else F32)
        for p in range(row_n)
    ]
    results = pl.pallas_call(
        functools.partial(outer_kernel, i_n, j_n),
        in_specs=[in_vmem()] * len(operands),
        out_specs=[in_vmem()] * len(shapes),
        out_shape=shapes,
        scratch_shapes=[
            pltpu.VMEM((sequences, j_n * depth), F32),
            pltpu.VMEM((i_n // GROUP * depth, GROUP * sequences), BF16),
            pltpu.VMEM((channels, PAIR_FEATURES), F32),
        ],
        compiler_params=params(sequences),
        cost_estimate=pl.CostEstimate(
            flops=4 * pairs * channels * PAIR_FEATURES,
            bytes_accessed=2 * pairs * channels,
            transcendentals=0,
        ),
    )(*operands)
    return *results[:3], results[3:]


def gradient_kernel(axis, plan, kept, positions, others, sequences, *refs):
    depth = PROJECTED_DEPTH
    wide, source = refs[:2]
    outs, (result, grown, grad) = refs[3:-3], refs[-3:]
    parts = lax.axis_size(axis)
    per_step = depth // CHUNKS
    span = GROUP * others

    result[...] = jnp.zeros(result.shape, F32)

    @chunks
    def _(t):
        size = per_step * depth
        rows = pl.ds(t * size if CHUNKS == 1 else pl.multiple_of(t * size, size), size)
        part = source.at[rows]
        for n in range(0, per_step, 2):
            blocks = [
                jnp.concatenate(
                    [
                        part[m * depth : (m + 1) * depth, k * span : (k + 1) * span]
                        for m in (n, n + 1)
                    ],
                    axis=1,
                )
                for k in range(positions // GROUP)
            ]
            right = [
                diagonal_of(wide, t * per_step + m, others, sequences) for m in (n, n + 1)
            ]
            result[...] += dot(jnp.concatenate(blocks, axis=0), jnp.concatenate(right, axis=0))

    scaled = (result[...] * (1.0 / sequences)).astype(BF16)
    for l in range(scaled.shape[1] // LANES):
        members = dict(tiles_of(sequences, l))
        for k in range(positions // GROUP):
            block = scaled[k * depth : (k + 1) * depth, l * LANES : (l + 1) * LANES]
            for m in range(GROUP):
                start = (k * GROUP + m) * depth
                grown[start : start + depth, l * LANES : (l + 1) * LANES] = (
                    block * members[m].astype(F32).astype(BF16)
                    if m in members
                    else jnp.zeros((depth, LANES), BF16)
                )
    grad[...] = dot(repeat_matrix(sequences), grown[...], ROWS_BY_ROWS)
    share = sequences // parts

    def rows_of(p):
        mine = grad[pl.ds(pl.multiple_of(p * share, share), share), :]
        return jnp.concatenate(
            [mine[:, l * LANES : (l + 1) * LANES] for l in range(mine.shape[1] // LANES)], axis=0
        )

    stay, go = plan(lax.axis_index(axis))
    for p, out in zip(stay, outs[:kept], strict=True):
        out[...] = rows_of(p)
    for group, out in zip(go, outs[kept:], strict=True):
        size = out.shape[0] // len(group)
        for n, p in enumerate(group):
            out[n * size : (n + 1) * size, :] = rows_of(p).astype(BF16)


def gradient(wide, source, after, axis, plan, kept, groups, positions, others, sequences):
    depth = PROJECTED_DEPTH
    parts = lax.axis_size(axis)
    rows = sequences // parts * positions * depth // LANES
    shapes = [jax.ShapeDtypeStruct((rows, LANES), F32)] * kept
    group = (parts - kept) // groups
    shapes += [jax.ShapeDtypeStruct((group * rows, LANES), BF16)] * groups
    results = pl.pallas_call(
        functools.partial(gradient_kernel, axis, plan, kept, positions, others, sequences),
        in_specs=[in_vmem(), in_vmem(), pl.BlockSpec(memory_space=pl.ANY)],
        out_specs=[in_vmem()] * len(shapes),
        out_shape=shapes,
        scratch_shapes=[
            pltpu.VMEM((positions // GROUP * depth, GROUP * sequences), F32),
            pltpu.VMEM((positions * depth, GROUP * sequences), BF16),
            pltpu.VMEM((sequences, positions * depth), F32),
        ],
        compiler_params=params(sequences),
        cost_estimate=pl.CostEstimate(
            flops=2 * source.size * PAIR_FEATURES,
            bytes_accessed=2 * source.size,
            transcendentals=0,
        ),
    )(wide, source, after)
    return results[:kept], results[kept:]


def product_kernel(left_ref, right_ref, held, _, out_ref, wide):
    spread(held, wide)
    multiply(left_ref, right_ref, out_ref)


def product(left, right, held, after):
    shape = (left.shape[0], right.shape[0])
    spread_shape = (tile_count(held.shape[0])[1], held.shape[1], LANES)
    return pl.pallas_call(
        product_kernel,
        in_specs=[in_vmem()] * 3 + [pl.BlockSpec(memory_space=pl.ANY)],
        out_specs=[in_vmem()] * 2,
        out_shape=[jax.ShapeDtypeStruct(shape, BF16), jax.ShapeDtypeStruct(spread_shape, F32)],
        compiler_params=params(32),
        cost_estimate=pl.CostEstimate(
            flops=2 * shape[0] * shape[1] * left.shape[1],
            bytes_accessed=4 * shape[0] * shape[1],
            transcendentals=0,
        ),
    )(left, right, held, after)


def pair_kernel(sequences, x_ref, wt_ref, bias_ref, _after, *refs):
    out_ref, done_ref = refs[-2:]
    done_ref[...] = jnp.zeros(done_ref.shape, F32)
    product = dot(wt_ref[...], x_ref[...])
    out_ref[...] = (product.T * (1.0 / sequences) + bias_ref[...]).astype(BF16)


def pair(x, wt, output_bias, after, sequences, first, last, before=None):
    channels, pairs = x.shape
    size = pairs // PAIR_BLOCKS
    anywhere = pl.BlockSpec(memory_space=pl.ANY)
    done = jax.ShapeDtypeStruct((8, LANES), F32)
    return pl.pallas_call(
        functools.partial(pair_kernel, sequences),
        grid=(last - first,),
        in_specs=[
            pl.BlockSpec((channels, size), lambda t: (0, t + first)),
            whole(wt.shape),
            whole((1, PAIR_FEATURES)),
            anywhere,
        ]
        + [anywhere] * (before is not None),
        out_specs=[
            pl.BlockSpec((size, PAIR_FEATURES), lambda t: (t + first, 0)),
            whole(done.shape),
        ],
        out_shape=[jax.ShapeDtypeStruct((pairs, PAIR_FEATURES), BF16), done],
        input_output_aliases={} if before is None else {4: 0},
        compiler_params=params(),
        cost_estimate=pl.CostEstimate(
            flops=(last - first) * size * channels * PAIR_FEATURES,
            bytes_accessed=2 * (last - first) * size * channels,
            transcendentals=0,
        ),
    )(x, wt, output_bias.reshape(1, PAIR_FEATURES), after, *([] if before is None else [before]))


def unfold(total, share, out):
    for l in range(out.shape[1] // LANES):
        out[:, l * LANES : (l + 1) * LANES] = total[l * share : (l + 1) * share, :]


def call(kernel, operands, shapes, after=(), scratch=()):
    specs = [in_vmem()] * len(operands) + [pl.BlockSpec(memory_space=pl.ANY)] * len(after)
    return pl.pallas_call(
        kernel,
        in_specs=specs,
        out_specs=[in_vmem()] * len(shapes),
        out_shape=[jax.ShapeDtypeStruct(shape, kind) for shape, kind in shapes],
        scratch_shapes=scratch,
        compiler_params=params(),
    )(*operands, *after)


def partners(count):
    return [0, *range(count - 1, 0, -1)]


def row_sum(parts, after, share):
    count = len(parts)

    def kernel(*refs):
        parts, (_, message, held) = refs[:count], refs[count:]
        me = lax.axis_index("row")
        total = parts[0][0:share, :]
        for p, part in zip(partners(count), parts, strict=True):
            held[lax.bitwise_xor(me, p)] = part[share:, :].astype(F32)
            if p > 0:
                total += part[0:share, :].astype(F32)
        bias = joined(held[0])
        for n in range(1, count):
            bias += joined(held[n])
        message[0:share, :] = total.astype(BF16)
        message[share:, :] = split(bias)

    scratch = [pltpu.VMEM((count, BIAS_ROWS, LANES), F32)]
    (message,) = call(kernel, parts, [((share + BIAS_ROWS, LANES), BF16)], [after], scratch)
    return message


def column_pair_sum(own, near, after, share):
    def kernel(own, near, _, message):
        total = own[0:share, :].astype(F32) + near[0:share, :].astype(F32)
        message[0:share, :] = total.astype(BF16)
        message[share:, :] = split(joined(own[share:, :]) + joined(near[share:, :]))

    (message,) = call(kernel, [own, near], [(own.shape, BF16)], [after])
    return message


def column_sum(parts, grads, kept, near, share):
    rows = share + BIAS_ROWS
    count, sent, kept_n = len(parts), len(grads), len(kept)

    def kernel(near, *refs):
        parts, grads, refs = refs[:count], refs[count : count + sent], refs[count + sent :]
        kept, refs = refs[:kept_n], refs[kept_n:]
        messages, (piece_out, bias_out, left_own, *left_messages, held) = refs[:sent], refs[sent:]
        home = lax.div(lax.axis_index("col"), 2)
        for p, part in enumerate(parts):
            held[lax.bitwise_xor(home, p)] = part[...]
        total, bias = held[0, 0:share, :].astype(F32), joined(held[0, share:, :])
        for n in range(1, count):
            total += held[n, 0:share, :].astype(F32)
            bias += joined(held[n, share:, :])
        piece = total.astype(BF16)
        piece_out[...] = piece
        for message, grad in zip(messages, grads, strict=True):
            message[0:share, :] = piece
            message[share:, :] = grad[...]
        bias_out[...] = jnp.broadcast_to(bias, bias_out.shape)
        size = left_own.shape[0]
        for p, part in enumerate(kept):
            both = part[...] + near[p * size : (p + 1) * size, :].astype(F32)
            if p == 0:
                left_own[...] = both
            else:
                left_messages[p - 1][...] = both.astype(BF16)

    shapes = [((share + grad.shape[0], LANES), BF16) for grad in grads]
    shapes += [((share, LANES), BF16), ((8, LANES), F32), (kept[0].shape, F32)]
    shapes += [(kept[0].shape, BF16)] * (kept_n - 1)
    scratch = [pltpu.VMEM((count, rows, LANES), BF16)]
    results = call(kernel, [near, *parts, *grads, *kept], shapes, scratch=scratch)
    return results[:sent], *results[sent : sent + 3], results[sent + 3 :]


def hand_on(arrays, after):
    def kernel(*refs):
        for ref, out in zip(refs[: len(arrays)], refs[len(arrays) + 1 :], strict=True):
            out[...] = ref[...]

    return call(kernel, arrays, [(x.shape, x.dtype) for x in arrays], [after])


def finish(pieces, left, right_own, bias, left_shape, right_shape, scale, bias_scale):
    count, left_n = len(pieces), len(left)
    share = pieces[0].shape[0]

    def kernel(*refs):
        pieces, left, refs = refs[:count], refs[count : count + left_n], refs[count + left_n :]
        right_own, bias, projection, left_out, right_out, bias_out = refs
        me = lax.axis_index("row")
        right_total = right_own[...]
        for p, piece in zip(partners(count), pieces, strict=True):
            rows = pl.ds(pl.multiple_of(lax.bitwise_xor(me, p) * share, share), share)
            projection[rows, :] = piece[0:share, :].astype(F32) * scale
            if p > 0:
                right_total += piece[share:, :].astype(F32)
        left_total = left[0][...]
        for term in left[1:]:
            left_total += term[...].astype(F32)
        unfold(left_total, left_out.shape[0], left_out)
        unfold(right_total, right_out.shape[0], right_out)
        bias_out[...] = bias[0:1, :] * bias_scale

    shapes = [
        ((count * share, PAIR_FEATURES), F32),
        (left_shape, F32),
        (right_shape, F32),
        ((1, PAIR_FEATURES), F32),
    ]
    return call(kernel, [*pieces, *left, right_own, bias], shapes)


def swap(x, axis, p):
    return lax.ppermute(x, axis, [(n, n ^ p) for n in range(lax.axis_size(axis))])


def swap_each(parts, axis, step=1):
    count = len(parts)
    return [swap(parts[n - 1], axis, n * step) for n in range(count, 0, -1)][::-1]


def from_evens(x, axis):
    return swap_each([x] * (lax.axis_size(axis) // 2 - 1), axis, 2)


def local(
    first_homolog_features, second_homolog_features, final_projection_matrix, output_bias, cotangent
):
    i_n, j_n, _ = cotangent.shape
    row_n, col_n = lax.axis_size("row"), lax.axis_size("col")
    sequences = second_homolog_features.shape[0] * row_n
    channels = final_projection_matrix.shape[0]
    res_total = i_n * row_n
    a_far = from_evens(first_homolog_features, "col")
    b_far = from_evens(second_homolog_features, "row")
    we, wt, a, b, w, g = load(
        first_homolog_features,
        second_homolog_features,
        final_projection_matrix,
        cotangent.reshape(i_n * j_n, PAIR_FEATURES),
    )
    a, b = stack([a, *a_far], [b, *b_far])
    a_pieces = [a, swap(a, "col", 1)]
    b_pieces = [b, swap(b, "row", 1)]
    y, gt, bias_rows = prepare(we, g, i_n, j_n)

    x, a_held, b_wide, (own, *messages) = outer(
        a_pieces, b_pieces, g, bias_rows, i_n, j_n, sequences
    )
    share = channels // row_n

    parts = [own] + swap_each(messages, "row")[::-1]
    left_kept, (message,) = gradient(
        b_wide, y, own, "col", in_pairs(col_n), col_n // 2, 1, i_n, j_n, sequences
    )
    left_near = swap(message, "col", 1)

    message = row_sum(parts, message, share)
    near = swap(message, "col", 1)
    y2, a_wide = product(w, gt, a_held, left_near)

    message = column_pair_sum(message, near, y2, share)
    parts = [message] + from_evens(message, "col")
    (right_own,), right_sent = gradient(
        a_wide, y2, message, "row", alone(row_n), 1, row_n - 1, j_n, i_n, sequences
    )

    messages, piece, bias, left_own, left_messages = column_sum(
        parts, right_sent, left_kept, left_near, share
    )
    pieces = [piece] + swap_each(messages, "row")[::-1]
    pair_map, pair_done = pair(x, wt, output_bias, piece, sequences, 0, 1)
    left = [left_own] + swap_each(hand_on(left_messages, pair_done), "col", 2)
    pair_map, _ = pair(x, wt, output_bias, pair_done, sequences, 1, PAIR_BLOCKS, pair_map)
    projection, left_grad, right_grad, bias_grad = finish(
        pieces,
        left,
        right_own,
        bias,
        first_homolog_features.shape,
        second_homolog_features.shape,
        1.0 / (sequences * res_total),
        1.0 / res_total,
    )
    return (
        pair_map.reshape(i_n, j_n, PAIR_FEATURES),
        left_grad,
        right_grad,
        projection,
        bias_grad.reshape(PAIR_FEATURES),
    )


def solution(mesh):
    return jax.shard_map(
        local,
        mesh=mesh,
        in_specs=(
            P(("dp", "col"), "row"),
            P(("dp", "row"), "col"),
            P(),
            P(),
            P(("dp", "row"), "col", None),
        ),
        out_specs=(
            P(("dp", "row"), "col", None),
            P(("dp", "col"), "row"),
            P(("dp", "row"), "col"),
            P("dp", None),
            P("dp"),
        ),
        check_vma=False,
    )
```

```python
import functools

import jax
import jax.numpy as jnp
from jax import lax
from jax.experimental import pallas as pl
from jax.experimental.pallas import tpu as pltpu
from jax.sharding import PartitionSpec as P

PROJECTED_DEPTH = 32
PAIR_FEATURES = 128
GROUP = 8
MULTIPLY_ROWS = 384
CHUNKS = 2
BIAS_ROWS = 16
LANES = 128
F32 = jnp.float32
BF16 = jnp.bfloat16
MIB = 1024 * 1024

ROWS_BY_ROWS = (((1,), (1,)), ((), ()))
COLS_BY_COLS = (((0,), (0,)), ((), ()))


def params(sequences=0):
    return pltpu.CompilerParams(vmem_limit_bytes=min(10 + 10 * sequences // 32, 50) * MIB + 2 * MIB)


def whole(shape):
    return pl.BlockSpec(shape, lambda t: (0,) * len(shape))


def dot(x, y, dims=(((1,), (0,)), ((), ()))):
    return lax.dot_general(x, y, dims, preferred_element_type=F32)


def load_kernel(a_hbm, b_hbm, w_hbm, g_hbm, we_ref, wt_ref, a_ref, b_ref, w_ref, g_ref, w32, sems):
    depth = PROJECTED_DEPTH
    copies = [
        pltpu.make_async_copy(source, target, sems.at[n])
        for n, (source, target) in enumerate(
            [(w_hbm, w_ref), (g_hbm, g_ref), (a_hbm, a_ref), (b_hbm, b_ref)]
        )
    ]
    for copy in copies:
        copy.start()
    copies[0].wait()
    w32[...] = w_ref[...].astype(F32)
    for e in range(depth):
        block = w32[pl.ds(e, depth, stride=depth), :]
        we_ref[e * depth : (e + 1) * depth, :] = block.astype(BF16)
    turned = we_ref[...].astype(F32).T.astype(BF16)
    for n in range(wt_ref.shape[0]):
        wt_ref[n] = turned[:, n * wt_ref.shape[2] : (n + 1) * wt_ref.shape[2]]
    for copy in copies[1:]:
        copy.wait()


def in_vmem():
    return pl.BlockSpec(memory_space=pltpu.VMEM)


def load(a, b, w, g, shares):
    shapes = [
        jax.ShapeDtypeStruct(w.shape, BF16),
        jax.ShapeDtypeStruct((shares, w.shape[1], w.shape[0] // shares), BF16),
        *[jax.ShapeDtypeStruct(x.shape, BF16) for x in (a, b, w, g)],
    ]
    return pl.pallas_call(
        load_kernel,
        in_specs=[pl.BlockSpec(memory_space=pltpu.HBM)] * 4,
        out_specs=[in_vmem()] * len(shapes),
        out_shape=shapes,
        scratch_shapes=[pltpu.VMEM(w.shape, F32), pltpu.SemaphoreType.DMA((4,))],
        compiler_params=params(),
        cost_estimate=pl.CostEstimate(
            flops=1000 * w.size, bytes_accessed=16 * w.size, transcendentals=0
        ),
    )(*[pltpu.with_memory_space_constraint(x, pltpu.HBM) for x in (a, b, w, g)])


def stack(*groups):
    def kernel(*refs):
        refs, outs = refs[: -len(groups)], refs[-len(groups) :]
        for group, out in zip(groups, outs, strict=True):
            blocks = [ref[...].astype(F32) for ref in refs[: len(group)]]
            refs = refs[len(group) :]
            out[...] = jnp.concatenate(blocks, axis=0).astype(BF16)

    shapes = [((len(group) * group[0].shape[0], group[0].shape[1]), BF16) for group in groups]
    return call(kernel, [x for group in groups for x in group], shapes)


def split(total):
    high = total.astype(BF16).astype(F32)
    row = lax.broadcasted_iota(jnp.int32, (BIAS_ROWS, PAIR_FEATURES), 0)
    return jnp.where(row == 0, high, jnp.where(row == 1, total - high, 0.0)).astype(BF16)


def joined(block):
    block = block.astype(F32)
    return block[0:1] + block[1:2]


def multiply(left_ref, right_ref, out_ref):
    for n in range(0, right_ref.shape[0], MULTIPLY_ROWS):
        rows = slice(n, n + MULTIPLY_ROWS)
        out_ref[:, rows] = dot(left_ref[...], right_ref[rows, :], ROWS_BY_ROWS).astype(BF16)


def prepare_kernel(i_n, j_n, we_ref, g_ref, y_ref, gt_ref, bias_ref, g32):
    g32[...] = g_ref[...].astype(F32)
    bias_ref[...] = split(jnp.sum(g32[...], axis=0, keepdims=True))
    multiply(we_ref, g_ref, y_ref)

    for j in range(j_n):
        gt_ref[j * i_n : (j + 1) * i_n, :] = g32[pl.ds(j, i_n, stride=j_n), :].astype(BF16)


def prepare(we, g, i_n, j_n):
    pairs = i_n * j_n
    channels = we.shape[0]
    shapes = [
        jax.ShapeDtypeStruct((channels, pairs), BF16),
        jax.ShapeDtypeStruct(g.shape, BF16),
        jax.ShapeDtypeStruct((BIAS_ROWS, PAIR_FEATURES), BF16),
    ]
    return pl.pallas_call(
        functools.partial(prepare_kernel, i_n, j_n),
        in_specs=[in_vmem()] * 2,
        out_specs=[in_vmem()] * len(shapes),
        out_shape=shapes,
        scratch_shapes=[pltpu.VMEM(g.shape, F32)],
        compiler_params=params(16),
        cost_estimate=pl.CostEstimate(
            flops=2 * pairs * channels * PAIR_FEATURES,
            bytes_accessed=4 * pairs * channels,
            transcendentals=0,
        ),
    )(we, g)


def join(pieces, axis, held):
    half = lax.axis_size(axis) // 2
    depth = pieces[0].shape[0] // half
    me = lax.axis_index(axis)
    odd, home = lax.rem(me, 2), lax.div(me, 2)
    for piece, parity in zip(pieces, (odd, 1 - odd), strict=True):
        block = piece[...].astype(F32)
        for p in range(half):
            place = (2 * lax.bitwise_xor(home, p) + parity) * depth
            held[pl.ds(pl.multiple_of(place, depth), depth), :] = block[p * depth : (p + 1) * depth]


def repeat_matrix(sequences):
    shape = (sequences, GROUP * sequences)
    lane = lax.broadcasted_iota(jnp.int32, shape, 1)
    row = lax.broadcasted_iota(jnp.int32, shape, 0)
    return (lax.rem(lane, sequences) == row).astype(BF16)


def tile_count(sequences):
    return GROUP * sequences // LANES, max(1, sequences // LANES)


def spread(held, wide):
    repeated = repeat_matrix(held.shape[0])[:, : wide.shape[0] * LANES]
    both = dot(held[...].T.astype(BF16), repeated)
    for l in range(wide.shape[0]):
        wide[l] = both[:, l * LANES : (l + 1) * LANES]


def tiles_of(sequences, tile):
    lane = lax.broadcasted_iota(jnp.int32, (1, LANES), 1) + tile * LANES
    return [
        (m, lax.div(lane, sequences) == m)
        for m in range(GROUP)
        if m * sequences < (tile + 1) * LANES and (m + 1) * sequences > tile * LANES
    ]


def chunks(body):
    if CHUNKS == 1:
        body(0)
    else:
        pl.loop(0, CHUNKS)(body)


def diagonal_of(wide, channel, positions, sequences):
    columns = []
    blocks = [
        wide[l, pl.ds(channel, positions, stride=PROJECTED_DEPTH), :].astype(BF16)
        for l in range(wide.shape[0])
    ]
    for l in range(tile_count(sequences)[0]):
        block = blocks[l % len(blocks)]
        members = dict(tiles_of(sequences, l))
        columns.append(
            jnp.concatenate(
                [
                    block * members[m].astype(F32).astype(BF16)
                    if m in members
                    else jnp.zeros(block.shape, BF16)
                    for m in range(GROUP)
                ],
                axis=0,
            )
        )
    return jnp.concatenate(columns, axis=1)


def alone(count):
    return lambda me: ([me], [[lax.bitwise_xor(me, d)] for d in range(1, count)])


def in_pairs(count):
    def plan(me):
        evens = range(0, count, 2)
        return [lax.bitwise_xor(me, d) for d in evens], [
            [lax.bitwise_xor(me, d + 1) for d in evens]
        ]

    return plan


def outer_share(left, wide, g_ref, x_part, share, i_n, j_n, sequences):
    depth = PROJECTED_DEPTH
    span = GROUP * j_n
    per_share = x_part.shape[0] // depth
    for e in range(0, per_share, 2):
        right = [diagonal_of(wide, share * per_share + e + n, j_n, sequences) for n in range(2)]
        product = dot(left[...], jnp.concatenate(right, axis=0), ROWS_BY_ROWS).astype(BF16)
        for n in range(2):
            for k in range(i_n // GROUP):
                x_part[(e + n) * depth : (e + n + 1) * depth, k * span : (k + 1) * span] = product[
                    k * depth : (k + 1) * depth, n * span : (n + 1) * span
                ]
    return dot(x_part[...], g_ref[...])


def outer_shares(partner_list, left, wide, g_ref, bias_ref, x_ref, messages, i_n, j_n, sequences):
    rows = x_ref.shape[0] // len(partner_list)
    me = lax.axis_index("row")
    for n, (p, message) in enumerate(zip(partner_list, messages, strict=True)):
        part = x_ref.at[n * rows : (n + 1) * rows]
        share = lax.bitwise_xor(me, p)
        total = outer_share(left, wide, g_ref, part, share, i_n, j_n, sequences)
        message[0:rows, :] = total.astype(message.dtype)
        message[rows:, :] = bias_ref[...].astype(message.dtype)


def outer_start_kernel(i_n, j_n, *refs):
    depth = PROJECTED_DEPTH
    far = partners(lax.axis_size("row"))[1:-1]
    a_pieces, b_pieces, (g_ref, bias_ref), refs = refs[:2], refs[2:4], refs[4:6], refs[6:]
    (x_ref, a_held, b_wide, left), messages, b_held = refs[:4], refs[4:-1], refs[-1]
    sequences = a_held.shape[0]
    join(a_pieces, "col", a_held)
    join(b_pieces, "row", b_held)
    spread(b_held, b_wide)
    turned = a_held[...].T.astype(BF16)
    shape = (sequences, GROUP * sequences)
    shifted = lax.broadcasted_iota(jnp.int32, shape, 1) - lax.broadcasted_iota(jnp.int32, shape, 0)
    value = jnp.zeros(left.shape, F32)
    for m in range(GROUP):
        rows = [
            turned[(k * GROUP + m) * depth : (k * GROUP + m + 1) * depth, :]
            for k in range(i_n // GROUP)
        ]
        value += dot(jnp.concatenate(rows, axis=0), (shifted == m * sequences).astype(BF16))
    left[...] = value.astype(BF16)
    outer_shares(far, left, b_wide, g_ref, bias_ref, x_ref, messages, i_n, j_n, sequences)


def outer_end_kernel(i_n, j_n, sequences, left, b_wide, g_ref, bias_ref, x_ref, *messages):
    outer_shares((1, 0), left, b_wide, g_ref, bias_ref, x_ref, messages, i_n, j_n, sequences)


def outer_call(kernel, operands, shapes, scratch, rows, pairs, sequences):
    return pl.pallas_call(
        kernel,
        in_specs=[in_vmem()] * len(operands),
        out_specs=[in_vmem()] * len(shapes),
        out_shape=[jax.ShapeDtypeStruct(shape, kind) for shape, kind in shapes],
        scratch_shapes=scratch,
        compiler_params=params(sequences),
        cost_estimate=pl.CostEstimate(
            flops=4 * pairs * rows * PAIR_FEATURES,
            bytes_accessed=2 * pairs * rows,
            transcendentals=0,
        ),
    )(*operands)


def outer_start(a_pieces, b_pieces, g, bias_rows, i_n, j_n, sequences):
    row_n = lax.axis_size("row")
    depth = PROJECTED_DEPTH
    share = depth * depth // row_n
    rows = share * (row_n - 2)
    shapes = [
        ((rows, i_n * j_n), BF16),
        ((sequences, i_n * depth), F32),
        ((tile_count(sequences)[1], j_n * depth, LANES), F32),
        ((i_n // GROUP * depth, GROUP * sequences), BF16),
    ]
    shapes += [((share + BIAS_ROWS, LANES), BF16)] * (row_n - 2)
    results = outer_call(
        functools.partial(outer_start_kernel, i_n, j_n),
        [*a_pieces, *b_pieces, g, bias_rows],
        shapes,
        [pltpu.VMEM((sequences, j_n * depth), F32)],
        rows,
        i_n * j_n,
        sequences,
    )
    return *results[:4], results[4:]


def outer_end(left, b_wide, g, bias_rows, i_n, j_n, sequences):
    share = PROJECTED_DEPTH * PROJECTED_DEPTH // lax.axis_size("row")
    shapes = [((2 * share, i_n * j_n), BF16)]
    shapes += [((share + BIAS_ROWS, LANES), kind) for kind in (BF16, F32)]
    return outer_call(
        functools.partial(outer_end_kernel, i_n, j_n, sequences),
        [left, b_wide, g, bias_rows],
        shapes,
        [],
        2 * share,
        i_n * j_n,
        sequences,
    )


def gradient_kernel(axis, plan, kept, positions, others, sequences, *refs):
    depth = PROJECTED_DEPTH
    wide, source = refs[:2]
    outs, (result, grown, grad) = refs[3:-3], refs[-3:]
    parts = lax.axis_size(axis)
    per_step = depth // CHUNKS
    span = GROUP * others

    result[...] = jnp.zeros(result.shape, F32)

    @chunks
    def _(t):
        size = per_step * depth
        rows = pl.ds(t * size if CHUNKS == 1 else pl.multiple_of(t * size, size), size)
        part = source.at[rows]
        for n in range(0, per_step, 2):
            blocks = [
                jnp.concatenate(
                    [
                        part[m * depth : (m + 1) * depth, k * span : (k + 1) * span]
                        for m in (n, n + 1)
                    ],
                    axis=1,
                )
                for k in range(positions // GROUP)
            ]
            right = [
                diagonal_of(wide, t * per_step + m, others, sequences) for m in (n, n + 1)
            ]
            result[...] += dot(jnp.concatenate(blocks, axis=0), jnp.concatenate(right, axis=0))

    scaled = (result[...] * (1.0 / sequences)).astype(BF16)
    for l in range(scaled.shape[1] // LANES):
        members = dict(tiles_of(sequences, l))
        for k in range(positions // GROUP):
            block = scaled[k * depth : (k + 1) * depth, l * LANES : (l + 1) * LANES]
            for m in range(GROUP):
                start = (k * GROUP + m) * depth
                grown[start : start + depth, l * LANES : (l + 1) * LANES] = (
                    block * members[m].astype(F32).astype(BF16)
                    if m in members
                    else jnp.zeros((depth, LANES), BF16)
                )
    grad[...] = dot(repeat_matrix(sequences), grown[...], ROWS_BY_ROWS)
    share = sequences // parts

    def rows_of(p):
        mine = grad[pl.ds(pl.multiple_of(p * share, share), share), :]
        return jnp.concatenate(
            [mine[:, l * LANES : (l + 1) * LANES] for l in range(mine.shape[1] // LANES)], axis=0
        )

    stay, go = plan(lax.axis_index(axis))
    for p, out in zip(stay, outs[:kept], strict=True):
        out[...] = rows_of(p)
    for group, out in zip(go, outs[kept:], strict=True):
        size = out.shape[0] // len(group)
        for n, p in enumerate(group):
            out[n * size : (n + 1) * size, :] = rows_of(p).astype(BF16)


def gradient(wide, source, after, axis, plan, kept, groups, positions, others, sequences):
    depth = PROJECTED_DEPTH
    parts = lax.axis_size(axis)
    rows = sequences // parts * positions * depth // LANES
    shapes = [jax.ShapeDtypeStruct((rows, LANES), F32)] * kept
    group = (parts - kept) // groups
    shapes += [jax.ShapeDtypeStruct((group * rows, LANES), BF16)] * groups
    results = pl.pallas_call(
        functools.partial(gradient_kernel, axis, plan, kept, positions, others, sequences),
        in_specs=[in_vmem(), in_vmem(), pl.BlockSpec(memory_space=pl.ANY)],
        out_specs=[in_vmem()] * len(shapes),
        out_shape=shapes,
        scratch_shapes=[
            pltpu.VMEM((positions // GROUP * depth, GROUP * sequences), F32),
            pltpu.VMEM((positions * depth, GROUP * sequences), BF16),
            pltpu.VMEM((sequences, positions * depth), F32),
        ],
        compiler_params=params(sequences),
        cost_estimate=pl.CostEstimate(
            flops=2 * source.size * PAIR_FEATURES,
            bytes_accessed=2 * source.size,
            transcendentals=0,
        ),
    )(wide, source, after)
    return results[:kept], results[kept:]


def product_kernel(left_ref, right_ref, held, *refs):
    out_ref, wide = refs[-2:]
    spread(held, wide)
    multiply(left_ref, right_ref, out_ref)


def product(left, right, held, after):
    shape = (left.shape[0], right.shape[0])
    spread_shape = (tile_count(held.shape[0])[1], held.shape[1], LANES)
    return pl.pallas_call(
        product_kernel,
        in_specs=[in_vmem()] * 3 + [pl.BlockSpec(memory_space=pl.ANY)] * len(after),
        out_specs=[in_vmem()] * 2,
        out_shape=[jax.ShapeDtypeStruct(shape, BF16), jax.ShapeDtypeStruct(spread_shape, F32)],
        compiler_params=params(32),
        cost_estimate=pl.CostEstimate(
            flops=2 * shape[0] * shape[1] * left.shape[1],
            bytes_accessed=4 * shape[0] * shape[1],
            transcendentals=0,
        ),
    )(left, right, held, *after)


def pair_kernel(sequences, far_ref, near_ref, wt_ref, bias_ref, _, out_ref):
    me = lax.axis_index("row")
    count = wt_ref.shape[0]
    product = None
    for x_ref, ps in ((far_ref, partners(count)[1:-1]), (near_ref, (1, 0))):
        weights = [wt_ref[lax.bitwise_xor(me, p)] for p in ps]
        term = dot(jnp.concatenate(weights, axis=1), x_ref[...])
        product = term if product is None else product + term
    out_ref[...] = (product.T * (1.0 / sequences) + bias_ref[...]).astype(BF16)


def pair(x_far, x_near, wt, output_bias, after, sequences):
    pairs = x_far.shape[1]
    count = 3
    size = pairs // count
    return pl.pallas_call(
        functools.partial(pair_kernel, sequences),
        grid=(count,),
        in_specs=[
            pl.BlockSpec((x_far.shape[0], size), lambda t: (0, t)),
            pl.BlockSpec((x_near.shape[0], size), lambda t: (0, t)),
            whole(wt.shape),
            whole((1, PAIR_FEATURES)),
            pl.BlockSpec(memory_space=pl.ANY),
        ],
        out_specs=pl.BlockSpec((size, PAIR_FEATURES), lambda t: (t, 0)),
        out_shape=jax.ShapeDtypeStruct((pairs, PAIR_FEATURES), BF16),
        compiler_params=params(),
        cost_estimate=pl.CostEstimate(
            flops=4 * pairs * wt.size, bytes_accessed=16 * pairs * wt.shape[2], transcendentals=0
        ),
    )(x_far, x_near, wt, output_bias.reshape(1, PAIR_FEATURES), after)


def unfold(total, share, out):
    for l in range(out.shape[1] // LANES):
        out[:, l * LANES : (l + 1) * LANES] = total[l * share : (l + 1) * share, :]


def call(kernel, operands, shapes, after=(), scratch=()):
    specs = [in_vmem()] * len(operands) + [pl.BlockSpec(memory_space=pl.ANY)] * len(after)
    return pl.pallas_call(
        kernel,
        in_specs=specs,
        out_specs=[in_vmem()] * len(shapes),
        out_shape=[jax.ShapeDtypeStruct(shape, kind) for shape, kind in shapes],
        scratch_shapes=scratch,
        compiler_params=params(),
    )(*operands, *after)


def partners(count):
    return [0, *range(count - 1, 0, -1)]


def row_sum(parts, after, share):
    count = len(parts)

    def kernel(*refs):
        parts, (_, message, held) = refs[:count], refs[count:]
        me = lax.axis_index("row")
        total = parts[0][0:share, :]
        for p, part in zip(partners(count), parts, strict=True):
            held[lax.bitwise_xor(me, p)] = part[share:, :].astype(F32)
            if p > 0:
                total += part[0:share, :].astype(F32)
        bias = joined(held[0])
        for n in range(1, count):
            bias += joined(held[n])
        message[0:share, :] = total.astype(BF16)
        message[share:, :] = split(bias)

    scratch = [pltpu.VMEM((count, BIAS_ROWS, LANES), F32)]
    (message,) = call(kernel, parts, [((share + BIAS_ROWS, LANES), BF16)], [after], scratch)
    return message


def pair_sum(kept, near, after):
    def kernel(*refs):
        kept, near, (own, *messages) = refs[:count], refs[count], refs[count + 2 :]
        size = own.shape[0]
        for p, part in enumerate(kept):
            both = part[...] + near[p * size : (p + 1) * size, :].astype(F32)
            if p == 0:
                own[...] = both
            else:
                messages[p - 1][...] = both.astype(BF16)

    count = len(kept)
    shapes = [(kept[0].shape, F32)] + [(kept[0].shape, BF16)] * (count - 1)
    own, *messages = call(kernel, [*kept, near], shapes, [after])
    return own, messages


def column_pair_sum(own, near, after, share):
    def kernel(own, near, _, message):
        total = own[0:share, :].astype(F32) + near[0:share, :].astype(F32)
        message[0:share, :] = total.astype(BF16)
        message[share:, :] = split(joined(own[share:, :]) + joined(near[share:, :]))

    (message,) = call(kernel, [own, near], [(own.shape, BF16)], [after])
    return message


def column_sum(parts, grads, after, share):
    rows = share + BIAS_ROWS
    count, sent = len(parts), len(grads)

    def kernel(*refs):
        parts, grads, refs = refs[:count], refs[count : count + sent], refs[count + sent + 1 :]
        messages, (piece_out, bias_out, held) = refs[:sent], refs[sent:]
        home = lax.div(lax.axis_index("col"), 2)
        for p, part in enumerate(parts):
            held[lax.bitwise_xor(home, p)] = part[...]
        total, bias = held[0, 0:share, :].astype(F32), joined(held[0, share:, :])
        for n in range(1, count):
            total += held[n, 0:share, :].astype(F32)
            bias += joined(held[n, share:, :])
        piece = total.astype(BF16)
        piece_out[...] = piece
        for message, grad in zip(messages, grads, strict=True):
            message[0:share, :] = piece
            message[share:, :] = grad[...]
        bias_out[...] = jnp.broadcast_to(bias, bias_out.shape)

    shapes = [((share + grad.shape[0], LANES), BF16) for grad in grads]
    shapes += [((share, LANES), BF16), ((8, LANES), F32)]
    scratch = [pltpu.VMEM((count, rows, LANES), BF16)]
    *messages, piece, bias = call(kernel, [*parts, *grads], shapes, [after], scratch)
    return messages, piece, bias


def finish(pieces, left, right_own, bias, left_shape, right_shape, scale, bias_scale):
    count, left_n = len(pieces), len(left)
    share = pieces[0].shape[0]

    def kernel(*refs):
        pieces, left, refs = refs[:count], refs[count : count + left_n], refs[count + left_n :]
        right_own, bias, projection, left_out, right_out, bias_out, ordered = refs
        me = lax.axis_index("row")
        right_total = right_own[...]
        for p, piece in zip(partners(count), pieces, strict=True):
            rows = pl.ds(pl.multiple_of(lax.bitwise_xor(me, p) * share, share), share)
            ordered[rows, :] = piece[0:share, :].astype(F32) * scale
            if p > 0:
                right_total += piece[share:, :].astype(F32)
        depth = PROJECTED_DEPTH
        for c in range(depth):
            block = ordered[pl.ds(c, depth, stride=depth), :]
            projection[c * depth : (c + 1) * depth, :] = block
        left_total = left[0][...]
        for term in left[1:]:
            left_total += term[...].astype(F32)
        unfold(left_total, left_out.shape[0], left_out)
        unfold(right_total, right_out.shape[0], right_out)
        bias_out[...] = bias[0:1, :] * bias_scale

    shapes = [
        ((count * share, PAIR_FEATURES), F32),
        (left_shape, F32),
        (right_shape, F32),
        ((1, PAIR_FEATURES), F32),
    ]
    scratch = [pltpu.VMEM(shapes[0][0], F32)]
    return call(kernel, [*pieces, *left, right_own, bias], shapes, scratch=scratch)


def swap(x, axis, p):
    return lax.ppermute(x, axis, [(n, n ^ p) for n in range(lax.axis_size(axis))])


def swap_each(parts, axis, step=1):
    count = len(parts)
    return [swap(parts[n - 1], axis, n * step) for n in range(count, 0, -1)][::-1]


def from_evens(x, axis):
    return swap_each([x] * (lax.axis_size(axis) // 2 - 1), axis, 2)


def local(
    first_homolog_features, second_homolog_features, final_projection_matrix, output_bias, cotangent
):
    i_n, j_n, _ = cotangent.shape
    row_n, col_n = lax.axis_size("row"), lax.axis_size("col")
    sequences = second_homolog_features.shape[0] * row_n
    channels = final_projection_matrix.shape[0]
    res_total = i_n * row_n
    a_far = from_evens(first_homolog_features, "col")
    b_far = from_evens(second_homolog_features, "row")
    we, wt, a, b, w, g = load(
        first_homolog_features,
        second_homolog_features,
        final_projection_matrix,
        cotangent.reshape(i_n * j_n, PAIR_FEATURES),
        row_n,
    )
    a, b = stack([a, *a_far], [b, *b_far])
    a_pieces = [a, swap(a, "col", 1)]
    b_pieces = [b, swap(b, "row", 1)]
    y, gt, bias_rows = prepare(we, g, i_n, j_n)

    x_far, a_held, b_wide, left_operand, messages = outer_start(
        a_pieces, b_pieces, g, bias_rows, i_n, j_n, sequences
    )
    share = channels // row_n
    parts = [
        swap(message, "row", p)
        for message, p in zip(messages, partners(row_n)[1:-1], strict=True)
    ]
    x_near, message, own = outer_end(left_operand, b_wide, g, bias_rows, i_n, j_n, sequences)
    parts = [own, *parts, swap(message, "row", 1)]
    y2, a_wide = product(w, gt, a_held, parts[1:-1])

    message = row_sum(parts, y2, share)
    near = swap(message, "col", 1)
    left_kept, (left_sent,) = gradient(
        b_wide, y, message, "col", in_pairs(col_n), col_n // 2, 1, i_n, j_n, sequences
    )
    left_near = swap(left_sent, "col", 1)

    message = column_pair_sum(message, near, left_sent, share)
    parts = [message] + from_evens(message, "col")
    (right_own,), right_sent = gradient(
        a_wide, y2, message, "row", alone(row_n), 1, row_n - 1, j_n, i_n, sequences
    )
    left_own, left_messages = pair_sum(left_kept, left_near, right_own)
    left = [left_own] + swap_each(left_messages, "col", 2)

    messages, piece, bias = column_sum(parts, right_sent, left_own, share)
    pieces = [piece] + swap_each(messages, "row")[::-1]
    pair_map = pair(x_far, x_near, wt, output_bias, piece, sequences)
    projection, left_grad, right_grad, bias_grad = finish(
        pieces,
        left,
        right_own,
        bias,
        first_homolog_features.shape,
        second_homolog_features.shape,
        1.0 / (sequences * res_total),
        1.0 / res_total,
    )
    return (
        pair_map.reshape(i_n, j_n, PAIR_FEATURES),
        left_grad,
        right_grad,
        projection,
        bias_grad.reshape(PAIR_FEATURES),
    )


def solution(mesh):
    return jax.shard_map(
        local,
        mesh=mesh,
        in_specs=(
            P(("dp", "col"), "row"),
            P(("dp", "row"), "col"),
            P(),
            P(),
            P(("dp", "row"), "col", None),
        ),
        out_specs=(
            P(("dp", "row"), "col", None),
            P(("dp", "col"), "row"),
            P(("dp", "row"), "col"),
            P("dp", None),
            P("dp"),
        ),
        check_vma=False,
    )
```

```python
import functools

import jax
import jax.numpy as jnp
from jax import lax
from jax.experimental import pallas as pl
from jax.experimental.pallas import tpu as pltpu
from jax.sharding import PartitionSpec as P

PROJECTED_DEPTH = 32
PAIR_FEATURES = 128
GROUP = 8
MULTIPLY_ROWS = 384
CHUNKS = 2
BIAS_ROWS = 16
LANES = 128
F32 = jnp.float32
BF16 = jnp.bfloat16
MIB = 1024 * 1024

ROWS_BY_ROWS = (((1,), (1,)), ((), ()))
COLS_BY_COLS = (((0,), (0,)), ((), ()))


def params(sequences=0):
    return pltpu.CompilerParams(vmem_limit_bytes=min(10 + 10 * sequences // 32, 50) * MIB + 2 * MIB)


def whole(shape):
    return pl.BlockSpec(shape, lambda t: (0,) * len(shape))


def dot(x, y, dims=(((1,), (0,)), ((), ()))):
    return lax.dot_general(x, y, dims, preferred_element_type=F32)


def load_kernel(a_hbm, b_hbm, w_hbm, g_hbm, we_ref, wt_ref, a_ref, b_ref, w_ref, g_ref, w32, sems):
    depth = PROJECTED_DEPTH
    copies = [
        pltpu.make_async_copy(source, target, sems.at[n])
        for n, (source, target) in enumerate(
            [(w_hbm, w_ref), (g_hbm, g_ref), (a_hbm, a_ref), (b_hbm, b_ref)]
        )
    ]
    for copy in copies:
        copy.start()
    copies[0].wait()
    w32[...] = w_ref[...].astype(F32)
    for e in range(depth):
        block = w32[pl.ds(e, depth, stride=depth), :]
        we_ref[e * depth : (e + 1) * depth, :] = block.astype(BF16)
    wt_ref[...] = we_ref[...].astype(F32).T.astype(BF16)
    for copy in copies[1:]:
        copy.wait()


def in_vmem():
    return pl.BlockSpec(memory_space=pltpu.VMEM)


def load(a, b, w, g):
    shapes = [
        jax.ShapeDtypeStruct(w.shape, BF16),
        jax.ShapeDtypeStruct(w.shape[::-1], BF16),
        *[jax.ShapeDtypeStruct(x.shape, BF16) for x in (a, b, w, g)],
    ]
    return pl.pallas_call(
        load_kernel,
        in_specs=[pl.BlockSpec(memory_space=pltpu.HBM)] * 4,
        out_specs=[in_vmem()] * len(shapes),
        out_shape=shapes,
        scratch_shapes=[pltpu.VMEM(w.shape, F32), pltpu.SemaphoreType.DMA((4,))],
        compiler_params=params(),
        cost_estimate=pl.CostEstimate(
            flops=1000 * w.size, bytes_accessed=16 * w.size, transcendentals=0
        ),
    )(*[pltpu.with_memory_space_constraint(x, pltpu.HBM) for x in (a, b, w, g)])


def stack(*groups):
    def kernel(*refs):
        refs, outs = refs[: -len(groups)], refs[-len(groups) :]
        for group, out in zip(groups, outs, strict=True):
            blocks = [ref[...].astype(F32) for ref in refs[: len(group)]]
            refs = refs[len(group) :]
            out[...] = jnp.concatenate(blocks, axis=0).astype(BF16)

    shapes = [((len(group) * group[0].shape[0], group[0].shape[1]), BF16) for group in groups]
    return call(kernel, [x for group in groups for x in group], shapes)


def split(total):
    high = total.astype(BF16).astype(F32)
    row = lax.broadcasted_iota(jnp.int32, (BIAS_ROWS, PAIR_FEATURES), 0)
    return jnp.where(row == 0, high, jnp.where(row == 1, total - high, 0.0)).astype(BF16)


def joined(block):
    block = block.astype(F32)
    return block[0:1] + block[1:2]


def multiply(left_ref, right_ref, out_ref):
    for n in range(0, right_ref.shape[0], MULTIPLY_ROWS):
        rows = slice(n, n + MULTIPLY_ROWS)
        out_ref[:, rows] = dot(left_ref[...], right_ref[rows, :], ROWS_BY_ROWS).astype(BF16)


def prepare_kernel(i_n, j_n, we_ref, g_ref, y_ref, gt_ref, bias_ref, g32):
    g32[...] = g_ref[...].astype(F32)
    bias_ref[...] = split(jnp.sum(g32[...], axis=0, keepdims=True))
    multiply(we_ref, g_ref, y_ref)

    for j in range(j_n):
        gt_ref[j * i_n : (j + 1) * i_n, :] = g32[pl.ds(j, i_n, stride=j_n), :].astype(BF16)


def prepare(we, g, i_n, j_n):
    pairs = i_n * j_n
    channels = we.shape[0]
    shapes = [
        jax.ShapeDtypeStruct((channels, pairs), BF16),
        jax.ShapeDtypeStruct(g.shape, BF16),
        jax.ShapeDtypeStruct((BIAS_ROWS, PAIR_FEATURES), BF16),
    ]
    return pl.pallas_call(
        functools.partial(prepare_kernel, i_n, j_n),
        in_specs=[in_vmem()] * 2,
        out_specs=[in_vmem()] * len(shapes),
        out_shape=shapes,
        scratch_shapes=[pltpu.VMEM(g.shape, F32)],
        compiler_params=params(16),
        cost_estimate=pl.CostEstimate(
            flops=2 * pairs * channels * PAIR_FEATURES,
            bytes_accessed=4 * pairs * channels,
            transcendentals=0,
        ),
    )(we, g)


def join(pieces, axis, held):
    half = lax.axis_size(axis) // 2
    depth = pieces[0].shape[0] // half
    me = lax.axis_index(axis)
    odd, home = lax.rem(me, 2), lax.div(me, 2)
    for piece, parity in zip(pieces, (odd, 1 - odd), strict=True):
        block = piece[...].astype(F32)
        for p in range(half):
            place = (2 * lax.bitwise_xor(home, p) + parity) * depth
            held[pl.ds(pl.multiple_of(place, depth), depth), :] = block[p * depth : (p + 1) * depth]


def repeat_matrix(sequences):
    shape = (sequences, GROUP * sequences)
    lane = lax.broadcasted_iota(jnp.int32, shape, 1)
    row = lax.broadcasted_iota(jnp.int32, shape, 0)
    return (lax.rem(lane, sequences) == row).astype(BF16)


def tile_count(sequences):
    return GROUP * sequences // LANES, max(1, sequences // LANES)


def spread(held, wide):
    repeated = repeat_matrix(held.shape[0])[:, : wide.shape[0] * LANES]
    both = dot(held[...].T.astype(BF16), repeated)
    for l in range(wide.shape[0]):
        wide[l] = both[:, l * LANES : (l + 1) * LANES]


def tiles_of(sequences, tile):
    lane = lax.broadcasted_iota(jnp.int32, (1, LANES), 1) + tile * LANES
    return [
        (m, lax.div(lane, sequences) == m)
        for m in range(GROUP)
        if m * sequences < (tile + 1) * LANES and (m + 1) * sequences > tile * LANES
    ]


def chunks(body):
    if CHUNKS == 1:
        body(0)
    else:
        pl.loop(0, CHUNKS)(body)


def diagonal_of(wide, channel, positions, sequences):
    columns = []
    blocks = [
        wide[l, pl.ds(channel, positions, stride=PROJECTED_DEPTH), :].astype(BF16)
        for l in range(wide.shape[0])
    ]
    for l in range(tile_count(sequences)[0]):
        block = blocks[l % len(blocks)]
        members = dict(tiles_of(sequences, l))
        columns.append(
            jnp.concatenate(
                [
                    block * members[m].astype(F32).astype(BF16)
                    if m in members
                    else jnp.zeros(block.shape, BF16)
                    for m in range(GROUP)
                ],
                axis=0,
            )
        )
    return jnp.concatenate(columns, axis=1)


def alone(count):
    return lambda me: ([me], [[lax.bitwise_xor(me, d)] for d in range(1, count)])


def in_pairs(count):
    def plan(me):
        evens = range(0, count, 2)
        return [lax.bitwise_xor(me, d) for d in evens], [
            [lax.bitwise_xor(me, d + 1) for d in evens]
        ]

    return plan


def outer_kernel(i_n, j_n, *refs):
    depth = PROJECTED_DEPTH
    row_n = lax.axis_size("row")
    a_pieces, b_pieces, refs = refs[:2], refs[2:4], refs[4:]
    g_ref, bias_ref, x_ref, a_held, b_wide = refs[:5]
    messages, (b_held, left, total) = refs[5 : 5 + row_n], refs[5 + row_n :]
    sequences = a_held.shape[0]
    groups = i_n // GROUP
    per_step = depth // CHUNKS
    span = GROUP * j_n

    join(a_pieces, "col", a_held)
    join(b_pieces, "row", b_held)
    spread(b_held, b_wide)
    turned = a_held[...].T.astype(BF16)
    shape = (sequences, GROUP * sequences)
    shifted = lax.broadcasted_iota(jnp.int32, shape, 1) - lax.broadcasted_iota(jnp.int32, shape, 0)
    value = jnp.zeros(left.shape, F32)
    for m in range(GROUP):
        rows = [
            turned[(k * GROUP + m) * depth : (k * GROUP + m + 1) * depth, :] for k in range(groups)
        ]
        value += dot(jnp.concatenate(rows, axis=0), (shifted == m * sequences).astype(BF16))
    left[...] = value.astype(BF16)

    @chunks
    def _(t):
        size = per_step * depth
        rows = pl.ds(t * size if CHUNKS == 1 else pl.multiple_of(t * size, size), size)
        x_part = x_ref.at[rows]
        for e in range(0, per_step, 2):
            right = [diagonal_of(b_wide, t * per_step + e + n, j_n, sequences) for n in range(2)]
            product = dot(
                left[...], jnp.concatenate(right, axis=0), ROWS_BY_ROWS
            ).astype(BF16)
            for n in range(2):
                for k in range(groups):
                    x_part[(e + n) * depth : (e + n + 1) * depth, k * span : (k + 1) * span] = product[
                        k * depth : (k + 1) * depth, n * span : (n + 1) * span
                    ]
        total[rows, :] = dot(x_part[...], g_ref[...])

    share = total.shape[0] // row_n
    me = lax.axis_index("row")
    for p, message in enumerate(messages):
        part = pl.ds(pl.multiple_of(lax.bitwise_xor(me, p) * share, share), share)
        message[0:share, :] = total[part, :].astype(message.dtype)
        message[share:, :] = bias_ref[...].astype(message.dtype)


def outer(a_pieces, b_pieces, g, bias_rows, i_n, j_n, sequences):
    row_n = lax.axis_size("row")
    depth = PROJECTED_DEPTH
    channels = depth * depth
    pairs = i_n * j_n
    tiles = tile_count(sequences)[1]
    operands = [*a_pieces, *b_pieces, g, bias_rows]
    shapes = [jax.ShapeDtypeStruct((channels, pairs), BF16)]
    shapes += [
        jax.ShapeDtypeStruct((sequences, i_n * depth), F32),
        jax.ShapeDtypeStruct((tiles, j_n * depth, LANES), F32),
    ]
    shapes += [
        jax.ShapeDtypeStruct((channels // row_n + BIAS_ROWS, LANES), BF16 if p else F32)
        for p in range(row_n)
    ]
    results = pl.pallas_call(
        functools.partial(outer_kernel, i_n, j_n),
        in_specs=[in_vmem()] * len(operands),
        out_specs=[in_vmem()] * len(shapes),
        out_shape=shapes,
        scratch_shapes=[
            pltpu.VMEM((sequences, j_n * depth), F32),
            pltpu.VMEM((i_n // GROUP * depth, GROUP * sequences), BF16),
            pltpu.VMEM((channels, PAIR_FEATURES), F32),
        ],
        compiler_params=params(sequences),
        cost_estimate=pl.CostEstimate(
            flops=4 * pairs * channels * PAIR_FEATURES,
            bytes_accessed=2 * pairs * channels,
            transcendentals=0,
        ),
    )(*operands)
    return *results[:3], results[3:]


def gradient_kernel(axis, plan, kept, positions, others, sequences, *refs):
    depth = PROJECTED_DEPTH
    wide, source = refs[:2]
    outs, (result, grown, grad) = refs[3:-3], refs[-3:]
    parts = lax.axis_size(axis)
    per_step = depth // CHUNKS
    span = GROUP * others

    result[...] = jnp.zeros(result.shape, F32)

    @chunks
    def _(t):
        size = per_step * depth
        rows = pl.ds(t * size if CHUNKS == 1 else pl.multiple_of(t * size, size), size)
        part = source.at[rows]
        for n in range(0, per_step, 2):
            blocks = [
                jnp.concatenate(
                    [
                        part[m * depth : (m + 1) * depth, k * span : (k + 1) * span]
                        for m in (n, n + 1)
                    ],
                    axis=1,
                )
                for k in range(positions // GROUP)
            ]
            right = [
                diagonal_of(wide, t * per_step + m, others, sequences) for m in (n, n + 1)
            ]
            result[...] += dot(jnp.concatenate(blocks, axis=0), jnp.concatenate(right, axis=0))

    scaled = (result[...] * (1.0 / sequences)).astype(BF16)
    for l in range(scaled.shape[1] // LANES):
        members = dict(tiles_of(sequences, l))
        for k in range(positions // GROUP):
            block = scaled[k * depth : (k + 1) * depth, l * LANES : (l + 1) * LANES]
            for m in range(GROUP):
                start = (k * GROUP + m) * depth
                grown[start : start + depth, l * LANES : (l + 1) * LANES] = (
                    block * members[m].astype(F32).astype(BF16)
                    if m in members
                    else jnp.zeros((depth, LANES), BF16)
                )
    grad[...] = dot(repeat_matrix(sequences), grown[...], ROWS_BY_ROWS)
    share = sequences // parts

    def rows_of(p):
        mine = grad[pl.ds(pl.multiple_of(p * share, share), share), :]
        return jnp.concatenate(
            [mine[:, l * LANES : (l + 1) * LANES] for l in range(mine.shape[1] // LANES)], axis=0
        )

    stay, go = plan(lax.axis_index(axis))
    for p, out in zip(stay, outs[:kept], strict=True):
        out[...] = rows_of(p)
    for group, out in zip(go, outs[kept:], strict=True):
        size = out.shape[0] // len(group)
        for n, p in enumerate(group):
            out[n * size : (n + 1) * size, :] = rows_of(p).astype(BF16)


def gradient(wide, source, after, axis, plan, kept, groups, positions, others, sequences):
    depth = PROJECTED_DEPTH
    parts = lax.axis_size(axis)
    rows = sequences // parts * positions * depth // LANES
    shapes = [jax.ShapeDtypeStruct((rows, LANES), F32)] * kept
    group = (parts - kept) // groups
    shapes += [jax.ShapeDtypeStruct((group * rows, LANES), BF16)] * groups
    results = pl.pallas_call(
        functools.partial(gradient_kernel, axis, plan, kept, positions, others, sequences),
        in_specs=[in_vmem(), in_vmem(), pl.BlockSpec(memory_space=pl.ANY)],
        out_specs=[in_vmem()] * len(shapes),
        out_shape=shapes,
        scratch_shapes=[
            pltpu.VMEM((positions // GROUP * depth, GROUP * sequences), F32),
            pltpu.VMEM((positions * depth, GROUP * sequences), BF16),
            pltpu.VMEM((sequences, positions * depth), F32),
        ],
        compiler_params=params(sequences),
        cost_estimate=pl.CostEstimate(
            flops=2 * source.size * PAIR_FEATURES,
            bytes_accessed=2 * source.size,
            transcendentals=0,
        ),
    )(wide, source, after)
    return results[:kept], results[kept:]


def product_kernel(left_ref, right_ref, held, _, out_ref, wide):
    spread(held, wide)
    multiply(left_ref, right_ref, out_ref)


def product(left, right, held, after):
    shape = (left.shape[0], right.shape[0])
    spread_shape = (tile_count(held.shape[0])[1], held.shape[1], LANES)
    return pl.pallas_call(
        product_kernel,
        in_specs=[in_vmem()] * 3 + [pl.BlockSpec(memory_space=pl.ANY)],
        out_specs=[in_vmem()] * 2,
        out_shape=[jax.ShapeDtypeStruct(shape, BF16), jax.ShapeDtypeStruct(spread_shape, F32)],
        compiler_params=params(32),
        cost_estimate=pl.CostEstimate(
            flops=2 * shape[0] * shape[1] * left.shape[1],
            bytes_accessed=4 * shape[0] * shape[1],
            transcendentals=0,
        ),
    )(left, right, held, after)


def pair_kernel(sequences, x_ref, wt_ref, bias_ref, _, out_ref):
    product = dot(wt_ref[...], x_ref[...])
    out_ref[...] = (product.T * (1.0 / sequences) + bias_ref[...]).astype(BF16)


def pair(x, wt, output_bias, after, sequences):
    channels, pairs = x.shape
    count = 3
    size = pairs // count
    return pl.pallas_call(
        functools.partial(pair_kernel, sequences),
        grid=(count,),
        in_specs=[
            pl.BlockSpec((channels, size), lambda t: (0, t)),
            whole(wt.shape),
            whole((1, PAIR_FEATURES)),
            pl.BlockSpec(memory_space=pl.ANY),
        ],
        out_specs=pl.BlockSpec((size, PAIR_FEATURES), lambda t: (t, 0)),
        out_shape=jax.ShapeDtypeStruct((pairs, PAIR_FEATURES), BF16),
        compiler_params=params(),
        cost_estimate=pl.CostEstimate(
            flops=4 * pairs * channels * PAIR_FEATURES,
            bytes_accessed=2 * pairs * channels,
            transcendentals=0,
        ),
    )(x, wt, output_bias.reshape(1, PAIR_FEATURES), after)


def unfold(total, share, out):
    for l in range(out.shape[1] // LANES):
        out[:, l * LANES : (l + 1) * LANES] = total[l * share : (l + 1) * share, :]


def call(kernel, operands, shapes, after=(), scratch=()):
    specs = [in_vmem()] * len(operands) + [pl.BlockSpec(memory_space=pl.ANY)] * len(after)
    return pl.pallas_call(
        kernel,
        in_specs=specs,
        out_specs=[in_vmem()] * len(shapes),
        out_shape=[jax.ShapeDtypeStruct(shape, kind) for shape, kind in shapes],
        scratch_shapes=scratch,
        compiler_params=params(),
    )(*operands, *after)


def partners(count):
    return [0, *range(count - 1, 0, -1)]


def row_sum(parts, after, share):
    count = len(parts)

    def kernel(*refs):
        parts, (_, message, held) = refs[:count], refs[count:]
        me = lax.axis_index("row")
        total = parts[0][0:share, :]
        for p, part in zip(partners(count), parts, strict=True):
            held[lax.bitwise_xor(me, p)] = part[share:, :].astype(F32)
            if p > 0:
                total += part[0:share, :].astype(F32)
        bias = joined(held[0])
        for n in range(1, count):
            bias += joined(held[n])
        message[0:share, :] = total.astype(BF16)
        message[share:, :] = split(bias)

    scratch = [pltpu.VMEM((count, BIAS_ROWS, LANES), F32)]
    (message,) = call(kernel, parts, [((share + BIAS_ROWS, LANES), BF16)], [after], scratch)
    return message


def pair_sum(kept, near, after):
    def kernel(*refs):
        kept, near, (own, *messages) = refs[:count], refs[count], refs[count + 2 :]
        size = own.shape[0]
        for p, part in enumerate(kept):
            both = part[...] + near[p * size : (p + 1) * size, :].astype(F32)
            if p == 0:
                own[...] = both
            else:
                messages[p - 1][...] = both.astype(BF16)

    count = len(kept)
    shapes = [(kept[0].shape, F32)] + [(kept[0].shape, BF16)] * (count - 1)
    own, *messages = call(kernel, [*kept, near], shapes, [after])
    return own, messages


def column_pair_sum(own, near, after, share):
    def kernel(own, near, _, message):
        total = own[0:share, :].astype(F32) + near[0:share, :].astype(F32)
        message[0:share, :] = total.astype(BF16)
        message[share:, :] = split(joined(own[share:, :]) + joined(near[share:, :]))

    (message,) = call(kernel, [own, near], [(own.shape, BF16)], [after])
    return message


def column_sum(parts, grads, share):
    rows = share + BIAS_ROWS
    count, sent = len(parts), len(grads)

    def kernel(*refs):
        parts, grads, refs = refs[:count], refs[count : count + sent], refs[count + sent :]
        messages, (piece_out, bias_out, held, by_e, by_c) = refs[:sent], refs[sent:]
        home = lax.div(lax.axis_index("col"), 2)
        for p, part in enumerate(parts):
            held[lax.bitwise_xor(home, p)] = part[...]
        total, bias = held[0, 0:share, :].astype(F32), joined(held[0, share:, :])
        for n in range(1, count):
            total += held[n, 0:share, :].astype(F32)
            bias += joined(held[n, share:, :])
        by_e[...] = total
        depth = PROJECTED_DEPTH
        width = share // depth
        for c in range(depth):
            by_c[c * width : (c + 1) * width, :] = by_e[pl.ds(c, width, stride=depth), :]
        piece = by_c[...].astype(BF16)
        piece_out[...] = piece
        for message, grad in zip(messages, grads, strict=True):
            message[0:share, :] = piece
            message[share:, :] = grad[...]
        bias_out[...] = jnp.broadcast_to(bias, bias_out.shape)

    shapes = [((share + grad.shape[0], LANES), BF16) for grad in grads]
    shapes += [((share, LANES), BF16), ((8, LANES), F32)]
    scratch = [pltpu.VMEM((count, rows, LANES), BF16)] + [pltpu.VMEM((share, LANES), F32)] * 2
    *messages, piece, bias = call(kernel, [*parts, *grads], shapes, scratch=scratch)
    return messages, piece, bias


def finish(pieces, left, right_own, bias, left_shape, right_shape, scale, bias_scale):
    count, left_n = len(pieces), len(left)
    share = pieces[0].shape[0]

    def kernel(*refs):
        pieces, left, refs = refs[:count], refs[count : count + left_n], refs[count + left_n :]
        right_own, bias, projection, left_out, right_out, bias_out = refs
        me = lax.axis_index("row")
        right_total = right_own[...]
        depth = PROJECTED_DEPTH
        width = share // depth
        for p, piece in zip(partners(count), pieces, strict=True):
            block = piece[0:share, :].astype(F32) * scale
            for c in range(depth):
                start = c * depth + pl.multiple_of(lax.bitwise_xor(me, p) * width, width)
                projection[pl.ds(start, width), :] = block[c * width : (c + 1) * width]
            if p > 0:
                right_total += piece[share:, :].astype(F32)
        left_total = left[0][...]
        for term in left[1:]:
            left_total += term[...].astype(F32)
        unfold(left_total, left_out.shape[0], left_out)
        unfold(right_total, right_out.shape[0], right_out)
        bias_out[...] = bias[0:1, :] * bias_scale

    shapes = [
        ((count * share, PAIR_FEATURES), F32),
        (left_shape, F32),
        (right_shape, F32),
        ((1, PAIR_FEATURES), F32),
    ]
    return call(kernel, [*pieces, *left, right_own, bias], shapes)


def swap(x, axis, p):
    return lax.ppermute(x, axis, [(n, n ^ p) for n in range(lax.axis_size(axis))])


def swap_each(parts, axis, step=1):
    count = len(parts)
    return [swap(parts[n - 1], axis, n * step) for n in range(count, 0, -1)][::-1]


def from_evens(x, axis):
    return swap_each([x] * (lax.axis_size(axis) // 2 - 1), axis, 2)


def local(
    first_homolog_features, second_homolog_features, final_projection_matrix, output_bias, cotangent
):
    i_n, j_n, _ = cotangent.shape
    row_n, col_n = lax.axis_size("row"), lax.axis_size("col")
    sequences = second_homolog_features.shape[0] * row_n
    channels = final_projection_matrix.shape[0]
    res_total = i_n * row_n
    a_far = from_evens(first_homolog_features, "col")
    b_far = from_evens(second_homolog_features, "row")
    we, wt, a, b, w, g = load(
        first_homolog_features,
        second_homolog_features,
        final_projection_matrix,
        cotangent.reshape(i_n * j_n, PAIR_FEATURES),
    )
    a, b = stack([a, *a_far], [b, *b_far])
    a_pieces = [a, swap(a, "col", 1)]
    b_pieces = [b, swap(b, "row", 1)]
    y, gt, bias_rows = prepare(we, g, i_n, j_n)

    x, a_held, b_wide, (own, *messages) = outer(
        a_pieces, b_pieces, g, bias_rows, i_n, j_n, sequences
    )
    share = channels // row_n

    parts = [own] + swap_each(messages, "row")[::-1]
    left_kept, (message,) = gradient(
        b_wide, y, own, "col", in_pairs(col_n), col_n // 2, 1, i_n, j_n, sequences
    )
    left_near = swap(message, "col", 1)

    message = row_sum(parts, message, share)
    near = swap(message, "col", 1)
    left_own, left_messages = pair_sum(left_kept, left_near, message)
    left = [left_own] + swap_each(left_messages, "col", 2)
    y2, a_wide = product(w, gt, a_held, left_own)

    message = column_pair_sum(message, near, y2, share)
    parts = [message] + from_evens(message, "col")
    (right_own,), right_sent = gradient(
        a_wide, y2, message, "row", alone(row_n), 1, row_n - 1, j_n, i_n, sequences
    )

    messages, piece, bias = column_sum(parts, right_sent, share)
    pieces = [piece] + swap_each(messages, "row")[::-1]
    pair_map = pair(x, wt, output_bias, piece, sequences)
    projection, left_grad, right_grad, bias_grad = finish(
        pieces,
        left,
        right_own,
        bias,
        first_homolog_features.shape,
        second_homolog_features.shape,
        1.0 / (sequences * res_total),
        1.0 / res_total,
    )
    return (
        pair_map.reshape(i_n, j_n, PAIR_FEATURES),
        left_grad,
        right_grad,
        projection,
        bias_grad.reshape(PAIR_FEATURES),
    )


def solution(mesh):
    return jax.shard_map(
        local,
        mesh=mesh,
        in_specs=(
            P(("dp", "col"), "row"),
            P(("dp", "row"), "col"),
            P(),
            P(),
            P(("dp", "row"), "col", None),
        ),
        out_specs=(
            P(("dp", "row"), "col", None),
            P(("dp", "col"), "row"),
            P(("dp", "row"), "col"),
            P("dp", None),
            P("dp"),
        ),
        check_vma=False,
    )
```

```python
import functools

import jax
import jax.numpy as jnp
from jax import lax
from jax.experimental import pallas as pl
from jax.experimental.pallas import tpu as pltpu
from jax.sharding import PartitionSpec as P

PROJECTED_DEPTH = 32
PAIR_FEATURES = 128
GROUP = 8
MULTIPLY_ROWS = 768
CHUNKS = 4
BIAS_ROWS = 16
LANES = 128
F32 = jnp.float32
BF16 = jnp.bfloat16
MIB = 1024 * 1024

ROWS_BY_ROWS = (((1,), (1,)), ((), ()))
COLS_BY_COLS = (((0,), (0,)), ((), ()))


def params(sequences=0):
    return pltpu.CompilerParams(vmem_limit_bytes=min(10 + 10 * sequences // 32, 50) * MIB + 2 * MIB)


def whole(shape):
    return pl.BlockSpec(shape, lambda t: (0,) * len(shape))


def dot(x, y, dims=(((1,), (0,)), ((), ()))):
    return lax.dot_general(x, y, dims, preferred_element_type=F32)


def load_kernel(a_hbm, b_hbm, w_hbm, g_hbm, we_ref, wt_ref, a_ref, b_ref, w_ref, g_ref, w32, sems):
    depth = PROJECTED_DEPTH
    copies = [
        pltpu.make_async_copy(source, target, sems.at[n])
        for n, (source, target) in enumerate(
            [(w_hbm, w_ref), (g_hbm, g_ref), (a_hbm, a_ref), (b_hbm, b_ref)]
        )
    ]
    for copy in copies:
        copy.start()
    copies[0].wait()
    w32[...] = w_ref[...].astype(F32)
    for e in range(depth):
        block = w32[pl.ds(e, depth, stride=depth), :]
        we_ref[e * depth : (e + 1) * depth, :] = block.astype(BF16)
    wt_ref[...] = we_ref[...].astype(F32).T.astype(BF16)
    for copy in copies[1:]:
        copy.wait()


def in_vmem():
    return pl.BlockSpec(memory_space=pltpu.VMEM)


def load(a, b, w, g):
    shapes = [
        jax.ShapeDtypeStruct(w.shape, BF16),
        jax.ShapeDtypeStruct(w.shape[::-1], BF16),
        *[jax.ShapeDtypeStruct(x.shape, BF16) for x in (a, b, w, g)],
    ]
    return pl.pallas_call(
        load_kernel,
        in_specs=[pl.BlockSpec(memory_space=pltpu.HBM)] * 4,
        out_specs=[in_vmem()] * len(shapes),
        out_shape=shapes,
        scratch_shapes=[pltpu.VMEM(w.shape, F32), pltpu.SemaphoreType.DMA((4,))],
        compiler_params=params(),
        cost_estimate=pl.CostEstimate(
            flops=1000 * w.size, bytes_accessed=16 * w.size, transcendentals=0
        ),
    )(*[pltpu.with_memory_space_constraint(x, pltpu.HBM) for x in (a, b, w, g)])


def stack(*groups):
    def kernel(*refs):
        refs, outs = refs[: -len(groups)], refs[-len(groups) :]
        for group, out in zip(groups, outs, strict=True):
            blocks = [ref[...].astype(F32) for ref in refs[: len(group)]]
            refs = refs[len(group) :]
            out[...] = jnp.concatenate(blocks, axis=0).astype(BF16)

    shapes = [((len(group) * group[0].shape[0], group[0].shape[1]), BF16) for group in groups]
    return call(kernel, [x for group in groups for x in group], shapes)


def split(total):
    high = total.astype(BF16).astype(F32)
    row = lax.broadcasted_iota(jnp.int32, (BIAS_ROWS, PAIR_FEATURES), 0)
    return jnp.where(row == 0, high, jnp.where(row == 1, total - high, 0.0)).astype(BF16)


def joined(block):
    block = block.astype(F32)
    return block[0:1] + block[1:2]


def multiply(left_ref, right_ref, out_ref):
    for n in range(0, right_ref.shape[0], MULTIPLY_ROWS):
        rows = slice(n, n + MULTIPLY_ROWS)
        out_ref[:, rows] = dot(left_ref[...], right_ref[rows, :], ROWS_BY_ROWS).astype(BF16)


def prepare_kernel(i_n, j_n, we_ref, g_ref, y_ref, gt_ref, bias_ref, g32):
    g32[...] = g_ref[...].astype(F32)
    bias_ref[...] = split(jnp.sum(g32[...], axis=0, keepdims=True))
    multiply(we_ref, g_ref, y_ref)

    for j in range(j_n):
        gt_ref[j * i_n : (j + 1) * i_n, :] = g32[pl.ds(j, i_n, stride=j_n), :].astype(BF16)


def prepare(we, g, i_n, j_n):
    pairs = i_n * j_n
    channels = we.shape[0]
    shapes = [
        jax.ShapeDtypeStruct((channels, pairs), BF16),
        jax.ShapeDtypeStruct(g.shape, BF16),
        jax.ShapeDtypeStruct((BIAS_ROWS, PAIR_FEATURES), BF16),
    ]
    return pl.pallas_call(
        functools.partial(prepare_kernel, i_n, j_n),
        in_specs=[in_vmem()] * 2,
        out_specs=[in_vmem()] * len(shapes),
        out_shape=shapes,
        scratch_shapes=[pltpu.VMEM(g.shape, F32)],
        compiler_params=params(16),
        cost_estimate=pl.CostEstimate(
            flops=2 * pairs * channels * PAIR_FEATURES,
            bytes_accessed=4 * pairs * channels,
            transcendentals=0,
        ),
    )(we, g)


def join(pieces, axis, held):
    half = lax.axis_size(axis) // 2
    depth = pieces[0].shape[0] // half
    me = lax.axis_index(axis)
    odd, home = lax.rem(me, 2), lax.div(me, 2)
    for piece, parity in zip(pieces, (odd, 1 - odd), strict=True):
        block = piece[...].astype(F32)
        for p in range(half):
            place = (2 * lax.bitwise_xor(home, p) + parity) * depth
            held[pl.ds(pl.multiple_of(place, depth), depth), :] = block[p * depth : (p + 1) * depth]


def repeat_matrix(sequences):
    shape = (sequences, GROUP * sequences)
    lane = lax.broadcasted_iota(jnp.int32, shape, 1)
    row = lax.broadcasted_iota(jnp.int32, shape, 0)
    return (lax.rem(lane, sequences) == row).astype(BF16)


def tile_count(sequences):
    return GROUP * sequences // LANES, max(1, sequences // LANES)


def spread(held, wide):
    repeated = repeat_matrix(held.shape[0])[:, : wide.shape[0] * LANES]
    both = dot(held[...].T.astype(BF16), repeated)
    for l in range(wide.shape[0]):
        wide[l] = both[:, l * LANES : (l + 1) * LANES]


def tiles_of(sequences, tile):
    lane = lax.broadcasted_iota(jnp.int32, (1, LANES), 1) + tile * LANES
    return [
        (m, lax.div(lane, sequences) == m)
        for m in range(GROUP)
        if m * sequences < (tile + 1) * LANES and (m + 1) * sequences > tile * LANES
    ]


def chunks(body):
    if CHUNKS == 1:
        body(0)
    else:
        pl.loop(0, CHUNKS)(body)


def diagonal_of(wide, channel, positions, sequences):
    columns = []
    blocks = [
        wide[l, pl.ds(channel, positions, stride=PROJECTED_DEPTH), :].astype(BF16)
        for l in range(wide.shape[0])
    ]
    for l in range(tile_count(sequences)[0]):
        block = blocks[l % len(blocks)]
        members = dict(tiles_of(sequences, l))
        columns.append(
            jnp.concatenate(
                [
                    block * members[m].astype(F32).astype(BF16)
                    if m in members
                    else jnp.zeros(block.shape, BF16)
                    for m in range(GROUP)
                ],
                axis=0,
            )
        )
    return jnp.concatenate(columns, axis=1)


def alone(count):
    return lambda me: ([me], [[lax.bitwise_xor(me, d)] for d in range(1, count)])


def in_pairs(count):
    def plan(me):
        evens = range(0, count, 2)
        return [lax.bitwise_xor(me, d) for d in evens], [
            [lax.bitwise_xor(me, d + 1) for d in evens]
        ]

    return plan


def outer_kernel(i_n, j_n, *refs):
    depth = PROJECTED_DEPTH
    row_n = lax.axis_size("row")
    a_pieces, b_pieces, refs = refs[:2], refs[2:4], refs[4:]
    g_ref, bias_ref, x_ref, a_held, b_wide = refs[:5]
    messages, (b_held, left, total) = refs[5 : 5 + row_n], refs[5 + row_n :]
    sequences = a_held.shape[0]
    groups = i_n // GROUP
    per_step = depth // CHUNKS
    span = GROUP * j_n

    join(a_pieces, "col", a_held)
    join(b_pieces, "row", b_held)
    spread(b_held, b_wide)
    turned = a_held[...].T.astype(BF16)
    shape = (sequences, GROUP * sequences)
    shifted = lax.broadcasted_iota(jnp.int32, shape, 1) - lax.broadcasted_iota(jnp.int32, shape, 0)
    value = jnp.zeros(left.shape, F32)
    for m in range(GROUP):
        rows = [
            turned[(k * GROUP + m) * depth : (k * GROUP + m + 1) * depth, :] for k in range(groups)
        ]
        value += dot(jnp.concatenate(rows, axis=0), (shifted == m * sequences).astype(BF16))
    left[...] = value.astype(BF16)

    @chunks
    def _(t):
        size = per_step * depth
        rows = pl.ds(t * size if CHUNKS == 1 else pl.multiple_of(t * size, size), size)
        x_part = x_ref.at[rows]
        for e in range(0, per_step, 2):
            right = [diagonal_of(b_wide, t * per_step + e + n, j_n, sequences) for n in range(2)]
            product = dot(
                left[...], jnp.concatenate(right, axis=0), ROWS_BY_ROWS
            ).astype(BF16)
            for n in range(2):
                for k in range(groups):
                    x_part[(e + n) * depth : (e + n + 1) * depth, k * span : (k + 1) * span] = product[
                        k * depth : (k + 1) * depth, n * span : (n + 1) * span
                    ]
        total[rows, :] = dot(x_part[...], g_ref[...])

    share = total.shape[0] // row_n
    me = lax.axis_index("row")
    for p, message in enumerate(messages):
        part = pl.ds(pl.multiple_of(lax.bitwise_xor(me, p) * share, share), share)
        message[0:share, :] = total[part, :].astype(message.dtype)
        message[share:, :] = bias_ref[...].astype(message.dtype)


def outer(a_pieces, b_pieces, g, bias_rows, i_n, j_n, sequences):
    row_n = lax.axis_size("row")
    depth = PROJECTED_DEPTH
    channels = depth * depth
    pairs = i_n * j_n
    tiles = tile_count(sequences)[1]
    operands = [*a_pieces, *b_pieces, g, bias_rows]
    shapes = [jax.ShapeDtypeStruct((channels, pairs), BF16)]
    shapes += [
        jax.ShapeDtypeStruct((sequences, i_n * depth), F32),
        jax.ShapeDtypeStruct((tiles, j_n * depth, LANES), F32),
    ]
    shapes += [
        jax.ShapeDtypeStruct((channels // row_n + BIAS_ROWS, LANES), BF16 if p else F32)
        for p in range(row_n)
    ]
    results = pl.pallas_call(
        functools.partial(outer_kernel, i_n, j_n),
        in_specs=[in_vmem()] * len(operands),
        out_specs=[in_vmem()] * len(shapes),
        out_shape=shapes,
        scratch_shapes=[
            pltpu.VMEM((sequences, j_n * depth), F32),
            pltpu.VMEM((i_n // GROUP * depth, GROUP * sequences), BF16),
            pltpu.VMEM((channels, PAIR_FEATURES), F32),
        ],
        compiler_params=params(sequences),
        cost_estimate=pl.CostEstimate(
            flops=4 * pairs * channels * PAIR_FEATURES,
            bytes_accessed=2 * pairs * channels,
            transcendentals=0,
        ),
    )(*operands)
    return *results[:3], results[3:]


def gradient_kernel(axis, plan, kept, positions, others, sequences, *refs):
    depth = PROJECTED_DEPTH
    wide, source = refs[:2]
    outs, (result, grown, grad) = refs[3:-3], refs[-3:]
    parts = lax.axis_size(axis)
    per_step = depth // CHUNKS
    span = GROUP * others

    result[...] = jnp.zeros(result.shape, F32)

    @chunks
    def _(t):
        size = per_step * depth
        rows = pl.ds(t * size if CHUNKS == 1 else pl.multiple_of(t * size, size), size)
        part = source.at[rows]
        for n in range(0, per_step, 2):
            blocks = [
                jnp.concatenate(
                    [
                        part[m * depth : (m + 1) * depth, k * span : (k + 1) * span]
                        for m in (n, n + 1)
                    ],
                    axis=1,
                )
                for k in range(positions // GROUP)
            ]
            right = [
                diagonal_of(wide, t * per_step + m, others, sequences) for m in (n, n + 1)
            ]
            result[...] += dot(jnp.concatenate(blocks, axis=0), jnp.concatenate(right, axis=0))

    scaled = (result[...] * (1.0 / sequences)).astype(BF16)
    for l in range(scaled.shape[1] // LANES):
        members = dict(tiles_of(sequences, l))
        for k in range(positions // GROUP):
            block = scaled[k * depth : (k + 1) * depth, l * LANES : (l + 1) * LANES]
            for m in range(GROUP):
                start = (k * GROUP + m) * depth
                grown[start : start + depth, l * LANES : (l + 1) * LANES] = (
                    block * members[m].astype(F32).astype(BF16)
                    if m in members
                    else jnp.zeros((depth, LANES), BF16)
                )
    grad[...] = dot(repeat_matrix(sequences), grown[...], ROWS_BY_ROWS)
    share = sequences // parts

    def rows_of(p):
        mine = grad[pl.ds(pl.multiple_of(p * share, share), share), :]
        return jnp.concatenate(
            [mine[:, l * LANES : (l + 1) * LANES] for l in range(mine.shape[1] // LANES)], axis=0
        )

    stay, go = plan(lax.axis_index(axis))
    for p, out in zip(stay, outs[:kept], strict=True):
        out[...] = rows_of(p)
    for group, out in zip(go, outs[kept:], strict=True):
        size = out.shape[0] // len(group)
        for n, p in enumerate(group):
            out[n * size : (n + 1) * size, :] = rows_of(p).astype(BF16)


def gradient(wide, source, after, axis, plan, kept, groups, positions, others, sequences):
    depth = PROJECTED_DEPTH
    parts = lax.axis_size(axis)
    rows = sequences // parts * positions * depth // LANES
    shapes = [jax.ShapeDtypeStruct((rows, LANES), F32)] * kept
    group = (parts - kept) // groups
    shapes += [jax.ShapeDtypeStruct((group * rows, LANES), BF16)] * groups
    results = pl.pallas_call(
        functools.partial(gradient_kernel, axis, plan, kept, positions, others, sequences),
        in_specs=[in_vmem(), in_vmem(), pl.BlockSpec(memory_space=pl.ANY)],
        out_specs=[in_vmem()] * len(shapes),
        out_shape=shapes,
        scratch_shapes=[
            pltpu.VMEM((positions // GROUP * depth, GROUP * sequences), F32),
            pltpu.VMEM((positions * depth, GROUP * sequences), BF16),
            pltpu.VMEM((sequences, positions * depth), F32),
        ],
        compiler_params=params(sequences),
        cost_estimate=pl.CostEstimate(
            flops=2 * source.size * PAIR_FEATURES,
            bytes_accessed=2 * source.size,
            transcendentals=0,
        ),
    )(wide, source, after)
    return results[:kept], results[kept:]


def product_kernel(left_ref, right_ref, held, _, out_ref, wide):
    spread(held, wide)
    multiply(left_ref, right_ref, out_ref)


def product(left, right, held, after):
    shape = (left.shape[0], right.shape[0])
    spread_shape = (tile_count(held.shape[0])[1], held.shape[1], LANES)
    return pl.pallas_call(
        product_kernel,
        in_specs=[in_vmem()] * 3 + [pl.BlockSpec(memory_space=pl.ANY)],
        out_specs=[in_vmem()] * 2,
        out_shape=[jax.ShapeDtypeStruct(shape, BF16), jax.ShapeDtypeStruct(spread_shape, F32)],
        compiler_params=params(32),
        cost_estimate=pl.CostEstimate(
            flops=2 * shape[0] * shape[1] * left.shape[1],
            bytes_accessed=4 * shape[0] * shape[1],
            transcendentals=0,
        ),
    )(left, right, held, after)


def pair_kernel(sequences, x_ref, wt_ref, bias_ref, _, out_ref):
    product = dot(wt_ref[...], x_ref[...])
    out_ref[...] = (product.T * (1.0 / sequences) + bias_ref[...]).astype(BF16)


def pair(x, wt, output_bias, after, sequences):
    channels, pairs = x.shape
    count = 3
    size = pairs // count
    return pl.pallas_call(
        functools.partial(pair_kernel, sequences),
        grid=(count,),
        in_specs=[
            pl.BlockSpec((channels, size), lambda t: (0, t)),
            whole(wt.shape),
            whole((1, PAIR_FEATURES)),
            pl.BlockSpec(memory_space=pl.ANY),
        ],
        out_specs=pl.BlockSpec((size, PAIR_FEATURES), lambda t: (t, 0)),
        out_shape=jax.ShapeDtypeStruct((pairs, PAIR_FEATURES), BF16),
        compiler_params=params(),
        cost_estimate=pl.CostEstimate(
            flops=4 * pairs * channels * PAIR_FEATURES,
            bytes_accessed=2 * pairs * channels,
            transcendentals=0,
        ),
    )(x, wt, output_bias.reshape(1, PAIR_FEATURES), after)


def unfold(total, share, out):
    for l in range(out.shape[1] // LANES):
        out[:, l * LANES : (l + 1) * LANES] = total[l * share : (l + 1) * share, :]


def call(kernel, operands, shapes, after=(), scratch=()):
    specs = [in_vmem()] * len(operands) + [pl.BlockSpec(memory_space=pl.ANY)] * len(after)
    return pl.pallas_call(
        kernel,
        in_specs=specs,
        out_specs=[in_vmem()] * len(shapes),
        out_shape=[jax.ShapeDtypeStruct(shape, kind) for shape, kind in shapes],
        scratch_shapes=scratch,
        compiler_params=params(),
    )(*operands, *after)


def partners(count):
    return [0, *range(count - 1, 0, -1)]


def row_sum(parts, after, share):
    count = len(parts)

    def kernel(*refs):
        parts, (_, message, held) = refs[:count], refs[count:]
        me = lax.axis_index("row")
        total = parts[0][0:share, :]
        for p, part in zip(partners(count), parts, strict=True):
            held[lax.bitwise_xor(me, p)] = part[share:, :].astype(F32)
            if p > 0:
                total += part[0:share, :].astype(F32)
        bias = joined(held[0])
        for n in range(1, count):
            bias += joined(held[n])
        message[0:share, :] = total.astype(BF16)
        message[share:, :] = split(bias)

    scratch = [pltpu.VMEM((count, BIAS_ROWS, LANES), F32)]
    (message,) = call(kernel, parts, [((share + BIAS_ROWS, LANES), BF16)], [after], scratch)
    return message


def pair_sum(kept, near, after):
    def kernel(*refs):
        kept, near, (own, *messages) = refs[:count], refs[count], refs[count + 2 :]
        size = own.shape[0]
        for p, part in enumerate(kept):
            both = part[...] + near[p * size : (p + 1) * size, :].astype(F32)
            if p == 0:
                own[...] = both
            else:
                messages[p - 1][...] = both.astype(BF16)

    count = len(kept)
    shapes = [(kept[0].shape, F32)] + [(kept[0].shape, BF16)] * (count - 1)
    own, *messages = call(kernel, [*kept, near], shapes, [after])
    return own, messages


def column_pair_sum(own, near, after, share):
    def kernel(own, near, _, message):
        total = own[0:share, :].astype(F32) + near[0:share, :].astype(F32)
        message[0:share, :] = total.astype(BF16)
        message[share:, :] = split(joined(own[share:, :]) + joined(near[share:, :]))

    (message,) = call(kernel, [own, near], [(own.shape, BF16)], [after])
    return message


def column_sum(parts, grads, share):
    rows = share + BIAS_ROWS
    count, sent = len(parts), len(grads)

    def kernel(*refs):
        parts, grads, refs = refs[:count], refs[count : count + sent], refs[count + sent :]
        messages, (piece_out, bias_out, held, by_e, by_c) = refs[:sent], refs[sent:]
        home = lax.div(lax.axis_index("col"), 2)
        for p, part in enumerate(parts):
            held[lax.bitwise_xor(home, p)] = part[...]
        total, bias = held[0, 0:share, :].astype(F32), joined(held[0, share:, :])
        for n in range(1, count):
            total += held[n, 0:share, :].astype(F32)
            bias += joined(held[n, share:, :])
        by_e[...] = total
        depth = PROJECTED_DEPTH
        width = share // depth
        for c in range(depth):
            by_c[c * width : (c + 1) * width, :] = by_e[pl.ds(c, width, stride=depth), :]
        piece = by_c[...].astype(BF16)
        piece_out[...] = piece
        for message, grad in zip(messages, grads, strict=True):
            message[0:share, :] = piece
            message[share:, :] = grad[...]
        bias_out[...] = jnp.broadcast_to(bias, bias_out.shape)

    shapes = [((share + grad.shape[0], LANES), BF16) for grad in grads]
    shapes += [((share, LANES), BF16), ((8, LANES), F32)]
    scratch = [pltpu.VMEM((count, rows, LANES), BF16)] + [pltpu.VMEM((share, LANES), F32)] * 2
    *messages, piece, bias = call(kernel, [*parts, *grads], shapes, scratch=scratch)
    return messages, piece, bias


def finish(pieces, left, right_own, bias, left_shape, right_shape, scale, bias_scale):
    count, left_n = len(pieces), len(left)
    share = pieces[0].shape[0]

    def kernel(*refs):
        pieces, left, refs = refs[:count], refs[count : count + left_n], refs[count + left_n :]
        right_own, bias, projection, left_out, right_out, bias_out = refs
        me = lax.axis_index("row")
        right_total = right_own[...]
        depth = PROJECTED_DEPTH
        width = share // depth
        for p, piece in zip(partners(count), pieces, strict=True):
            block = piece[0:share, :].astype(F32) * scale
            for c in range(depth):
                start = c * depth + pl.multiple_of(lax.bitwise_xor(me, p) * width, width)
                projection[pl.ds(start, width), :] = block[c * width : (c + 1) * width]
            if p > 0:
                right_total += piece[share:, :].astype(F32)
        left_total = left[0][...]
        for term in left[1:]:
            left_total += term[...].astype(F32)
        unfold(left_total, left_out.shape[0], left_out)
        unfold(right_total, right_out.shape[0], right_out)
        bias_out[...] = bias[0:1, :] * bias_scale

    shapes = [
        ((count * share, PAIR_FEATURES), F32),
        (left_shape, F32),
        (right_shape, F32),
        ((1, PAIR_FEATURES), F32),
    ]
    return call(kernel, [*pieces, *left, right_own, bias], shapes)


def swap(x, axis, p):
    return lax.ppermute(x, axis, [(n, n ^ p) for n in range(lax.axis_size(axis))])


def swap_each(parts, axis, step=1):
    count = len(parts)
    return [swap(parts[n - 1], axis, n * step) for n in range(count, 0, -1)][::-1]


def from_evens(x, axis):
    return swap_each([x] * (lax.axis_size(axis) // 2 - 1), axis, 2)


def local(
    first_homolog_features, second_homolog_features, final_projection_matrix, output_bias, cotangent
):
    i_n, j_n, _ = cotangent.shape
    row_n, col_n = lax.axis_size("row"), lax.axis_size("col")
    sequences = second_homolog_features.shape[0] * row_n
    channels = final_projection_matrix.shape[0]
    res_total = i_n * row_n
    a_far = from_evens(first_homolog_features, "col")
    b_far = from_evens(second_homolog_features, "row")
    we, wt, a, b, w, g = load(
        first_homolog_features,
        second_homolog_features,
        final_projection_matrix,
        cotangent.reshape(i_n * j_n, PAIR_FEATURES),
    )
    a, b = stack([a, *a_far], [b, *b_far])
    a_pieces = [a, swap(a, "col", 1)]
    b_pieces = [b, swap(b, "row", 1)]
    y, gt, bias_rows = prepare(we, g, i_n, j_n)

    x, a_held, b_wide, (own, *messages) = outer(
        a_pieces, b_pieces, g, bias_rows, i_n, j_n, sequences
    )
    share = channels // row_n

    parts = [own] + swap_each(messages, "row")[::-1]
    left_kept, (message,) = gradient(
        b_wide, y, own, "col", in_pairs(col_n), col_n // 2, 1, i_n, j_n, sequences
    )
    left_near = swap(message, "col", 1)

    message = row_sum(parts, message, share)
    near = swap(message, "col", 1)
    left_own, left_messages = pair_sum(left_kept, left_near, message)
    left = [left_own] + swap_each(left_messages, "col", 2)
    y2, a_wide = product(w, gt, a_held, left_own)

    message = column_pair_sum(message, near, y2, share)
    parts = [message] + from_evens(message, "col")
    (right_own,), right_sent = gradient(
        a_wide, y2, message, "row", alone(row_n), 1, row_n - 1, j_n, i_n, sequences
    )

    messages, piece, bias = column_sum(parts, right_sent, share)
    pieces = [piece] + swap_each(messages, "row")[::-1]
    pair_map = pair(x, wt, output_bias, piece, sequences)
    projection, left_grad, right_grad, bias_grad = finish(
        pieces,
        left,
        right_own,
        bias,
        first_homolog_features.shape,
        second_homolog_features.shape,
        1.0 / (sequences * res_total),
        1.0 / res_total,
    )
    return (
        pair_map.reshape(i_n, j_n, PAIR_FEATURES),
        left_grad,
        right_grad,
        projection,
        bias_grad.reshape(PAIR_FEATURES),
    )


def solution(mesh):
    return jax.shard_map(
        local,
        mesh=mesh,
        in_specs=(
            P(("dp", "col"), "row"),
            P(("dp", "row"), "col"),
            P(),
            P(),
            P(("dp", "row"), "col", None),
        ),
        out_specs=(
            P(("dp", "row"), "col", None),
            P(("dp", "col"), "row"),
            P(("dp", "row"), "col"),
            P("dp", None),
            P("dp"),
        ),
        check_vma=False,
    )
```

```python
import functools

import jax
import jax.numpy as jnp
from jax import lax
from jax.experimental import pallas as pl
from jax.experimental.pallas import tpu as pltpu
from jax.sharding import PartitionSpec as P

PROJECTED_DEPTH = 32
PAIR_FEATURES = 128
GROUP = 8
MULTIPLY_ROWS = 384
CHUNKS = 2
BIAS_ROWS = 16
LANES = 128
F32 = jnp.float32
BF16 = jnp.bfloat16
MIB = 1024 * 1024

ROWS_BY_ROWS = (((1,), (1,)), ((), ()))
COLS_BY_COLS = (((0,), (0,)), ((), ()))


def params(sequences=0):
    return pltpu.CompilerParams(vmem_limit_bytes=min(10 + 10 * sequences // 32, 50) * MIB + 2 * MIB)


def whole(shape):
    return pl.BlockSpec(shape, lambda t: (0,) * len(shape))


def dot(x, y, dims=(((1,), (0,)), ((), ()))):
    return lax.dot_general(x, y, dims, preferred_element_type=F32)


def load_kernel(a_hbm, b_hbm, w_hbm, g_hbm, we_ref, wt_ref, a_ref, b_ref, w_ref, g_ref, w32, sems):
    depth = PROJECTED_DEPTH
    copies = [
        pltpu.make_async_copy(source, target, sems.at[n])
        for n, (source, target) in enumerate(
            [(w_hbm, w_ref), (g_hbm, g_ref), (a_hbm, a_ref), (b_hbm, b_ref)]
        )
    ]
    for copy in copies:
        copy.start()
    copies[0].wait()
    w32[...] = w_ref[...].astype(F32)
    for e in range(depth):
        block = w32[pl.ds(e, depth, stride=depth), :]
        we_ref[e * depth : (e + 1) * depth, :] = block.astype(BF16)
    wt_ref[...] = we_ref[...].astype(F32).T.astype(BF16)
    for copy in copies[1:]:
        copy.wait()


def in_vmem():
    return pl.BlockSpec(memory_space=pltpu.VMEM)


def load(a, b, w, g):
    shapes = [
        jax.ShapeDtypeStruct(w.shape, BF16),
        jax.ShapeDtypeStruct(w.shape[::-1], BF16),
        *[jax.ShapeDtypeStruct(x.shape, BF16) for x in (a, b, w, g)],
    ]
    return pl.pallas_call(
        load_kernel,
        in_specs=[pl.BlockSpec(memory_space=pltpu.HBM)] * 4,
        out_specs=[in_vmem()] * len(shapes),
        out_shape=shapes,
        scratch_shapes=[pltpu.VMEM(w.shape, F32), pltpu.SemaphoreType.DMA((4,))],
        compiler_params=params(),
        cost_estimate=pl.CostEstimate(
            flops=1000 * w.size, bytes_accessed=16 * w.size, transcendentals=0
        ),
    )(*[pltpu.with_memory_space_constraint(x, pltpu.HBM) for x in (a, b, w, g)])


def stack(*groups):
    def kernel(*refs):
        refs, outs = refs[: -len(groups)], refs[-len(groups) :]
        for group, out in zip(groups, outs, strict=True):
            blocks = [ref[...].astype(F32) for ref in refs[: len(group)]]
            refs = refs[len(group) :]
            out[...] = jnp.concatenate(blocks, axis=0).astype(BF16)

    shapes = [((len(group) * group[0].shape[0], group[0].shape[1]), BF16) for group in groups]
    return call(kernel, [x for group in groups for x in group], shapes)


def split(total):
    high = total.astype(BF16).astype(F32)
    row = lax.broadcasted_iota(jnp.int32, (BIAS_ROWS, PAIR_FEATURES), 0)
    return jnp.where(row == 0, high, jnp.where(row == 1, total - high, 0.0)).astype(BF16)


def joined(block):
    block = block.astype(F32)
    return block[0:1] + block[1:2]


def multiply(left_ref, right_ref, out_ref):
    for n in range(0, right_ref.shape[0], MULTIPLY_ROWS):
        rows = slice(n, n + MULTIPLY_ROWS)
        out_ref[:, rows] = dot(left_ref[...], right_ref[rows, :], ROWS_BY_ROWS).astype(BF16)


def prepare_kernel(i_n, j_n, we_ref, g_ref, y_ref, gt_ref, bias_ref, g32):
    g32[...] = g_ref[...].astype(F32)
    bias_ref[...] = split(jnp.sum(g32[...], axis=0, keepdims=True))
    multiply(we_ref, g_ref, y_ref)

    for j in range(j_n):
        gt_ref[j * i_n : (j + 1) * i_n, :] = g32[pl.ds(j, i_n, stride=j_n), :].astype(BF16)


def prepare(we, g, i_n, j_n):
    pairs = i_n * j_n
    channels = we.shape[0]
    shapes = [
        jax.ShapeDtypeStruct((channels, pairs), BF16),
        jax.ShapeDtypeStruct(g.shape, BF16),
        jax.ShapeDtypeStruct((BIAS_ROWS, PAIR_FEATURES), BF16),
    ]
    return pl.pallas_call(
        functools.partial(prepare_kernel, i_n, j_n),
        in_specs=[in_vmem()] * 2,
        out_specs=[in_vmem()] * len(shapes),
        out_shape=shapes,
        scratch_shapes=[pltpu.VMEM(g.shape, F32)],
        compiler_params=params(16),
        cost_estimate=pl.CostEstimate(
            flops=2 * pairs * channels * PAIR_FEATURES,
            bytes_accessed=4 * pairs * channels,
            transcendentals=0,
        ),
    )(we, g)


def join(pieces, axis, held):
    half = lax.axis_size(axis) // 2
    depth = pieces[0].shape[0] // half
    me = lax.axis_index(axis)
    odd, home = lax.rem(me, 2), lax.div(me, 2)
    for piece, parity in zip(pieces, (odd, 1 - odd), strict=True):
        block = piece[...].astype(F32)
        for p in range(half):
            place = (2 * lax.bitwise_xor(home, p) + parity) * depth
            held[pl.ds(pl.multiple_of(place, depth), depth), :] = block[p * depth : (p + 1) * depth]


def repeat_matrix(sequences):
    shape = (sequences, GROUP * sequences)
    lane = lax.broadcasted_iota(jnp.int32, shape, 1)
    row = lax.broadcasted_iota(jnp.int32, shape, 0)
    return (lax.rem(lane, sequences) == row).astype(BF16)


def tile_count(sequences):
    return GROUP * sequences // LANES, max(1, sequences // LANES)


def spread(held, wide):
    repeated = repeat_matrix(held.shape[0])[:, : wide.shape[0] * LANES]
    both = dot(held[...].T.astype(BF16), repeated)
    for l in range(wide.shape[0]):
        wide[l] = both[:, l * LANES : (l + 1) * LANES]


def tiles_of(sequences, tile):
    lane = lax.broadcasted_iota(jnp.int32, (1, LANES), 1) + tile * LANES
    return [
        (m, lax.div(lane, sequences) == m)
        for m in range(GROUP)
        if m * sequences < (tile + 1) * LANES and (m + 1) * sequences > tile * LANES
    ]


def chunks(body):
    if CHUNKS == 1:
        body(0)
    else:
        pl.loop(0, CHUNKS)(body)


def diagonal_of(wide, channel, positions, sequences):
    columns = []
    blocks = [
        wide[l, pl.ds(channel, positions, stride=PROJECTED_DEPTH), :].astype(BF16)
        for l in range(wide.shape[0])
    ]
    for l in range(tile_count(sequences)[0]):
        block = blocks[l % len(blocks)]
        members = dict(tiles_of(sequences, l))
        columns.append(
            jnp.concatenate(
                [
                    block * members[m].astype(F32).astype(BF16)
                    if m in members
                    else jnp.zeros(block.shape, BF16)
                    for m in range(GROUP)
                ],
                axis=0,
            )
        )
    return jnp.concatenate(columns, axis=1)


def alone(count):
    return lambda me: ([me], [[lax.bitwise_xor(me, d)] for d in range(1, count)])


def in_pairs(count):
    def plan(me):
        evens = range(0, count, 2)
        return [lax.bitwise_xor(me, d) for d in evens], [
            [lax.bitwise_xor(me, d + 1) for d in evens]
        ]

    return plan


def outer_kernel(i_n, j_n, *refs):
    depth = PROJECTED_DEPTH
    row_n = lax.axis_size("row")
    a_pieces, b_pieces, refs = refs[:2], refs[2:4], refs[4:]
    g_ref, bias_ref, x_ref, a_held, b_wide = refs[:5]
    messages, (b_held, left, total) = refs[5 : 5 + row_n], refs[5 + row_n :]
    sequences = a_held.shape[0]
    groups = i_n // GROUP
    per_step = depth // CHUNKS
    span = GROUP * j_n

    join(a_pieces, "col", a_held)
    join(b_pieces, "row", b_held)
    spread(b_held, b_wide)
    turned = a_held[...].T.astype(BF16)
    shape = (sequences, GROUP * sequences)
    shifted = lax.broadcasted_iota(jnp.int32, shape, 1) - lax.broadcasted_iota(jnp.int32, shape, 0)
    value = jnp.zeros(left.shape, F32)
    for m in range(GROUP):
        rows = [
            turned[(k * GROUP + m) * depth : (k * GROUP + m + 1) * depth, :] for k in range(groups)
        ]
        value += dot(jnp.concatenate(rows, axis=0), (shifted == m * sequences).astype(BF16))
    left[...] = value.astype(BF16)

    @chunks
    def _(t):
        size = per_step * depth
        rows = pl.ds(t * size if CHUNKS == 1 else pl.multiple_of(t * size, size), size)
        x_part, total_part = x_ref.at[rows], total.at[rows]
        half = per_step // 2
        for e in range(0, per_step, 2):
            right = [diagonal_of(b_wide, t * per_step + e + n, j_n, sequences) for n in range(2)]
            product = dot(
                left[...], jnp.concatenate(right, axis=0), ROWS_BY_ROWS
            ).astype(BF16)
            for n in range(2):
                for k in range(groups):
                    x_part[(e + n) * depth : (e + n + 1) * depth, k * span : (k + 1) * span] = product[
                        k * depth : (k + 1) * depth, n * span : (n + 1) * span
                    ]
            if (e + 2) % half == 0:
                done = slice((e + 2 - half) * depth, (e + 2) * depth)
                total_part[done, :] = dot(x_part[done, :], g_ref[...])

    share = total.shape[0] // row_n
    me = lax.axis_index("row")
    for p, message in enumerate(messages):
        part = pl.ds(pl.multiple_of(lax.bitwise_xor(me, p) * share, share), share)
        message[0:share, :] = total[part, :].astype(message.dtype)
        message[share:, :] = bias_ref[...].astype(message.dtype)


def outer(a_pieces, b_pieces, g, bias_rows, i_n, j_n, sequences):
    row_n = lax.axis_size("row")
    depth = PROJECTED_DEPTH
    channels = depth * depth
    pairs = i_n * j_n
    tiles = tile_count(sequences)[1]
    operands = [*a_pieces, *b_pieces, g, bias_rows]
    shapes = [jax.ShapeDtypeStruct((channels, pairs), BF16)]
    shapes += [
        jax.ShapeDtypeStruct((sequences, i_n * depth), F32),
        jax.ShapeDtypeStruct((tiles, j_n * depth, LANES), F32),
    ]
    shapes += [
        jax.ShapeDtypeStruct((channels // row_n + BIAS_ROWS, LANES), BF16 if p else F32)
        for p in range(row_n)
    ]
    results = pl.pallas_call(
        functools.partial(outer_kernel, i_n, j_n),
        in_specs=[in_vmem()] * len(operands),
        out_specs=[in_vmem()] * len(shapes),
        out_shape=shapes,
        scratch_shapes=[
            pltpu.VMEM((sequences, j_n * depth), F32),
            pltpu.VMEM((i_n // GROUP * depth, GROUP * sequences), BF16),
            pltpu.VMEM((channels, PAIR_FEATURES), F32),
        ],
        compiler_params=params(sequences),
        cost_estimate=pl.CostEstimate(
            flops=4 * pairs * channels * PAIR_FEATURES,
            bytes_accessed=2 * pairs * channels,
            transcendentals=0,
        ),
    )(*operands)
    return *results[:3], results[3:]


def gradient_kernel(axis, plan, kept, positions, others, sequences, *refs):
    depth = PROJECTED_DEPTH
    wide, source = refs[:2]
    outs, (result, grown, grad) = refs[3:-3], refs[-3:]
    parts = lax.axis_size(axis)
    per_step = depth // CHUNKS
    span = GROUP * others

    result[...] = jnp.zeros(result.shape, F32)

    @chunks
    def _(t):
        size = per_step * depth
        rows = pl.ds(t * size if CHUNKS == 1 else pl.multiple_of(t * size, size), size)
        part = source.at[rows]
        for n in range(0, per_step, 2):
            blocks = [
                jnp.concatenate(
                    [
                        part[m * depth : (m + 1) * depth, k * span : (k + 1) * span]
                        for m in (n, n + 1)
                    ],
                    axis=1,
                )
                for k in range(positions // GROUP)
            ]
            right = [
                diagonal_of(wide, t * per_step + m, others, sequences) for m in (n, n + 1)
            ]
            result[...] += dot(jnp.concatenate(blocks, axis=0), jnp.concatenate(right, axis=0))

    scaled = (result[...] * (1.0 / sequences)).astype(BF16)
    for l in range(scaled.shape[1] // LANES):
        members = dict(tiles_of(sequences, l))
        for k in range(positions // GROUP):
            block = scaled[k * depth : (k + 1) * depth, l * LANES : (l + 1) * LANES]
            for m in range(GROUP):
                start = (k * GROUP + m) * depth
                grown[start : start + depth, l * LANES : (l + 1) * LANES] = (
                    block * members[m].astype(F32).astype(BF16)
                    if m in members
                    else jnp.zeros((depth, LANES), BF16)
                )
    grad[...] = dot(repeat_matrix(sequences), grown[...], ROWS_BY_ROWS)
    share = sequences // parts

    def rows_of(p):
        mine = grad[pl.ds(pl.multiple_of(p * share, share), share), :]
        return jnp.concatenate(
            [mine[:, l * LANES : (l + 1) * LANES] for l in range(mine.shape[1] // LANES)], axis=0
        )

    stay, go = plan(lax.axis_index(axis))
    for p, out in zip(stay, outs[:kept], strict=True):
        out[...] = rows_of(p)
    for group, out in zip(go, outs[kept:], strict=True):
        size = out.shape[0] // len(group)
        for n, p in enumerate(group):
            out[n * size : (n + 1) * size, :] = rows_of(p).astype(BF16)


def gradient(wide, source, after, axis, plan, kept, groups, positions, others, sequences):
    depth = PROJECTED_DEPTH
    parts = lax.axis_size(axis)
    rows = sequences // parts * positions * depth // LANES
    shapes = [jax.ShapeDtypeStruct((rows, LANES), F32)] * kept
    group = (parts - kept) // groups
    shapes += [jax.ShapeDtypeStruct((group * rows, LANES), BF16)] * groups
    results = pl.pallas_call(
        functools.partial(gradient_kernel, axis, plan, kept, positions, others, sequences),
        in_specs=[in_vmem(), in_vmem(), pl.BlockSpec(memory_space=pl.ANY)],
        out_specs=[in_vmem()] * len(shapes),
        out_shape=shapes,
        scratch_shapes=[
            pltpu.VMEM((positions // GROUP * depth, GROUP * sequences), F32),
            pltpu.VMEM((positions * depth, GROUP * sequences), BF16),
            pltpu.VMEM((sequences, positions * depth), F32),
        ],
        compiler_params=params(sequences),
        cost_estimate=pl.CostEstimate(
            flops=2 * source.size * PAIR_FEATURES,
            bytes_accessed=2 * source.size,
            transcendentals=0,
        ),
    )(wide, source, after)
    return results[:kept], results[kept:]


def product_kernel(left_ref, right_ref, held, _, out_ref, wide):
    spread(held, wide)
    multiply(left_ref, right_ref, out_ref)


def product(left, right, held, after):
    shape = (left.shape[0], right.shape[0])
    spread_shape = (tile_count(held.shape[0])[1], held.shape[1], LANES)
    return pl.pallas_call(
        product_kernel,
        in_specs=[in_vmem()] * 3 + [pl.BlockSpec(memory_space=pl.ANY)],
        out_specs=[in_vmem()] * 2,
        out_shape=[jax.ShapeDtypeStruct(shape, BF16), jax.ShapeDtypeStruct(spread_shape, F32)],
        compiler_params=params(32),
        cost_estimate=pl.CostEstimate(
            flops=2 * shape[0] * shape[1] * left.shape[1],
            bytes_accessed=4 * shape[0] * shape[1],
            transcendentals=0,
        ),
    )(left, right, held, after)


def pair_kernel(sequences, x_ref, wt_ref, bias_ref, _, out_ref):
    product = dot(wt_ref[...], x_ref[...])
    out_ref[...] = (product.T * (1.0 / sequences) + bias_ref[...]).astype(BF16)


def pair(x, wt, output_bias, after, sequences):
    channels, pairs = x.shape
    count = 3
    size = pairs // count
    return pl.pallas_call(
        functools.partial(pair_kernel, sequences),
        grid=(count,),
        in_specs=[
            pl.BlockSpec((channels, size), lambda t: (0, t)),
            whole(wt.shape),
            whole((1, PAIR_FEATURES)),
            pl.BlockSpec(memory_space=pl.ANY),
        ],
        out_specs=pl.BlockSpec((size, PAIR_FEATURES), lambda t: (t, 0)),
        out_shape=jax.ShapeDtypeStruct((pairs, PAIR_FEATURES), BF16),
        compiler_params=params(),
        cost_estimate=pl.CostEstimate(
            flops=4 * pairs * channels * PAIR_FEATURES,
            bytes_accessed=2 * pairs * channels,
            transcendentals=0,
        ),
    )(x, wt, output_bias.reshape(1, PAIR_FEATURES), after)


def unfold(total, share, out):
    for l in range(out.shape[1] // LANES):
        out[:, l * LANES : (l + 1) * LANES] = total[l * share : (l + 1) * share, :]


def call(kernel, operands, shapes, after=(), scratch=()):
    specs = [in_vmem()] * len(operands) + [pl.BlockSpec(memory_space=pl.ANY)] * len(after)
    return pl.pallas_call(
        kernel,
        in_specs=specs,
        out_specs=[in_vmem()] * len(shapes),
        out_shape=[jax.ShapeDtypeStruct(shape, kind) for shape, kind in shapes],
        scratch_shapes=scratch,
        compiler_params=params(),
    )(*operands, *after)


def partners(count):
    return [0, *range(count - 1, 0, -1)]


def row_sum(parts, after, share):
    count = len(parts)

    def kernel(*refs):
        parts, (_, message, held) = refs[:count], refs[count:]
        me = lax.axis_index("row")
        total = parts[0][0:share, :]
        for p, part in zip(partners(count), parts, strict=True):
            held[lax.bitwise_xor(me, p)] = part[share:, :].astype(F32)
            if p > 0:
                total += part[0:share, :].astype(F32)
        bias = joined(held[0])
        for n in range(1, count):
            bias += joined(held[n])
        message[0:share, :] = total.astype(BF16)
        message[share:, :] = split(bias)

    scratch = [pltpu.VMEM((count, BIAS_ROWS, LANES), F32)]
    (message,) = call(kernel, parts, [((share + BIAS_ROWS, LANES), BF16)], [after], scratch)
    return message


def pair_sum(kept, near, after):
    def kernel(*refs):
        kept, near, (own, *messages) = refs[:count], refs[count], refs[count + 2 :]
        size = own.shape[0]
        for p, part in enumerate(kept):
            both = part[...] + near[p * size : (p + 1) * size, :].astype(F32)
            if p == 0:
                own[...] = both
            else:
                messages[p - 1][...] = both.astype(BF16)

    count = len(kept)
    shapes = [(kept[0].shape, F32)] + [(kept[0].shape, BF16)] * (count - 1)
    own, *messages = call(kernel, [*kept, near], shapes, [after])
    return own, messages


def column_pair_sum(own, near, after, share):
    def kernel(own, near, _, message):
        total = own[0:share, :].astype(F32) + near[0:share, :].astype(F32)
        message[0:share, :] = total.astype(BF16)
        message[share:, :] = split(joined(own[share:, :]) + joined(near[share:, :]))

    (message,) = call(kernel, [own, near], [(own.shape, BF16)], [after])
    return message


def column_sum(parts, grads, share):
    rows = share + BIAS_ROWS
    count, sent = len(parts), len(grads)

    def kernel(*refs):
        parts, grads, refs = refs[:count], refs[count : count + sent], refs[count + sent :]
        messages, (piece_out, bias_out, held, by_e, by_c) = refs[:sent], refs[sent:]
        home = lax.div(lax.axis_index("col"), 2)
        for p, part in enumerate(parts):
            held[lax.bitwise_xor(home, p)] = part[...]
        total, bias = held[0, 0:share, :].astype(F32), joined(held[0, share:, :])
        for n in range(1, count):
            total += held[n, 0:share, :].astype(F32)
            bias += joined(held[n, share:, :])
        by_e[...] = total
        depth = PROJECTED_DEPTH
        width = share // depth
        for c in range(depth):
            by_c[c * width : (c + 1) * width, :] = by_e[pl.ds(c, width, stride=depth), :]
        piece = by_c[...].astype(BF16)
        piece_out[...] = piece
        for message, grad in zip(messages, grads, strict=True):
            message[0:share, :] = piece
            message[share:, :] = grad[...]
        bias_out[...] = jnp.broadcast_to(bias, bias_out.shape)

    shapes = [((share + grad.shape[0], LANES), BF16) for grad in grads]
    shapes += [((share, LANES), BF16), ((8, LANES), F32)]
    scratch = [pltpu.VMEM((count, rows, LANES), BF16)] + [pltpu.VMEM((share, LANES), F32)] * 2
    *messages, piece, bias = call(kernel, [*parts, *grads], shapes, scratch=scratch)
    return messages, piece, bias


def finish(pieces, left, right_own, bias, left_shape, right_shape, scale, bias_scale):
    count, left_n = len(pieces), len(left)
    share = pieces[0].shape[0]

    def kernel(*refs):
        pieces, left, refs = refs[:count], refs[count : count + left_n], refs[count + left_n :]
        right_own, bias, projection, left_out, right_out, bias_out = refs
        me = lax.axis_index("row")
        right_total = right_own[...]
        depth = PROJECTED_DEPTH
        width = share // depth
        for p, piece in zip(partners(count), pieces, strict=True):
            block = piece[0:share, :].astype(F32) * scale
            for c in range(depth):
                start = c * depth + pl.multiple_of(lax.bitwise_xor(me, p) * width, width)
                projection[pl.ds(start, width), :] = block[c * width : (c + 1) * width]
            if p > 0:
                right_total += piece[share:, :].astype(F32)
        left_total = left[0][...]
        for term in left[1:]:
            left_total += term[...].astype(F32)
        unfold(left_total, left_out.shape[0], left_out)
        unfold(right_total, right_out.shape[0], right_out)
        bias_out[...] = bias[0:1, :] * bias_scale

    shapes = [
        ((count * share, PAIR_FEATURES), F32),
        (left_shape, F32),
        (right_shape, F32),
        ((1, PAIR_FEATURES), F32),
    ]
    return call(kernel, [*pieces, *left, right_own, bias], shapes)


def swap(x, axis, p):
    return lax.ppermute(x, axis, [(n, n ^ p) for n in range(lax.axis_size(axis))])


def swap_each(parts, axis, step=1):
    count = len(parts)
    return [swap(parts[n - 1], axis, n * step) for n in range(count, 0, -1)][::-1]


def from_evens(x, axis):
    return swap_each([x] * (lax.axis_size(axis) // 2 - 1), axis, 2)


def local(
    first_homolog_features, second_homolog_features, final_projection_matrix, output_bias, cotangent
):
    i_n, j_n, _ = cotangent.shape
    row_n, col_n = lax.axis_size("row"), lax.axis_size("col")
    sequences = second_homolog_features.shape[0] * row_n
    channels = final_projection_matrix.shape[0]
    res_total = i_n * row_n
    a_far = from_evens(first_homolog_features, "col")
    b_far = from_evens(second_homolog_features, "row")
    we, wt, a, b, w, g = load(
        first_homolog_features,
        second_homolog_features,
        final_projection_matrix,
        cotangent.reshape(i_n * j_n, PAIR_FEATURES),
    )
    a, b = stack([a, *a_far], [b, *b_far])
    a_pieces = [a, swap(a, "col", 1)]
    b_pieces = [b, swap(b, "row", 1)]
    y, gt, bias_rows = prepare(we, g, i_n, j_n)

    x, a_held, b_wide, (own, *messages) = outer(
        a_pieces, b_pieces, g, bias_rows, i_n, j_n, sequences
    )
    share = channels // row_n

    parts = [own] + swap_each(messages, "row")[::-1]
    left_kept, (message,) = gradient(
        b_wide, y, own, "col", in_pairs(col_n), col_n // 2, 1, i_n, j_n, sequences
    )
    left_near = swap(message, "col", 1)

    message = row_sum(parts, message, share)
    near = swap(message, "col", 1)
    left_own, left_messages = pair_sum(left_kept, left_near, message)
    left = [left_own] + swap_each(left_messages, "col", 2)
    y2, a_wide = product(w, gt, a_held, left_own)

    message = column_pair_sum(message, near, y2, share)
    parts = [message] + from_evens(message, "col")
    (right_own,), right_sent = gradient(
        a_wide, y2, message, "row", alone(row_n), 1, row_n - 1, j_n, i_n, sequences
    )

    messages, piece, bias = column_sum(parts, right_sent, share)
    pieces = [piece] + swap_each(messages, "row")[::-1]
    pair_map = pair(x, wt, output_bias, piece, sequences)
    projection, left_grad, right_grad, bias_grad = finish(
        pieces,
        left,
        right_own,
        bias,
        first_homolog_features.shape,
        second_homolog_features.shape,
        1.0 / (sequences * res_total),
        1.0 / res_total,
    )
    return (
        pair_map.reshape(i_n, j_n, PAIR_FEATURES),
        left_grad,
        right_grad,
        projection,
        bias_grad.reshape(PAIR_FEATURES),
    )


def solution(mesh):
    return jax.shard_map(
        local,
        mesh=mesh,
        in_specs=(
            P(("dp", "col"), "row"),
            P(("dp", "row"), "col"),
            P(),
            P(),
            P(("dp", "row"), "col", None),
        ),
        out_specs=(
            P(("dp", "row"), "col", None),
            P(("dp", "col"), "row"),
            P(("dp", "row"), "col"),
            P("dp", None),
            P("dp"),
        ),
        check_vma=False,
    )
```

```python
import functools

import jax
import jax.numpy as jnp
from jax import lax
from jax.experimental import pallas as pl
from jax.experimental.pallas import tpu as pltpu
from jax.sharding import PartitionSpec as P

PROJECTED_DEPTH = 32
PAIR_FEATURES = 128
GROUP = 8
MULTIPLY_ROWS = 384
CHUNKS = 2
BIAS_ROWS = 16
LANES = 128
F32 = jnp.float32
BF16 = jnp.bfloat16
MIB = 1024 * 1024

ROWS_BY_ROWS = (((1,), (1,)), ((), ()))
COLS_BY_COLS = (((0,), (0,)), ((), ()))


def params(sequences=0):
    return pltpu.CompilerParams(vmem_limit_bytes=min(10 + 10 * sequences // 32, 50) * MIB + 2 * MIB)


def whole(shape):
    return pl.BlockSpec(shape, lambda t: (0,) * len(shape))


def dot(x, y, dims=(((1,), (0,)), ((), ()))):
    return lax.dot_general(x, y, dims, preferred_element_type=F32)


def load_kernel(a_hbm, b_hbm, w_hbm, g_hbm, we_ref, wt_ref, a_ref, b_ref, w_ref, g_ref, w32, sems):
    depth = PROJECTED_DEPTH
    copies = [
        pltpu.make_async_copy(source, target, sems.at[n])
        for n, (source, target) in enumerate(
            [(w_hbm, w_ref), (g_hbm, g_ref), (a_hbm, a_ref), (b_hbm, b_ref)]
        )
    ]
    for copy in copies:
        copy.start()
    copies[0].wait()
    w32[...] = w_ref[...].astype(F32)
    for e in range(depth):
        block = w32[pl.ds(e, depth, stride=depth), :]
        we_ref[e * depth : (e + 1) * depth, :] = block.astype(BF16)
    wt_ref[...] = we_ref[...].astype(F32).T.astype(BF16)
    for copy in copies[1:]:
        copy.wait()


def in_vmem():
    return pl.BlockSpec(memory_space=pltpu.VMEM)


def load(a, b, w, g):
    shapes = [
        jax.ShapeDtypeStruct(w.shape, BF16),
        jax.ShapeDtypeStruct(w.shape[::-1], BF16),
        *[jax.ShapeDtypeStruct(x.shape, BF16) for x in (a, b, w, g)],
    ]
    return pl.pallas_call(
        load_kernel,
        in_specs=[pl.BlockSpec(memory_space=pltpu.HBM)] * 4,
        out_specs=[in_vmem()] * len(shapes),
        out_shape=shapes,
        scratch_shapes=[pltpu.VMEM(w.shape, F32), pltpu.SemaphoreType.DMA((4,))],
        compiler_params=params(),
        cost_estimate=pl.CostEstimate(
            flops=1000 * w.size, bytes_accessed=16 * w.size, transcendentals=0
        ),
    )(*[pltpu.with_memory_space_constraint(x, pltpu.HBM) for x in (a, b, w, g)])


def stack(*groups):
    def kernel(*refs):
        refs, outs = refs[: -len(groups)], refs[-len(groups) :]
        for group, out in zip(groups, outs, strict=True):
            blocks = [ref[...].astype(F32) for ref in refs[: len(group)]]
            refs = refs[len(group) :]
            out[...] = jnp.concatenate(blocks, axis=0).astype(BF16)

    shapes = [((len(group) * group[0].shape[0], group[0].shape[1]), BF16) for group in groups]
    return call(kernel, [x for group in groups for x in group], shapes)


def split(total):
    high = total.astype(BF16).astype(F32)
    row = lax.broadcasted_iota(jnp.int32, (BIAS_ROWS, PAIR_FEATURES), 0)
    return jnp.where(row == 0, high, jnp.where(row == 1, total - high, 0.0)).astype(BF16)


def joined(block):
    block = block.astype(F32)
    return block[0:1] + block[1:2]


def multiply(left_ref, right_ref, out_ref):
    for n in range(0, right_ref.shape[0], MULTIPLY_ROWS):
        rows = slice(n, n + MULTIPLY_ROWS)
        out_ref[:, rows] = dot(left_ref[...], right_ref[rows, :], ROWS_BY_ROWS).astype(BF16)


def prepare_kernel(i_n, j_n, we_ref, g_ref, y_ref, gt_ref, bias_ref, g32):
    g32[...] = g_ref[...].astype(F32)
    bias_ref[...] = split(jnp.sum(g32[...], axis=0, keepdims=True))
    multiply(we_ref, g_ref, y_ref)

    for j in range(j_n):
        gt_ref[j * i_n : (j + 1) * i_n, :] = g32[pl.ds(j, i_n, stride=j_n), :].astype(BF16)


def prepare(we, g, i_n, j_n):
    pairs = i_n * j_n
    channels = we.shape[0]
    shapes = [
        jax.ShapeDtypeStruct((channels, pairs), BF16),
        jax.ShapeDtypeStruct(g.shape, BF16),
        jax.ShapeDtypeStruct((BIAS_ROWS, PAIR_FEATURES), BF16),
    ]
    return pl.pallas_call(
        functools.partial(prepare_kernel, i_n, j_n),
        in_specs=[in_vmem()] * 2,
        out_specs=[in_vmem()] * len(shapes),
        out_shape=shapes,
        scratch_shapes=[pltpu.VMEM(g.shape, F32)],
        compiler_params=params(16),
        cost_estimate=pl.CostEstimate(
            flops=2 * pairs * channels * PAIR_FEATURES,
            bytes_accessed=4 * pairs * channels,
            transcendentals=0,
        ),
    )(we, g)


def join(pieces, axis, held):
    depth = pieces[0].shape[0] // 2
    me = lax.axis_index(axis)
    for p, piece in enumerate(pieces):
        block = piece[...].astype(F32)
        for n in range(2):
            place = lax.bitwise_xor(me, 2 * p + n) * depth
            held[pl.ds(pl.multiple_of(place, depth), depth), :] = block[n * depth : (n + 1) * depth]


def repeat_matrix(sequences):
    shape = (sequences, GROUP * sequences)
    lane = lax.broadcasted_iota(jnp.int32, shape, 1)
    row = lax.broadcasted_iota(jnp.int32, shape, 0)
    return (lax.rem(lane, sequences) == row).astype(BF16)


def tile_count(sequences):
    return GROUP * sequences // LANES, max(1, sequences // LANES)


def spread(held, wide):
    repeated = repeat_matrix(held.shape[0])[:, : wide.shape[0] * LANES]
    both = dot(held[...].T.astype(BF16), repeated)
    for l in range(wide.shape[0]):
        wide[l] = both[:, l * LANES : (l + 1) * LANES]


def tiles_of(sequences, tile):
    lane = lax.broadcasted_iota(jnp.int32, (1, LANES), 1) + tile * LANES
    return [
        (m, lax.div(lane, sequences) == m)
        for m in range(GROUP)
        if m * sequences < (tile + 1) * LANES and (m + 1) * sequences > tile * LANES
    ]


def chunks(body):
    if CHUNKS == 1:
        body(0)
    else:
        pl.loop(0, CHUNKS)(body)


def diagonal_of(wide, channel, positions, sequences):
    columns = []
    blocks = [
        wide[l, pl.ds(channel, positions, stride=PROJECTED_DEPTH), :].astype(BF16)
        for l in range(wide.shape[0])
    ]
    for l in range(tile_count(sequences)[0]):
        block = blocks[l % len(blocks)]
        members = dict(tiles_of(sequences, l))
        columns.append(
            jnp.concatenate(
                [
                    block * members[m].astype(F32).astype(BF16)
                    if m in members
                    else jnp.zeros(block.shape, BF16)
                    for m in range(GROUP)
                ],
                axis=0,
            )
        )
    return jnp.concatenate(columns, axis=1)


def alone(count):
    return lambda me: ([me], [[lax.bitwise_xor(me, d)] for d in range(1, count)])


def in_pairs(count):
    def plan(me):
        evens = range(0, count, 2)
        return [lax.bitwise_xor(me, d) for d in evens], [
            [lax.bitwise_xor(me, d + 1) for d in evens]
        ]

    return plan


def outer_kernel(i_n, j_n, *refs):
    depth = PROJECTED_DEPTH
    row_n = lax.axis_size("row")
    halves = [lax.axis_size("col") // 2, row_n // 2]
    a_pieces, refs = refs[: halves[0]], refs[halves[0] :]
    b_pieces, refs = refs[: halves[1]], refs[halves[1] :]
    g_ref, bias_ref, x_ref, a_held, b_wide = refs[:5]
    messages, (b_held, left, total) = refs[5 : 5 + row_n], refs[5 + row_n :]
    sequences = a_held.shape[0]
    groups = i_n // GROUP
    per_step = depth // CHUNKS
    span = GROUP * j_n

    join(a_pieces, "col", a_held)
    join(b_pieces, "row", b_held)
    spread(b_held, b_wide)
    turned = a_held[...].T.astype(BF16)
    shape = (sequences, GROUP * sequences)
    shifted = lax.broadcasted_iota(jnp.int32, shape, 1) - lax.broadcasted_iota(jnp.int32, shape, 0)
    value = jnp.zeros(left.shape, F32)
    for m in range(GROUP):
        rows = [
            turned[(k * GROUP + m) * depth : (k * GROUP + m + 1) * depth, :] for k in range(groups)
        ]
        value += dot(jnp.concatenate(rows, axis=0), (shifted == m * sequences).astype(BF16))
    left[...] = value.astype(BF16)

    @chunks
    def _(t):
        size = per_step * depth
        rows = pl.ds(t * size if CHUNKS == 1 else pl.multiple_of(t * size, size), size)
        x_part = x_ref.at[rows]
        for e in range(0, per_step, 2):
            right = [diagonal_of(b_wide, t * per_step + e + n, j_n, sequences) for n in range(2)]
            product = dot(
                left[...], jnp.concatenate(right, axis=0), ROWS_BY_ROWS
            ).astype(BF16)
            for n in range(2):
                for k in range(groups):
                    x_part[(e + n) * depth : (e + n + 1) * depth, k * span : (k + 1) * span] = product[
                        k * depth : (k + 1) * depth, n * span : (n + 1) * span
                    ]
        total[rows, :] = dot(x_part[...], g_ref[...])

    share = total.shape[0] // row_n
    me = lax.axis_index("row")
    for p, message in enumerate(messages):
        part = pl.ds(pl.multiple_of(lax.bitwise_xor(me, p) * share, share), share)
        message[0:share, :] = total[part, :].astype(message.dtype)
        message[share:, :] = bias_ref[...].astype(message.dtype)


def outer(a_pieces, b_pieces, g, bias_rows, i_n, j_n, sequences):
    row_n = lax.axis_size("row")
    depth = PROJECTED_DEPTH
    channels = depth * depth
    pairs = i_n * j_n
    tiles = tile_count(sequences)[1]
    operands = [*a_pieces, *b_pieces, g, bias_rows]
    shapes = [jax.ShapeDtypeStruct((channels, pairs), BF16)]
    shapes += [
        jax.ShapeDtypeStruct((sequences, i_n * depth), F32),
        jax.ShapeDtypeStruct((tiles, j_n * depth, LANES), F32),
    ]
    shapes += [
        jax.ShapeDtypeStruct((channels // row_n + BIAS_ROWS, LANES), BF16 if p else F32)
        for p in range(row_n)
    ]
    results = pl.pallas_call(
        functools.partial(outer_kernel, i_n, j_n),
        in_specs=[in_vmem()] * len(operands),
        out_specs=[in_vmem()] * len(shapes),
        out_shape=shapes,
        scratch_shapes=[
            pltpu.VMEM((sequences, j_n * depth), F32),
            pltpu.VMEM((i_n // GROUP * depth, GROUP * sequences), BF16),
            pltpu.VMEM((channels, PAIR_FEATURES), F32),
        ],
        compiler_params=params(sequences),
        cost_estimate=pl.CostEstimate(
            flops=4 * pairs * channels * PAIR_FEATURES,
            bytes_accessed=2 * pairs * channels,
            transcendentals=0,
        ),
    )(*operands)
    return *results[:3], results[3:]


def gradient_kernel(axis, plan, kept, positions, others, sequences, *refs):
    depth = PROJECTED_DEPTH
    wide, source = refs[:2]
    outs, (result, grown, grad) = refs[3:-3], refs[-3:]
    parts = lax.axis_size(axis)
    per_step = depth // CHUNKS
    span = GROUP * others

    result[...] = jnp.zeros(result.shape, F32)

    @chunks
    def _(t):
        size = per_step * depth
        rows = pl.ds(t * size if CHUNKS == 1 else pl.multiple_of(t * size, size), size)
        part = source.at[rows]
        for n in range(0, per_step, 2):
            blocks = [
                jnp.concatenate(
                    [
                        part[m * depth : (m + 1) * depth, k * span : (k + 1) * span]
                        for m in (n, n + 1)
                    ],
                    axis=1,
                )
                for k in range(positions // GROUP)
            ]
            right = [
                diagonal_of(wide, t * per_step + m, others, sequences) for m in (n, n + 1)
            ]
            result[...] += dot(jnp.concatenate(blocks, axis=0), jnp.concatenate(right, axis=0))

    scaled = (result[...] * (1.0 / sequences)).astype(BF16)
    for l in range(scaled.shape[1] // LANES):
        members = dict(tiles_of(sequences, l))
        for k in range(positions // GROUP):
            block = scaled[k * depth : (k + 1) * depth, l * LANES : (l + 1) * LANES]
            for m in range(GROUP):
                start = (k * GROUP + m) * depth
                grown[start : start + depth, l * LANES : (l + 1) * LANES] = (
                    block * members[m].astype(F32).astype(BF16)
                    if m in members
                    else jnp.zeros((depth, LANES), BF16)
                )
    grad[...] = dot(repeat_matrix(sequences), grown[...], ROWS_BY_ROWS)
    share = sequences // parts

    def rows_of(p):
        mine = grad[pl.ds(pl.multiple_of(p * share, share), share), :]
        return jnp.concatenate(
            [mine[:, l * LANES : (l + 1) * LANES] for l in range(mine.shape[1] // LANES)], axis=0
        )

    stay, go = plan(lax.axis_index(axis))
    for p, out in zip(stay, outs[:kept], strict=True):
        out[...] = rows_of(p)
    for group, out in zip(go, outs[kept:], strict=True):
        size = out.shape[0] // len(group)
        for n, p in enumerate(group):
            out[n * size : (n + 1) * size, :] = rows_of(p).astype(BF16)


def gradient(wide, source, after, axis, plan, kept, groups, positions, others, sequences):
    depth = PROJECTED_DEPTH
    parts = lax.axis_size(axis)
    rows = sequences // parts * positions * depth // LANES
    shapes = [jax.ShapeDtypeStruct((rows, LANES), F32)] * kept
    group = (parts - kept) // groups
    shapes += [jax.ShapeDtypeStruct((group * rows, LANES), BF16)] * groups
    results = pl.pallas_call(
        functools.partial(gradient_kernel, axis, plan, kept, positions, others, sequences),
        in_specs=[in_vmem(), in_vmem(), pl.BlockSpec(memory_space=pl.ANY)],
        out_specs=[in_vmem()] * len(shapes),
        out_shape=shapes,
        scratch_shapes=[
            pltpu.VMEM((positions // GROUP * depth, GROUP * sequences), F32),
            pltpu.VMEM((positions * depth, GROUP * sequences), BF16),
            pltpu.VMEM((sequences, positions * depth), F32),
        ],
        compiler_params=params(sequences),
        cost_estimate=pl.CostEstimate(
            flops=2 * source.size * PAIR_FEATURES,
            bytes_accessed=2 * source.size,
            transcendentals=0,
        ),
    )(wide, source, after)
    return results[:kept], results[kept:]


def product_kernel(left_ref, right_ref, held, _, out_ref, wide):
    spread(held, wide)
    multiply(left_ref, right_ref, out_ref)


def product(left, right, held, after):
    shape = (left.shape[0], right.shape[0])
    spread_shape = (tile_count(held.shape[0])[1], held.shape[1], LANES)
    return pl.pallas_call(
        product_kernel,
        in_specs=[in_vmem()] * 3 + [pl.BlockSpec(memory_space=pl.ANY)],
        out_specs=[in_vmem()] * 2,
        out_shape=[jax.ShapeDtypeStruct(shape, BF16), jax.ShapeDtypeStruct(spread_shape, F32)],
        compiler_params=params(32),
        cost_estimate=pl.CostEstimate(
            flops=2 * shape[0] * shape[1] * left.shape[1],
            bytes_accessed=4 * shape[0] * shape[1],
            transcendentals=0,
        ),
    )(left, right, held, after)


def pair_kernel(sequences, x_ref, wt_ref, bias_ref, _, out_ref):
    product = dot(wt_ref[...], x_ref[...])
    out_ref[...] = (product.T * (1.0 / sequences) + bias_ref[...]).astype(BF16)


def pair(x, wt, output_bias, after, sequences):
    channels, pairs = x.shape
    count = 3
    size = pairs // count
    return pl.pallas_call(
        functools.partial(pair_kernel, sequences),
        grid=(count,),
        in_specs=[
            pl.BlockSpec((channels, size), lambda t: (0, t)),
            whole(wt.shape),
            whole((1, PAIR_FEATURES)),
            pl.BlockSpec(memory_space=pl.ANY),
        ],
        out_specs=pl.BlockSpec((size, PAIR_FEATURES), lambda t: (t, 0)),
        out_shape=jax.ShapeDtypeStruct((pairs, PAIR_FEATURES), BF16),
        compiler_params=params(),
        cost_estimate=pl.CostEstimate(
            flops=4 * pairs * channels * PAIR_FEATURES,
            bytes_accessed=2 * pairs * channels,
            transcendentals=0,
        ),
    )(x, wt, output_bias.reshape(1, PAIR_FEATURES), after)


def unfold(total, share, out):
    for l in range(out.shape[1] // LANES):
        out[:, l * LANES : (l + 1) * LANES] = total[l * share : (l + 1) * share, :]


def call(kernel, operands, shapes, after=(), scratch=()):
    specs = [in_vmem()] * len(operands) + [pl.BlockSpec(memory_space=pl.ANY)] * len(after)
    return pl.pallas_call(
        kernel,
        in_specs=specs,
        out_specs=[in_vmem()] * len(shapes),
        out_shape=[jax.ShapeDtypeStruct(shape, kind) for shape, kind in shapes],
        scratch_shapes=scratch,
        compiler_params=params(),
    )(*operands, *after)


def partners(count):
    return [0, *range(count - 1, 0, -1)]


def row_sum(parts, after, share):
    count = len(parts)

    def kernel(*refs):
        parts, (_, message, held) = refs[:count], refs[count:]
        me = lax.axis_index("row")
        total = parts[0][0:share, :]
        for p, part in zip(partners(count), parts, strict=True):
            held[lax.bitwise_xor(me, p)] = part[share:, :].astype(F32)
            if p > 0:
                total += part[0:share, :].astype(F32)
        bias = joined(held[0])
        for n in range(1, count):
            bias += joined(held[n])
        message[0:share, :] = total.astype(BF16)
        message[share:, :] = split(bias)

    scratch = [pltpu.VMEM((count, BIAS_ROWS, LANES), F32)]
    (message,) = call(kernel, parts, [((share + BIAS_ROWS, LANES), BF16)], [after], scratch)
    return message


def pair_sum(kept, near, after):
    def kernel(*refs):
        kept, near, (own, *messages) = refs[:count], refs[count], refs[count + 2 :]
        size = own.shape[0]
        for p, part in enumerate(kept):
            both = part[...] + near[p * size : (p + 1) * size, :].astype(F32)
            if p == 0:
                own[...] = both
            else:
                messages[p - 1][...] = both.astype(BF16)

    count = len(kept)
    shapes = [(kept[0].shape, F32)] + [(kept[0].shape, BF16)] * (count - 1)
    own, *messages = call(kernel, [*kept, near], shapes, [after])
    return own, messages


def column_pair_sum(own, near, after, share):
    def kernel(own, near, _, message):
        total = own[0:share, :].astype(F32) + near[0:share, :].astype(F32)
        message[0:share, :] = total.astype(BF16)
        message[share:, :] = split(joined(own[share:, :]) + joined(near[share:, :]))

    (message,) = call(kernel, [own, near], [(own.shape, BF16)], [after])
    return message


def column_sum(parts, grads, share):
    rows = share + BIAS_ROWS
    count, sent = len(parts), len(grads)

    def kernel(*refs):
        parts, grads, refs = refs[:count], refs[count : count + sent], refs[count + sent :]
        messages, (piece_out, bias_out, held, by_e, by_c) = refs[:sent], refs[sent:]
        home = lax.div(lax.axis_index("col"), 2)
        for p, part in enumerate(parts):
            held[lax.bitwise_xor(home, p)] = part[...]
        total, bias = held[0, 0:share, :].astype(F32), joined(held[0, share:, :])
        for n in range(1, count):
            total += held[n, 0:share, :].astype(F32)
            bias += joined(held[n, share:, :])
        by_e[...] = total
        depth = PROJECTED_DEPTH
        width = share // depth
        for c in range(depth):
            by_c[c * width : (c + 1) * width, :] = by_e[pl.ds(c, width, stride=depth), :]
        piece = by_c[...].astype(BF16)
        piece_out[...] = piece
        for message, grad in zip(messages, grads, strict=True):
            message[0:share, :] = piece
            message[share:, :] = grad[...]
        bias_out[...] = jnp.broadcast_to(bias, bias_out.shape)

    shapes = [((share + grad.shape[0], LANES), BF16) for grad in grads]
    shapes += [((share, LANES), BF16), ((8, LANES), F32)]
    scratch = [pltpu.VMEM((count, rows, LANES), BF16)] + [pltpu.VMEM((share, LANES), F32)] * 2
    *messages, piece, bias = call(kernel, [*parts, *grads], shapes, scratch=scratch)
    return messages, piece, bias


def finish(pieces, left, right_own, bias, left_shape, right_shape, scale, bias_scale):
    count, left_n = len(pieces), len(left)
    share = pieces[0].shape[0]

    def kernel(*refs):
        pieces, left, refs = refs[:count], refs[count : count + left_n], refs[count + left_n :]
        right_own, bias, projection, left_out, right_out, bias_out = refs
        me = lax.axis_index("row")
        right_total = right_own[...]
        depth = PROJECTED_DEPTH
        width = share // depth
        for p, piece in zip(partners(count), pieces, strict=True):
            block = piece[0:share, :].astype(F32) * scale
            for c in range(depth):
                start = c * depth + pl.multiple_of(lax.bitwise_xor(me, p) * width, width)
                projection[pl.ds(start, width), :] = block[c * width : (c + 1) * width]
            if p > 0:
                right_total += piece[share:, :].astype(F32)
        left_total = left[0][...]
        for term in left[1:]:
            left_total += term[...].astype(F32)
        unfold(left_total, left_out.shape[0], left_out)
        unfold(right_total, right_out.shape[0], right_out)
        bias_out[...] = bias[0:1, :] * bias_scale

    shapes = [
        ((count * share, PAIR_FEATURES), F32),
        (left_shape, F32),
        (right_shape, F32),
        ((1, PAIR_FEATURES), F32),
    ]
    return call(kernel, [*pieces, *left, right_own, bias], shapes)


def swap(x, axis, p):
    return lax.ppermute(x, axis, [(n, n ^ p) for n in range(lax.axis_size(axis))])


def swap_each(parts, axis, step=1):
    count = len(parts)
    return [swap(parts[n - 1], axis, n * step) for n in range(count, 0, -1)][::-1]


def from_evens(x, axis):
    return swap_each([x] * (lax.axis_size(axis) // 2 - 1), axis, 2)


def local(
    first_homolog_features, second_homolog_features, final_projection_matrix, output_bias, cotangent
):
    i_n, j_n, _ = cotangent.shape
    row_n, col_n = lax.axis_size("row"), lax.axis_size("col")
    sequences = second_homolog_features.shape[0] * row_n
    channels = final_projection_matrix.shape[0]
    res_total = i_n * row_n
    a_near = swap(first_homolog_features, "col", 1)
    b_near = swap(second_homolog_features, "row", 1)
    we, wt, a, b, w, g = load(
        first_homolog_features,
        second_homolog_features,
        final_projection_matrix,
        cotangent.reshape(i_n * j_n, PAIR_FEATURES),
    )
    a, b = stack([a, a_near], [b, b_near])
    a_pieces = [a] + from_evens(a, "col")
    b_pieces = [b] + from_evens(b, "row")
    y, gt, bias_rows = prepare(we, g, i_n, j_n)

    x, a_held, b_wide, (own, *messages) = outer(
        a_pieces, b_pieces, g, bias_rows, i_n, j_n, sequences
    )
    share = channels // row_n

    parts = [own] + swap_each(messages, "row")[::-1]
    left_kept, (message,) = gradient(
        b_wide, y, own, "col", in_pairs(col_n), col_n // 2, 1, i_n, j_n, sequences
    )
    left_near = swap(message, "col", 1)

    message = row_sum(parts, message, share)
    near = swap(message, "col", 1)
    left_own, left_messages = pair_sum(left_kept, left_near, message)
    left = [left_own] + swap_each(left_messages, "col", 2)
    y2, a_wide = product(w, gt, a_held, left_own)

    message = column_pair_sum(message, near, y2, share)
    parts = [message] + from_evens(message, "col")
    (right_own,), right_sent = gradient(
        a_wide, y2, message, "row", alone(row_n), 1, row_n - 1, j_n, i_n, sequences
    )

    messages, piece, bias = column_sum(parts, right_sent, share)
    pieces = [piece] + swap_each(messages, "row")[::-1]
    pair_map = pair(x, wt, output_bias, piece, sequences)
    projection, left_grad, right_grad, bias_grad = finish(
        pieces,
        left,
        right_own,
        bias,
        first_homolog_features.shape,
        second_homolog_features.shape,
        1.0 / (sequences * res_total),
        1.0 / res_total,
    )
    return (
        pair_map.reshape(i_n, j_n, PAIR_FEATURES),
        left_grad,
        right_grad,
        projection,
        bias_grad.reshape(PAIR_FEATURES),
    )


def solution(mesh):
    return jax.shard_map(
        local,
        mesh=mesh,
        in_specs=(
            P(("dp", "col"), "row"),
            P(("dp", "row"), "col"),
            P(),
            P(),
            P(("dp", "row"), "col", None),
        ),
        out_specs=(
            P(("dp", "row"), "col", None),
            P(("dp", "col"), "row"),
            P(("dp", "row"), "col"),
            P("dp", None),
            P("dp"),
        ),
        check_vma=False,
    )
```

```python
import functools

import jax
import jax.numpy as jnp
from jax import lax
from jax.experimental import pallas as pl
from jax.experimental.pallas import tpu as pltpu
from jax.sharding import PartitionSpec as P

PROJECTED_DEPTH = 32
PAIR_FEATURES = 128
GROUP = 8
MULTIPLY_ROWS = 384
CHUNKS = 2
BIAS_ROWS = 16
LANES = 128
F32 = jnp.float32
BF16 = jnp.bfloat16
MIB = 1024 * 1024

ROWS_BY_ROWS = (((1,), (1,)), ((), ()))
COLS_BY_COLS = (((0,), (0,)), ((), ()))


def params(sequences=0):
    return pltpu.CompilerParams(vmem_limit_bytes=min(10 + 10 * sequences // 32, 50) * MIB + 2 * MIB)


def whole(shape):
    return pl.BlockSpec(shape, lambda t: (0,) * len(shape))


def dot(x, y, dims=(((1,), (0,)), ((), ()))):
    return lax.dot_general(x, y, dims, preferred_element_type=F32)


def load_kernel(a_hbm, b_hbm, w_hbm, g_hbm, we_ref, wt_ref, a_ref, b_ref, w_ref, g_ref, w32, sems):
    depth = PROJECTED_DEPTH
    copies = [
        pltpu.make_async_copy(source, target, sems.at[n])
        for n, (source, target) in enumerate(
            [(w_hbm, w_ref), (g_hbm, g_ref), (a_hbm, a_ref), (b_hbm, b_ref)]
        )
    ]
    for copy in copies:
        copy.start()
    copies[0].wait()
    w32[...] = w_ref[...].astype(F32)
    for e in range(depth):
        block = w32[pl.ds(e, depth, stride=depth), :]
        we_ref[e * depth : (e + 1) * depth, :] = block.astype(BF16)
    wt_ref[...] = we_ref[...].astype(F32).T.astype(BF16)
    for copy in copies[1:]:
        copy.wait()


def in_vmem():
    return pl.BlockSpec(memory_space=pltpu.VMEM)


def load(a, b, w, g):
    shapes = [
        jax.ShapeDtypeStruct(w.shape, BF16),
        jax.ShapeDtypeStruct(w.shape[::-1], BF16),
        *[jax.ShapeDtypeStruct(x.shape, BF16) for x in (a, b, w, g)],
    ]
    return pl.pallas_call(
        load_kernel,
        in_specs=[pl.BlockSpec(memory_space=pltpu.HBM)] * 4,
        out_specs=[in_vmem()] * len(shapes),
        out_shape=shapes,
        scratch_shapes=[pltpu.VMEM(w.shape, F32), pltpu.SemaphoreType.DMA((4,))],
        compiler_params=params(),
        cost_estimate=pl.CostEstimate(
            flops=1000 * w.size, bytes_accessed=16 * w.size, transcendentals=0
        ),
    )(*[pltpu.with_memory_space_constraint(x, pltpu.HBM) for x in (a, b, w, g)])


def stack(*groups):
    def kernel(*refs):
        refs, outs = refs[: -len(groups)], refs[-len(groups) :]
        for group, out in zip(groups, outs, strict=True):
            blocks = [ref[...].astype(F32) for ref in refs[: len(group)]]
            refs = refs[len(group) :]
            out[...] = jnp.concatenate(blocks, axis=0).astype(BF16)

    shapes = [((len(group) * group[0].shape[0], group[0].shape[1]), BF16) for group in groups]
    return call(kernel, [x for group in groups for x in group], shapes)


def split(total):
    high = total.astype(BF16).astype(F32)
    row = lax.broadcasted_iota(jnp.int32, (BIAS_ROWS, PAIR_FEATURES), 0)
    return jnp.where(row == 0, high, jnp.where(row == 1, total - high, 0.0)).astype(BF16)


def joined(block):
    block = block.astype(F32)
    return block[0:1] + block[1:2]


def multiply(left_ref, right_ref, out_ref):
    for n in range(0, right_ref.shape[0], MULTIPLY_ROWS):
        rows = slice(n, n + MULTIPLY_ROWS)
        out_ref[:, rows] = dot(left_ref[...], right_ref[rows, :], ROWS_BY_ROWS).astype(BF16)


def prepare_kernel(i_n, j_n, we_ref, g_ref, y_ref, gt_ref, bias_ref, g32):
    g32[...] = g_ref[...].astype(F32)
    bias_ref[...] = split(jnp.sum(g32[...], axis=0, keepdims=True))
    multiply(we_ref, g_ref, y_ref)

    for j in range(j_n):
        gt_ref[j * i_n : (j + 1) * i_n, :] = g32[pl.ds(j, i_n, stride=j_n), :].astype(BF16)


def prepare(we, g, i_n, j_n):
    pairs = i_n * j_n
    channels = we.shape[0]
    shapes = [
        jax.ShapeDtypeStruct((channels, pairs), BF16),
        jax.ShapeDtypeStruct(g.shape, BF16),
        jax.ShapeDtypeStruct((BIAS_ROWS, PAIR_FEATURES), BF16),
    ]
    return pl.pallas_call(
        functools.partial(prepare_kernel, i_n, j_n),
        in_specs=[in_vmem()] * 2,
        out_specs=[in_vmem()] * len(shapes),
        out_shape=shapes,
        scratch_shapes=[pltpu.VMEM(g.shape, F32)],
        compiler_params=params(16),
        cost_estimate=pl.CostEstimate(
            flops=2 * pairs * channels * PAIR_FEATURES,
            bytes_accessed=4 * pairs * channels,
            transcendentals=0,
        ),
    )(we, g)


def join(pieces, axis, held):
    depth = pieces[0].shape[0] // 2
    me = lax.axis_index(axis)
    for p, piece in enumerate(pieces):
        block = piece[...].astype(F32)
        for n in range(2):
            place = lax.bitwise_xor(me, 2 * p + n) * depth
            held[pl.ds(pl.multiple_of(place, depth), depth), :] = block[n * depth : (n + 1) * depth]


def repeat_matrix(sequences):
    shape = (sequences, GROUP * sequences)
    lane = lax.broadcasted_iota(jnp.int32, shape, 1)
    row = lax.broadcasted_iota(jnp.int32, shape, 0)
    return (lax.rem(lane, sequences) == row).astype(BF16)


def tile_count(sequences):
    return GROUP * sequences // LANES, max(1, sequences // LANES)


def spread(held, wide):
    repeated = repeat_matrix(held.shape[0])[:, : wide.shape[0] * LANES]
    both = dot(held[...].T.astype(BF16), repeated)
    for l in range(wide.shape[0]):
        wide[l] = both[:, l * LANES : (l + 1) * LANES]


def tiles_of(sequences, tile):
    lane = lax.broadcasted_iota(jnp.int32, (1, LANES), 1) + tile * LANES
    return [
        (m, lax.div(lane, sequences) == m)
        for m in range(GROUP)
        if m * sequences < (tile + 1) * LANES and (m + 1) * sequences > tile * LANES
    ]


def chunks(body):
    if CHUNKS == 1:
        body(0)
    else:
        pl.loop(0, CHUNKS)(body)


def diagonal_of(wide, channel, positions, sequences):
    columns = []
    blocks = [
        wide[l, pl.ds(channel, positions, stride=PROJECTED_DEPTH), :].astype(BF16)
        for l in range(wide.shape[0])
    ]
    for l in range(tile_count(sequences)[0]):
        block = blocks[l % len(blocks)]
        members = dict(tiles_of(sequences, l))
        columns.append(
            jnp.concatenate(
                [
                    block * members[m].astype(F32).astype(BF16)
                    if m in members
                    else jnp.zeros(block.shape, BF16)
                    for m in range(GROUP)
                ],
                axis=0,
            )
        )
    return jnp.concatenate(columns, axis=1)


def alone(count):
    return lambda me: ([me], [[lax.bitwise_xor(me, d)] for d in range(1, count)])


def in_pairs(count):
    def plan(me):
        evens = range(0, count, 2)
        return [lax.bitwise_xor(me, d) for d in evens], [
            [lax.bitwise_xor(me, d + 1) for d in evens]
        ]

    return plan


def outer_kernel(i_n, j_n, *refs):
    depth = PROJECTED_DEPTH
    row_n = lax.axis_size("row")
    halves = [lax.axis_size("col") // 2, row_n // 2]
    a_pieces, refs = refs[: halves[0]], refs[halves[0] :]
    b_pieces, refs = refs[: halves[1]], refs[halves[1] :]
    g_ref, bias_ref, x_ref, a_held, b_wide = refs[:5]
    messages, (b_held, left, total) = refs[5 : 5 + row_n], refs[5 + row_n :]
    sequences = a_held.shape[0]
    groups = i_n // GROUP
    per_step = depth // CHUNKS
    span = GROUP * j_n

    join(a_pieces, "col", a_held)
    join(b_pieces, "row", b_held)
    spread(b_held, b_wide)
    turned = a_held[...].T.astype(BF16)
    shape = (sequences, GROUP * sequences)
    shifted = lax.broadcasted_iota(jnp.int32, shape, 1) - lax.broadcasted_iota(jnp.int32, shape, 0)
    value = jnp.zeros(left.shape, F32)
    for m in range(GROUP):
        rows = [
            turned[(k * GROUP + m) * depth : (k * GROUP + m + 1) * depth, :] for k in range(groups)
        ]
        value += dot(jnp.concatenate(rows, axis=0), (shifted == m * sequences).astype(BF16))
    left[...] = value.astype(BF16)

    @chunks
    def _(t):
        size = per_step * depth
        rows = pl.ds(t * size if CHUNKS == 1 else pl.multiple_of(t * size, size), size)
        x_part = x_ref.at[rows]
        for e in range(0, per_step, 2):
            right = [diagonal_of(b_wide, t * per_step + e + n, j_n, sequences) for n in range(2)]
            product = dot(
                left[...], jnp.concatenate(right, axis=0), ROWS_BY_ROWS
            ).astype(BF16)
            for n in range(2):
                for k in range(groups):
                    x_part[(e + n) * depth : (e + n + 1) * depth, k * span : (k + 1) * span] = product[
                        k * depth : (k + 1) * depth, n * span : (n + 1) * span
                    ]
        total[rows, :] = dot(x_part[...], g_ref[...])

    share = total.shape[0] // row_n
    me = lax.axis_index("row")
    for p, message in enumerate(messages):
        part = pl.ds(pl.multiple_of(lax.bitwise_xor(me, p) * share, share), share)
        message[0:share, :] = total[part, :].astype(message.dtype)
        message[share:, :] = bias_ref[...].astype(message.dtype)


def outer(a_pieces, b_pieces, g, bias_rows, i_n, j_n, sequences):
    row_n = lax.axis_size("row")
    depth = PROJECTED_DEPTH
    channels = depth * depth
    pairs = i_n * j_n
    tiles = tile_count(sequences)[1]
    operands = [*a_pieces, *b_pieces, g, bias_rows]
    shapes = [jax.ShapeDtypeStruct((channels, pairs), BF16)]
    shapes += [
        jax.ShapeDtypeStruct((sequences, i_n * depth), F32),
        jax.ShapeDtypeStruct((tiles, j_n * depth, LANES), F32),
    ]
    shapes += [
        jax.ShapeDtypeStruct((channels // row_n + BIAS_ROWS, LANES), BF16 if p else F32)
        for p in range(row_n)
    ]
    results = pl.pallas_call(
        functools.partial(outer_kernel, i_n, j_n),
        in_specs=[in_vmem()] * len(operands),
        out_specs=[in_vmem()] * len(shapes),
        out_shape=shapes,
        scratch_shapes=[
            pltpu.VMEM((sequences, j_n * depth), F32),
            pltpu.VMEM((i_n // GROUP * depth, GROUP * sequences), BF16),
            pltpu.VMEM((channels, PAIR_FEATURES), F32),
        ],
        compiler_params=params(sequences),
        cost_estimate=pl.CostEstimate(
            flops=4 * pairs * channels * PAIR_FEATURES,
            bytes_accessed=2 * pairs * channels,
            transcendentals=0,
        ),
    )(*operands)
    return *results[:3], results[3:]


def add_channels(wide, source, result, steps, positions, others, sequences):
    depth = PROJECTED_DEPTH
    per_step = depth // CHUNKS
    span = GROUP * others

    def step(t):
        size = per_step * depth
        part = source.at[pl.ds(t * size if len(steps) == 1 else pl.multiple_of(t * size, size), size)]
        for n in range(0, per_step, 2):
            blocks = [
                jnp.concatenate(
                    [
                        part[m * depth : (m + 1) * depth, k * span : (k + 1) * span]
                        for m in (n, n + 1)
                    ],
                    axis=1,
                )
                for k in range(positions // GROUP)
            ]
            right = [
                diagonal_of(wide, t * per_step + m, others, sequences) for m in (n, n + 1)
            ]
            result[...] += dot(jnp.concatenate(blocks, axis=0), jnp.concatenate(right, axis=0))

    if len(steps) == 1:
        step(steps[0])
    else:
        pl.loop(steps[0], steps[-1] + 1)(step)


def gradient_start_kernel(positions, others, sequences, wide, source, result):
    result[...] = jnp.zeros(result.shape, F32)
    steps = range(CHUNKS // 2)
    add_channels(wide, source, result, steps, positions, others, sequences)


def gradient_start(wide, source, positions, others, sequences):
    shape = (positions // GROUP * PROJECTED_DEPTH, GROUP * sequences)
    return pl.pallas_call(
        functools.partial(gradient_start_kernel, positions, others, sequences),
        in_specs=[in_vmem()] * 2,
        out_specs=in_vmem(),
        out_shape=jax.ShapeDtypeStruct(shape, F32),
        compiler_params=params(sequences),
        cost_estimate=pl.CostEstimate(
            flops=source.size * PAIR_FEATURES, bytes_accessed=source.size, transcendentals=0
        ),
    )(wide, source)


def gradient_kernel(axis, plan, kept, positions, others, sequences, started, *refs):
    depth = PROJECTED_DEPTH
    wide, source = refs[:2]
    outs, (result, grown, grad) = refs[3 + started : -3], refs[-3:]
    parts = lax.axis_size(axis)
    result[...] = refs[3][...] if started else jnp.zeros(result.shape, F32)
    steps = range(CHUNKS // 2 if started else 0, CHUNKS)
    add_channels(wide, source, result, steps, positions, others, sequences)

    scaled = (result[...] * (1.0 / sequences)).astype(BF16)
    for l in range(scaled.shape[1] // LANES):
        members = dict(tiles_of(sequences, l))
        for k in range(positions // GROUP):
            block = scaled[k * depth : (k + 1) * depth, l * LANES : (l + 1) * LANES]
            for m in range(GROUP):
                start = (k * GROUP + m) * depth
                grown[start : start + depth, l * LANES : (l + 1) * LANES] = (
                    block * members[m].astype(F32).astype(BF16)
                    if m in members
                    else jnp.zeros((depth, LANES), BF16)
                )
    grad[...] = dot(repeat_matrix(sequences), grown[...], ROWS_BY_ROWS)
    share = sequences // parts

    def rows_of(p):
        mine = grad[pl.ds(pl.multiple_of(p * share, share), share), :]
        return jnp.concatenate(
            [mine[:, l * LANES : (l + 1) * LANES] for l in range(mine.shape[1] // LANES)], axis=0
        )

    stay, go = plan(lax.axis_index(axis))
    for p, out in zip(stay, outs[:kept], strict=True):
        out[...] = rows_of(p)
    for group, out in zip(go, outs[kept:], strict=True):
        size = out.shape[0] // len(group)
        for n, p in enumerate(group):
            out[n * size : (n + 1) * size, :] = rows_of(p).astype(BF16)


def gradient(
    wide, source, after, axis, plan, kept, groups, positions, others, sequences, before=()
):
    depth = PROJECTED_DEPTH
    parts = lax.axis_size(axis)
    rows = sequences // parts * positions * depth // LANES
    shapes = [jax.ShapeDtypeStruct((rows, LANES), F32)] * kept
    group = (parts - kept) // groups
    shapes += [jax.ShapeDtypeStruct((group * rows, LANES), BF16)] * groups
    results = pl.pallas_call(
        functools.partial(
            gradient_kernel, axis, plan, kept, positions, others, sequences, len(before)
        ),
        in_specs=[in_vmem(), in_vmem(), pl.BlockSpec(memory_space=pl.ANY)]
        + [in_vmem()] * len(before),
        out_specs=[in_vmem()] * len(shapes),
        out_shape=shapes,
        scratch_shapes=[
            pltpu.VMEM((positions // GROUP * depth, GROUP * sequences), F32),
            pltpu.VMEM((positions * depth, GROUP * sequences), BF16),
            pltpu.VMEM((sequences, positions * depth), F32),
        ],
        compiler_params=params(sequences),
        cost_estimate=pl.CostEstimate(
            flops=2 * source.size * PAIR_FEATURES,
            bytes_accessed=2 * source.size,
            transcendentals=0,
        ),
    )(wide, source, after, *before)
    return results[:kept], results[kept:]


def product_kernel(left_ref, right_ref, held, _, out_ref, wide):
    spread(held, wide)
    multiply(left_ref, right_ref, out_ref)


def product(left, right, held, after):
    shape = (left.shape[0], right.shape[0])
    spread_shape = (tile_count(held.shape[0])[1], held.shape[1], LANES)
    return pl.pallas_call(
        product_kernel,
        in_specs=[in_vmem()] * 3 + [pl.BlockSpec(memory_space=pl.ANY)],
        out_specs=[in_vmem()] * 2,
        out_shape=[jax.ShapeDtypeStruct(shape, BF16), jax.ShapeDtypeStruct(spread_shape, F32)],
        compiler_params=params(32),
        cost_estimate=pl.CostEstimate(
            flops=2 * shape[0] * shape[1] * left.shape[1],
            bytes_accessed=4 * shape[0] * shape[1],
            transcendentals=0,
        ),
    )(left, right, held, after)


def pair_kernel(sequences, x_ref, wt_ref, bias_ref, _, out_ref):
    product = dot(wt_ref[...], x_ref[...])
    out_ref[...] = (product.T * (1.0 / sequences) + bias_ref[...]).astype(BF16)


def pair(x, wt, output_bias, after, sequences):
    channels, pairs = x.shape
    count = 3
    size = pairs // count
    return pl.pallas_call(
        functools.partial(pair_kernel, sequences),
        grid=(count,),
        in_specs=[
            pl.BlockSpec((channels, size), lambda t: (0, t)),
            whole(wt.shape),
            whole((1, PAIR_FEATURES)),
            pl.BlockSpec(memory_space=pl.ANY),
        ],
        out_specs=pl.BlockSpec((size, PAIR_FEATURES), lambda t: (t, 0)),
        out_shape=jax.ShapeDtypeStruct((pairs, PAIR_FEATURES), BF16),
        compiler_params=params(),
        cost_estimate=pl.CostEstimate(
            flops=4 * pairs * channels * PAIR_FEATURES,
            bytes_accessed=2 * pairs * channels,
            transcendentals=0,
        ),
    )(x, wt, output_bias.reshape(1, PAIR_FEATURES), after)


def unfold(total, share, out):
    for l in range(out.shape[1] // LANES):
        out[:, l * LANES : (l + 1) * LANES] = total[l * share : (l + 1) * share, :]


def call(kernel, operands, shapes, after=(), scratch=()):
    specs = [in_vmem()] * len(operands) + [pl.BlockSpec(memory_space=pl.ANY)] * len(after)
    return pl.pallas_call(
        kernel,
        in_specs=specs,
        out_specs=[in_vmem()] * len(shapes),
        out_shape=[jax.ShapeDtypeStruct(shape, kind) for shape, kind in shapes],
        scratch_shapes=scratch,
        compiler_params=params(),
    )(*operands, *after)


def partners(count):
    return [0, *range(count - 1, 0, -1)]


def row_sum(parts, after, share):
    count = len(parts)

    def kernel(*refs):
        parts, (_, message, held) = refs[:count], refs[count:]
        me = lax.axis_index("row")
        total = parts[0][0:share, :]
        for p, part in zip(partners(count), parts, strict=True):
            held[lax.bitwise_xor(me, p)] = part[share:, :].astype(F32)
            if p > 0:
                total += part[0:share, :].astype(F32)
        bias = joined(held[0])
        for n in range(1, count):
            bias += joined(held[n])
        message[0:share, :] = total.astype(BF16)
        message[share:, :] = split(bias)

    scratch = [pltpu.VMEM((count, BIAS_ROWS, LANES), F32)]
    (message,) = call(kernel, parts, [((share + BIAS_ROWS, LANES), BF16)], [after], scratch)
    return message


def pair_sum(kept, near, after):
    def kernel(*refs):
        kept, near, (own, *messages) = refs[:count], refs[count], refs[count + 2 :]
        size = own.shape[0]
        for p, part in enumerate(kept):
            both = part[...] + near[p * size : (p + 1) * size, :].astype(F32)
            if p == 0:
                own[...] = both
            else:
                messages[p - 1][...] = both.astype(BF16)

    count = len(kept)
    shapes = [(kept[0].shape, F32)] + [(kept[0].shape, BF16)] * (count - 1)
    own, *messages = call(kernel, [*kept, near], shapes, [after])
    return own, messages


def column_pair_sum(own, near, after, share):
    def kernel(own, near, _, message):
        total = own[0:share, :].astype(F32) + near[0:share, :].astype(F32)
        message[0:share, :] = total.astype(BF16)
        message[share:, :] = split(joined(own[share:, :]) + joined(near[share:, :]))

    (message,) = call(kernel, [own, near], [(own.shape, BF16)], [after])
    return message


def column_sum(parts, grads, share):
    rows = share + BIAS_ROWS
    count, sent = len(parts), len(grads)

    def kernel(*refs):
        parts, grads, refs = refs[:count], refs[count : count + sent], refs[count + sent :]
        messages, (piece_out, bias_out, held, by_e, by_c) = refs[:sent], refs[sent:]
        home = lax.div(lax.axis_index("col"), 2)
        for p, part in enumerate(parts):
            held[lax.bitwise_xor(home, p)] = part[...]
        total, bias = held[0, 0:share, :].astype(F32), joined(held[0, share:, :])
        for n in range(1, count):
            total += held[n, 0:share, :].astype(F32)
            bias += joined(held[n, share:, :])
        by_e[...] = total
        depth = PROJECTED_DEPTH
        width = share // depth
        for c in range(depth):
            by_c[c * width : (c + 1) * width, :] = by_e[pl.ds(c, width, stride=depth), :]
        piece = by_c[...].astype(BF16)
        piece_out[...] = piece
        for message, grad in zip(messages, grads, strict=True):
            message[0:share, :] = piece
            message[share:, :] = grad[...]
        bias_out[...] = jnp.broadcast_to(bias, bias_out.shape)

    shapes = [((share + grad.shape[0], LANES), BF16) for grad in grads]
    shapes += [((share, LANES), BF16), ((8, LANES), F32)]
    scratch = [pltpu.VMEM((count, rows, LANES), BF16)] + [pltpu.VMEM((share, LANES), F32)] * 2
    *messages, piece, bias = call(kernel, [*parts, *grads], shapes, scratch=scratch)
    return messages, piece, bias


def finish(pieces, left, right_own, bias, left_shape, right_shape, scale, bias_scale):
    count, left_n = len(pieces), len(left)
    share = pieces[0].shape[0]

    def kernel(*refs):
        pieces, left, refs = refs[:count], refs[count : count + left_n], refs[count + left_n :]
        right_own, bias, projection, left_out, right_out, bias_out = refs
        me = lax.axis_index("row")
        right_total = right_own[...]
        depth = PROJECTED_DEPTH
        width = share // depth
        for p, piece in zip(partners(count), pieces, strict=True):
            block = piece[0:share, :].astype(F32) * scale
            for c in range(depth):
                start = c * depth + pl.multiple_of(lax.bitwise_xor(me, p) * width, width)
                projection[pl.ds(start, width), :] = block[c * width : (c + 1) * width]
            if p > 0:
                right_total += piece[share:, :].astype(F32)
        left_total = left[0][...]
        for term in left[1:]:
            left_total += term[...].astype(F32)
        unfold(left_total, left_out.shape[0], left_out)
        unfold(right_total, right_out.shape[0], right_out)
        bias_out[...] = bias[0:1, :] * bias_scale

    shapes = [
        ((count * share, PAIR_FEATURES), F32),
        (left_shape, F32),
        (right_shape, F32),
        ((1, PAIR_FEATURES), F32),
    ]
    return call(kernel, [*pieces, *left, right_own, bias], shapes)


def swap(x, axis, p):
    return lax.ppermute(x, axis, [(n, n ^ p) for n in range(lax.axis_size(axis))])


def swap_each(parts, axis, step=1):
    count = len(parts)
    return [swap(parts[n - 1], axis, n * step) for n in range(count, 0, -1)][::-1]


def from_evens(x, axis):
    return swap_each([x] * (lax.axis_size(axis) // 2 - 1), axis, 2)


def local(
    first_homolog_features, second_homolog_features, final_projection_matrix, output_bias, cotangent
):
    i_n, j_n, _ = cotangent.shape
    row_n, col_n = lax.axis_size("row"), lax.axis_size("col")
    sequences = second_homolog_features.shape[0] * row_n
    channels = final_projection_matrix.shape[0]
    res_total = i_n * row_n
    a_near = swap(first_homolog_features, "col", 1)
    b_near = swap(second_homolog_features, "row", 1)
    we, wt, a, b, w, g = load(
        first_homolog_features,
        second_homolog_features,
        final_projection_matrix,
        cotangent.reshape(i_n * j_n, PAIR_FEATURES),
    )
    a, b = stack([a, a_near], [b, b_near])
    a_pieces = [a] + from_evens(a, "col")
    b_pieces = [b] + from_evens(b, "row")
    y, gt, bias_rows = prepare(we, g, i_n, j_n)

    x, a_held, b_wide, (own, *messages) = outer(
        a_pieces, b_pieces, g, bias_rows, i_n, j_n, sequences
    )
    share = channels // row_n

    parts = [own] + swap_each(messages, "row")[::-1]
    left_kept, (message,) = gradient(
        b_wide, y, own, "col", in_pairs(col_n), col_n // 2, 1, i_n, j_n, sequences
    )
    left_near = swap(message, "col", 1)

    message = row_sum(parts, message, share)
    near = swap(message, "col", 1)
    left_own, left_messages = pair_sum(left_kept, left_near, message)
    left = [left_own] + swap_each(left_messages, "col", 2)
    y2, a_wide = product(w, gt, a_held, left_own)

    before = gradient_start(a_wide, y2, j_n, i_n, sequences)
    message = column_pair_sum(message, near, before, share)
    parts = [message] + from_evens(message, "col")
    (right_own,), right_sent = gradient(
        a_wide, y2, message, "row", alone(row_n), 1, row_n - 1, j_n, i_n, sequences, [before]
    )

    messages, piece, bias = column_sum(parts, right_sent, share)
    pieces = [piece] + swap_each(messages, "row")[::-1]
    pair_map = pair(x, wt, output_bias, piece, sequences)
    projection, left_grad, right_grad, bias_grad = finish(
        pieces,
        left,
        right_own,
        bias,
        first_homolog_features.shape,
        second_homolog_features.shape,
        1.0 / (sequences * res_total),
        1.0 / res_total,
    )
    return (
        pair_map.reshape(i_n, j_n, PAIR_FEATURES),
        left_grad,
        right_grad,
        projection,
        bias_grad.reshape(PAIR_FEATURES),
    )


def solution(mesh):
    return jax.shard_map(
        local,
        mesh=mesh,
        in_specs=(
            P(("dp", "col"), "row"),
            P(("dp", "row"), "col"),
            P(),
            P(),
            P(("dp", "row"), "col", None),
        ),
        out_specs=(
            P(("dp", "row"), "col", None),
            P(("dp", "col"), "row"),
            P(("dp", "row"), "col"),
            P("dp", None),
            P("dp"),
        ),
        check_vma=False,
    )
```

```python
import functools

import jax
import jax.numpy as jnp
from jax import lax
from jax.experimental import pallas as pl
from jax.experimental.pallas import tpu as pltpu
from jax.sharding import PartitionSpec as P

PROJECTED_DEPTH = 32
PAIR_FEATURES = 128
GROUP = 8
MULTIPLY_ROWS = 384
CHUNKS = 2
BIAS_ROWS = 16
LANES = 128
F32 = jnp.float32
BF16 = jnp.bfloat16
MIB = 1024 * 1024

ROWS_BY_ROWS = (((1,), (1,)), ((), ()))
COLS_BY_COLS = (((0,), (0,)), ((), ()))


def params(sequences=0):
    return pltpu.CompilerParams(vmem_limit_bytes=min(10 + 10 * sequences // 32, 50) * MIB + 2 * MIB)


def whole(shape):
    return pl.BlockSpec(shape, lambda t: (0,) * len(shape))


def dot(x, y, dims=(((1,), (0,)), ((), ()))):
    return lax.dot_general(x, y, dims, preferred_element_type=F32)


def load_kernel(a_hbm, b_hbm, w_hbm, g_hbm, we_ref, wt_ref, a_ref, b_ref, w_ref, g_ref, w32, sems):
    depth = PROJECTED_DEPTH
    copies = [
        pltpu.make_async_copy(source, target, sems.at[n])
        for n, (source, target) in enumerate(
            [(w_hbm, w_ref), (g_hbm, g_ref), (a_hbm, a_ref), (b_hbm, b_ref)]
        )
    ]
    for copy in copies:
        copy.start()
    copies[0].wait()
    w32[...] = w_ref[...].astype(F32)
    for e in range(depth):
        block = w32[pl.ds(e, depth, stride=depth), :]
        we_ref[e * depth : (e + 1) * depth, :] = block.astype(BF16)
    wt_ref[...] = we_ref[...].astype(F32).T.astype(BF16)
    for copy in copies[1:]:
        copy.wait()


def in_vmem():
    return pl.BlockSpec(memory_space=pltpu.VMEM)


def load(a, b, w, g):
    shapes = [
        jax.ShapeDtypeStruct(w.shape, BF16),
        jax.ShapeDtypeStruct(w.shape[::-1], BF16),
        *[jax.ShapeDtypeStruct(x.shape, BF16) for x in (a, b, w, g)],
    ]
    return pl.pallas_call(
        load_kernel,
        in_specs=[pl.BlockSpec(memory_space=pltpu.HBM)] * 4,
        out_specs=[in_vmem()] * len(shapes),
        out_shape=shapes,
        scratch_shapes=[pltpu.VMEM(w.shape, F32), pltpu.SemaphoreType.DMA((4,))],
        compiler_params=params(),
        cost_estimate=pl.CostEstimate(
            flops=1000 * w.size, bytes_accessed=16 * w.size, transcendentals=0
        ),
    )(*[pltpu.with_memory_space_constraint(x, pltpu.HBM) for x in (a, b, w, g)])


def stack(*groups):
    def kernel(*refs):
        refs, outs = refs[: -len(groups)], refs[-len(groups) :]
        for group, out in zip(groups, outs, strict=True):
            blocks = [ref[...].astype(F32) for ref in refs[: len(group)]]
            refs = refs[len(group) :]
            out[...] = jnp.concatenate(blocks, axis=0).astype(BF16)

    shapes = [((len(group) * group[0].shape[0], group[0].shape[1]), BF16) for group in groups]
    return call(kernel, [x for group in groups for x in group], shapes)


def split(total):
    high = total.astype(BF16).astype(F32)
    row = lax.broadcasted_iota(jnp.int32, (BIAS_ROWS, PAIR_FEATURES), 0)
    return jnp.where(row == 0, high, jnp.where(row == 1, total - high, 0.0)).astype(BF16)


def joined(block):
    block = block.astype(F32)
    return block[0:1] + block[1:2]


def multiply(left_ref, right_ref, out_ref):
    for n in range(0, right_ref.shape[0], MULTIPLY_ROWS):
        rows = slice(n, n + MULTIPLY_ROWS)
        out_ref[:, rows] = dot(left_ref[...], right_ref[rows, :], ROWS_BY_ROWS).astype(BF16)


def prepare_kernel(i_n, j_n, we_ref, g_ref, y_ref, gt_ref, bias_ref, g32):
    g32[...] = g_ref[...].astype(F32)
    bias_ref[...] = split(jnp.sum(g32[...], axis=0, keepdims=True))
    multiply(we_ref, g_ref, y_ref)

    for j in range(j_n):
        gt_ref[j * i_n : (j + 1) * i_n, :] = g32[pl.ds(j, i_n, stride=j_n), :].astype(BF16)


def prepare(we, g, i_n, j_n):
    pairs = i_n * j_n
    channels = we.shape[0]
    shapes = [
        jax.ShapeDtypeStruct((channels, pairs), BF16),
        jax.ShapeDtypeStruct(g.shape, BF16),
        jax.ShapeDtypeStruct((BIAS_ROWS, PAIR_FEATURES), BF16),
    ]
    return pl.pallas_call(
        functools.partial(prepare_kernel, i_n, j_n),
        in_specs=[in_vmem()] * 2,
        out_specs=[in_vmem()] * len(shapes),
        out_shape=shapes,
        scratch_shapes=[pltpu.VMEM(g.shape, F32)],
        compiler_params=params(16),
        cost_estimate=pl.CostEstimate(
            flops=2 * pairs * channels * PAIR_FEATURES,
            bytes_accessed=4 * pairs * channels,
            transcendentals=0,
        ),
    )(we, g)


def join(pieces, axis, held):
    depth = pieces[0].shape[0] // 2
    me = lax.axis_index(axis)
    for p, piece in enumerate(pieces):
        block = piece[...].astype(F32)
        for n in range(2):
            place = lax.bitwise_xor(me, 2 * p + n) * depth
            held[pl.ds(pl.multiple_of(place, depth), depth), :] = block[n * depth : (n + 1) * depth]


def join_far(pieces, axis, held):
    half = lax.axis_size(axis) // 2
    depth = pieces[0].shape[0] // half
    me = lax.axis_index(axis)
    for n, piece in enumerate(pieces):
        block = piece[...].astype(F32)
        for p in range(half):
            place = lax.bitwise_xor(me, 2 * p + n) * depth
            held[pl.ds(pl.multiple_of(place, depth), depth), :] = block[p * depth : (p + 1) * depth]


def repeat_matrix(sequences):
    shape = (sequences, GROUP * sequences)
    lane = lax.broadcasted_iota(jnp.int32, shape, 1)
    row = lax.broadcasted_iota(jnp.int32, shape, 0)
    return (lax.rem(lane, sequences) == row).astype(BF16)


def tile_count(sequences):
    return GROUP * sequences // LANES, max(1, sequences // LANES)


def spread(held, wide):
    repeated = repeat_matrix(held.shape[0])[:, : wide.shape[0] * LANES]
    both = dot(held[...].T.astype(BF16), repeated)
    for l in range(wide.shape[0]):
        wide[l] = both[:, l * LANES : (l + 1) * LANES]


def tiles_of(sequences, tile):
    lane = lax.broadcasted_iota(jnp.int32, (1, LANES), 1) + tile * LANES
    return [
        (m, lax.div(lane, sequences) == m)
        for m in range(GROUP)
        if m * sequences < (tile + 1) * LANES and (m + 1) * sequences > tile * LANES
    ]


def chunks(body):
    if CHUNKS == 1:
        body(0)
    else:
        pl.loop(0, CHUNKS)(body)


def diagonal_of(wide, channel, positions, sequences):
    columns = []
    blocks = [
        wide[l, pl.ds(channel, positions, stride=PROJECTED_DEPTH), :].astype(BF16)
        for l in range(wide.shape[0])
    ]
    for l in range(tile_count(sequences)[0]):
        block = blocks[l % len(blocks)]
        members = dict(tiles_of(sequences, l))
        columns.append(
            jnp.concatenate(
                [
                    block * members[m].astype(F32).astype(BF16)
                    if m in members
                    else jnp.zeros(block.shape, BF16)
                    for m in range(GROUP)
                ],
                axis=0,
            )
        )
    return jnp.concatenate(columns, axis=1)


def alone(count):
    return lambda me: ([me], [[lax.bitwise_xor(me, d)] for d in range(1, count)])


def in_pairs(count):
    def plan(me):
        evens = range(0, count, 2)
        return [lax.bitwise_xor(me, d) for d in evens], [
            [lax.bitwise_xor(me, d + 1) for d in evens]
        ]

    return plan


def outer_kernel(i_n, j_n, *refs):
    depth = PROJECTED_DEPTH
    row_n = lax.axis_size("row")
    half = lax.axis_size("col") // 2
    a_pieces, b_pieces, refs = refs[:half], refs[half : half + 2], refs[half + 2 :]
    g_ref, bias_ref, x_ref, a_held, b_wide = refs[:5]
    messages, (b_held, left, total) = refs[5 : 5 + row_n], refs[5 + row_n :]
    sequences = a_held.shape[0]
    groups = i_n // GROUP
    per_step = depth // CHUNKS
    span = GROUP * j_n

    join(a_pieces, "col", a_held)
    join_far(b_pieces, "row", b_held)
    spread(b_held, b_wide)
    turned = a_held[...].T.astype(BF16)
    shape = (sequences, GROUP * sequences)
    shifted = lax.broadcasted_iota(jnp.int32, shape, 1) - lax.broadcasted_iota(jnp.int32, shape, 0)
    value = jnp.zeros(left.shape, F32)
    for m in range(GROUP):
        rows = [
            turned[(k * GROUP + m) * depth : (k * GROUP + m + 1) * depth, :] for k in range(groups)
        ]
        value += dot(jnp.concatenate(rows, axis=0), (shifted == m * sequences).astype(BF16))
    left[...] = value.astype(BF16)

    @chunks
    def _(t):
        size = per_step * depth
        rows = pl.ds(t * size if CHUNKS == 1 else pl.multiple_of(t * size, size), size)
        x_part = x_ref.at[rows]
        for e in range(0, per_step, 2):
            right = [diagonal_of(b_wide, t * per_step + e + n, j_n, sequences) for n in range(2)]
            product = dot(
                left[...], jnp.concatenate(right, axis=0), ROWS_BY_ROWS
            ).astype(BF16)
            for n in range(2):
                for k in range(groups):
                    x_part[(e + n) * depth : (e + n + 1) * depth, k * span : (k + 1) * span] = product[
                        k * depth : (k + 1) * depth, n * span : (n + 1) * span
                    ]
        total[rows, :] = dot(x_part[...], g_ref[...])

    share = total.shape[0] // row_n
    me = lax.axis_index("row")
    for p, message in enumerate(messages):
        part = pl.ds(pl.multiple_of(lax.bitwise_xor(me, p) * share, share), share)
        message[0:share, :] = total[part, :].astype(message.dtype)
        message[share:, :] = bias_ref[...].astype(message.dtype)


def outer(a_pieces, b_pieces, g, bias_rows, i_n, j_n, sequences):
    row_n = lax.axis_size("row")
    depth = PROJECTED_DEPTH
    channels = depth * depth
    pairs = i_n * j_n
    tiles = tile_count(sequences)[1]
    operands = [*a_pieces, *b_pieces, g, bias_rows]
    shapes = [jax.ShapeDtypeStruct((channels, pairs), BF16)]
    shapes += [
        jax.ShapeDtypeStruct((sequences, i_n * depth), F32),
        jax.ShapeDtypeStruct((tiles, j_n * depth, LANES), F32),
    ]
    shapes += [
        jax.ShapeDtypeStruct((channels // row_n + BIAS_ROWS, LANES), BF16 if p else F32)
        for p in range(row_n)
    ]
    results = pl.pallas_call(
        functools.partial(outer_kernel, i_n, j_n),
        in_specs=[in_vmem()] * len(operands),
        out_specs=[in_vmem()] * len(shapes),
        out_shape=shapes,
        scratch_shapes=[
            pltpu.VMEM((sequences, j_n * depth), F32),
            pltpu.VMEM((i_n // GROUP * depth, GROUP * sequences), BF16),
            pltpu.VMEM((channels, PAIR_FEATURES), F32),
        ],
        compiler_params=params(sequences),
        cost_estimate=pl.CostEstimate(
            flops=4 * pairs * channels * PAIR_FEATURES,
            bytes_accessed=2 * pairs * channels,
            transcendentals=0,
        ),
    )(*operands)
    return *results[:3], results[3:]


def gradient_kernel(axis, plan, kept, positions, others, sequences, *refs):
    depth = PROJECTED_DEPTH
    wide, source = refs[:2]
    outs, (result, grown, grad) = refs[3:-3], refs[-3:]
    parts = lax.axis_size(axis)
    per_step = depth // CHUNKS
    span = GROUP * others

    result[...] = jnp.zeros(result.shape, F32)

    @chunks
    def _(t):
        size = per_step * depth
        rows = pl.ds(t * size if CHUNKS == 1 else pl.multiple_of(t * size, size), size)
        part = source.at[rows]
        for n in range(0, per_step, 2):
            blocks = [
                jnp.concatenate(
                    [
                        part[m * depth : (m + 1) * depth, k * span : (k + 1) * span]
                        for m in (n, n + 1)
                    ],
                    axis=1,
                )
                for k in range(positions // GROUP)
            ]
            right = [
                diagonal_of(wide, t * per_step + m, others, sequences) for m in (n, n + 1)
            ]
            result[...] += dot(jnp.concatenate(blocks, axis=0), jnp.concatenate(right, axis=0))

    scaled = (result[...] * (1.0 / sequences)).astype(BF16)
    for l in range(scaled.shape[1] // LANES):
        members = dict(tiles_of(sequences, l))
        for k in range(positions // GROUP):
            block = scaled[k * depth : (k + 1) * depth, l * LANES : (l + 1) * LANES]
            for m in range(GROUP):
                start = (k * GROUP + m) * depth
                grown[start : start + depth, l * LANES : (l + 1) * LANES] = (
                    block * members[m].astype(F32).astype(BF16)
                    if m in members
                    else jnp.zeros((depth, LANES), BF16)
                )
    grad[...] = dot(repeat_matrix(sequences), grown[...], ROWS_BY_ROWS)
    share = sequences // parts

    def rows_of(p):
        mine = grad[pl.ds(pl.multiple_of(p * share, share), share), :]
        return jnp.concatenate(
            [mine[:, l * LANES : (l + 1) * LANES] for l in range(mine.shape[1] // LANES)], axis=0
        )

    stay, go = plan(lax.axis_index(axis))
    for p, out in zip(stay, outs[:kept], strict=True):
        out[...] = rows_of(p)
    for group, out in zip(go, outs[kept:], strict=True):
        size = out.shape[0] // len(group)
        for n, p in enumerate(group):
            out[n * size : (n + 1) * size, :] = rows_of(p).astype(BF16)


def gradient(wide, source, after, axis, plan, kept, groups, positions, others, sequences):
    depth = PROJECTED_DEPTH
    parts = lax.axis_size(axis)
    rows = sequences // parts * positions * depth // LANES
    shapes = [jax.ShapeDtypeStruct((rows, LANES), F32)] * kept
    group = (parts - kept) // groups
    shapes += [jax.ShapeDtypeStruct((group * rows, LANES), BF16)] * groups
    results = pl.pallas_call(
        functools.partial(gradient_kernel, axis, plan, kept, positions, others, sequences),
        in_specs=[in_vmem(), in_vmem(), pl.BlockSpec(memory_space=pl.ANY)],
        out_specs=[in_vmem()] * len(shapes),
        out_shape=shapes,
        scratch_shapes=[
            pltpu.VMEM((positions // GROUP * depth, GROUP * sequences), F32),
            pltpu.VMEM((positions * depth, GROUP * sequences), BF16),
            pltpu.VMEM((sequences, positions * depth), F32),
        ],
        compiler_params=params(sequences),
        cost_estimate=pl.CostEstimate(
            flops=2 * source.size * PAIR_FEATURES,
            bytes_accessed=2 * source.size,
            transcendentals=0,
        ),
    )(wide, source, after)
    return results[:kept], results[kept:]


def product_kernel(left_ref, right_ref, held, _, out_ref, wide):
    spread(held, wide)
    multiply(left_ref, right_ref, out_ref)


def product(left, right, held, after):
    shape = (left.shape[0], right.shape[0])
    spread_shape = (tile_count(held.shape[0])[1], held.shape[1], LANES)
    return pl.pallas_call(
        product_kernel,
        in_specs=[in_vmem()] * 3 + [pl.BlockSpec(memory_space=pl.ANY)],
        out_specs=[in_vmem()] * 2,
        out_shape=[jax.ShapeDtypeStruct(shape, BF16), jax.ShapeDtypeStruct(spread_shape, F32)],
        compiler_params=params(32),
        cost_estimate=pl.CostEstimate(
            flops=2 * shape[0] * shape[1] * left.shape[1],
            bytes_accessed=4 * shape[0] * shape[1],
            transcendentals=0,
        ),
    )(left, right, held, after)


def pair_kernel(sequences, x_ref, wt_ref, bias_ref, _, out_ref):
    product = dot(wt_ref[...], x_ref[...])
    out_ref[...] = (product.T * (1.0 / sequences) + bias_ref[...]).astype(BF16)


def pair(x, wt, output_bias, after, sequences):
    channels, pairs = x.shape
    count = 3
    size = pairs // count
    return pl.pallas_call(
        functools.partial(pair_kernel, sequences),
        grid=(count,),
        in_specs=[
            pl.BlockSpec((channels, size), lambda t: (0, t)),
            whole(wt.shape),
            whole((1, PAIR_FEATURES)),
            pl.BlockSpec(memory_space=pl.ANY),
        ],
        out_specs=pl.BlockSpec((size, PAIR_FEATURES), lambda t: (t, 0)),
        out_shape=jax.ShapeDtypeStruct((pairs, PAIR_FEATURES), BF16),
        compiler_params=params(),
        cost_estimate=pl.CostEstimate(
            flops=4 * pairs * channels * PAIR_FEATURES,
            bytes_accessed=2 * pairs * channels,
            transcendentals=0,
        ),
    )(x, wt, output_bias.reshape(1, PAIR_FEATURES), after)


def unfold(total, share, out):
    for l in range(out.shape[1] // LANES):
        out[:, l * LANES : (l + 1) * LANES] = total[l * share : (l + 1) * share, :]


def call(kernel, operands, shapes, after=(), scratch=()):
    specs = [in_vmem()] * len(operands) + [pl.BlockSpec(memory_space=pl.ANY)] * len(after)
    return pl.pallas_call(
        kernel,
        in_specs=specs,
        out_specs=[in_vmem()] * len(shapes),
        out_shape=[jax.ShapeDtypeStruct(shape, kind) for shape, kind in shapes],
        scratch_shapes=scratch,
        compiler_params=params(),
    )(*operands, *after)


def partners(count):
    return [0, *range(count - 1, 0, -1)]


def row_sum(parts, after, share):
    count = len(parts)

    def kernel(*refs):
        parts, (_, message, held) = refs[:count], refs[count:]
        me = lax.axis_index("row")
        total = parts[0][0:share, :]
        for p, part in zip(partners(count), parts, strict=True):
            held[lax.bitwise_xor(me, p)] = part[share:, :].astype(F32)
            if p > 0:
                total += part[0:share, :].astype(F32)
        bias = joined(held[0])
        for n in range(1, count):
            bias += joined(held[n])
        message[0:share, :] = total.astype(BF16)
        message[share:, :] = split(bias)

    scratch = [pltpu.VMEM((count, BIAS_ROWS, LANES), F32)]
    (message,) = call(kernel, parts, [((share + BIAS_ROWS, LANES), BF16)], [after], scratch)
    return message


def pair_sum(kept, near, after):
    def kernel(*refs):
        kept, near, (own, *messages) = refs[:count], refs[count], refs[count + 2 :]
        size = own.shape[0]
        for p, part in enumerate(kept):
            both = part[...] + near[p * size : (p + 1) * size, :].astype(F32)
            if p == 0:
                own[...] = both
            else:
                messages[p - 1][...] = both.astype(BF16)

    count = len(kept)
    shapes = [(kept[0].shape, F32)] + [(kept[0].shape, BF16)] * (count - 1)
    own, *messages = call(kernel, [*kept, near], shapes, [after])
    return own, messages


def column_pair_sum(own, near, after, share):
    def kernel(own, near, _, message):
        total = own[0:share, :].astype(F32) + near[0:share, :].astype(F32)
        message[0:share, :] = total.astype(BF16)
        message[share:, :] = split(joined(own[share:, :]) + joined(near[share:, :]))

    (message,) = call(kernel, [own, near], [(own.shape, BF16)], [after])
    return message


def column_sum(parts, grads, share):
    rows = share + BIAS_ROWS
    count, sent = len(parts), len(grads)

    def kernel(*refs):
        parts, grads, refs = refs[:count], refs[count : count + sent], refs[count + sent :]
        messages, (piece_out, bias_out, held, by_e, by_c) = refs[:sent], refs[sent:]
        home = lax.div(lax.axis_index("col"), 2)
        for p, part in enumerate(parts):
            held[lax.bitwise_xor(home, p)] = part[...]
        total, bias = held[0, 0:share, :].astype(F32), joined(held[0, share:, :])
        for n in range(1, count):
            total += held[n, 0:share, :].astype(F32)
            bias += joined(held[n, share:, :])
        by_e[...] = total
        depth = PROJECTED_DEPTH
        width = share // depth
        for c in range(depth):
            by_c[c * width : (c + 1) * width, :] = by_e[pl.ds(c, width, stride=depth), :]
        piece = by_c[...].astype(BF16)
        piece_out[...] = piece
        for message, grad in zip(messages, grads, strict=True):
            message[0:share, :] = piece
            message[share:, :] = grad[...]
        bias_out[...] = jnp.broadcast_to(bias, bias_out.shape)

    shapes = [((share + grad.shape[0], LANES), BF16) for grad in grads]
    shapes += [((share, LANES), BF16), ((8, LANES), F32)]
    scratch = [pltpu.VMEM((count, rows, LANES), BF16)] + [pltpu.VMEM((share, LANES), F32)] * 2
    *messages, piece, bias = call(kernel, [*parts, *grads], shapes, scratch=scratch)
    return messages, piece, bias


def finish(pieces, left, right_own, bias, left_shape, right_shape, scale, bias_scale):
    count, left_n = len(pieces), len(left)
    share = pieces[0].shape[0]

    def kernel(*refs):
        pieces, left, refs = refs[:count], refs[count : count + left_n], refs[count + left_n :]
        right_own, bias, projection, left_out, right_out, bias_out = refs
        me = lax.axis_index("row")
        right_total = right_own[...]
        depth = PROJECTED_DEPTH
        width = share // depth
        for p, piece in zip(partners(count), pieces, strict=True):
            block = piece[0:share, :].astype(F32) * scale
            for c in range(depth):
                start = c * depth + pl.multiple_of(lax.bitwise_xor(me, p) * width, width)
                projection[pl.ds(start, width), :] = block[c * width : (c + 1) * width]
            if p > 0:
                right_total += piece[share:, :].astype(F32)
        left_total = left[0][...]
        for term in left[1:]:
            left_total += term[...].astype(F32)
        unfold(left_total, left_out.shape[0], left_out)
        unfold(right_total, right_out.shape[0], right_out)
        bias_out[...] = bias[0:1, :] * bias_scale

    shapes = [
        ((count * share, PAIR_FEATURES), F32),
        (left_shape, F32),
        (right_shape, F32),
        ((1, PAIR_FEATURES), F32),
    ]
    return call(kernel, [*pieces, *left, right_own, bias], shapes)


def swap(x, axis, p):
    return lax.ppermute(x, axis, [(n, n ^ p) for n in range(lax.axis_size(axis))])


def swap_each(parts, axis, step=1):
    count = len(parts)
    return [swap(parts[n - 1], axis, n * step) for n in range(count, 0, -1)][::-1]


def from_evens(x, axis):
    return swap_each([x] * (lax.axis_size(axis) // 2 - 1), axis, 2)


def local(
    first_homolog_features, second_homolog_features, final_projection_matrix, output_bias, cotangent
):
    i_n, j_n, _ = cotangent.shape
    row_n, col_n = lax.axis_size("row"), lax.axis_size("col")
    sequences = second_homolog_features.shape[0] * row_n
    channels = final_projection_matrix.shape[0]
    res_total = i_n * row_n
    a_near = swap(first_homolog_features, "col", 1)
    b_far = from_evens(second_homolog_features, "row")
    we, wt, a, b, w, g = load(
        first_homolog_features,
        second_homolog_features,
        final_projection_matrix,
        cotangent.reshape(i_n * j_n, PAIR_FEATURES),
    )
    a, b = stack([a, a_near], [b, *b_far])
    a_pieces = [a] + from_evens(a, "col")
    b_pieces = [b, swap(b, "row", 1)]
    y, gt, bias_rows = prepare(we, g, i_n, j_n)

    x, a_held, b_wide, (own, *messages) = outer(
        a_pieces, b_pieces, g, bias_rows, i_n, j_n, sequences
    )
    share = channels // row_n

    parts = [own] + swap_each(messages, "row")[::-1]
    left_kept, (message,) = gradient(
        b_wide, y, own, "col", in_pairs(col_n), col_n // 2, 1, i_n, j_n, sequences
    )
    left_near = swap(message, "col", 1)

    message = row_sum(parts, message, share)
    near = swap(message, "col", 1)
    left_own, left_messages = pair_sum(left_kept, left_near, message)
    left = [left_own] + swap_each(left_messages, "col", 2)
    y2, a_wide = product(w, gt, a_held, left_own)

    message = column_pair_sum(message, near, y2, share)
    parts = [message] + from_evens(message, "col")
    (right_own,), right_sent = gradient(
        a_wide, y2, message, "row", alone(row_n), 1, row_n - 1, j_n, i_n, sequences
    )

    messages, piece, bias = column_sum(parts, right_sent, share)
    pieces = [piece] + swap_each(messages, "row")[::-1]
    pair_map = pair(x, wt, output_bias, piece, sequences)
    projection, left_grad, right_grad, bias_grad = finish(
        pieces,
        left,
        right_own,
        bias,
        first_homolog_features.shape,
        second_homolog_features.shape,
        1.0 / (sequences * res_total),
        1.0 / res_total,
    )
    return (
        pair_map.reshape(i_n, j_n, PAIR_FEATURES),
        left_grad,
        right_grad,
        projection,
        bias_grad.reshape(PAIR_FEATURES),
    )


def solution(mesh):
    return jax.shard_map(
        local,
        mesh=mesh,
        in_specs=(
            P(("dp", "col"), "row"),
            P(("dp", "row"), "col"),
            P(),
            P(),
            P(("dp", "row"), "col", None),
        ),
        out_specs=(
            P(("dp", "row"), "col", None),
            P(("dp", "col"), "row"),
            P(("dp", "row"), "col"),
            P("dp", None),
            P("dp"),
        ),
        check_vma=False,
    )
```

```python
import functools

import jax
import jax.numpy as jnp
from jax import lax
from jax.experimental import pallas as pl
from jax.experimental.pallas import tpu as pltpu
from jax.sharding import PartitionSpec as P

PROJECTED_DEPTH = 32
PAIR_FEATURES = 128
GROUP = 8
MULTIPLY_ROWS = 384
CHUNKS = 2
BIAS_ROWS = 16
LANES = 128
F32 = jnp.float32
BF16 = jnp.bfloat16
MIB = 1024 * 1024

ROWS_BY_ROWS = (((1,), (1,)), ((), ()))
COLS_BY_COLS = (((0,), (0,)), ((), ()))


def params(sequences=0):
    return pltpu.CompilerParams(vmem_limit_bytes=min(10 + 10 * sequences // 32, 50) * MIB + 2 * MIB)


def whole(shape):
    return pl.BlockSpec(shape, lambda t: (0,) * len(shape))


def dot(x, y, dims=(((1,), (0,)), ((), ()))):
    return lax.dot_general(x, y, dims, preferred_element_type=F32)


def load_kernel(a_hbm, b_hbm, w_hbm, g_hbm, we_ref, wt_ref, a_ref, b_ref, w_ref, g_ref, w32, sems):
    depth = PROJECTED_DEPTH
    copies = [
        pltpu.make_async_copy(source, target, sems.at[n])
        for n, (source, target) in enumerate(
            [(w_hbm, w_ref), (g_hbm, g_ref), (a_hbm, a_ref), (b_hbm, b_ref)]
        )
    ]
    for copy in copies:
        copy.start()
    copies[0].wait()
    w32[...] = w_ref[...].astype(F32)
    for e in range(depth):
        block = w32[pl.ds(e, depth, stride=depth), :]
        we_ref[e * depth : (e + 1) * depth, :] = block.astype(BF16)
    wt_ref[...] = we_ref[...].astype(F32).T.astype(BF16)
    for copy in copies[1:]:
        copy.wait()


def in_vmem():
    return pl.BlockSpec(memory_space=pltpu.VMEM)


def load(a, b, w, g):
    shapes = [
        jax.ShapeDtypeStruct(w.shape, BF16),
        jax.ShapeDtypeStruct(w.shape[::-1], BF16),
        *[jax.ShapeDtypeStruct(x.shape, BF16) for x in (a, b, w, g)],
    ]
    return pl.pallas_call(
        load_kernel,
        in_specs=[pl.BlockSpec(memory_space=pltpu.HBM)] * 4,
        out_specs=[in_vmem()] * len(shapes),
        out_shape=shapes,
        scratch_shapes=[pltpu.VMEM(w.shape, F32), pltpu.SemaphoreType.DMA((4,))],
        compiler_params=params(),
        cost_estimate=pl.CostEstimate(
            flops=1000 * w.size, bytes_accessed=16 * w.size, transcendentals=0
        ),
    )(*[pltpu.with_memory_space_constraint(x, pltpu.HBM) for x in (a, b, w, g)])


def stack(*groups):
    def kernel(*refs):
        refs, outs = refs[: -len(groups)], refs[-len(groups) :]
        for group, out in zip(groups, outs, strict=True):
            blocks = [ref[...].astype(F32) for ref in refs[: len(group)]]
            refs = refs[len(group) :]
            out[...] = jnp.concatenate(blocks, axis=0).astype(BF16)

    shapes = [((len(group) * group[0].shape[0], group[0].shape[1]), BF16) for group in groups]
    return call(kernel, [x for group in groups for x in group], shapes)


def split(total):
    high = total.astype(BF16).astype(F32)
    row = lax.broadcasted_iota(jnp.int32, (BIAS_ROWS, PAIR_FEATURES), 0)
    return jnp.where(row == 0, high, jnp.where(row == 1, total - high, 0.0)).astype(BF16)


def joined(block):
    block = block.astype(F32)
    return block[0:1] + block[1:2]


def multiply(left_ref, right_ref, out_ref):
    for n in range(0, right_ref.shape[0], MULTIPLY_ROWS):
        rows = slice(n, n + MULTIPLY_ROWS)
        out_ref[:, rows] = dot(left_ref[...], right_ref[rows, :], ROWS_BY_ROWS).astype(BF16)


def prepare_kernel(i_n, j_n, we_ref, g_ref, y_ref, gt_ref, bias_ref, g32):
    g32[...] = g_ref[...].astype(F32)
    bias_ref[...] = split(jnp.sum(g32[...], axis=0, keepdims=True))
    multiply(we_ref, g_ref, y_ref)

    for j in range(j_n):
        gt_ref[j * i_n : (j + 1) * i_n, :] = g32[pl.ds(j, i_n, stride=j_n), :].astype(BF16)


def prepare(we, g, i_n, j_n):
    pairs = i_n * j_n
    channels = we.shape[0]
    shapes = [
        jax.ShapeDtypeStruct((channels, pairs), BF16),
        jax.ShapeDtypeStruct(g.shape, BF16),
        jax.ShapeDtypeStruct((BIAS_ROWS, PAIR_FEATURES), BF16),
    ]
    return pl.pallas_call(
        functools.partial(prepare_kernel, i_n, j_n),
        in_specs=[in_vmem()] * 2,
        out_specs=[in_vmem()] * len(shapes),
        out_shape=shapes,
        scratch_shapes=[pltpu.VMEM(g.shape, F32)],
        compiler_params=params(16),
        cost_estimate=pl.CostEstimate(
            flops=2 * pairs * channels * PAIR_FEATURES,
            bytes_accessed=4 * pairs * channels,
            transcendentals=0,
        ),
    )(we, g)


def join(pieces, axis, held):
    depth = pieces[0].shape[0] // 2
    me = lax.axis_index(axis)
    for p, piece in enumerate(pieces):
        block = piece[...].astype(F32)
        for n in range(2):
            place = lax.bitwise_xor(me, 2 * p + n) * depth
            held[pl.ds(pl.multiple_of(place, depth), depth), :] = block[n * depth : (n + 1) * depth]


def repeat_matrix(sequences):
    shape = (sequences, GROUP * sequences)
    lane = lax.broadcasted_iota(jnp.int32, shape, 1)
    row = lax.broadcasted_iota(jnp.int32, shape, 0)
    return (lax.rem(lane, sequences) == row).astype(BF16)


def tile_count(sequences):
    return GROUP * sequences // LANES, max(1, sequences // LANES)


def spread(held, wide):
    repeated = repeat_matrix(held.shape[0])[:, : wide.shape[0] * LANES]
    both = dot(held[...].T.astype(BF16), repeated)
    for l in range(wide.shape[0]):
        wide[l] = both[:, l * LANES : (l + 1) * LANES]


def tiles_of(sequences, tile):
    lane = lax.broadcasted_iota(jnp.int32, (1, LANES), 1) + tile * LANES
    return [
        (m, lax.div(lane, sequences) == m)
        for m in range(GROUP)
        if m * sequences < (tile + 1) * LANES and (m + 1) * sequences > tile * LANES
    ]


def chunks(body):
    if CHUNKS == 1:
        body(0)
    else:
        pl.loop(0, CHUNKS)(body)


def diagonal_of(wide, channel, positions, sequences):
    columns = []
    blocks = [
        wide[l, pl.ds(channel, positions, stride=PROJECTED_DEPTH), :].astype(BF16)
        for l in range(wide.shape[0])
    ]
    for l in range(tile_count(sequences)[0]):
        block = blocks[l % len(blocks)]
        members = dict(tiles_of(sequences, l))
        columns.append(
            jnp.concatenate(
                [
                    block * members[m].astype(F32).astype(BF16)
                    if m in members
                    else jnp.zeros(block.shape, BF16)
                    for m in range(GROUP)
                ],
                axis=0,
            )
        )
    return jnp.concatenate(columns, axis=1)


def alone(count):
    return lambda me: ([me], [[lax.bitwise_xor(me, d)] for d in range(1, count)])


def in_pairs(count):
    def plan(me):
        evens = range(0, count, 2)
        return [lax.bitwise_xor(me, d) for d in evens], [
            [lax.bitwise_xor(me, d + 1) for d in evens]
        ]

    return plan


def outer_kernel(i_n, j_n, *refs):
    depth = PROJECTED_DEPTH
    row_n = lax.axis_size("row")
    halves = [lax.axis_size("col") // 2, row_n // 2]
    a_pieces, refs = refs[: halves[0]], refs[halves[0] :]
    b_pieces, refs = refs[: halves[1]], refs[halves[1] :]
    g_ref, bias_ref, x_ref, a_held, b_wide = refs[:5]
    messages, (b_held, left, total) = refs[5 : 5 + row_n], refs[5 + row_n :]
    sequences = a_held.shape[0]
    groups = i_n // GROUP
    per_step = depth // CHUNKS
    span = GROUP * j_n

    join(a_pieces, "col", a_held)
    join(b_pieces, "row", b_held)
    spread(b_held, b_wide)
    turned = a_held[...].T.astype(BF16)
    shape = (sequences, GROUP * sequences)
    shifted = lax.broadcasted_iota(jnp.int32, shape, 1) - lax.broadcasted_iota(jnp.int32, shape, 0)
    value = jnp.zeros(left.shape, F32)
    for m in range(GROUP):
        rows = [
            turned[(k * GROUP + m) * depth : (k * GROUP + m + 1) * depth, :] for k in range(groups)
        ]
        value += dot(jnp.concatenate(rows, axis=0), (shifted == m * sequences).astype(BF16))
    left[...] = value.astype(BF16)

    @chunks
    def _(t):
        size = per_step * depth
        rows = pl.ds(t * size if CHUNKS == 1 else pl.multiple_of(t * size, size), size)
        x_part = x_ref.at[rows]
        for e in range(0, per_step, 2):
            right = [diagonal_of(b_wide, t * per_step + e + n, j_n, sequences) for n in range(2)]
            product = dot(
                left[...], jnp.concatenate(right, axis=0), ROWS_BY_ROWS
            ).astype(BF16)
            for n in range(2):
                for k in range(groups):
                    x_part[(e + n) * depth : (e + n + 1) * depth, k * span : (k + 1) * span] = product[
                        k * depth : (k + 1) * depth, n * span : (n + 1) * span
                    ]
        total[rows, :] = dot(x_part[...], g_ref[...])

    share = total.shape[0] // row_n
    me = lax.axis_index("row")
    for p, message in enumerate(messages):
        part = pl.ds(pl.multiple_of(lax.bitwise_xor(me, p) * share, share), share)
        message[0:share, :] = total[part, :].astype(message.dtype)
        message[share:, :] = bias_ref[...].astype(message.dtype)


def outer(a_pieces, b_pieces, g, bias_rows, i_n, j_n, sequences):
    row_n = lax.axis_size("row")
    depth = PROJECTED_DEPTH
    channels = depth * depth
    pairs = i_n * j_n
    tiles = tile_count(sequences)[1]
    operands = [*a_pieces, *b_pieces, g, bias_rows]
    shapes = [jax.ShapeDtypeStruct((channels, pairs), BF16)]
    shapes += [
        jax.ShapeDtypeStruct((sequences, i_n * depth), F32),
        jax.ShapeDtypeStruct((tiles, j_n * depth, LANES), F32),
    ]
    shapes += [
        jax.ShapeDtypeStruct((channels // row_n + BIAS_ROWS, LANES), BF16 if p else F32)
        for p in range(row_n)
    ]
    results = pl.pallas_call(
        functools.partial(outer_kernel, i_n, j_n),
        in_specs=[in_vmem()] * len(operands),
        out_specs=[in_vmem()] * len(shapes),
        out_shape=shapes,
        scratch_shapes=[
            pltpu.VMEM((sequences, j_n * depth), F32),
            pltpu.VMEM((i_n // GROUP * depth, GROUP * sequences), BF16),
            pltpu.VMEM((channels, PAIR_FEATURES), F32),
        ],
        compiler_params=params(sequences),
        cost_estimate=pl.CostEstimate(
            flops=4 * pairs * channels * PAIR_FEATURES,
            bytes_accessed=2 * pairs * channels,
            transcendentals=0,
        ),
    )(*operands)
    return *results[:3], results[3:]


def gradient_kernel(axis, plan, kept, positions, others, sequences, *refs):
    depth = PROJECTED_DEPTH
    wide, source = refs[:2]
    outs, (result, grown, grad) = refs[3:-3], refs[-3:]
    parts = lax.axis_size(axis)
    per_step = depth // CHUNKS
    span = GROUP * others

    result[...] = jnp.zeros(result.shape, F32)

    @chunks
    def _(t):
        size = per_step * depth
        rows = pl.ds(t * size if CHUNKS == 1 else pl.multiple_of(t * size, size), size)
        part = source.at[rows]
        for n in range(0, per_step, 2):
            blocks = [
                jnp.concatenate(
                    [
                        part[m * depth : (m + 1) * depth, k * span : (k + 1) * span]
                        for m in (n, n + 1)
                    ],
                    axis=1,
                )
                for k in range(positions // GROUP)
            ]
            right = [
                diagonal_of(wide, t * per_step + m, others, sequences) for m in (n, n + 1)
            ]
            result[...] += dot(jnp.concatenate(blocks, axis=0), jnp.concatenate(right, axis=0))

    scaled = (result[...] * (1.0 / sequences)).astype(BF16)
    for l in range(scaled.shape[1] // LANES):
        members = dict(tiles_of(sequences, l))
        for k in range(positions // GROUP):
            block = scaled[k * depth : (k + 1) * depth, l * LANES : (l + 1) * LANES]
            for m in range(GROUP):
                start = (k * GROUP + m) * depth
                grown[start : start + depth, l * LANES : (l + 1) * LANES] = (
                    block * members[m].astype(F32).astype(BF16)
                    if m in members
                    else jnp.zeros((depth, LANES), BF16)
                )
    grad[...] = dot(repeat_matrix(sequences), grown[...], ROWS_BY_ROWS)
    share = sequences // parts

    def rows_of(p):
        mine = grad[pl.ds(pl.multiple_of(p * share, share), share), :]
        return jnp.concatenate(
            [mine[:, l * LANES : (l + 1) * LANES] for l in range(mine.shape[1] // LANES)], axis=0
        )

    stay, go = plan(lax.axis_index(axis))
    for p, out in zip(stay, outs[:kept], strict=True):
        out[...] = rows_of(p)
    for group, out in zip(go, outs[kept:], strict=True):
        size = out.shape[0] // len(group)
        for n, p in enumerate(group):
            out[n * size : (n + 1) * size, :] = rows_of(p).astype(BF16)


def gradient(wide, source, after, axis, plan, kept, groups, positions, others, sequences):
    depth = PROJECTED_DEPTH
    parts = lax.axis_size(axis)
    rows = sequences // parts * positions * depth // LANES
    shapes = [jax.ShapeDtypeStruct((rows, LANES), F32)] * kept
    group = (parts - kept) // groups
    shapes += [jax.ShapeDtypeStruct((group * rows, LANES), BF16)] * groups
    results = pl.pallas_call(
        functools.partial(gradient_kernel, axis, plan, kept, positions, others, sequences),
        in_specs=[in_vmem(), in_vmem(), pl.BlockSpec(memory_space=pl.ANY)],
        out_specs=[in_vmem()] * len(shapes),
        out_shape=shapes,
        scratch_shapes=[
            pltpu.VMEM((positions // GROUP * depth, GROUP * sequences), F32),
            pltpu.VMEM((positions * depth, GROUP * sequences), BF16),
            pltpu.VMEM((sequences, positions * depth), F32),
        ],
        compiler_params=params(sequences),
        cost_estimate=pl.CostEstimate(
            flops=2 * source.size * PAIR_FEATURES,
            bytes_accessed=2 * source.size,
            transcendentals=0,
        ),
    )(wide, source, after)
    return results[:kept], results[kept:]


def product_kernel(left_ref, right_ref, held, _, out_ref, wide):
    spread(held, wide)
    multiply(left_ref, right_ref, out_ref)


def product(left, right, held, after):
    shape = (left.shape[0], right.shape[0])
    spread_shape = (tile_count(held.shape[0])[1], held.shape[1], LANES)
    return pl.pallas_call(
        product_kernel,
        in_specs=[in_vmem()] * 3 + [pl.BlockSpec(memory_space=pl.ANY)],
        out_specs=[in_vmem()] * 2,
        out_shape=[jax.ShapeDtypeStruct(shape, BF16), jax.ShapeDtypeStruct(spread_shape, F32)],
        compiler_params=params(32),
        cost_estimate=pl.CostEstimate(
            flops=2 * shape[0] * shape[1] * left.shape[1],
            bytes_accessed=4 * shape[0] * shape[1],
            transcendentals=0,
        ),
    )(left, right, held, after)


def pair_kernel(sequences, x_ref, wt_ref, bias_ref, _, out_ref):
    product = dot(wt_ref[...], x_ref[...])
    out_ref[...] = (product.T * (1.0 / sequences) + bias_ref[...]).astype(BF16)


def pair(x, wt, output_bias, after, sequences):
    channels, pairs = x.shape
    count = 3
    size = pairs // count
    return pl.pallas_call(
        functools.partial(pair_kernel, sequences),
        grid=(count,),
        in_specs=[
            pl.BlockSpec((channels, size), lambda t: (0, t)),
            whole(wt.shape),
            whole((1, PAIR_FEATURES)),
            pl.BlockSpec(memory_space=pl.ANY),
        ],
        out_specs=pl.BlockSpec((size, PAIR_FEATURES), lambda t: (t, 0)),
        out_shape=jax.ShapeDtypeStruct((pairs, PAIR_FEATURES), BF16),
        compiler_params=params(),
        cost_estimate=pl.CostEstimate(
            flops=4 * pairs * channels * PAIR_FEATURES,
            bytes_accessed=2 * pairs * channels,
            transcendentals=0,
        ),
    )(x, wt, output_bias.reshape(1, PAIR_FEATURES), after)


def unfold(total, share, out):
    for l in range(out.shape[1] // LANES):
        out[:, l * LANES : (l + 1) * LANES] = total[l * share : (l + 1) * share, :]


def call(kernel, operands, shapes, after=(), scratch=()):
    specs = [in_vmem()] * len(operands) + [pl.BlockSpec(memory_space=pl.ANY)] * len(after)
    return pl.pallas_call(
        kernel,
        in_specs=specs,
        out_specs=[in_vmem()] * len(shapes),
        out_shape=[jax.ShapeDtypeStruct(shape, kind) for shape, kind in shapes],
        scratch_shapes=scratch,
        compiler_params=params(),
    )(*operands, *after)


def partners(count):
    return [0, *[p ^ 1 for p in range(count - 1, 1, -1)], 1]


def row_sum(parts, after, share):
    count = len(parts)

    def kernel(*refs):
        parts, (_, message, held) = refs[:count], refs[count:]
        me = lax.axis_index("row")
        total = parts[0][0:share, :]
        for p, part in zip(partners(count), parts, strict=True):
            held[lax.bitwise_xor(me, p)] = part[share:, :].astype(F32)
            if p > 0:
                total += part[0:share, :].astype(F32)
        bias = joined(held[0])
        for n in range(1, count):
            bias += joined(held[n])
        message[0:share, :] = total.astype(BF16)
        message[share:, :] = split(bias)

    scratch = [pltpu.VMEM((count, BIAS_ROWS, LANES), F32)]
    (message,) = call(kernel, parts, [((share + BIAS_ROWS, LANES), BF16)], [after], scratch)
    return message


def pair_sum(kept, near, after):
    def kernel(*refs):
        kept, near, (own, *messages) = refs[:count], refs[count], refs[count + 2 :]
        size = own.shape[0]
        for p, part in enumerate(kept):
            both = part[...] + near[p * size : (p + 1) * size, :].astype(F32)
            if p == 0:
                own[...] = both
            else:
                messages[p - 1][...] = both.astype(BF16)

    count = len(kept)
    shapes = [(kept[0].shape, F32)] + [(kept[0].shape, BF16)] * (count - 1)
    own, *messages = call(kernel, [*kept, near], shapes, [after])
    return own, messages


def column_pair_sum(own, near, after, share):
    def kernel(own, near, _, message):
        total = own[0:share, :].astype(F32) + near[0:share, :].astype(F32)
        message[0:share, :] = total.astype(BF16)
        message[share:, :] = split(joined(own[share:, :]) + joined(near[share:, :]))

    (message,) = call(kernel, [own, near], [(own.shape, BF16)], [after])
    return message


def column_sum(parts, grads, share):
    rows = share + BIAS_ROWS
    count, sent = len(parts), len(grads)

    def kernel(*refs):
        parts, grads, refs = refs[:count], refs[count : count + sent], refs[count + sent :]
        messages, (piece_out, bias_out, held, by_e, by_c) = refs[:sent], refs[sent:]
        home = lax.div(lax.axis_index("col"), 2)
        for p, part in enumerate(parts):
            held[lax.bitwise_xor(home, p)] = part[...]
        total, bias = held[0, 0:share, :].astype(F32), joined(held[0, share:, :])
        for n in range(1, count):
            total += held[n, 0:share, :].astype(F32)
            bias += joined(held[n, share:, :])
        by_e[...] = total
        depth = PROJECTED_DEPTH
        width = share // depth
        for c in range(depth):
            by_c[c * width : (c + 1) * width, :] = by_e[pl.ds(c, width, stride=depth), :]
        piece = by_c[...].astype(BF16)
        piece_out[...] = piece
        for message, grad in zip(messages, grads, strict=True):
            message[0:share, :] = piece
            message[share:, :] = grad[...]
        bias_out[...] = jnp.broadcast_to(bias, bias_out.shape)

    shapes = [((share + grad.shape[0], LANES), BF16) for grad in grads]
    shapes += [((share, LANES), BF16), ((8, LANES), F32)]
    scratch = [pltpu.VMEM((count, rows, LANES), BF16)] + [pltpu.VMEM((share, LANES), F32)] * 2
    *messages, piece, bias = call(kernel, [*parts, *grads], shapes, scratch=scratch)
    return messages, piece, bias


def finish(pieces, left, right_own, bias, left_shape, right_shape, scale, bias_scale):
    count, left_n = len(pieces), len(left)
    share = pieces[0].shape[0]

    def kernel(*refs):
        pieces, left, refs = refs[:count], refs[count : count + left_n], refs[count + left_n :]
        right_own, bias, projection, left_out, right_out, bias_out = refs
        me = lax.axis_index("row")
        right_total = right_own[...]
        depth = PROJECTED_DEPTH
        width = share // depth
        for p, piece in zip(partners(count), pieces, strict=True):
            block = piece[0:share, :].astype(F32) * scale
            for c in range(depth):
                start = c * depth + pl.multiple_of(lax.bitwise_xor(me, p) * width, width)
                projection[pl.ds(start, width), :] = block[c * width : (c + 1) * width]
            if p > 0:
                right_total += piece[share:, :].astype(F32)
        left_total = left[0][...]
        for term in left[1:]:
            left_total += term[...].astype(F32)
        unfold(left_total, left_out.shape[0], left_out)
        unfold(right_total, right_out.shape[0], right_out)
        bias_out[...] = bias[0:1, :] * bias_scale

    shapes = [
        ((count * share, PAIR_FEATURES), F32),
        (left_shape, F32),
        (right_shape, F32),
        ((1, PAIR_FEATURES), F32),
    ]
    return call(kernel, [*pieces, *left, right_own, bias], shapes)


def swap(x, axis, p):
    return lax.ppermute(x, axis, [(n, n ^ p) for n in range(lax.axis_size(axis))])


def in_turn(parts):
    return [parts[p - 1] for p in partners(len(parts) + 1)[1:]]


def swap_each(parts, axis, step=1):
    count = len(parts)
    return [swap(parts[n - 1], axis, n * step) for n in range(count, 0, -1)][::-1]


def from_evens(x, axis):
    return swap_each([x] * (lax.axis_size(axis) // 2 - 1), axis, 2)


def local(
    first_homolog_features, second_homolog_features, final_projection_matrix, output_bias, cotangent
):
    i_n, j_n, _ = cotangent.shape
    row_n, col_n = lax.axis_size("row"), lax.axis_size("col")
    sequences = second_homolog_features.shape[0] * row_n
    channels = final_projection_matrix.shape[0]
    res_total = i_n * row_n
    a_near = swap(first_homolog_features, "col", 1)
    b_near = swap(second_homolog_features, "row", 1)
    we, wt, a, b, w, g = load(
        first_homolog_features,
        second_homolog_features,
        final_projection_matrix,
        cotangent.reshape(i_n * j_n, PAIR_FEATURES),
    )
    a, b = stack([a, a_near], [b, b_near])
    a_pieces = [a] + from_evens(a, "col")
    b_pieces = [b] + from_evens(b, "row")
    y, gt, bias_rows = prepare(we, g, i_n, j_n)

    x, a_held, b_wide, (own, *messages) = outer(
        a_pieces, b_pieces, g, bias_rows, i_n, j_n, sequences
    )
    share = channels // row_n

    parts = [own] + in_turn(swap_each(messages, "row"))
    left_kept, (message,) = gradient(
        b_wide, y, own, "col", in_pairs(col_n), col_n // 2, 1, i_n, j_n, sequences
    )
    left_near = swap(message, "col", 1)

    message = row_sum(parts, message, share)
    near = swap(message, "col", 1)
    left_own, left_messages = pair_sum(left_kept, left_near, message)
    left = [left_own] + swap_each(left_messages, "col", 2)
    y2, a_wide = product(w, gt, a_held, left_own)

    message = column_pair_sum(message, near, y2, share)
    parts = [message] + from_evens(message, "col")
    (right_own,), right_sent = gradient(
        a_wide, y2, message, "row", alone(row_n), 1, row_n - 1, j_n, i_n, sequences
    )

    messages, piece, bias = column_sum(parts, right_sent, share)
    pieces = [piece] + in_turn(swap_each(messages, "row"))
    pair_map = pair(x, wt, output_bias, piece, sequences)
    projection, left_grad, right_grad, bias_grad = finish(
        pieces,
        left,
        right_own,
        bias,
        first_homolog_features.shape,
        second_homolog_features.shape,
        1.0 / (sequences * res_total),
        1.0 / res_total,
    )
    return (
        pair_map.reshape(i_n, j_n, PAIR_FEATURES),
        left_grad,
        right_grad,
        projection,
        bias_grad.reshape(PAIR_FEATURES),
    )


def solution(mesh):
    return jax.shard_map(
        local,
        mesh=mesh,
        in_specs=(
            P(("dp", "col"), "row"),
            P(("dp", "row"), "col"),
            P(),
            P(),
            P(("dp", "row"), "col", None),
        ),
        out_specs=(
            P(("dp", "row"), "col", None),
            P(("dp", "col"), "row"),
            P(("dp", "row"), "col"),
            P("dp", None),
            P("dp"),
        ),
        check_vma=False,
    )
```
